32 devices in a mesh: batch: 4 (over y, x), seq: 8 (over z, core).
Axes of the slice: x: 2, y: 2, z: 4, core: 2. Of those that a mesh axis runs over, the one named last changes fastest.
Arguments:
- latents: float32 [4, 32, 64, 320], P('batch', 'seq'), may hold values from -16 to 16
- heights: int32 [4], P('batch'), may hold values from 16 to 32, as said below
- time_vector: bfloat16 [4, 1280], P('batch'), may hold values from -6 to 6
- text_states: bfloat16 [4, 77, 768], P('batch'), may hold values from -6 to 6
- gain_in: float32 [320], replicated, may hold values from 0.25 to 1.75
- conv_first: bfloat16 [3, 3, 320, 320], replicated, may hold values from -0.109375 to 0.109375
- time_weight: bfloat16 [1280, 320], replicated, may hold values from -0.15625 to 0.15625
- gain_mid: float32 [320], replicated, may hold values from 0.25 to 1.75
- conv_second: bfloat16 [3, 3, 320, 320], replicated, may hold values from -0.109375 to 0.109375
- gain_block: float32 [320], replicated, may hold values from 0.25 to 1.75
- project_in: bfloat16 [320, 320], replicated, may hold values from -0.3125 to 0.3125
- gain_self: float32 [320], replicated, may hold values from 0.25 to 1.75
- query_self: bfloat16 [320, 320], replicated, may hold values from -0.3125 to 0.3125
- key_self: bfloat16 [320, 320], replicated, may hold values from -0.3125 to 0.3125
- value_self: bfloat16 [320, 320], replicated, may hold values from -0.3125 to 0.3125
- out_self: bfloat16 [320, 320], replicated, may hold values from -6 to 6
- gain_cross: float32 [320], replicated, may hold values from 0.25 to 1.75
- query_cross: bfloat16 [320, 320], replicated, may hold values from -0.3125 to 0.3125
- key_cross: bfloat16 [768, 320], replicated, may hold values from -0.21875 to 0.21875
- value_cross: bfloat16 [768, 320], replicated, may hold values from -0.21875 to 0.21875
- out_cross: bfloat16 [320, 320], replicated, may hold values from -4 to 4
- gain_feed: float32 [320], replicated, may hold values from 0.25 to 1.75
- feed_up: bfloat16 [320, 2560], replicated, may hold values from -0.3125 to 0.3125
- feed_down: bfloat16 [1280, 320], replicated, may hold values from -0.3125 to 0.3125
- project_out: bfloat16 [320, 320], replicated, may hold values from -0.3125 to 0.3125
- cotangent: float32 [4, 32, 64, 320], P('batch', 'seq'), may hold values from -6 to 6
Outputs:
- output: float32 [4, 32, 64, 320], P('batch', 'seq')
- latent_grad: float32 [4, 32, 64, 320], P('batch', 'seq')
- grad_gain_in: float32 [320], P('seq')
- grad_conv_first: float32 [3, 3, 320, 320], P(None, None, None, 'seq')
- grad_time_weight: float32 [1280, 320], P(None, 'seq')
- grad_gain_mid: float32 [320], P('seq')
- grad_conv_second: float32 [3, 3, 320, 320], P(None, None, None, 'seq')
- grad_gain_block: float32 [320], P('seq')
- grad_project_in: float32 [320, 320], P(None, 'seq')
- grad_gain_self: float32 [320], P('seq')
- grad_query_self: float32 [320, 320], P(None, 'seq')
- grad_key_self: float32 [320, 320], P(None, 'seq')
- grad_value_self: float32 [320, 320], P(None, 'seq')
- grad_out_self: float32 [320, 320], P(None, 'seq')
- grad_gain_cross: float32 [320], P('seq')
- grad_query_cross: float32 [320, 320], P(None, 'seq')
- grad_key_cross: float32 [768, 320], P(None, 'seq')
- grad_value_cross: float32 [768, 320], P(None, 'seq')
- grad_out_cross: float32 [320, 320], P(None, 'seq')
- grad_gain_feed: float32 [320], P('seq')
- grad_feed_up: float32 [320, 2560], P(None, 'seq')
- grad_feed_down: float32 [1280, 320], P(None, 'seq')
- grad_project_out: float32 [320, 320], P(None, 'seq')
The draws below stay inside these ranges and needn't reach their ends.
Inputs may be any that keep to these rules, and one draw needn't show every extreme that they name: `heights`: in each aligned run of two images, or of 1 images where that is more, at least one image has all 32 rows.
All inputs are finite; a program needn't handle non-finite values.
Results may differ from the reference program's by a relative error of at most 0.028.
Values may be sent and summed in bfloat16 or wider, within the bound.
A program may use at most 384 MiB of HBM per device.

```python
import math
import jax
import jax.numpy as jnp
from jax import lax

CH = 320
HEADS = 8
HEAD = 40
GROUPS = 32
CTX = 768
TXT = 77
FF = 1280
TEMB = 1280
WIDTH = 64
IMG_GROUP = 1
HMAX = 32
KEYS = 2048
IMAGES = 4


def draw_latents(key, part):
    key = jax.random.fold_in(key, 11)
    noise_key, chan_key, row_key = jax.random.split(key, 3)
    positions = jnp.arange(HMAX, dtype=jnp.float32) / max(HMAX - 1, 1)
    chan_scale = jnp.exp(jax.random.uniform(chan_key, (IMAGES, 1, 1, CH), jnp.float32, jnp.log(0.4), jnp.log(4.0)))
    rough_rows = jax.random.uniform(row_key, (IMAGES, HMAX, 1, 1), jnp.float32, 0.7, 1.4)
    base_draw = jax.random.normal(noise_key, (IMAGES, HMAX, WIDTH, CH), jnp.float32)
    row_scale = 0.6 * 3.0 ** positions
    values = base_draw * row_scale[None, :, None, None] * rough_rows * chan_scale
    return jnp.clip(values, -16.0, 16.0)


def draw_heights(key, part):
    key = jax.random.fold_in(key, 23)
    base_key, pick_key = jax.random.split(key)
    run_length = max(IMG_GROUP, 2)
    base_draw = jax.random.randint(base_key, (IMAGES,), HMAX // 2, HMAX + 1)
    picked = jax.random.randint(pick_key, (IMAGES // run_length,), 0, run_length)
    slot_index = jnp.arange(IMAGES, dtype=jnp.int32) % run_length
    full_image = slot_index == jnp.repeat(picked, run_length)
    return jnp.where(full_image, HMAX, base_draw).astype(jnp.int32)


def shard_levels(own_key, extent, shards, smallest, top_value):
    level = 1.0
    for dim, shards_of in shards:
        draws = jax.random.uniform(jax.random.fold_in(jax.random.fold_in(own_key, 6), dim), (shards_of,), jnp.float32, smallest / len(shards), top_value / len(shards))
        level = level * jnp.repeat(jnp.exp(draws), extent[dim] // shards_of).reshape((-1,) + (1,) * (len(extent) - 1 - dim))
    return level


def gaussian(own_key, dims, width, limit, pieces=(), kind=jnp.bfloat16):
    values = width * jax.random.normal(own_key, dims, jnp.float32)
    if pieces:
        values = values * shard_levels(own_key, dims, pieces, -0.22, 0.18)
    return jnp.clip(values, -limit, limit).astype(kind)


def setup_inputs(seed: int = 0) -> dict:
    key_list = jax.random.split(jax.random.key(seed), 27)
    return {
        "latents": draw_latents(jax.random.fold_in(key_list[26], 71), 0),
        "heights": draw_heights(jax.random.fold_in(key_list[26], 71), 0),
        "time_vector": gaussian(key_list[2], (IMAGES, TEMB), 1.0, 6.0, ((0, 4),)),
        "text_states": gaussian(key_list[3], (IMAGES, TXT, CTX), 1.0, 6.0, ((0, 4),)),
        "gain_in": jnp.clip(1.0 + 0.15 * jax.random.normal(key_list[4], (CH,), jnp.float32), 0.25, 1.75),
        "conv_first": gaussian(key_list[5], (3, 3, CH, CH), (9 * CH) ** -0.5, 0.109375),
        "time_weight": gaussian(key_list[6], (TEMB, CH), TEMB ** -0.5, 0.15625),
        "gain_mid": jnp.clip(1.0 + 0.15 * jax.random.normal(key_list[7], (CH,), jnp.float32), 0.25, 1.75),
        "conv_second": gaussian(key_list[8], (3, 3, CH, CH), (9 * CH) ** -0.5, 0.109375),
        "gain_block": jnp.clip(1.0 + 0.15 * jax.random.normal(key_list[9], (CH,), jnp.float32), 0.25, 1.75),
        "project_in": gaussian(key_list[10], (CH, CH), CH ** -0.5, 0.3125),
        "gain_self": jnp.clip(1.0 + 0.15 * jax.random.normal(key_list[11], (CH,), jnp.float32), 0.25, 1.75),
        "query_self": gaussian(key_list[12], (CH, CH), CH ** -0.5, 0.3125),
        "key_self": gaussian(key_list[13], (CH, CH), CH ** -0.5, 0.3125),
        "value_self": gaussian(key_list[14], (CH, CH), CH ** -0.5, 0.3125),
        "out_self": gaussian(key_list[15], (CH, CH), (0.6 * KEYS ** 0.5 * CH ** -0.5), 6.0),
        "gain_cross": jnp.clip(1.0 + 0.15 * jax.random.normal(key_list[16], (CH,), jnp.float32), 0.25, 1.75),
        "query_cross": gaussian(key_list[17], (CH, CH), CH ** -0.5, 0.3125),
        "key_cross": gaussian(key_list[18], (CTX, CH), CTX ** -0.5, 0.21875),
        "value_cross": gaussian(key_list[19], (CTX, CH), CTX ** -0.5, 0.21875),
        "out_cross": gaussian(key_list[20], (CH, CH), (0.6 * TXT ** 0.5 * CH ** -0.5), 4.0),
        "gain_feed": jnp.clip(1.0 + 0.15 * jax.random.normal(key_list[21], (CH,), jnp.float32), 0.25, 1.75),
        "feed_up": gaussian(key_list[22], (CH, 2 * FF), CH ** -0.5, 0.3125),
        "feed_down": gaussian(key_list[23], (FF, CH), (FF // 4) ** -0.5, 0.3125),
        "project_out": gaussian(key_list[24], (CH, CH), CH ** -0.5, 0.3125),
        "cotangent": gaussian(key_list[25], (IMAGES, HMAX, WIDTH, CH), 1.0, 6.0, ((0, 4), (1, 8)), jnp.float32),
    }


@jax.custom_vjp
def low(v):
    return lax.optimization_barrier(v.astype(jnp.bfloat16)).astype(jnp.float32)

@jax.custom_vjp
def low_back(v):
    return v

def low_keep(v):
    return (low(v), None)

def low_pass(kept, grad):
    return (grad,)

def back_keep(v):
    return (v, None)

def back_low(kept, grad):
    return (low(grad),)
low.defvjp(low_keep, low_pass)
low_back.defvjp(back_keep, back_low)
highest = lax.Precision.HIGHEST
epsilon = 1e-05

def matmul(left_side, right_side):
    return jnp.dot(left_side, right_side, precision=highest, preferred_element_type=jnp.float32)

def layer_norm(values, norm_gain):
    centred = values - lax.optimization_barrier(jnp.mean(values, axis=-1, keepdims=True))
    spread = lax.optimization_barrier(jnp.mean(centred * centred, axis=-1, keepdims=True))
    return centred * lax.rsqrt(spread + epsilon) * norm_gain

def group_norm(values, norm_gain, row_mask):
    grouped = values.reshape(HMAX, WIDTH, GROUPS, CH // GROUPS)
    masked = grouped * row_mask[:, None, None, None]
    cell_total = jnp.sum(row_mask) * (WIDTH * (CH // GROUPS))
    group_mean = lax.optimization_barrier(jnp.sum(masked, axis=(0, 1, 3))) / cell_total
    spread = lax.optimization_barrier(jnp.sum(masked * grouped, axis=(0, 1, 3))) / cell_total - group_mean * group_mean
    normed = (grouped - group_mean[:, None]) * lax.rsqrt(spread + epsilon)[:, None]
    return normed.reshape(HMAX, WIDTH, CH) * norm_gain

def conv_same(values, weight):
    return lax.conv_general_dilated(values[None], weight, (1, 1), ((1, 1), (1, 1)), dimension_numbers=('NHWC', 'HWIO', 'NHWC'), precision=highest, preferred_element_type=jnp.float32)[0]

def attend(queries, keys_all, values_all, key_mask):
    row_count = queries.shape[0]
    key_count = keys_all.shape[0]
    raw_scores = jnp.einsum('qhd,khd->hqk', queries.reshape(row_count, HEADS, HEAD), keys_all.reshape(key_count, HEADS, HEAD), precision=highest) * HEAD ** (-0.5)
    scores = jnp.where(key_mask[None, None, :] > 0, low_back(raw_scores), -1e+30)
    attention = jnp.exp(scores - jax.nn.logsumexp(scores, axis=-1, keepdims=True))
    attn_mixed = jnp.einsum('hqk,khd->qhd', low(attention), values_all.reshape(key_count, HEADS, HEAD), precision=highest)
    return low(low_back(attn_mixed.reshape(row_count, CH)))

def attention_blocks(queries, keys_all, values_all, key_mask):
    block_rows = math.gcd(KEYS, 512)
    blocks = queries.reshape(KEYS // block_rows, block_rows, CH)
    checked = jax.checkpoint(attend)
    result = lax.map(lambda block_part: checked(block_part, keys_all, values_all, key_mask), blocks)
    return result.reshape(KEYS, CH)

def image_forward(latents, weights, time_vector, text_states, row_mask):
    gain_in, conv_first, time_weight, gain_mid, conv_second, gain_block, project_in, gain_self, query_self, key_self, value_self, out_self, gain_cross, query_cross, key_cross, value_cross, out_cross, gain_feed, feed_up, feed_down, project_out = weights
    cell_mask = row_mask[:, None, None]
    act_in = low(jax.nn.silu(group_norm(latents, gain_in, row_mask)) * cell_mask)
    conv_out = low_back(conv_same(act_in, conv_first))
    time_term = matmul(low(jax.nn.silu(time_vector))[None, :], time_weight)[0]
    mid_in = conv_out + time_term
    act_mid = low(jax.nn.silu(group_norm(mid_in, gain_mid, row_mask)) * cell_mask)
    resid = latents + low_back(conv_same(act_mid, conv_second))
    normed_block = low(group_norm(resid, gain_block, row_mask).reshape(KEYS, CH))
    stream_in = low_back(matmul(normed_block, project_in))
    normed_self = low(layer_norm(stream_in, gain_self))
    queries = low(low_back(matmul(normed_self, query_self)))
    keys_all = low(low_back(matmul(normed_self, key_self)))
    values_all = low(low_back(matmul(normed_self, value_self)))
    key_mask = jnp.repeat(row_mask, WIDTH)
    attn_mixed = attention_blocks(queries, keys_all, values_all, key_mask)
    stream_self = stream_in + low_back(matmul(attn_mixed, out_self))
    normed_cross = low(layer_norm(stream_self, gain_cross))
    query_text = low(low_back(matmul(normed_cross, query_cross)))
    text_keys = low(matmul(text_states, key_cross))
    text_values = low(matmul(text_states, value_cross))
    text_mask = jnp.ones((TXT,), jnp.float32)
    cross_mixed = attention_blocks(query_text, text_keys, text_values, text_mask)
    stream_cross = stream_self + low_back(matmul(cross_mixed, out_cross))
    normed_feed = low(layer_norm(stream_cross, gain_feed))
    joined = low_back(matmul(normed_feed, feed_up))
    gated = joined[:, :FF] * jax.nn.gelu(joined[:, FF:], approximate=False)
    stream_feed = stream_cross + low_back(matmul(low(gated), feed_down))
    branch_out = low_back(matmul(low(stream_feed), project_out)).reshape(HMAX, WIDTH, CH)
    return (resid + branch_out) * cell_mask

def reference(latents, heights, time_vector, text_states, gain_in, conv_first, time_weight, gain_mid, conv_second, gain_block, project_in, gain_self, query_self, key_self, value_self, out_self, gain_cross, query_cross, key_cross, value_cross, out_cross, gain_feed, feed_up, feed_down, project_out, cotangent):
    weights = tuple((entry.astype(jnp.float32) for entry in (gain_in, conv_first, time_weight, gain_mid, conv_second, gain_block, project_in, gain_self, query_self, key_self, value_self, out_self, gain_cross, query_cross, key_cross, value_cross, out_cross, gain_feed, feed_up, feed_down, project_out)))

    def step_image(running, bundle):
        image_latents, image_height, image_time, image_text, image_cot = bundle
        row_mask = (jnp.arange(HMAX, dtype=jnp.int32) < image_height).astype(jnp.float32)
        time_wide = image_time.astype(jnp.float32)
        text_wide = image_text.astype(jnp.float32)

        def forward_fn(inner_latents, *inner_weights):
            return image_forward(inner_latents, inner_weights, time_wide, text_wide, row_mask)
        image_out, pull_back = jax.vjp(forward_fn, image_latents, *weights)
        grads_all = pull_back(image_cot)
        updated = tuple((first_part + second_part for first_part, second_part in zip(running, grads_all[1:])))
        return (updated, (image_out, grads_all[0]))
    initial = tuple((jnp.zeros_like(entry) for entry in weights))
    totals, (outputs, latent_grads) = lax.scan(step_image, initial, (latents, heights, time_vector, text_states, cotangent))
    return (outputs, latent_grads, totals[0], totals[1], totals[2], totals[3], totals[4], totals[5], totals[6], totals[7], totals[8], totals[9], totals[10], totals[11], totals[12], totals[13], totals[14], totals[15], totals[16], totals[17], totals[18], totals[19], totals[20])
```

```python
import jax
import jax.numpy as jnp
from jax import lax
from jax.experimental import pallas as pl
from jax.experimental.pallas import tpu as pltpu
from jax.sharding import PartitionSpec as P

HEADS = 8
HEAD = 40
GROUPS = 32


epsilon = 1e-05
layout = ("NHWC", "HWIO", "NHWC")


def extended(block, sides, width):
    for axis, dim in sides:
        count = lax.axis_size(axis)
        forward = [(i, i + 1) for i in range(count - 1)]
        backward = [(target, source) for source, target in forward]
        low = lax.ppermute(
            lax.slice_in_dim(block, block.shape[dim] - width, None, axis=dim), axis, forward
        )
        high = lax.ppermute(lax.slice_in_dim(block, 0, width, axis=dim), axis, backward)
        block = jnp.concatenate([low, block, high], axis=dim)
    return block


def layer_norm(values, norm_gain):
    centred = values - jnp.mean(values, axis=-1, keepdims=True)
    spread = jnp.mean(centred * centred, axis=-1, keepdims=True)
    return centred * lax.rsqrt(spread + epsilon) * norm_gain


def geglu(joined):
    half_width = joined.shape[-1] // 2
    return joined[:, :half_width] * jax.nn.gelu(joined[:, half_width:], approximate=False)


def back_dot(left_side, weight):
    return lax.dot_general(
        left_side, weight, (((1,), (1,)), ((), ())), preferred_element_type=jnp.float32
    )


def grad_dot(left_side, right_side):
    return lax.dot_general(
        left_side, right_side, (((0,), (0,)), ((), ())), preferred_element_type=jnp.float32
    )


def exact_grad_dot(left_side, right_side):
    return lax.dot_general(
        left_side,
        right_side,
        (((0,), (0,)), ((), ())),
        precision=lax.Precision.HIGHEST,
        preferred_element_type=jnp.float32,
    )


def conv_rows(padded, weight):
    return lax.conv_general_dilated(
        padded,
        weight,
        (1, 1),
        ((0, 0), (1, 1)),
        dimension_numbers=layout,
        preferred_element_type=jnp.float32,
    )


def conv_weight_grad(padded, grad_output):
    row_count = grad_output.shape[1]
    col_count = grad_output.shape[2]
    padded_cols = jnp.pad(padded, ((0, 0), (0, 0), (1, 1), (0, 0)))
    flat_grad = grad_output.reshape(-1, grad_output.shape[3])
    tap_rows = []
    for shift_row in range(3):
        tap_line = []
        for shift_col in range(3):
            patch_rows = padded_cols[
                :, shift_row : shift_row + row_count, shift_col : shift_col + col_count
            ].reshape(-1, padded.shape[3])
            tap_line.append(grad_dot(patch_rows, flat_grad))
        tap_rows.append(jnp.stack(tap_line))
    return jnp.stack(tap_rows)


def flipped(weight):
    return jnp.swapaxes(weight[::-1, ::-1], 2, 3)


def group_sums(values, row_mask):
    full_shape = values.shape
    grouped = values.reshape(
        full_shape[0], full_shape[1], full_shape[2], GROUPS, full_shape[3] // GROUPS
    )
    masked = grouped * row_mask[:, :, None, None, None]
    return (jnp.sum(masked, axis=(1, 2, 4)), jnp.sum(masked * grouped, axis=(1, 2, 4)))


def group_apply(values, norm_gain, sum_first, sum_second, cell_counts):
    full_shape = values.shape
    grouped = values.reshape(
        full_shape[0], full_shape[1], full_shape[2], GROUPS, full_shape[3] // GROUPS
    )
    group_mean = sum_first / cell_counts[:, None]
    spread = sum_second / cell_counts[:, None] - group_mean * group_mean
    inverse = lax.rsqrt(spread + epsilon)
    normed = (grouped - group_mean[:, None, None, :, None]) * inverse[:, None, None, :, None]
    return normed.reshape(full_shape) * norm_gain


def norm_stats(values, row_mask, spread_fn, pick_fn):
    sum_first, sum_second = group_sums(values, row_mask)
    total_first, total_second = lax.psum((spread_fn(sum_first), spread_fn(sum_second)), "seq")
    return (pick_fn(total_first), pick_fn(total_second))


def norm_back(grad_first, grad_second, spread_fn, pick_fn):
    total_first, total_second = lax.psum((spread_fn(grad_first), spread_fn(grad_second)), "seq")
    return (pick_fn(total_first), pick_fn(total_second))


def rows_halo(values):
    return extended(values, (("seq", 1),), 1)


def grads_halo(values):
    return extended(values, (("seq", 1),), 1)


def norm_backward(
    piece_fn, values, norm_gain, sum_first, sum_second, grad_output, row_mask, spread_fn, pick_fn
):
    unused, pull_piece = jax.vjp(piece_fn, values, norm_gain, sum_first, sum_second)
    grad_values, grad_gain, grad_first, grad_second = pull_piece(grad_output)
    total_first, total_second = norm_back(grad_first, grad_second, spread_fn, pick_fn)
    unused, pull_sums = jax.vjp(lambda inner_vals: group_sums(inner_vals, row_mask), values)
    extra_part = pull_sums((total_first, total_second))[0]
    return (grad_values + extra_part, grad_gain)


def masked_scores(queries, keys_all, key_mask, score_scale):
    row_count = queries.shape[0]
    key_count = keys_all.shape[0]
    raw_scores = (
        jnp.einsum(
            "qhd,khd->hqk",
            queries.reshape(row_count, HEADS, HEAD),
            keys_all.reshape(key_count, HEADS, HEAD),
            preferred_element_type=jnp.float32,
        )
        * score_scale
    )
    return jnp.where(key_mask[None, None, :] > 0, raw_scores, -1e30)


def self_forward(bundle, score_scale):
    queries, keys_all, values_all, key_mask = bundle
    row_count = queries.shape[0]
    scores = masked_scores(queries, keys_all, key_mask, score_scale)
    log_total = jax.nn.logsumexp(scores, axis=-1)
    attention = jnp.exp(scores - log_total[:, :, None]).astype(jnp.bfloat16)
    attn_mixed = jnp.einsum(
        "hqk,khd->qhd",
        attention,
        values_all.reshape(keys_all.shape[0], HEADS, HEAD),
        preferred_element_type=jnp.float32,
    )
    return (attn_mixed.astype(jnp.bfloat16).reshape(row_count, -1), log_total)


def query_side(bundle, score_scale):
    queries, grad_mixed, log_total, keys_all, values_all, key_mask = bundle
    row_count = queries.shape[0]
    key_count = keys_all.shape[0]
    scores = masked_scores(queries, keys_all, key_mask, score_scale)
    attention = jnp.exp(scores - log_total[:, :, None])
    grad_attn = jnp.einsum(
        "qhd,khd->hqk",
        grad_mixed.reshape(row_count, HEADS, HEAD),
        values_all.reshape(key_count, HEADS, HEAD),
        preferred_element_type=jnp.float32,
    )
    row_delta = jnp.sum(attention * grad_attn, axis=-1)
    grad_scores = (attention * (grad_attn - row_delta[:, :, None])).astype(jnp.bfloat16)
    grad_queries = (
        jnp.einsum(
            "hqk,khd->qhd",
            grad_scores,
            keys_all.reshape(key_count, HEADS, HEAD),
            preferred_element_type=jnp.float32,
        )
        * score_scale
    )
    return (
        grad_queries.astype(jnp.bfloat16).reshape(row_count, -1),
        attention.astype(jnp.bfloat16),
        grad_scores,
    )

LANES = 128
MESH = pl.DeviceIdType.MESH


def reduce_kernel(chunks, batches, pack_ref, out_ref, recv_core, held, recv_batch, quart, recv_z, gather, sems):
    batch = lax.axis_index("batch")
    seq = lax.axis_index("seq")
    shards = pack_ref.shape[0]
    half = shards // 2
    z_pos = seq // 2
    core = lax.rem(seq, 2)
    partner = (batch, seq + 1 - 2 * core)
    others = [lax.rem(batch + step, batches) for step in range(1, batches)]
    z_others = [lax.rem(z_pos + step, half) for step in range(1, half)]
    barrier = pltpu.get_barrier_semaphore()
    pl.semaphore_signal(barrier, inc=1, device_id=partner, device_id_type=MESH)
    for other in others:
        pl.semaphore_signal(barrier, inc=1, device_id=(other, seq), device_id_type=MESH)
    for other in z_others:
        pl.semaphore_signal(barrier, inc=1, device_id=(batch, other * 2 + core), device_id_type=MESH)
    pl.semaphore_wait(barrier, batches + half - 1)

    def copy(source, target, index, device):
        return pltpu.make_async_remote_copy(
            src_ref=source,
            dst_ref=target,
            send_sem=sems.at[0, index],
            recv_sem=sems.at[1, index],
            device_id=device,
            device_id_type=MESH,
        )

    per_chunk = half + batches - 1 + half - 1 + batches - 1
    stage_one, stage_two, stage_three, stage_four = [], [], [], []
    for number, (start, size) in enumerate(chunks):
        rows = pl.ds(start, size)
        part = size // batches
        base = number * per_chunk
        stage_one.append(
            [
                copy(
                    pack_ref.at[2 * z + 1 - core, rows],
                    recv_core.at[z, rows],
                    base + z,
                    partner,
                )
                for z in range(half)
            ]
        )
        base += half
        stage_two.append(
            [
                copy(
                    held.at[:, pl.ds(pl.multiple_of(start + other * part, 16), part)],
                    recv_batch.at[step, :, pl.ds(start // batches, part)],
                    base + step,
                    (other, seq),
                )
                for step, other in enumerate(others)
            ]
        )
        base += batches - 1
        stage_three.append(
            [
                copy(
                    quart.at[other, pl.ds(start // batches, part)],
                    recv_z.at[step, pl.ds(start // batches, part)],
                    base + step,
                    (batch, other * 2 + core),
                )
                for step, other in enumerate(z_others)
            ]
        )
        base += half - 1
        stage_four.append(
            [
                copy(
                    gather.at[batch, pl.ds(start // batches, part)],
                    gather.at[batch, pl.ds(start // batches, part)],
                    base + step,
                    (other, seq),
                )
                for step, other in enumerate(others)
            ]
        )
    for copies in stage_one:
        for one in copies:
            one.start()

    def finish_three(number):
        start, size = chunks[number]
        rows = pl.ds(start // batches, size // batches)
        for one in stage_three[number]:
            one.wait()
        total = quart[z_pos, rows].astype(jnp.float32)
        for step in range(half - 1):
            total = total + recv_z[step, rows].astype(jnp.float32)
        gather[batch, rows] = total.astype(jnp.bfloat16)
        for one in stage_four[number]:
            one.start()

    for number, (start, size) in enumerate(chunks):
        rows = pl.ds(start, size)
        for one in stage_one[number]:
            one.wait()

        @pl.loop(0, half)
        def add_core(z):
            held[z, rows] = (
                pack_ref[2 * z + core, rows].astype(jnp.float32)
                + recv_core[z, rows].astype(jnp.float32)
            ).astype(jnp.bfloat16)

        for one in stage_two[number]:
            one.start()
    for number, (start, size) in enumerate(chunks):
        part = size // batches
        for one in stage_two[number]:
            one.wait()

        @pl.loop(0, half)
        def add_batch(z):
            total = held[z, pl.ds(pl.multiple_of(start + batch * part, 16), part)].astype(jnp.float32)
            for step in range(batches - 1):
                total = total + recv_batch[step, z, pl.ds(start // batches, part)].astype(jnp.float32)
            quart[z, pl.ds(start // batches, part)] = total.astype(jnp.bfloat16)

        for one in stage_three[number]:
            one.start()
        if number:
            finish_three(number - 1)
    finish_three(len(chunks) - 1)
    for number, (start, size) in enumerate(chunks):
        part = size // batches
        for one in stage_four[number]:
            one.wait()
        for quarter in range(batches):
            out_ref[pl.ds(start + quarter * part, part)] = gather[
                quarter, pl.ds(start // batches, part)
            ].astype(jnp.float32)


def reduce_packed(pack, chunk_sizes, batches):
    shards, rows, lanes = pack.shape
    half = shards // 2
    chunks = []
    start = 0
    for size in chunk_sizes:
        chunks.append((start, size))
        start += size
    count = len(chunks) * (half + batches - 1 + half - 1 + batches - 1)
    low = jnp.bfloat16
    return pl.pallas_call(
        lambda *refs: reduce_kernel(chunks, batches, *refs),
        out_shape=jax.ShapeDtypeStruct((rows, lanes), jnp.float32),
        in_specs=[pl.BlockSpec(memory_space=pltpu.VMEM)],
        out_specs=pl.BlockSpec(memory_space=pltpu.VMEM),
        scratch_shapes=[
            pltpu.VMEM((half, rows, lanes), low),
            pltpu.VMEM((half, rows, lanes), low),
            pltpu.VMEM((batches - 1, half, rows // batches, lanes), low),
            pltpu.VMEM((half, rows // batches, lanes), low),
            pltpu.VMEM((half - 1, rows // batches, lanes), low),
            pltpu.VMEM((batches, rows // batches, lanes), low),
            pltpu.SemaphoreType.DMA((2, count)),
        ],
        compiler_params=pltpu.CompilerParams(
            collective_id=5, has_side_effects=True, vmem_limit_bytes=56 << 20
        ),
    )(pack)


def slots(blocks, rows):
    parts = []
    for block in blocks:
        low = block.astype(jnp.bfloat16)
        parts.append(jnp.pad(low, ((0, rows - low.shape[0]), (0, 0))).reshape(rows, HEADS, HEAD))
    stacked = jnp.concatenate(parts, axis=2)
    stacked = jnp.pad(stacked, ((0, 0), (0, 0), (0, LANES - stacked.shape[2])))
    return jnp.swapaxes(stacked, 0, 1)


def slot(block, number):
    return block[:, number * HEAD : (number + 1) * HEAD]


def reduce_grads(grads, batches):
    (
        gain_in, conv_first, time_weight, gain_mid, conv_second, gain_block, project_in, gain_self,
        query_self, key_self, value_self, out_self, gain_cross, query_cross, key_cross,
        value_cross, out_cross, gain_feed, feed_up, feed_down, project_out,
    ) = grads
    channels = project_in.shape[0]
    gains = jnp.stack((gain_in, gain_mid, gain_block, gain_self, gain_cross, gain_feed))
    first = conv_first.reshape(3, 3 * channels, channels)
    second = conv_second.reshape(3, 3 * channels, channels)
    hidden = feed_down.shape[0]
    up_cols = feed_up.shape[1] // HEADS
    up_wide = -(-up_cols // LANES) * LANES
    up_low = jnp.pad(
        feed_up.astype(jnp.bfloat16).reshape(channels, HEADS, up_cols),
        ((0, 0), (0, 0), (0, up_wide - up_cols)),
    ).reshape(channels, HEADS, up_wide // LANES, LANES)
    up_pack = jnp.transpose(up_low, (1, 2, 0, 3)).reshape(HEADS, -1, LANES)
    long_rows = time_weight.shape[0]
    down_rows = 512
    packs = [
        up_pack,
        slots([feed_down[:down_rows], feed_down[down_rows : 2 * down_rows], feed_down[2 * down_rows :]], down_rows),
        slots([project_out, out_cross, query_cross], channels),
        slots([out_self, project_in, gains], channels + 64),
        slots([query_self, key_self, value_self], channels),
        slots([time_weight, key_cross, value_cross], long_rows),
        slots([second[0], second[1], second[2]], 3 * channels),
        slots([first[0], first[1], first[2]], 3 * channels),
    ]
    sizes = [part.shape[1] for part in packs]
    total = reduce_packed(jnp.concatenate(packs, axis=1), sizes, batches)
    pieces = []
    start = 0
    for size in sizes:
        pieces.append(total[start : start + size])
        start += size
    up, down, trio, pair, heads, longs, second, first = pieces
    up = jnp.swapaxes(up.reshape(-1, channels, LANES), 0, 1).reshape(channels, -1)[:, :up_cols]
    down = jnp.concatenate([slot(down, 0), slot(down, 1), slot(down, 2)])[:hidden]
    small = slot(pair, 2)

    def conv(piece):
        return jnp.stack([slot(piece, shift).reshape(3, channels, HEAD) for shift in range(3)])

    context = key_cross.shape[0]
    return (
        small[0], conv(first), slot(longs, 0), small[1], conv(second), small[2],
        slot(pair, 1)[:channels], small[3], slot(heads, 0), slot(heads, 1), slot(heads, 2),
        slot(pair, 0)[:channels], small[4], slot(trio, 2), slot(longs, 1)[:context],
        slot(longs, 2)[:context], slot(trio, 1), small[5], up, down, slot(trio, 0),
    )


def on_device(
    latents,
    heights,
    time_vector,
    text_states,
    gain_in,
    conv_first,
    time_weight,
    gain_mid,
    conv_second,
    gain_block,
    project_in,
    gain_self,
    query_self,
    key_self,
    value_self,
    out_self,
    gain_cross,
    query_cross,
    key_cross,
    value_cross,
    out_cross,
    gain_feed,
    feed_up,
    feed_down,
    project_out,
    cotangent,
):
    images_in, rows_in, col_count, channels = latents.shape
    seq_size = lax.axis_size("seq")
    seq_index = lax.axis_index("seq")
    block_rows = rows_in * col_count
    keys_count = block_rows * seq_size
    score_scale = HEAD ** (-0.5)
    row_ids = seq_index * rows_in + jnp.arange(rows_in, dtype=jnp.int32)

    def spread_fn(values):
        return values

    def pick_fn(values):
        return values

    images, row_count = (latents.shape[0], latents.shape[1])
    tok_rows = row_count * col_count
    tokens = images * tok_rows
    row_valid = (row_ids[None, :] < heights[:, None]).astype(jnp.int32)
    row_mask = row_valid.astype(jnp.float32)
    cell_mask = row_mask[:, :, None, None]
    key_rows = jnp.arange(keys_count, dtype=jnp.int32) // col_count
    key_mask = (key_rows[None, :] < heights[:, None]).astype(jnp.int32)
    cell_counts = (heights * (col_count * (channels // GROUPS))).astype(jnp.float32)

    def res_piece(values, norm_gain, sum_first, sum_second):
        return (
            jax.nn.silu(group_apply(values, norm_gain, sum_first, sum_second, cell_counts))
            * cell_mask
        )

    def block_piece(values, norm_gain, sum_first, sum_second):
        return group_apply(values, norm_gain, sum_first, sum_second, cell_counts)

    first_in, second_in = norm_stats(latents, row_mask, spread_fn, pick_fn)
    act_in = res_piece(latents, gain_in, first_in, second_in).astype(jnp.bfloat16)
    padded_in = rows_halo(act_in)
    conv_out = conv_rows(padded_in, conv_first)
    time_act = jax.nn.silu(time_vector.astype(jnp.float32)).astype(jnp.bfloat16)
    time_term = jnp.dot(time_act, time_weight, preferred_element_type=jnp.float32)
    mid_in = conv_out + time_term[:, None, None, :]
    first_mid, second_mid = norm_stats(mid_in, row_mask, spread_fn, pick_fn)
    act_mid = res_piece(mid_in, gain_mid, first_mid, second_mid).astype(jnp.bfloat16)
    padded_mid = rows_halo(act_mid)
    resid = latents + conv_rows(padded_mid, conv_second)
    first_block, second_block = norm_stats(resid, row_mask, spread_fn, pick_fn)
    normed_block = (
        block_piece(resid, gain_block, first_block, second_block)
        .reshape(tokens, channels)
        .astype(jnp.bfloat16)
    )
    stream_in = jnp.dot(normed_block, project_in, preferred_element_type=jnp.float32)
    normed_self = layer_norm(stream_in, gain_self).astype(jnp.bfloat16)
    joined_self = jnp.concatenate((query_self, key_self, value_self), axis=1)
    projected = (
        jnp.dot(normed_self, joined_self, preferred_element_type=jnp.float32)
        .astype(jnp.bfloat16)
        .reshape(images, tok_rows, 3 * channels)
    )
    queries = projected[:, :, :channels]
    keys_local = projected[:, :, channels : 2 * channels]
    values_local = projected[:, :, 2 * channels :]
    keys_all = lax.all_gather(keys_local, "seq", axis=1, tiled=True)
    values_all = lax.all_gather(values_local, "seq", axis=1, tiled=True)

    def forward_image(bundle):
        image_queries, image_keys, image_values, image_mask = bundle
        query_blocks = image_queries.reshape(-1, block_rows, channels)
        return lax.map(
            lambda part: self_forward((part, image_keys, image_values, image_mask), score_scale),
            query_blocks,
        )

    attn_mixed, log_totals = lax.map(forward_image, (queries, keys_all, values_all, key_mask))
    mixed_flat = attn_mixed.reshape(tokens, channels)
    stream_self = stream_in + jnp.dot(mixed_flat, out_self, preferred_element_type=jnp.float32)
    normed_cross = layer_norm(stream_self, gain_cross).astype(jnp.bfloat16)
    query_text = (
        jnp.dot(normed_cross, query_cross, preferred_element_type=jnp.float32)
        .astype(jnp.bfloat16)
        .reshape(images, tok_rows, HEADS, HEAD)
    )
    text_flat = text_states.reshape(-1, text_states.shape[2])
    text_pairs = (
        jnp.dot(
            text_flat,
            jnp.concatenate((key_cross, value_cross), axis=1),
            preferred_element_type=jnp.float32,
        )
        .astype(jnp.bfloat16)
        .reshape(images, -1, 2, HEADS, HEAD)
    )
    text_keys = text_pairs[:, :, 0]
    text_values = text_pairs[:, :, 1]
    cross_scores = (
        jnp.einsum("iqhd,ikhd->ihqk", query_text, text_keys, preferred_element_type=jnp.float32)
        * score_scale
    )
    cross_attn = jnp.exp(cross_scores - jax.nn.logsumexp(cross_scores, axis=-1, keepdims=True))
    cross_low = cross_attn.astype(jnp.bfloat16)
    cross_mixed = (
        jnp.einsum("ihqk,ikhd->iqhd", cross_low, text_values, preferred_element_type=jnp.float32)
        .astype(jnp.bfloat16)
        .reshape(tokens, channels)
    )
    stream_cross = stream_self + jnp.dot(cross_mixed, out_cross, preferred_element_type=jnp.float32)
    normed_feed = layer_norm(stream_cross, gain_feed).astype(jnp.bfloat16)
    joined_feed = jnp.dot(normed_feed, feed_up, preferred_element_type=jnp.float32)
    gated = geglu(joined_feed).astype(jnp.bfloat16)
    stream_feed = stream_cross + jnp.dot(gated, feed_down, preferred_element_type=jnp.float32)
    stream_low = stream_feed.astype(jnp.bfloat16)
    branch_out = jnp.dot(stream_low, project_out, preferred_element_type=jnp.float32).reshape(
        images, row_count, col_count, channels
    )
    output = (resid + branch_out) * cell_mask
    grad_output = cotangent * cell_mask
    grad_branch = grad_output.reshape(tokens, channels).astype(jnp.bfloat16)
    grad_project_out = grad_dot(stream_low, grad_branch)
    grad_stream = back_dot(grad_branch, project_out)
    grad_feed_low = grad_stream.astype(jnp.bfloat16)
    grad_feed_down = grad_dot(gated, grad_feed_low)
    grad_gated = back_dot(grad_feed_low, feed_down)
    unused, pull_geglu = jax.vjp(geglu, joined_feed)
    grad_joined = pull_geglu(grad_gated)[0].astype(jnp.bfloat16)
    grad_feed_up = grad_dot(normed_feed, grad_joined)
    unused, pull_norm = jax.vjp(layer_norm, stream_cross, gain_feed)
    grad_part, grad_gain_feed = pull_norm(back_dot(grad_joined, feed_up))
    grad_stream = grad_stream + grad_part
    grad_cross_low = grad_stream.astype(jnp.bfloat16)
    grad_out_cross = grad_dot(cross_mixed, grad_cross_low)
    grad_cross_mixed = (
        back_dot(grad_cross_low, out_cross)
        .astype(jnp.bfloat16)
        .reshape(images, tok_rows, HEADS, HEAD)
    )
    grad_text_values = jnp.einsum(
        "ihqk,iqhd->ikhd", cross_low, grad_cross_mixed, preferred_element_type=jnp.float32
    )
    grad_cross_attn = jnp.einsum(
        "iqhd,ikhd->ihqk", grad_cross_mixed, text_values, preferred_element_type=jnp.float32
    )
    cross_delta = jnp.sum(cross_attn * grad_cross_attn, axis=-1, keepdims=True)
    grad_cross_scores = (cross_attn * (grad_cross_attn - cross_delta)).astype(jnp.bfloat16)
    grad_query_text = (
        (
            jnp.einsum(
                "ihqk,ikhd->iqhd", grad_cross_scores, text_keys, preferred_element_type=jnp.float32
            )
            * score_scale
        )
        .astype(jnp.bfloat16)
        .reshape(tokens, channels)
    )
    grad_text_keys = (
        jnp.einsum(
            "ihqk,iqhd->ikhd", grad_cross_scores, query_text, preferred_element_type=jnp.float32
        )
        * score_scale
    )
    text_wide = text_flat.astype(jnp.float32)
    grad_key_cross = exact_grad_dot(text_wide, grad_text_keys.reshape(-1, channels))
    grad_value_cross = exact_grad_dot(text_wide, grad_text_values.reshape(-1, channels))
    grad_query_cross = grad_dot(normed_cross, grad_query_text)
    unused, pull_norm = jax.vjp(layer_norm, stream_self, gain_cross)
    grad_part, grad_gain_cross = pull_norm(back_dot(grad_query_text, query_cross))
    grad_stream = grad_stream + grad_part
    grad_self_low = grad_stream.astype(jnp.bfloat16)
    grad_out_self = grad_dot(mixed_flat, grad_self_low)
    grad_mixed = (
        back_dot(grad_self_low, out_self).astype(jnp.bfloat16).reshape(images, tok_rows, channels)
    )

    def backward_image(bundle):
        image_queries, image_grads, image_totals, image_keys, image_values, image_mask = bundle
        query_blocks = image_queries.reshape(-1, block_rows, channels)
        grad_blocks = image_grads.reshape(-1, block_rows, channels)
        return lax.map(
            lambda part: query_side(
                (part[0], part[1], part[2], image_keys, image_values, image_mask), score_scale
            ),
            (query_blocks, grad_blocks, image_totals),
        )

    grad_queries, kept_attn, kept_grads = lax.map(
        backward_image, (queries, grad_mixed, log_totals, keys_all, values_all, key_mask)
    )
    grads_four = grad_mixed.reshape(images, -1, block_rows, HEADS, HEAD)
    queries_four = queries.reshape(images, -1, block_rows, HEADS, HEAD)
    row_total = tok_rows * lax.axis_size("seq")
    value_terms = jnp.einsum(
        "inhqk,inqhd->kihd", kept_attn, grads_four, preferred_element_type=jnp.float32
    )
    key_terms_part = (
        jnp.einsum(
            "inhqk,inqhd->kihd", kept_grads, queries_four, preferred_element_type=jnp.float32
        )
        * score_scale
    )
    summed = lax.psum_scatter(
        jnp.stack(
            (
                key_terms_part.reshape(row_total, images, -1),
                value_terms.reshape(row_total, images, -1),
            ),
            2,
        ).astype(jnp.bfloat16),
        "seq",
        scatter_dimension=0,
        tiled=True,
    ).astype(jnp.float32)
    grad_keys = jnp.swapaxes(summed[:, :, 0], 0, 1)
    grad_values = jnp.swapaxes(summed[:, :, 1], 0, 1)
    grad_projected = jnp.concatenate(
        (
            grad_queries.reshape(images, tok_rows, channels),
            grad_keys.astype(jnp.bfloat16),
            grad_values.astype(jnp.bfloat16),
        ),
        axis=2,
    ).reshape(tokens, 3 * channels)
    grad_joined_self = grad_dot(normed_self, grad_projected)
    unused, pull_norm = jax.vjp(layer_norm, stream_in, gain_self)
    grad_part, grad_gain_self = pull_norm(back_dot(grad_projected, joined_self))
    grad_stream = grad_stream + grad_part
    grad_stream_low = grad_stream.astype(jnp.bfloat16)
    grad_project_in = grad_dot(normed_block, grad_stream_low)
    grad_block = back_dot(grad_stream_low, project_in).reshape(
        images, row_count, col_count, channels
    )
    grad_resid_part, grad_gain_block = norm_backward(
        block_piece,
        resid,
        gain_block,
        first_block,
        second_block,
        grad_block,
        row_mask,
        spread_fn,
        pick_fn,
    )
    grad_resid = grad_output + grad_resid_part
    grad_second_low = grad_resid.astype(jnp.bfloat16)
    grad_conv_second = conv_weight_grad(padded_mid, grad_second_low)
    grad_act_mid = conv_rows(grads_halo(grad_second_low), flipped(conv_second))
    grad_mid, grad_gain_mid = norm_backward(
        res_piece,
        mid_in,
        gain_mid,
        first_mid,
        second_mid,
        grad_act_mid,
        row_mask,
        spread_fn,
        pick_fn,
    )
    grad_time = jnp.sum(grad_mid, axis=(1, 2))
    grad_time_weight = exact_grad_dot(time_act.astype(jnp.float32), grad_time)
    grad_first_low = grad_mid.astype(jnp.bfloat16)
    grad_conv_first = conv_weight_grad(padded_in, grad_first_low)
    grad_act_in = conv_rows(grads_halo(grad_first_low), flipped(conv_first))
    grad_in_part, grad_gain_in = norm_backward(
        res_piece, latents, gain_in, first_in, second_in, grad_act_in, row_mask, spread_fn, pick_fn
    )
    latent_grad = grad_resid + grad_in_part
    if seq_size == HEADS:
        grads = reduce_grads(
            (
                grad_gain_in, grad_conv_first, grad_time_weight, grad_gain_mid, grad_conv_second,
                grad_gain_block, grad_project_in, grad_gain_self,
                grad_joined_self[:, :channels], grad_joined_self[:, channels : 2 * channels],
                grad_joined_self[:, 2 * channels :], grad_out_self, grad_gain_cross,
                grad_query_cross, grad_key_cross, grad_value_cross, grad_out_cross,
                grad_gain_feed, grad_feed_up, grad_feed_down, grad_project_out,
            ),
            lax.axis_size("batch"),
        )
        return (output, latent_grad) + grads
    shares = (
        lax.psum_scatter(
            grad_gain_in.reshape(1, -1).astype(jnp.bfloat16), "seq", scatter_dimension=1, tiled=True
        ).astype(jnp.float32),
        lax.psum_scatter(
            grad_conv_first.reshape(-1, channels).astype(jnp.bfloat16),
            "seq",
            scatter_dimension=1,
            tiled=True,
        ).astype(jnp.float32),
        lax.psum_scatter(
            grad_time_weight.astype(jnp.bfloat16), "seq", scatter_dimension=1, tiled=True
        ).astype(jnp.float32),
        lax.psum_scatter(
            grad_gain_mid.reshape(1, -1).astype(jnp.bfloat16),
            "seq",
            scatter_dimension=1,
            tiled=True,
        ).astype(jnp.float32),
        lax.psum_scatter(
            grad_conv_second.reshape(-1, channels).astype(jnp.bfloat16),
            "seq",
            scatter_dimension=1,
            tiled=True,
        ).astype(jnp.float32),
        lax.psum_scatter(
            grad_gain_block.reshape(1, -1).astype(jnp.bfloat16),
            "seq",
            scatter_dimension=1,
            tiled=True,
        ).astype(jnp.float32),
        lax.psum_scatter(
            grad_project_in.astype(jnp.bfloat16), "seq", scatter_dimension=1, tiled=True
        ).astype(jnp.float32),
        lax.psum_scatter(
            grad_gain_self.reshape(1, -1).astype(jnp.bfloat16),
            "seq",
            scatter_dimension=1,
            tiled=True,
        ).astype(jnp.float32),
        lax.psum_scatter(
            grad_joined_self[:, :channels].astype(jnp.bfloat16),
            "seq",
            scatter_dimension=1,
            tiled=True,
        ).astype(jnp.float32),
        lax.psum_scatter(
            grad_joined_self[:, channels : 2 * channels].astype(jnp.bfloat16),
            "seq",
            scatter_dimension=1,
            tiled=True,
        ).astype(jnp.float32),
        lax.psum_scatter(
            grad_joined_self[:, 2 * channels :].astype(jnp.bfloat16),
            "seq",
            scatter_dimension=1,
            tiled=True,
        ).astype(jnp.float32),
        lax.psum_scatter(
            grad_out_self.astype(jnp.bfloat16), "seq", scatter_dimension=1, tiled=True
        ).astype(jnp.float32),
        lax.psum_scatter(
            grad_gain_cross.reshape(1, -1).astype(jnp.bfloat16),
            "seq",
            scatter_dimension=1,
            tiled=True,
        ).astype(jnp.float32),
        lax.psum_scatter(
            grad_query_cross.astype(jnp.bfloat16), "seq", scatter_dimension=1, tiled=True
        ).astype(jnp.float32),
        lax.psum_scatter(
            grad_key_cross.astype(jnp.bfloat16), "seq", scatter_dimension=1, tiled=True
        ).astype(jnp.float32),
        lax.psum_scatter(
            grad_value_cross.astype(jnp.bfloat16), "seq", scatter_dimension=1, tiled=True
        ).astype(jnp.float32),
        lax.psum_scatter(
            grad_out_cross.astype(jnp.bfloat16), "seq", scatter_dimension=1, tiled=True
        ).astype(jnp.float32),
        lax.psum_scatter(
            grad_gain_feed.reshape(1, -1).astype(jnp.bfloat16),
            "seq",
            scatter_dimension=1,
            tiled=True,
        ).astype(jnp.float32),
        lax.psum_scatter(
            grad_feed_up.astype(jnp.bfloat16), "seq", scatter_dimension=1, tiled=True
        ).astype(jnp.float32),
        lax.psum_scatter(
            grad_feed_down.astype(jnp.bfloat16), "seq", scatter_dimension=1, tiled=True
        ).astype(jnp.float32),
        lax.psum_scatter(
            grad_project_out.astype(jnp.bfloat16), "seq", scatter_dimension=1, tiled=True
        ).astype(jnp.float32),
    )
    totals = (
        lax.psum(shares[0].astype(jnp.bfloat16), "batch").astype(jnp.float32),
        lax.psum(shares[1].astype(jnp.bfloat16), "batch").astype(jnp.float32),
        lax.psum(shares[2].astype(jnp.bfloat16), "batch").astype(jnp.float32),
        lax.psum(shares[3].astype(jnp.bfloat16), "batch").astype(jnp.float32),
        lax.psum(shares[4].astype(jnp.bfloat16), "batch").astype(jnp.float32),
        lax.psum(shares[5].astype(jnp.bfloat16), "batch").astype(jnp.float32),
        lax.psum(shares[6].astype(jnp.bfloat16), "batch").astype(jnp.float32),
        lax.psum(shares[7].astype(jnp.bfloat16), "batch").astype(jnp.float32),
        lax.psum(shares[8].astype(jnp.bfloat16), "batch").astype(jnp.float32),
        lax.psum(shares[9].astype(jnp.bfloat16), "batch").astype(jnp.float32),
        lax.psum(shares[10].astype(jnp.bfloat16), "batch").astype(jnp.float32),
        lax.psum(shares[11].astype(jnp.bfloat16), "batch").astype(jnp.float32),
        lax.psum(shares[12].astype(jnp.bfloat16), "batch").astype(jnp.float32),
        lax.psum(shares[13].astype(jnp.bfloat16), "batch").astype(jnp.float32),
        lax.psum(shares[14].astype(jnp.bfloat16), "batch").astype(jnp.float32),
        lax.psum(shares[15].astype(jnp.bfloat16), "batch").astype(jnp.float32),
        lax.psum(shares[16].astype(jnp.bfloat16), "batch").astype(jnp.float32),
        lax.psum(shares[17].astype(jnp.bfloat16), "batch").astype(jnp.float32),
        lax.psum(shares[18].astype(jnp.bfloat16), "batch").astype(jnp.float32),
        lax.psum(shares[19].astype(jnp.bfloat16), "batch").astype(jnp.float32),
        lax.psum(shares[20].astype(jnp.bfloat16), "batch").astype(jnp.float32),
    )
    return (
        output,
        latent_grad,
        totals[0].reshape(-1),
        totals[1].reshape(3, 3, channels, -1),
        totals[2],
        totals[3].reshape(-1),
        totals[4].reshape(3, 3, channels, -1),
        totals[5].reshape(-1),
        totals[6],
        totals[7].reshape(-1),
        totals[8],
        totals[9],
        totals[10],
        totals[11],
        totals[12].reshape(-1),
        totals[13],
        totals[14],
        totals[15],
        totals[16],
        totals[17].reshape(-1),
        totals[18],
        totals[19],
        totals[20],
    )


def solution(mesh):
    in_specs = (
        P("batch", "seq", None, None),
        P("batch"),
        P("batch", None),
        P("batch", None, None),
        P(),
        P(),
        P(),
        P(),
        P(),
        P(),
        P(),
        P(),
        P(),
        P(),
        P(),
        P(),
        P(),
        P(),
        P(),
        P(),
        P(),
        P(),
        P(),
        P(),
        P(),
        P("batch", "seq", None, None),
    )
    out_specs = (
        P("batch", "seq", None, None),
        P("batch", "seq", None, None),
        P("seq"),
        P(None, None, None, "seq"),
        P(None, "seq"),
        P("seq"),
        P(None, None, None, "seq"),
        P("seq"),
        P(None, "seq"),
        P("seq"),
        P(None, "seq"),
        P(None, "seq"),
        P(None, "seq"),
        P(None, "seq"),
        P("seq"),
        P(None, "seq"),
        P(None, "seq"),
        P(None, "seq"),
        P(None, "seq"),
        P("seq"),
        P(None, "seq"),
        P(None, "seq"),
        P(None, "seq"),
    )
    return jax.shard_map(
        on_device, mesh=mesh, in_specs=in_specs, out_specs=out_specs, check_vma=False
    )
```

```python
import types
import typing

import jax
import jax.numpy as jnp
from jax import lax
from jax.experimental import pallas as pl
from jax.experimental.pallas import tpu as pltpu
from jax.sharding import PartitionSpec as P

BATCH, SEQ = "batch", "seq"
HEADS = 8
HEAD = 40
GROUPS = 32


epsilon = 1e-05
layout = ("NHWC", "HWIO", "NHWC")


def extended(block, sides, width):
    for axis, dim in sides:
        count = lax.axis_size(axis)
        forward = [(i, i + 1) for i in range(count - 1)]
        backward = [(target, source) for source, target in forward]
        low = lax.ppermute(
            lax.slice_in_dim(block, block.shape[dim] - width, None, axis=dim), axis, forward
        )
        high = lax.ppermute(lax.slice_in_dim(block, 0, width, axis=dim), axis, backward)
        block = jnp.concatenate([low, block, high], axis=dim)
    return block


def layer_norm(values, norm_gain):
    centred = values - jnp.mean(values, axis=-1, keepdims=True)
    spread = jnp.mean(centred * centred, axis=-1, keepdims=True)
    return centred * lax.rsqrt(spread + epsilon) * norm_gain


def geglu(joined):
    half_width = joined.shape[-1] // 2
    return joined[:, :half_width] * jax.nn.gelu(joined[:, half_width:], approximate=False)


def back_dot(left_side, weight):
    return lax.dot_general(
        left_side, weight, (((1,), (1,)), ((), ())), preferred_element_type=jnp.float32
    )


def grad_dot(left_side, right_side):
    return lax.dot_general(
        left_side, right_side, (((0,), (0,)), ((), ())), preferred_element_type=jnp.float32
    )


def exact_grad_dot(left_side, right_side):
    return lax.dot_general(
        left_side,
        right_side,
        (((0,), (0,)), ((), ())),
        precision=lax.Precision.HIGHEST,
        preferred_element_type=jnp.float32,
    )


def conv_rows(padded, weight):
    return lax.conv_general_dilated(
        padded,
        weight,
        (1, 1),
        ((0, 0), (1, 1)),
        dimension_numbers=layout,
        preferred_element_type=jnp.float32,
    )


def conv_weight_grad(padded, grad_output):
    row_count = grad_output.shape[1]
    col_count = grad_output.shape[2]
    padded_cols = jnp.pad(padded, ((0, 0), (0, 0), (1, 1), (0, 0)))
    flat_grad = grad_output.reshape(-1, grad_output.shape[3])
    tap_rows = []
    for shift_row in range(3):
        tap_line = []
        for shift_col in range(3):
            patch_rows = padded_cols[
                :, shift_row : shift_row + row_count, shift_col : shift_col + col_count
            ].reshape(-1, padded.shape[3])
            tap_line.append(grad_dot(patch_rows, flat_grad))
        tap_rows.append(jnp.stack(tap_line))
    return jnp.stack(tap_rows)


def flipped(weight):
    return jnp.swapaxes(weight[::-1, ::-1], 2, 3)


def group_sums(values, row_mask):
    full_shape = values.shape
    grouped = values.reshape(
        full_shape[0], full_shape[1], full_shape[2], GROUPS, full_shape[3] // GROUPS
    )
    masked = grouped * row_mask[:, :, None, None, None]
    return (jnp.sum(masked, axis=(1, 2, 4)), jnp.sum(masked * grouped, axis=(1, 2, 4)))


def group_apply(values, norm_gain, sum_first, sum_second, cell_counts):
    full_shape = values.shape
    grouped = values.reshape(
        full_shape[0], full_shape[1], full_shape[2], GROUPS, full_shape[3] // GROUPS
    )
    group_mean = sum_first / cell_counts[:, None]
    spread = sum_second / cell_counts[:, None] - group_mean * group_mean
    inverse = lax.rsqrt(spread + epsilon)
    normed = (grouped - group_mean[:, None, None, :, None]) * inverse[:, None, None, :, None]
    return normed.reshape(full_shape) * norm_gain


def norm_stats(values, row_mask, spread_fn, pick_fn):
    sum_first, sum_second = group_sums(values, row_mask)
    total_first, total_second = lax.psum((spread_fn(sum_first), spread_fn(sum_second)), SEQ)
    return (pick_fn(total_first), pick_fn(total_second))


def norm_back(grad_first, grad_second, spread_fn, pick_fn):
    total_first, total_second = lax.psum((spread_fn(grad_first), spread_fn(grad_second)), SEQ)
    return (pick_fn(total_first), pick_fn(total_second))


def rows_halo(values):
    return extended(values, ((SEQ, 1),), 1)


def grads_halo(values):
    return extended(values, ((SEQ, 1),), 1)


def norm_backward(
    piece_fn, values, norm_gain, sum_first, sum_second, grad_output, row_mask, spread_fn, pick_fn
):
    unused, pull_piece = jax.vjp(piece_fn, values, norm_gain, sum_first, sum_second)
    grad_values, grad_gain, grad_first, grad_second = pull_piece(grad_output)
    total_first, total_second = norm_back(grad_first, grad_second, spread_fn, pick_fn)
    unused, pull_sums = jax.vjp(lambda inner_vals: group_sums(inner_vals, row_mask), values)
    extra_part = pull_sums((total_first, total_second))[0]
    return (grad_values + extra_part, grad_gain)


def masked_scores(queries, keys_all, key_mask, score_scale):
    row_count = queries.shape[0]
    key_count = keys_all.shape[0]
    raw_scores = (
        jnp.einsum(
            "qhd,khd->hqk",
            queries.reshape(row_count, HEADS, HEAD),
            keys_all.reshape(key_count, HEADS, HEAD),
            preferred_element_type=jnp.float32,
        )
        * score_scale
    )
    return jnp.where(key_mask[None, None, :] > 0, raw_scores, -1e30)


def self_forward(bundle, score_scale):
    queries, keys_all, values_all, key_mask = bundle
    row_count = queries.shape[0]
    scores = masked_scores(queries, keys_all, key_mask, score_scale)
    log_total = jax.nn.logsumexp(scores, axis=-1)
    attention = jnp.exp(scores - log_total[:, :, None]).astype(jnp.bfloat16)
    attn_mixed = jnp.einsum(
        "hqk,khd->qhd",
        attention,
        values_all.reshape(keys_all.shape[0], HEADS, HEAD),
        preferred_element_type=jnp.float32,
    )
    return (attn_mixed.astype(jnp.bfloat16).reshape(row_count, -1), log_total)


def query_side(bundle, score_scale):
    queries, grad_mixed, log_total, keys_all, values_all, key_mask = bundle
    row_count = queries.shape[0]
    key_count = keys_all.shape[0]
    scores = masked_scores(queries, keys_all, key_mask, score_scale)
    attention = jnp.exp(scores - log_total[:, :, None])
    grad_attn = jnp.einsum(
        "qhd,khd->hqk",
        grad_mixed.reshape(row_count, HEADS, HEAD),
        values_all.reshape(key_count, HEADS, HEAD),
        preferred_element_type=jnp.float32,
    )
    row_delta = jnp.sum(attention * grad_attn, axis=-1)
    grad_scores = (attention * (grad_attn - row_delta[:, :, None])).astype(jnp.bfloat16)
    grad_queries = (
        jnp.einsum(
            "hqk,khd->qhd",
            grad_scores,
            keys_all.reshape(key_count, HEADS, HEAD),
            preferred_element_type=jnp.float32,
        )
        * score_scale
    )
    return (
        grad_queries.astype(jnp.bfloat16).reshape(row_count, -1),
        attention.astype(jnp.bfloat16),
        grad_scores,
    )


LANES = 128
MESH = pl.DeviceIdType.MESH
LOW = jnp.bfloat16
F32 = jnp.float32
TILE = 64


def dot_nn(left, right):
    return jnp.dot(left, right, preferred_element_type=F32)


def dot_nt(left, right):
    return lax.dot_general(left, right, (((1,), (1,)), ((), ())), preferred_element_type=F32)


def dot_tn(left, right):
    return lax.dot_general(left, right, (((0,), (0,)), ((), ())), preferred_element_type=F32)


def iota(shape, dim):
    return lax.broadcasted_iota(jnp.int32, shape, dim)


def floor_div(values, by):
    return jnp.floor((values.astype(F32) + 0.5) * (1.0 / by)).astype(jnp.int32)


def split_three(values):
    high = values.astype(LOW).astype(F32)
    rest = values - high
    middle = rest.astype(LOW).astype(F32)
    return jnp.concatenate([high, middle, rest - middle], axis=0).astype(LOW)


def sum_three(values):
    rows = values.shape[0] // 3
    return values[:rows] + values[rows : 2 * rows] + values[2 * rows :]


def row_of(ref):
    return ref[...].reshape(1, -1)


def sigmoid(values):
    return 1.0 / (1.0 + jnp.exp(-values))


def col_sum(values):
    return jnp.sum(values, axis=0, keepdims=True)


ROUNDS = 6


class Packs(typing.NamedTuple):
    up: typing.Any
    down: typing.Any
    trio: typing.Any
    pair: typing.Any
    heads: typing.Any
    second: typing.Any
    first: typing.Any


class Sizes:
    def __init__(self, mesh_batch, mesh_seq, latents, time_vector, text_states, feed_down):
        self.batches = mesh_batch
        self.seqs = mesh_seq
        self.rows = latents.shape[1]
        self.width = latents.shape[2]
        self.channels = latents.shape[3]
        self.tokens = self.rows * self.width
        self.wide = self.tokens + 2 * self.width
        self.keys = self.tokens * mesh_seq
        self.emb = time_vector.shape[1]
        self.text = text_states.shape[1]
        self.text_pad = -(-self.text // 16) * 16
        self.context = text_states.shape[2]
        self.hidden = feed_down.shape[0]
        self.slot = 48
        self.packed = HEADS * LANES
        self.down_rows = 512
        channels = self.channels
        sizes = Packs(
            up=3 * channels,
            down=self.down_rows,
            trio=channels,
            pair=HEADS * self.slot,
            heads=channels,
            second=3 * channels,
            first=3 * channels,
        )
        starts = [sum(sizes[:place]) for place in range(len(sizes))]
        self.start = Packs(*starts)
        self.pack_rows = sum(sizes)
        self.sizes = sizes
        self.chunks = [
            (0, sizes.up + sizes.down + sizes.trio),
            (self.start.pair, sizes.pair + sizes.heads),
            (self.start.second, sizes.second),
            (self.start.first, sizes.first),
        ]


class Inputs(typing.NamedTuple):
    latents: typing.Any
    heights: typing.Any
    time_vector: typing.Any
    text_states: typing.Any
    gain_in: typing.Any
    conv_first: typing.Any
    time_weight: typing.Any
    gain_mid: typing.Any
    conv_second: typing.Any
    gain_block: typing.Any
    project_in: typing.Any
    gain_self: typing.Any
    query_self: typing.Any
    key_self: typing.Any
    value_self: typing.Any
    out_self: typing.Any
    gain_cross: typing.Any
    query_cross: typing.Any
    key_cross: typing.Any
    value_cross: typing.Any
    out_cross: typing.Any
    gain_feed: typing.Any
    feed_up: typing.Any
    feed_down: typing.Any
    project_out: typing.Any
    cotangent: typing.Any


class Fetched(typing.NamedTuple):
    query_self: typing.Any
    key_self: typing.Any
    value_self: typing.Any
    time_weight: typing.Any
    conv_first: typing.Any
    conv_second: typing.Any
    project_in: typing.Any
    key_cross: typing.Any
    value_cross: typing.Any
    out_self: typing.Any
    query_cross: typing.Any
    out_cross: typing.Any
    feed_up: typing.Any
    feed_down: typing.Any
    project_out: typing.Any


def buffers(sz):
    c, t, w, k = sz.channels, sz.tokens, sz.wide, sz.keys
    half = sz.seqs // 2
    others = sz.batches - 1
    return dict(
        lat6=((w, c), F32),
        cot6=((w, c), F32),
        mid6=((w, c), F32),
        res6=((w, c), F32),
        gblk6=((w, c), F32),
        gact6=((w, c), F32),
        shift_in=((3, w, c), LOW),
        shift_mid=((3, w, c), LOW),
        shift_grad=((3, w, c), LOW),
        stat_send=((ROUNDS, 8, c), F32),
        stat_recv=((ROUNDS, sz.seqs, 8, c), F32),
        norms=((3, 8, c), F32),
        gain_parts=((8, c), F32),
        final_send=((8, c), F32),
        group=((c, c), LOW),
        place=((3, c, sz.packed), LOW),
        wqkv=((c, sz.packed), LOW),
        osp=((HEADS * sz.slot, c), LOW),
        time_send=((8, sz.emb), F32),
        normed_block=((t, c), LOW),
        stream_in=((t, c), F32),
        normed_self=((t, c), LOW),
        qkv_send=((t, sz.packed), LOW),
        qkv=((k, LANES), LOW),
        qh=((k, LANES), LOW),
        kh=((k, LANES), LOW),
        vh=((k, sz.slot), LOW),
        vt=((sz.slot, k), LOW),
        kt=((sz.slot, k), LOW),
        scores=((max(k, 2 * sz.hidden), t), F32),
        probs=((2, k, t), LOW),
        mixed_full=((sz.seqs, sz.slot, t), F32),
        inverse=((sz.seqs, 8, t), F32),
        mixed_send=((sz.seqs, sz.slot, t), LOW),
        mixed=((HEADS * sz.slot, t), LOW),
        stream=((t, c), F32),
        centred_cross=((t, c), F32),
        scale_cross=((t, LANES), F32),
        normed_cross=((t, c), LOW),
        query_text=((t, c), LOW),
        text_rows=((2, sz.text_pad, c), F32),
        text_key=((HEADS * sz.text_pad, c), LOW),
        text_value=((HEADS * sz.text_pad, c), LOW),
        cross=((HEADS * sz.text_pad, t), F32),
        cross_low=((HEADS * sz.text_pad, t), LOW),
        cross_scores=((HEADS * sz.text_pad, t), LOW),
        cross_mixed=((t, c), LOW),
        scale_feed=((t, LANES), F32),
        normed_feed=((t, c), LOW),
        gated=((t, sz.hidden), LOW),
        grad_gated=((t, 2 * LANES), F32),
        grad_joined=((t, 2 * sz.hidden), LOW),
        stream_low=((t, c), LOW),
        grad_branch=((t, c), LOW),
        grad=((t, c), F32),
        tmp=((t, c), F32),
        grad_feed_low=((t, c), LOW),
        grad_cross_low=((t, c), LOW),
        grad_cross_mixed=((t, c), LOW),
        grad_query_text=((t, c), LOW),
        grad_self_low=((t, c), LOW),
        grad_in_low=((t, c), LOW),
        text_send=((sz.text_pad, sz.packed), LOW),
        text_recv=((sz.seqs, sz.text_pad, LANES), LOW),
        gm_send=((HEADS * sz.slot, t), LOW),
        gm=((sz.seqs, sz.slot, t), LOW),
        dscores=((k, t), LOW),
        gp=((t, sz.packed), LOW),
        pack=((sz.seqs, sz.pack_rows, LANES), LOW),
        recv_core=((half, sz.pack_rows, LANES), LOW),
        recv_batch=((others, half, sz.pack_rows // sz.batches, LANES), LOW),
        recv_z=((half - 1, sz.pack_rows // sz.batches, LANES), LOW),
    )


class Fused:
    def __init__(self, sz, refs, local):
        self.sz = sz
        self.r = refs
        self.v = local
        self.used = 0
        self.batch = lax.axis_index(BATCH)
        self.seq = lax.axis_index(SEQ)
        self.z_pos = self.seq // 2
        self.core = lax.rem(self.seq, 2)
        self.partner = (self.batch, self.seq + 1 - 2 * self.core)
        self.seq_others = [lax.rem(self.seq + step, sz.seqs) for step in range(1, sz.seqs)]
        self.batch_others = [lax.rem(self.batch + step, sz.batches) for step in range(1, sz.batches)]
        half = sz.seqs // 2
        self.z_others = [lax.rem(self.z_pos + step, half) for step in range(1, half)]
        self.height = refs.heights[0]
        self.scale = HEAD ** (-0.5)

    def remote(self, source, target, device, index=None):
        if index is None:
            index = self.used
            self.used += 1
        return pltpu.make_async_remote_copy(
            src_ref=source,
            dst_ref=target,
            send_sem=self.r.sems.at[0, index],
            recv_sem=self.r.sems.at[1, index],
            device_id=device,
            device_id_type=MESH,
        )

    def to_seq(self, source, target):
        return [self.remote(source(other), target, (self.batch, other)) for other in self.seq_others]

    def to_batch(self, source, target):
        return [self.remote(source, target, (other, self.seq)) for other in self.batch_others]

    def start(self, copies):
        for one in copies:
            one.start()

    def wait(self, copies):
        for one in copies:
            one.wait()

    def entry(self):
        r = self.r
        barrier = pltpu.get_barrier_semaphore()
        for other in self.seq_others:
            pl.semaphore_signal(barrier, inc=1, device_id=(self.batch, other), device_id_type=MESH)
        for other in self.batch_others:
            pl.semaphore_signal(barrier, inc=1, device_id=(other, self.seq), device_id_type=MESH)
        self.local = {}
        self.named = {id(getattr(r, name)): name for name in Fetched._fields}
        for number, name in enumerate(Fetched._fields):
            self.local[name] = pltpu.make_async_copy(
                getattr(r, name), getattr(self.v, name), r.local_sems.at[number]
            )
            self.local[name].start()
        own = pl.ds(self.sz.width, self.sz.tokens)
        self.images = [
            pltpu.make_async_copy(source, target.at[own], r.local_sems.at[len(Fetched._fields) + place])
            for place, (source, target) in enumerate(((r.latents, r.lat6), (r.cotangent, r.cot6)))
        ]
        self.start(self.images)
        pl.semaphore_wait(barrier, self.sz.seqs - 1 + self.sz.batches - 1)

    def weight(self, ref):
        name = self.named[id(ref)]
        if name in self.local:
            self.local.pop(name).wait()
        return getattr(self.v, name)

    def wide_row(self, start, size):
        rows = floor_div(iota((size, 1), 0) + start, self.sz.width) - 1
        return rows + self.seq * self.sz.rows

    def wide_mask(self, start, size):
        rows = self.wide_row(start, size)
        return jnp.where((rows >= 0) & (rows < self.height), 1.0, 0.0)

    def inside_mask(self, start, size):
        rows = self.wide_row(start, size)
        return jnp.where((rows >= 0) & (rows < self.sz.rows * self.sz.seqs), 1.0, 0.0)

    def chunks(self, total):
        return [(start, TILE) for start in range(0, total, TILE)]

    def halo(self, ref):
        r, sz = self.r, self.sz
        after = lax.rem(self.seq + 1, sz.seqs)
        before = lax.rem(self.seq + sz.seqs - 1, sz.seqs)
        width = sz.width
        return [
            self.remote(ref.at[pl.ds(sz.tokens, width)], ref.at[pl.ds(0, width)], (self.batch, after)),
            self.remote(
                ref.at[pl.ds(width, width)],
                ref.at[pl.ds(width + sz.tokens, width)],
                (self.batch, before),
            ),
        ]

    def stats_start(self, number, rows):
        r = self.r
        r.stat_send[number] = jnp.zeros(r.stat_send.shape[1:], F32)
        for place, row in enumerate(rows):
            r.stat_send[number, place : place + 1] = row
        r.stat_recv[number, self.seq] = r.stat_send[number]
        copies = self.to_seq(lambda other: r.stat_send.at[number], r.stat_recv.at[number, self.seq])
        self.start(copies)
        return copies

    def stats_total(self, number):
        r = self.r
        total = r.stat_recv[number, 0]
        for place in range(1, self.sz.seqs):
            total = total + r.stat_recv[number, place]
        return total

    def grouped(self, rows):
        return sum_three(dot_nn(split_three(rows), self.r.group[...]))

    def count(self):
        per_row = self.sz.width * (self.sz.channels // GROUPS)
        return (self.height * per_row).astype(F32)

    def set_norm(self, number, total):
        sums = self.grouped(total) / self.count()
        mean = sums[0:1]
        spread = sums[1:2] - mean * mean
        self.r.norms[number, 0:1] = mean
        self.r.norms[number, 1:2] = lax.rsqrt(spread + epsilon)

    def norm(self, number):
        return self.r.norms[number, 0:1], self.r.norms[number, 1:2]

    def value_sums(self, ref):
        r, sz = self.r, self.sz
        first = second = None
        for start, size in self.chunks(sz.tokens):
            start += sz.width
            values = ref[start : start + size]
            masked = values * self.wide_mask(start, size)
            one, two = col_sum(masked), col_sum(masked * values)
            first = one if first is None else first + one
            second = two if second is None else second + two
        return first, second

    def shifts(self, ref, start, size, values):
        column = lax.rem(iota((size, 1), 0), self.sz.width)
        ref[1, start : start + size] = values.astype(LOW)
        left = jnp.where(column == 0, 0.0, pltpu.roll(values, 1, 0))
        ref[0, start : start + size] = left.astype(LOW)
        right = jnp.where(column == self.sz.width - 1, 0.0, pltpu.roll(values, size - 1, 0))
        ref[2, start : start + size] = right.astype(LOW)

    def activate(self, source, number, gain, target):
        mean, inverse = self.norm(number)
        factor = inverse * row_of(gain)
        for start, size in self.chunks(self.sz.wide):
            normed = (source[start : start + size] - mean) * factor
            values = normed * sigmoid(normed) * self.wide_mask(start, size)
            self.shifts(target, start, size, values)

    def conv(self, ref, weight):
        sz = self.sz
        total = None
        for row in range(3):
            for col in range(3):
                part = dot_nn(ref[col, row * sz.width : row * sz.width + sz.tokens], weight[row, col])
                total = part if total is None else total + part
        return total

    def conv_back(self, ref, weight):
        sz = self.sz
        total = None
        for row in range(3):
            for col in range(3):
                part = dot_nt(
                    ref[col, row * sz.width : row * sz.width + sz.tokens], weight[2 - row, 2 - col]
                )
                total = part if total is None else total + part
        return total

    def constants(self):
        r, sz = self.r, self.sz
        channels = sz.channels
        size = channels // GROUPS
        r.group[...] = jnp.where(
            floor_div(iota((channels, 1), 0), size) == floor_div(iota((1, channels), 1), size), 1.0, 0.0
        ).astype(LOW)
        rows = iota((channels, 1), 0)
        target = rows + (LANES - HEAD) * floor_div(rows, HEAD)
        lanes = iota((1, sz.packed), 1)
        for number in range(3):
            r.place[number] = jnp.where(lanes == target + number * HEAD, 1.0, 0.0).astype(LOW)

    def residual(self):
        r, sz = self.r, self.sz
        width, tokens = sz.width, sz.tokens
        self.wait(self.images)
        halo = self.halo(r.lat6)
        self.start(halo)
        stats = self.stats_start(0, self.value_sums(r.lat6))
        late = self.halo(r.cot6)
        act = r.time_vector[...].astype(F32)
        act = (act * sigmoid(act)).astype(LOW)
        r.time_send[...] = jnp.zeros(r.time_send.shape, F32)
        r.time_send[0:1] = act.astype(F32)
        r.time_all[self.batch] = r.time_send[...]
        late += self.to_batch(r.time_send, r.time_all.at[self.batch])
        r.text_all[self.batch] = jnp.zeros(r.text_all.shape[1:], LOW)
        r.text_all[self.batch, 0 : sz.text] = r.text_states[...]
        late += self.to_batch(r.text_all.at[self.batch], r.text_all.at[self.batch])
        self.start(late)
        self.late = late
        self.constants()
        time_weight = self.weight(self.r.time_weight)
        time_term = dot_nt(jnp.broadcast_to(act, (16, sz.emb)), time_weight[...])[0:1]
        wqkv = None
        for number, name in enumerate((r.query_self, r.key_self, r.value_self)):
            part = dot_nn(self.weight(name)[...], r.place[number])
            wqkv = part if wqkv is None else wqkv + part
        r.wqkv[...] = wqkv.astype(LOW)
        self.wait(halo)
        self.wait(stats)
        self.set_norm(0, self.stats_total(0))
        self.activate(r.lat6, 0, r.gain_in, r.shift_in)
        r.mid6[width : width + tokens] = self.conv(r.shift_in, self.weight(self.r.conv_first)) + time_term
        halo = self.halo(r.mid6)
        self.start(halo)
        stats = self.stats_start(1, self.value_sums(r.mid6))
        self.weight(self.r.conv_second)
        self.wait(halo)
        self.wait(stats)
        self.set_norm(1, self.stats_total(1))
        self.activate(r.mid6, 1, r.gain_mid, r.shift_mid)
        r.res6[width : width + tokens] = r.lat6[width : width + tokens] + self.conv(
            r.shift_mid, self.v.conv_second
        )
        halo = self.halo(r.res6)
        stats = self.stats_start(2, self.value_sums(r.res6))
        self.start(halo)
        self.late += halo
        project_in = self.weight(self.r.project_in)
        self.wait(stats)
        self.set_norm(2, self.stats_total(2))
        mean, inverse = self.norm(2)
        factor = inverse * row_of(r.gain_block)
        for start, size in self.chunks(tokens):
            values = r.res6[width + start : width + start + size]
            r.normed_block[start : start + size] = ((values - mean) * factor).astype(LOW)
        r.stream_in[...] = dot_nn(r.normed_block[...], project_in[...])
        for start, size in self.chunks(tokens):
            values = r.stream_in[start : start + size]
            centred, scale = self.layer_parts(values)
            r.normed_self[start : start + size] = (centred * scale * row_of(r.gain_self)).astype(LOW)
        r.qkv_send[...] = dot_nn(r.normed_self[...], r.wqkv[...]).astype(LOW)
        rows = pl.ds(pl.multiple_of(self.seq * tokens, tokens), tokens)
        copies = [
            self.remote(
                r.qkv_send.at[:, pl.ds(pl.multiple_of(other * LANES, LANES), LANES)],
                r.qkv.at[rows],
                (self.batch, other),
            )
            for other in self.seq_others
        ]
        self.start(copies)
        r.qkv[rows] = r.qkv_send[:, pl.ds(pl.multiple_of(self.seq * LANES, LANES), LANES)]
        self.text_start()
        self.wait(copies)

    def layer_parts(self, values):
        centred = values - jnp.mean(values, axis=-1, keepdims=True)
        spread = jnp.mean(centred * centred, axis=-1, keepdims=True)
        return centred, lax.rsqrt(spread + epsilon)

    def layer_back(self, values, grad, gain):
        centred, scale = self.layer_parts(values)
        normed = centred * scale
        scaled = grad * gain
        first = jnp.mean(scaled, axis=-1, keepdims=True)
        second = jnp.mean(scaled * normed, axis=-1, keepdims=True)
        return scale * (scaled - first - normed * second), col_sum(grad * normed)

    def text_start(self):
        r, sz = self.r, self.sz
        r.text_rows[...] = jnp.zeros(r.text_rows.shape, F32)
        for number, (name, target) in enumerate(
            ((r.key_cross, r.text_key), (r.value_cross, r.text_value))
        ):
            r.text_rows[number, 0 : sz.text] = dot_nt(r.text_states[...], self.weight(name)[...])
            rows = r.text_rows[number]
            head = floor_div(iota((1, sz.channels), 1), HEAD)
            for one in range(HEADS):
                target[one * sz.text_pad : (one + 1) * sz.text_pad] = jnp.where(
                    head == one, rows, 0.0
                ).astype(LOW)
        spread = iota((HEADS * sz.slot, 1), 0)
        source = iota((1, sz.channels), 1)
        source = source + (sz.slot - HEAD) * floor_div(source, HEAD)
        one_hot = jnp.where(spread == source, 1.0, 0.0).astype(LOW)
        r.osp[...] = dot_nn(one_hot, self.weight(self.r.out_self)[...]).astype(LOW)

    def attention(self):
        r, sz = self.r, self.sz
        keys, tokens, slot = sz.keys, sz.tokens, sz.slot
        lane_in = iota((LANES, LANES), 0)
        lane_out = iota((LANES, LANES), 1)

        def shift(by):
            return jnp.where((lane_in == lane_out + by) & (lane_out < HEAD), 1.0, 0.0).astype(LOW)

        def shift_wide(by):
            source = iota((LANES, slot), 0)
            target = iota((LANES, slot), 1)
            return jnp.where((source == target + by) & (target < HEAD), 1.0, 0.0).astype(LOW)

        def shift_rows(by):
            source = iota((slot, LANES), 1)
            target = iota((slot, LANES), 0)
            return jnp.where((source == target + by) & (target < HEAD), 1.0, 0.0).astype(LOW)

        query_out = jnp.where((lane_in + HEAD == lane_out) & (lane_in < HEAD), 1.0, 0.0).astype(LOW)
        lane = iota((1, LANES), 1)
        for start in range(0, keys, 2 * tokens):
            rows = slice(start, start + 2 * tokens)
            block = r.qkv[rows]
            valid = iota((2 * tokens, 1), 0) + start < self.height * sz.width
            r.qh[rows] = jnp.where(
                lane < HEAD, block.astype(F32), jnp.where(lane == HEAD, 1.0, 0.0)
            ).astype(LOW)
            bias = jnp.where((lane == HEAD) & jnp.logical_not(valid), -1e30, 0.0)
            r.kh[rows] = (dot_nn(block, shift(HEAD)) + bias).astype(LOW)
            ones = jnp.where((iota((1, slot), 1) >= HEAD) & (iota((1, slot), 1) < HEAD + 3), 1.0, 0.0)
            r.vh[rows] = (dot_nn(block, shift_wide(2 * HEAD)) + ones).astype(LOW)
            one_row = jnp.where(iota((slot, 1), 0) == HEAD, 1.0, 0.0)
            r.vt[:, rows] = (dot_nt(shift_rows(2 * HEAD), block) + one_row).astype(LOW)
            r.kt[:, rows] = dot_nt(shift_rows(HEAD), block).astype(LOW)
            r.qkv[rows] = dot_nn(block, query_out).astype(LOW)
        factor = self.scale * 1.4426950408889634
        base = self.used
        self.used += sz.seqs

        def send(target, step):
            return self.remote(
                r.mixed_send.at[target],
                r.mixed.at[pl.ds(pl.multiple_of(self.seq * slot, 16), slot)],
                (self.batch, target),
                base + step,
            )

        def keep(step):
            return pltpu.make_async_copy(
                r.probs.at[lax.rem(step, 2)],
                r.kept_probs.at[lax.rem(self.seq + 1 + step, sz.seqs)],
                r.local_sems.at[len(Fetched._fields) + 2 + lax.rem(step, 2)],
            )

        def block(step, carry):
            target = lax.rem(self.seq + 1 + step, sz.seqs)
            slot_now = lax.rem(step, 2)

            @pl.when(step >= 2)
            def _():
                keep(step - 2).wait()

            queries = r.qh[pl.ds(pl.multiple_of(target * tokens, tokens), tokens)]
            top = None
            for start in range(0, keys, tokens):
                scores = dot_nt(r.kh[start : start + tokens], queries)
                r.scores[start : start + tokens] = scores
                part = jnp.max(scores.reshape(tokens // 8, 8, tokens), axis=0)
                top = part if top is None else jnp.maximum(top, part)
            offset = jnp.max(top, axis=0, keepdims=True) * factor
            for start in range(0, keys, LANES):
                powers = jnp.exp2(r.scores[start : start + LANES] * factor - offset)
                r.probs[slot_now, start : start + LANES] = powers.astype(LOW)
            keep(step).start()
            sums = dot_nn(r.vt[...], r.probs[slot_now])
            inverse = 1.0 / sums[HEAD : HEAD + 1]
            mixed = jnp.where(iota((slot, 1), 0) < HEAD, sums * inverse, 0.0)
            r.mixed_full[target] = mixed
            r.mixed_send[target] = mixed.astype(LOW)
            r.inverse[target] = jnp.broadcast_to(inverse, (8, tokens))

            @pl.when(step < sz.seqs - 1)
            def _():
                send(target, step).start()

            return carry

        lax.fori_loop(0, sz.seqs, block, 0)
        keep(sz.seqs - 2).wait()
        keep(sz.seqs - 1).wait()
        self.recall(0).start()
        r.mixed[pl.ds(pl.multiple_of(self.seq * slot, 16), slot)] = r.mixed_send[self.seq]
        for step in range(sz.seqs - 1):
            send(lax.rem(self.seq + 1 + step, sz.seqs), step).wait()

    def local_block(self):
        r, sz = self.r, self.sz
        tokens, channels = sz.tokens, sz.channels
        pad = sz.text_pad
        r.stream[...] = r.stream_in[...] + dot_tn(r.mixed[...], r.osp[...])
        for start, size in self.chunks(tokens):
            rows = slice(start, start + size)
            centred, scale = self.layer_parts(r.stream[rows])
            r.normed_cross[rows] = (centred * scale * row_of(r.gain_cross)).astype(LOW)
        r.query_text[...] = dot_nn(r.normed_cross[...], self.weight(self.r.query_cross)[...]).astype(LOW)
        r.cross[...] = dot_nt(r.text_key[...], r.query_text[...])
        for head in range(HEADS):
            rows = slice(head * pad, (head + 1) * pad)
            valid = iota((pad, 1), 0) < sz.text
            scores = jnp.where(valid, r.cross[rows] * self.scale, -1e30)
            powers = jnp.exp(scores - jnp.max(scores, axis=0, keepdims=True))
            attention = powers / jnp.sum(powers, axis=0, keepdims=True)
            r.cross[rows] = attention
            r.cross_low[rows] = attention.astype(LOW)
        r.cross_mixed[...] = dot_tn(r.cross_low[...], r.text_value[...]).astype(LOW)
        r.centred_cross[...] = r.stream[...]
        r.stream[...] = r.stream[...] + dot_nn(r.cross_mixed[...], self.weight(self.r.out_cross)[...])
        for start, size in self.chunks(tokens):
            rows = slice(start, start + size)
            centred, scale = self.layer_parts(r.stream[rows])
            r.normed_feed[rows] = (centred * scale * row_of(r.gain_feed)).astype(LOW)
        feed_up = self.weight(self.r.feed_up)
        joined = r.scores
        root = 0.7071067811865476
        block = 2 * LANES
        pieces = sz.hidden // block
        for piece in range(pieces):
            for place in (piece, piece + pieces):
                joined[place * tokens : (place + 1) * tokens] = dot_nn(
                    r.normed_feed[...], feed_up[:, place * block : (place + 1) * block]
                )
            for start, size in self.chunks(tokens):
                values = joined[piece * tokens + start : piece * tokens + start + size]
                gates_at = (piece + pieces) * tokens + start
                gates = joined[gates_at : gates_at + size]
                half = 0.5 * (1.0 + lax.erf(gates * root))
                r.gated[start : start + size, piece * block : (piece + 1) * block] = (
                    values * (gates * half)
                ).astype(LOW)

        low = (
            r.stream[...] + dot_nt(r.gated[...], self.weight(self.r.feed_down)[...])
        ).astype(LOW)
        r.stream_low[...] = low
        project_out = self.weight(self.r.project_out)
        r.tmp[...] = dot_nn(r.stream_low[...], project_out[...])
        for start, size in self.chunks(tokens):
            rows = slice(start, start + size)
            wide = slice(start + sz.width, start + sz.width + size)
            mask = self.wide_mask(start + sz.width, size)
            r.output[rows] = (r.res6[wide] + r.tmp[rows]) * mask
            r.grad_branch[rows] = (r.cot6[wide] * mask).astype(LOW)
        r.grad[...] = dot_nt(r.grad_branch[...], project_out[...])
        r.grad_feed_low[...] = r.grad[...].astype(LOW)
        for piece in range(pieces):
            lanes = slice(piece * block, (piece + 1) * block)
            gate_lanes = slice(sz.hidden + piece * block, sz.hidden + (piece + 1) * block)
            r.grad_gated[...] = dot_nn(r.grad_feed_low[...], self.v.feed_down[:, lanes])
            for start, size in self.chunks(tokens):
                rows = slice(start, start + size)
                values = joined[piece * tokens + start : piece * tokens + start + size]
                gates_at = (piece + pieces) * tokens + start
                gates = joined[gates_at : gates_at + size]
                grads = r.grad_gated[rows]
                half = 0.5 * (1.0 + lax.erf(gates * root))
                slope = half + gates * (jnp.exp(-0.5 * gates * gates) * 0.3989422804014327)
                r.grad_joined[rows, lanes] = (grads * (gates * half)).astype(LOW)
                r.grad_joined[rows, gate_lanes] = (grads * values * slope).astype(LOW)
        r.tmp[...] = dot_nt(r.grad_joined[...], self.v.feed_up[...])
        self.layer_step(r.stream, r.gain_feed, 3, r.grad_cross_low)
        r.grad_cross_mixed[...] = dot_nt(r.grad_cross_low[...], self.v.out_cross[...]).astype(LOW)
        r.scores[0 : HEADS * pad] = dot_nt(r.text_value[...], r.grad_cross_mixed[...])
        for head in range(HEADS):
            rows = slice(head * pad, (head + 1) * pad)
            attention = r.cross[rows]
            grads = r.scores[rows]
            delta = jnp.sum(attention * grads, axis=0, keepdims=True)
            r.cross_scores[rows] = (attention * (grads - delta)).astype(LOW)
        r.grad_query_text[...] = (
            dot_tn(r.cross_scores[...], r.text_key[...]) * self.scale
        ).astype(LOW)
        r.tmp[...] = dot_nt(r.grad_query_text[...], self.v.query_cross[...])
        self.layer_step(r.centred_cross, r.gain_cross, 4, r.grad_self_low)
        r.gm_send[...] = dot_nt(r.osp[...], r.grad_self_low[...]).astype(LOW)
        slot = sz.slot
        copies = [
            self.remote(
                r.gm_send.at[pl.ds(pl.multiple_of(other * slot, 16), slot)],
                r.gm.at[self.seq],
                (self.batch, other),
            )
            for other in self.seq_others
        ]
        self.start(copies)
        self.gm_copies = copies
        r.gm[self.seq] = r.gm_send[pl.ds(pl.multiple_of(self.seq * slot, 16), slot)]

    def layer_step(self, source, gain, place, target):
        r = self.r
        gains = None
        for start, size in self.chunks(self.sz.tokens):
            rows = slice(start, start + size)
            part, gain_part = self.layer_back(source[rows], r.tmp[rows], row_of(gain))
            total = r.grad[rows] + part
            r.grad[rows] = total
            target[rows] = total.astype(LOW)
            gains = gain_part if gains is None else gains + gain_part
        r.gain_parts[place : place + 1] = gains

    def text_grads(self):
        r, sz = self.r, self.sz
        pad = sz.text_pad
        head_of = floor_div(iota((1, sz.channels), 1), HEAD)
        keys = dot_nn(r.cross_scores[...], r.query_text[...]) * self.scale
        values = dot_nn(r.cross_low[...], r.grad_cross_mixed[...])
        packed = None
        for number, grads in enumerate((keys, values)):
            total = None
            for head in range(HEADS):
                part = jnp.where(head_of == head, grads[head * pad : (head + 1) * pad], 0.0)
                total = part if total is None else total + part
            part = dot_nn(total.astype(LOW), r.place[number])
            packed = part if packed is None else packed + part
        r.text_send[...] = packed.astype(LOW)
        copies = [
            self.remote(
                r.text_send.at[:, pl.ds(pl.multiple_of(other * LANES, LANES), LANES)],
                r.text_recv.at[self.seq],
                (self.batch, other),
            )
            for other in self.seq_others
        ]
        self.start(copies)
        r.text_recv[self.seq] = r.text_send[
            :, pl.ds(pl.multiple_of(self.seq * LANES, LANES), LANES)
        ]
        self.text_copies = copies

    def text_second(self):
        r = self.r
        self.wait(self.text_copies)
        total = r.text_recv[0].astype(F32)
        for place in range(1, self.sz.seqs):
            total = total + r.text_recv[place].astype(F32)
        r.text_total[self.batch] = total
        copies = self.to_batch(r.text_total.at[self.batch], r.text_total.at[self.batch])
        self.start(copies)
        self.text_copies = copies

    def store_pack(self, start, rows, values):
        for shard in range(self.sz.seqs):
            self.r.pack[shard, start + rows.start : start + rows.stop] = values[
                :, shard * LANES : (shard + 1) * LANES
            ].astype(LOW)

    def early_grads(self):
        r, sz = self.r, self.sz
        channels = sz.channels
        rows = iota((2 * channels, 1), 0)
        target = jnp.where(rows >= channels, rows + (3 * LANES - channels), rows)
        spread = jnp.where(iota((1, 6 * LANES), 1) == target, 1.0, 0.0).astype(LOW)
        for z in range(sz.seqs // 2):
            wide = 2 * channels
            grads = dot_nn(r.grad_joined[:, z * wide : (z + 1) * wide], spread).astype(LOW)
            sums = dot_tn(r.normed_feed[...], grads)
            for tile in range(6):
                start = sz.start.up + (tile % 3) * channels
                r.pack[2 * z + tile // 3, start : start + channels] = sums[
                    :, tile * LANES : (tile + 1) * LANES
                ].astype(LOW)
        size = sz.down_rows
        tail = sz.hidden - 2 * size
        placed = [dot_nn(r.grad_feed_low[...], r.place[number]).astype(LOW) for number in range(3)]
        sums = dot_tn(r.gated[:, 0:size], placed[0]) + dot_tn(r.gated[:, size : 2 * size], placed[1])
        extra = dot_tn(r.gated[:, 2 * size :], placed[2])
        self.store_pack(sz.start.down, slice(0, tail), sums[0:tail] + extra)
        self.store_pack(sz.start.down, slice(tail, size), sums[tail:])
        sums = (
            dot_tn(r.stream_low[...], dot_nn(r.grad_branch[...], r.place[0]).astype(LOW))
            + dot_tn(r.cross_mixed[...], dot_nn(r.grad_cross_low[...], r.place[1]).astype(LOW))
            + dot_tn(r.normed_cross[...], dot_nn(r.grad_query_text[...], r.place[2]).astype(LOW))
        )
        self.store_pack(sz.start.trio, slice(0, channels), sums)

    def recall(self, step):
        r = self.r
        return pltpu.make_async_copy(
            r.kept_probs.at[lax.rem(self.seq + step, self.sz.seqs)],
            r.probs.at[lax.rem(step, 2)],
            r.local_sems.at[len(Fetched._fields) + 2 + lax.rem(step, 2)],
        )

    def attention_back(self):
        r, sz = self.r, self.sz
        keys, tokens, slot = sz.keys, sz.tokens, sz.slot
        self.wait(self.gm_copies)
        r.scores[0:keys, 0:LANES] = jnp.zeros((keys, LANES), F32)
        row = iota((slot, 1), 0)
        to_lanes = jnp.where(
            (iota((slot, LANES), 0) == iota((slot, LANES), 1)) & (iota((slot, LANES), 0) < HEAD), 1.0, 0.0
        ).astype(LOW)
        to_values = jnp.where(
            (iota((slot, LANES), 0) + 2 * HEAD == iota((slot, LANES), 1))
            & (iota((slot, LANES), 0) < HEAD),
            1.0,
            0.0,
        ).astype(LOW)

        def block(step, carry):
            source = lax.rem(self.seq + step, sz.seqs)
            slot_now = lax.rem(step, 2)
            self.recall(step).wait()

            @pl.when(step < sz.seqs - 1)
            def _():
                self.recall(step + 1).start()

            scaled = (r.gm[source].astype(F32) * r.inverse[source, 0:1]).astype(LOW).astype(F32)
            delta = -jnp.sum(r.mixed_full[source] * scaled, axis=0, keepdims=True)
            high = delta.astype(LOW).astype(F32)
            middle = (delta - high).astype(LOW).astype(F32)
            rest = delta - high - middle
            extended = jnp.where(row == HEAD, high, scaled)
            extended = jnp.where(row == HEAD + 1, middle, extended)
            extended = jnp.where(row == HEAD + 2, rest, extended).astype(LOW)
            for start in range(0, keys, tokens):
                rows = slice(start, start + tokens)
                grads = dot_nn(r.vh[rows], extended)
                r.dscores[rows] = (r.probs[slot_now, rows].astype(F32) * grads).astype(LOW)
            query_rows = pl.ds(pl.multiple_of(source * tokens, tokens), tokens)
            grad_query = (dot_nn(r.kt[...], r.dscores[...]) * self.scale).astype(LOW)
            r.kh[query_rows] = dot_tn(grad_query, to_lanes).astype(LOW)
            token_grads = dot_tn(scaled.astype(LOW), to_values).astype(LOW)
            queries = r.qkv[query_rows]
            for start in range(0, keys, tokens):
                rows = slice(start, start + tokens)
                r.scores[rows, 0:LANES] += dot_nn(r.dscores[rows], queries) + dot_nn(
                    r.probs[slot_now, rows], token_grads
                )
            return carry

        lax.fori_loop(0, sz.seqs, block, 0)
        factor = jnp.where(iota((1, LANES), 1) < 2 * HEAD, self.scale, 1.0)
        for place in range(sz.seqs):
            rows = slice(place * tokens, (place + 1) * tokens)
            grads = r.scores[rows, 0:LANES] * factor
            r.qh[rows] = (grads + r.kh[rows].astype(F32)).astype(LOW)
        lanes = pl.ds(pl.multiple_of(self.seq * LANES, LANES), LANES)
        copies = [
            self.remote(
                r.qh.at[pl.ds(pl.multiple_of(other * tokens, tokens), tokens)],
                r.gp.at[:, lanes],
                (self.batch, other),
            )
            for other in self.seq_others
        ]
        self.start(copies)
        r.gp[:, lanes] = r.qh[pl.ds(pl.multiple_of(self.seq * tokens, tokens), tokens)]
        self.gp_copies = copies

    def norm_sums(self, number, rows_of):
        first = second = None
        mean, inverse = self.norm(number)
        for start, size in self.chunks(self.sz.tokens):
            grads, values = rows_of(start, size)
            one, two = col_sum(grads), col_sum(grads * ((values - mean) * inverse))
            first = one if first is None else first + one
            second = two if second is None else second + two
        return first, second

    def norm_factors(self, number, gain, total):
        gains = row_of(gain)
        sums = self.grouped(total * gains) / self.count()
        mean, inverse = self.norm(number)
        return mean, inverse, gains * inverse, sums[0:1] * inverse, sums[1:2] * inverse

    def slope(self, source, number, gain, start, size):
        mean, inverse = self.norm(number)
        normed = (source[start : start + size] - mean) * inverse
        values = normed * row_of(gain)
        gate = sigmoid(values)
        return normed, gate * (1.0 + values * (1.0 - gate)) * self.wide_mask(start, size)

    def residual_back(self):
        r, sz = self.r, self.sz
        width, tokens, channels = sz.width, sz.tokens, sz.channels
        self.wait(self.gp_copies)
        r.tmp[...] = dot_nt(r.gp[...], r.wqkv[...])
        self.layer_step(r.stream_in, r.gain_self, 5, r.grad_in_low)
        r.gblk6[width : width + tokens] = dot_nt(r.grad_in_low[...], self.v.project_in[...])
        halo = self.halo(r.gblk6)
        self.start(halo)

        def block_rows(start, size):
            wide = slice(start + width, start + width + size)
            return r.gblk6[wide], r.res6[wide]

        stats = self.stats_start(3, self.norm_sums(2, block_rows))
        self.wait(self.late)
        self.late = []
        self.middle_grads()
        self.wait(halo)
        self.wait(stats)
        total = self.stats_total(3)
        r.gain_parts[2:3] = total[1:2]
        mean, inverse, factor, first, second = self.norm_factors(2, r.gain_block, total)
        for start, size in self.chunks(sz.wide):
            rows = slice(start, start + size)
            mask = self.wide_mask(start, size)
            normed = (r.res6[rows] - mean) * inverse
            grads = r.cot6[rows] * mask + r.gblk6[rows] * factor - mask * (first + normed * second)
            r.cot6[rows] = grads
            self.shifts(r.shift_grad, start, size, grads * self.inside_mask(start, size))
        r.gact6[width : width + tokens] = self.conv_back(r.shift_grad, self.v.conv_second)
        halo = self.halo(r.gact6)
        self.start(halo)

        def mid_rows(start, size):
            wide = slice(start + width, start + width + size)
            normed, slope = self.slope(r.mid6, 1, r.gain_mid, start + width, size)
            return r.gact6[wide] * slope, r.mid6[wide]

        stats = self.stats_start(4, self.norm_sums(1, mid_rows))
        self.conv_grads(sz.start.second, r.shift_mid, r.shift_grad)
        self.wait(halo)
        self.wait(stats)
        total = self.stats_total(4)
        r.gain_parts[1:2] = total[1:2]
        mean, inverse, factor, first, second = self.norm_factors(1, r.gain_mid, total)
        time_total = None
        for start, size in self.chunks(sz.wide):
            rows = slice(start, start + size)
            normed, slope = self.slope(r.mid6, 1, r.gain_mid, start, size)
            grads = r.gact6[rows] * slope * factor - self.wide_mask(start, size) * (
                first + normed * second
            )
            self.shifts(r.shift_grad, start, size, grads)
            if width <= start < width + tokens:
                part = col_sum(grads)
                time_total = part if time_total is None else time_total + part
        r.gblk6[width : width + tokens] = self.conv_back(r.shift_grad, self.v.conv_first)

        def in_rows(start, size):
            wide = slice(start + width, start + width + size)
            normed, slope = self.slope(r.lat6, 0, r.gain_in, start + width, size)
            return r.gblk6[wide] * slope, r.lat6[wide]

        parts = r.gain_parts
        stats = self.stats_start(
            5,
            list(self.norm_sums(0, in_rows)) + [time_total, parts[3:4], parts[4:5], parts[5:6]],
        )
        self.conv_grads(sz.start.first, r.shift_in, r.shift_grad)
        self.wait(stats)
        total = self.stats_total(5)
        mean, inverse, factor, first, second = self.norm_factors(0, r.gain_in, total)
        r.final_send[...] = total
        r.final_send[0:1] = parts[1:2]
        r.final_send[6:7] = parts[2:3]
        r.final_recv[self.batch] = r.final_send[...]
        self.final_copies = self.to_batch(r.final_send, r.final_recv.at[self.batch])
        self.start(self.final_copies)
        for start, size in self.chunks(tokens):
            wide = slice(start + width, start + width + size)
            normed, slope = self.slope(r.lat6, 0, r.gain_in, start + width, size)
            r.latent_grad[start : start + size] = (
                r.cot6[wide]
                + r.gblk6[wide] * slope * factor
                - self.wide_mask(start + width, size) * (first + normed * second)
            )

    def middle_grads(self):
        r, sz = self.r, self.sz
        self.store_pack(sz.start.heads, slice(0, sz.channels), dot_tn(r.normed_self[...], r.gp[...]))
        outer = dot_nn(r.mixed[...], dot_nn(r.grad_self_low[...], r.place[0]).astype(LOW))
        inner = dot_tn(r.normed_block[...], dot_nn(r.grad_in_low[...], r.place[1]).astype(LOW))
        self.store_pack(sz.start.pair, slice(0, sz.channels), outer[0 : sz.channels] + inner)
        self.store_pack(sz.start.pair, slice(sz.channels, HEADS * sz.slot), outer[sz.channels :])

    def conv_grads(self, pack_start, shifted, grads):
        r, sz = self.r, self.sz
        own = grads[1, sz.width : sz.width + sz.tokens]
        placed = [dot_nn(own, r.place[number]).astype(LOW) for number in range(3)]
        for col in range(3):
            total = None
            for row in range(3):
                start = row * sz.width
                part = dot_tn(shifted[col, start : start + sz.tokens], placed[row])
                total = part if total is None else total + part
            self.store_pack(pack_start, slice(col * sz.channels, (col + 1) * sz.channels), total)

    def sums_setup(self):
        r, sz = self.r, self.sz
        half, batches = sz.seqs // 2, sz.batches
        self.stages = []
        for start, size in sz.chunks:
            rows = pl.ds(start, size)
            part = size // batches
            quarter = pl.ds(start // batches, part)
            one = [
                self.remote(r.pack.at[2 * z + 1 - self.core, rows], r.recv_core.at[z, rows], self.partner)
                for z in range(half)
            ]
            two = [
                self.remote(
                    r.recv_core.at[:, pl.ds(pl.multiple_of(start + other * part, 16), part)],
                    r.recv_batch.at[step, :, quarter],
                    (other, self.seq),
                )
                for step, other in enumerate(self.batch_others)
            ]
            three = [
                self.remote(
                    r.recv_batch.at[0, other, quarter],
                    r.recv_z.at[step, quarter],
                    (self.batch, other * 2 + self.core),
                )
                for step, other in enumerate(self.z_others)
            ]
            four = [
                self.remote(
                    r.gathered.at[pl.ds(pl.multiple_of(start + self.batch * part, 16), part)],
                    r.gathered.at[pl.ds(pl.multiple_of(start + self.batch * part, 16), part)],
                    (other, self.seq),
                )
                for other in self.batch_others
            ]
            self.stages.append((one, two, three, four))

    def sums_core(self, number):
        self.start(self.stages[number][0])

    def sums_batch(self, number):
        r, sz = self.r, self.sz
        start, size = sz.chunks[number]
        self.wait(self.stages[number][0])

        @pl.loop(0, sz.seqs // 2)
        def add(z):
            rows = pl.ds(start, size)
            r.recv_core[z, rows] = (
                r.pack[2 * z + self.core, rows].astype(F32) + r.recv_core[z, rows].astype(F32)
            ).astype(LOW)

        self.start(self.stages[number][1])

    def sums_z(self, number):
        r, sz = self.r, self.sz
        start, size = sz.chunks[number]
        part = size // sz.batches
        quarter = pl.ds(start // sz.batches, part)
        self.wait(self.stages[number][1])

        @pl.loop(0, sz.seqs // 2)
        def add(z):
            total = r.recv_core[z, pl.ds(pl.multiple_of(start + self.batch * part, 16), part)].astype(F32)
            for step in range(sz.batches - 1):
                total = total + r.recv_batch[step, z, quarter].astype(F32)
            r.recv_batch[0, z, quarter] = total.astype(LOW)

        self.start(self.stages[number][2])

    def sums_gather(self, number):
        r, sz = self.r, self.sz
        start, size = sz.chunks[number]
        quarter = pl.ds(start // sz.batches, size // sz.batches)
        self.wait(self.stages[number][2])
        total = r.recv_batch[0, self.z_pos, quarter].astype(F32)
        for step in range(sz.seqs // 2 - 1):
            total = total + r.recv_z[step, quarter].astype(F32)
        part = size // sz.batches
        own = pl.ds(pl.multiple_of(start + self.batch * part, 16), part)
        r.gathered[own] = total.astype(LOW)
        self.start(self.stages[number][3])

    def run(self):
        self.entry()
        self.sums_setup()
        self.residual()
        self.attention()
        self.local_block()
        self.text_grads()
        self.early_grads()
        self.sums_core(0)
        self.attention_back()
        self.sums_batch(0)
        self.text_second()
        self.residual_back()
        self.sums_core(1)
        self.sums_core(2)
        self.sums_core(3)
        self.sums_batch(1)
        self.sums_batch(2)
        self.sums_batch(3)
        self.wait(self.text_copies)
        self.wait(self.final_copies)
        count = len(self.sz.chunks)
        for number in range(count):
            self.sums_z(number)
            if number:
                self.sums_gather(number - 1)
        self.sums_gather(count - 1)
        for number in range(count):
            self.wait(self.stages[number][3])


def fused_call(sz, operands):
    t, c = sz.tokens, sz.channels
    outs = dict(
        output=((t, c), F32),
        latent_grad=((t, c), F32),
        final_recv=((sz.batches, 8, c), F32),
        time_all=((sz.batches, 8, sz.emb), F32),
        text_all=((sz.batches, sz.text_pad, sz.context), LOW),
        text_total=((sz.batches, sz.text_pad, LANES), F32),
        gathered=((sz.pack_rows, LANES), LOW),
        kept_probs=((sz.seqs, sz.keys, t), LOW),
    )
    scratch = buffers(sz)
    vmem = pl.BlockSpec(memory_space=pltpu.VMEM)
    anywhere = pl.BlockSpec(memory_space=pl.ANY)
    fetched = [getattr(operands, name) for name in Fetched._fields]
    specs = operands._replace(**{name: vmem for name in Inputs._fields})
    specs = specs._replace(**{name: anywhere for name in Fetched._fields})
    specs = specs._replace(
        latents=anywhere, cotangent=anywhere, heights=pl.BlockSpec(memory_space=pltpu.SMEM)
    )
    names = list(Inputs._fields) + list(outs) + list(scratch)
    shapes = [pltpu.VMEM(shape, kind) for shape, kind in scratch.values()]
    shapes += [pltpu.VMEM(operand.shape, operand.dtype) for operand in fetched]
    shapes += [pltpu.SemaphoreType.DMA((2, 192)), pltpu.SemaphoreType.DMA((len(fetched) + 4,))]

    def body(*refs):
        count = len(names)
        named = types.SimpleNamespace(**dict(zip(names, refs[:count])))
        named.sems, named.local_sems = refs[-2:]
        Fused(sz, named, Fetched(*refs[count:-2])).run()

    return pl.pallas_call(
        body,
        out_shape=tuple(jax.ShapeDtypeStruct(shape, kind) for shape, kind in outs.values()),
        in_specs=list(specs),
        out_specs=(vmem,) * (len(outs) - 1) + (anywhere,),
        scratch_shapes=shapes,
        compiler_params=pltpu.CompilerParams(
            collective_id=5, has_side_effects=True, vmem_limit_bytes=63 << 20
        ),
    )(*operands)


class Outputs(typing.NamedTuple):
    output: typing.Any
    latent_grad: typing.Any
    gain_in: typing.Any
    conv_first: typing.Any
    time_weight: typing.Any
    gain_mid: typing.Any
    conv_second: typing.Any
    gain_block: typing.Any
    project_in: typing.Any
    gain_self: typing.Any
    query_self: typing.Any
    key_self: typing.Any
    value_self: typing.Any
    out_self: typing.Any
    gain_cross: typing.Any
    query_cross: typing.Any
    key_cross: typing.Any
    value_cross: typing.Any
    out_cross: typing.Any
    gain_feed: typing.Any
    feed_up: typing.Any
    feed_down: typing.Any
    project_out: typing.Any


def unpack_kernel(
    sz, output, latent_grad, final_recv, time_all, text_all, text_total, gathered, *out_refs
):
    outs = Outputs(*out_refs)
    channels = sz.channels
    outs.output[...] = output[...]
    outs.latent_grad[...] = latent_grad[...]
    eye = jnp.where(iota((LANES, LANES), 0) == iota((LANES, LANES), 1), 1.0, 0.0).astype(LOW)

    def turned(start, rows):
        return dot_nt(eye, gathered[start : start + rows])

    def three(values, *targets):
        for place, target in enumerate(targets):
            target[...] = values[place * HEAD : (place + 1) * HEAD]

    for tile in range(3):
        lanes = slice(tile * LANES, min((tile + 1) * LANES, outs.feed_up.shape[1]))
        start = sz.start.up + tile * channels
        outs.feed_up[:, lanes] = gathered[start : start + channels, : lanes.stop - lanes.start].astype(F32)
    values = turned(sz.start.down, sz.down_rows)
    for place in range(3):
        lanes = slice(place * sz.down_rows, min((place + 1) * sz.down_rows, sz.hidden))
        outs.feed_down[:, lanes] = values[
            place * HEAD : (place + 1) * HEAD, : lanes.stop - lanes.start
        ]
    three(turned(sz.start.trio, channels), outs.project_out, outs.out_cross, outs.query_cross)
    three(turned(sz.start.heads, channels), outs.query_self, outs.key_self, outs.value_self)
    outs.project_in[...] = turned(sz.start.pair, channels)[HEAD : 2 * HEAD]
    wide = turned(sz.start.pair, HEADS * sz.slot)[:HEAD].astype(LOW)
    source = iota((1, channels), 1)
    target = source + (sz.slot - HEAD) * floor_div(source, HEAD)
    squeeze = jnp.where(iota((HEADS * sz.slot, 1), 0) == target, 1.0, 0.0).astype(LOW)
    outs.out_self[...] = dot_nn(wide, squeeze)
    for start, out in ((sz.start.second, outs.conv_second), (sz.start.first, outs.conv_first)):
        for col in range(3):
            values = turned(start + col * channels, channels)
            for row in range(3):
                out[row, col] = values[row * HEAD : (row + 1) * HEAD]
    text = None
    for place in range(sz.batches):
        grads = text_total[place]
        high = grads.astype(LOW)
        rest = (grads - high.astype(F32)).astype(LOW)
        part = dot_tn(high, text_all[place]) + dot_tn(rest, text_all[place])
        text = part if text is None else text + part
    three(text, outs.key_cross, outs.value_cross)
    pick = jnp.where(
        (iota((channels, LANES), 0) == iota((channels, LANES), 1) + lax.axis_index(SEQ) * HEAD)
        & (iota((channels, LANES), 1) < HEAD),
        1.0,
        0.0,
    ).astype(LOW)
    total = time = None
    for place in range(sz.batches):
        rows = final_recv[place]
        total = rows if total is None else total + rows
        picked = dot_nn(split_three(jnp.where(iota((8, 1), 0) == 2, rows, 0.0)), pick)
        act = time_all[place]
        act = pltpu.roll(act, 2, 0)
        part = dot_tn(picked.astype(LOW), jnp.concatenate([act, act, act], axis=0).astype(LOW))
        time = part if time is None else time + part
    outs.time_weight[...] = time[:HEAD]
    gains = sum_three(dot_nn(split_three(total), pick))
    order = (
        outs.gain_mid,
        outs.gain_in,
        None,
        outs.gain_feed,
        outs.gain_cross,
        outs.gain_self,
        outs.gain_block,
    )
    for place, out in enumerate(order):
        if out is not None:
            out[...] = gains[place : place + 1, :HEAD]


def unpack_call(sz, results):
    channels, hidden = sz.channels, sz.hidden
    square = jax.ShapeDtypeStruct((HEAD, channels), F32)
    gain = jax.ShapeDtypeStruct((1, HEAD), F32)
    image = jax.ShapeDtypeStruct((sz.tokens, channels), F32)
    conv = jax.ShapeDtypeStruct((3, 3, HEAD, channels), F32)
    context = jax.ShapeDtypeStruct((HEAD, sz.context), F32)
    shapes = Outputs(*[square] * len(Outputs._fields))._replace(
        output=image,
        latent_grad=image,
        gain_in=gain,
        gain_mid=gain,
        gain_block=gain,
        gain_self=gain,
        gain_cross=gain,
        gain_feed=gain,
        conv_first=conv,
        conv_second=conv,
        time_weight=jax.ShapeDtypeStruct((HEAD, sz.emb), F32),
        key_cross=context,
        value_cross=context,
        feed_up=jax.ShapeDtypeStruct((channels, 2 * hidden // sz.seqs), F32),
        feed_down=jax.ShapeDtypeStruct((HEAD, hidden), F32),
    )
    vmem = pl.BlockSpec(memory_space=pltpu.VMEM)
    return Outputs(
        *pl.pallas_call(
            lambda *refs: unpack_kernel(sz, *refs),
            out_shape=tuple(shapes),
            in_specs=[vmem] * len(results),
            out_specs=(vmem,) * len(shapes),
            compiler_params=pltpu.CompilerParams(vmem_limit_bytes=60 << 20),
        )(*results)
    )


def fast_device(*arguments):
    given = Inputs(*arguments)
    latents = given.latents
    sz = Sizes(
        lax.axis_size(BATCH),
        lax.axis_size(SEQ),
        latents,
        given.time_vector,
        given.text_states,
        given.feed_down,
    )
    channels = sz.channels
    flat = given._replace(
        latents=latents.reshape(sz.tokens, channels),
        cotangent=given.cotangent.reshape(sz.tokens, channels),
        text_states=given.text_states.reshape(sz.text, sz.context),
        time_weight=given.time_weight.T,
        key_cross=given.key_cross.T,
        value_cross=given.value_cross.T,
        feed_down=given.feed_down.T,
    )
    results = fused_call(sz, flat)[:-1]
    outs = unpack_call(sz, results)
    shaped = outs._replace(
        output=outs.output.reshape(latents.shape), latent_grad=outs.latent_grad.reshape(latents.shape)
    )
    shaped = [jnp.swapaxes(one, -2, -1) if one.shape[-2] == HEAD else one for one in shaped]
    return tuple(one.reshape(-1) if one.shape[0] == 1 and one.ndim == 2 else one for one in shaped)


def on_device(
    latents,
    heights,
    time_vector,
    text_states,
    gain_in,
    conv_first,
    time_weight,
    gain_mid,
    conv_second,
    gain_block,
    project_in,
    gain_self,
    query_self,
    key_self,
    value_self,
    out_self,
    gain_cross,
    query_cross,
    key_cross,
    value_cross,
    out_cross,
    gain_feed,
    feed_up,
    feed_down,
    project_out,
    cotangent,
):
    images_in, rows_in, col_count, channels = latents.shape
    seq_size = lax.axis_size(SEQ)
    seq_index = lax.axis_index(SEQ)
    block_rows = rows_in * col_count
    keys_count = block_rows * seq_size
    score_scale = HEAD ** (-0.5)
    row_ids = seq_index * rows_in + jnp.arange(rows_in, dtype=jnp.int32)

    def spread_fn(values):
        return values

    def pick_fn(values):
        return values

    images, row_count = (latents.shape[0], latents.shape[1])
    tok_rows = row_count * col_count
    tokens = images * tok_rows
    row_valid = (row_ids[None, :] < heights[:, None]).astype(jnp.int32)
    row_mask = row_valid.astype(jnp.float32)
    cell_mask = row_mask[:, :, None, None]
    key_rows = jnp.arange(keys_count, dtype=jnp.int32) // col_count
    key_mask = (key_rows[None, :] < heights[:, None]).astype(jnp.int32)
    cell_counts = (heights * (col_count * (channels // GROUPS))).astype(jnp.float32)

    def res_piece(values, norm_gain, sum_first, sum_second):
        return (
            jax.nn.silu(group_apply(values, norm_gain, sum_first, sum_second, cell_counts))
            * cell_mask
        )

    def block_piece(values, norm_gain, sum_first, sum_second):
        return group_apply(values, norm_gain, sum_first, sum_second, cell_counts)

    first_in, second_in = norm_stats(latents, row_mask, spread_fn, pick_fn)
    act_in = res_piece(latents, gain_in, first_in, second_in).astype(jnp.bfloat16)
    padded_in = rows_halo(act_in)
    conv_out = conv_rows(padded_in, conv_first)
    time_act = jax.nn.silu(time_vector.astype(jnp.float32)).astype(jnp.bfloat16)
    time_term = jnp.dot(time_act, time_weight, preferred_element_type=jnp.float32)
    mid_in = conv_out + time_term[:, None, None, :]
    first_mid, second_mid = norm_stats(mid_in, row_mask, spread_fn, pick_fn)
    act_mid = res_piece(mid_in, gain_mid, first_mid, second_mid).astype(jnp.bfloat16)
    padded_mid = rows_halo(act_mid)
    resid = latents + conv_rows(padded_mid, conv_second)
    first_block, second_block = norm_stats(resid, row_mask, spread_fn, pick_fn)
    normed_block = (
        block_piece(resid, gain_block, first_block, second_block)
        .reshape(tokens, channels)
        .astype(jnp.bfloat16)
    )
    stream_in = jnp.dot(normed_block, project_in, preferred_element_type=jnp.float32)
    normed_self = layer_norm(stream_in, gain_self).astype(jnp.bfloat16)
    joined_self = jnp.concatenate((query_self, key_self, value_self), axis=1)
    projected = (
        jnp.dot(normed_self, joined_self, preferred_element_type=jnp.float32)
        .astype(jnp.bfloat16)
        .reshape(images, tok_rows, 3 * channels)
    )
    queries = projected[:, :, :channels]
    keys_local = projected[:, :, channels : 2 * channels]
    values_local = projected[:, :, 2 * channels :]
    keys_all = lax.all_gather(keys_local, SEQ, axis=1, tiled=True)
    values_all = lax.all_gather(values_local, SEQ, axis=1, tiled=True)

    def forward_image(bundle):
        image_queries, image_keys, image_values, image_mask = bundle
        query_blocks = image_queries.reshape(-1, block_rows, channels)
        return lax.map(
            lambda part: self_forward((part, image_keys, image_values, image_mask), score_scale),
            query_blocks,
        )

    attn_mixed, log_totals = lax.map(forward_image, (queries, keys_all, values_all, key_mask))
    mixed_flat = attn_mixed.reshape(tokens, channels)
    stream_self = stream_in + jnp.dot(mixed_flat, out_self, preferred_element_type=jnp.float32)
    normed_cross = layer_norm(stream_self, gain_cross).astype(jnp.bfloat16)
    query_text = (
        jnp.dot(normed_cross, query_cross, preferred_element_type=jnp.float32)
        .astype(jnp.bfloat16)
        .reshape(images, tok_rows, HEADS, HEAD)
    )
    text_flat = text_states.reshape(-1, text_states.shape[2])
    text_pairs = (
        jnp.dot(
            text_flat,
            jnp.concatenate((key_cross, value_cross), axis=1),
            preferred_element_type=jnp.float32,
        )
        .astype(jnp.bfloat16)
        .reshape(images, -1, 2, HEADS, HEAD)
    )
    text_keys = text_pairs[:, :, 0]
    text_values = text_pairs[:, :, 1]
    cross_scores = (
        jnp.einsum("iqhd,ikhd->ihqk", query_text, text_keys, preferred_element_type=jnp.float32)
        * score_scale
    )
    cross_attn = jnp.exp(cross_scores - jax.nn.logsumexp(cross_scores, axis=-1, keepdims=True))
    cross_low = cross_attn.astype(jnp.bfloat16)
    cross_mixed = (
        jnp.einsum("ihqk,ikhd->iqhd", cross_low, text_values, preferred_element_type=jnp.float32)
        .astype(jnp.bfloat16)
        .reshape(tokens, channels)
    )
    stream_cross = stream_self + jnp.dot(cross_mixed, out_cross, preferred_element_type=jnp.float32)
    normed_feed = layer_norm(stream_cross, gain_feed).astype(jnp.bfloat16)
    joined_feed = jnp.dot(normed_feed, feed_up, preferred_element_type=jnp.float32)
    gated = geglu(joined_feed).astype(jnp.bfloat16)
    stream_feed = stream_cross + jnp.dot(gated, feed_down, preferred_element_type=jnp.float32)
    stream_low = stream_feed.astype(jnp.bfloat16)
    branch_out = jnp.dot(stream_low, project_out, preferred_element_type=jnp.float32).reshape(
        images, row_count, col_count, channels
    )
    output = (resid + branch_out) * cell_mask
    grad_output = cotangent * cell_mask
    grad_branch = grad_output.reshape(tokens, channels).astype(jnp.bfloat16)
    grad_project_out = grad_dot(stream_low, grad_branch)
    grad_stream = back_dot(grad_branch, project_out)
    grad_feed_low = grad_stream.astype(jnp.bfloat16)
    grad_feed_down = grad_dot(gated, grad_feed_low)
    grad_gated = back_dot(grad_feed_low, feed_down)
    unused, pull_geglu = jax.vjp(geglu, joined_feed)
    grad_joined = pull_geglu(grad_gated)[0].astype(jnp.bfloat16)
    grad_feed_up = grad_dot(normed_feed, grad_joined)
    unused, pull_norm = jax.vjp(layer_norm, stream_cross, gain_feed)
    grad_part, grad_gain_feed = pull_norm(back_dot(grad_joined, feed_up))
    grad_stream = grad_stream + grad_part
    grad_cross_low = grad_stream.astype(jnp.bfloat16)
    grad_out_cross = grad_dot(cross_mixed, grad_cross_low)
    grad_cross_mixed = (
        back_dot(grad_cross_low, out_cross)
        .astype(jnp.bfloat16)
        .reshape(images, tok_rows, HEADS, HEAD)
    )
    grad_text_values = jnp.einsum(
        "ihqk,iqhd->ikhd", cross_low, grad_cross_mixed, preferred_element_type=jnp.float32
    )
    grad_cross_attn = jnp.einsum(
        "iqhd,ikhd->ihqk", grad_cross_mixed, text_values, preferred_element_type=jnp.float32
    )
    cross_delta = jnp.sum(cross_attn * grad_cross_attn, axis=-1, keepdims=True)
    grad_cross_scores = (cross_attn * (grad_cross_attn - cross_delta)).astype(jnp.bfloat16)
    grad_query_text = (
        (
            jnp.einsum(
                "ihqk,ikhd->iqhd", grad_cross_scores, text_keys, preferred_element_type=jnp.float32
            )
            * score_scale
        )
        .astype(jnp.bfloat16)
        .reshape(tokens, channels)
    )
    grad_text_keys = (
        jnp.einsum(
            "ihqk,iqhd->ikhd", grad_cross_scores, query_text, preferred_element_type=jnp.float32
        )
        * score_scale
    )
    text_wide = text_flat.astype(jnp.float32)
    grad_key_cross = exact_grad_dot(text_wide, grad_text_keys.reshape(-1, channels))
    grad_value_cross = exact_grad_dot(text_wide, grad_text_values.reshape(-1, channels))
    grad_query_cross = grad_dot(normed_cross, grad_query_text)
    unused, pull_norm = jax.vjp(layer_norm, stream_self, gain_cross)
    grad_part, grad_gain_cross = pull_norm(back_dot(grad_query_text, query_cross))
    grad_stream = grad_stream + grad_part
    grad_self_low = grad_stream.astype(jnp.bfloat16)
    grad_out_self = grad_dot(mixed_flat, grad_self_low)
    grad_mixed = (
        back_dot(grad_self_low, out_self).astype(jnp.bfloat16).reshape(images, tok_rows, channels)
    )

    def backward_image(bundle):
        image_queries, image_grads, image_totals, image_keys, image_values, image_mask = bundle
        query_blocks = image_queries.reshape(-1, block_rows, channels)
        grad_blocks = image_grads.reshape(-1, block_rows, channels)
        return lax.map(
            lambda part: query_side(
                (part[0], part[1], part[2], image_keys, image_values, image_mask), score_scale
            ),
            (query_blocks, grad_blocks, image_totals),
        )

    grad_queries, kept_attn, kept_grads = lax.map(
        backward_image, (queries, grad_mixed, log_totals, keys_all, values_all, key_mask)
    )
    grads_four = grad_mixed.reshape(images, -1, block_rows, HEADS, HEAD)
    queries_four = queries.reshape(images, -1, block_rows, HEADS, HEAD)
    row_total = tok_rows * lax.axis_size(SEQ)
    value_terms = jnp.einsum(
        "inhqk,inqhd->kihd", kept_attn, grads_four, preferred_element_type=jnp.float32
    )
    key_terms_part = (
        jnp.einsum(
            "inhqk,inqhd->kihd", kept_grads, queries_four, preferred_element_type=jnp.float32
        )
        * score_scale
    )
    summed = lax.psum_scatter(
        jnp.stack(
            (
                key_terms_part.reshape(row_total, images, -1),
                value_terms.reshape(row_total, images, -1),
            ),
            2,
        ).astype(jnp.bfloat16),
        SEQ,
        scatter_dimension=0,
        tiled=True,
    ).astype(jnp.float32)
    grad_keys = jnp.swapaxes(summed[:, :, 0], 0, 1)
    grad_values = jnp.swapaxes(summed[:, :, 1], 0, 1)
    grad_projected = jnp.concatenate(
        (
            grad_queries.reshape(images, tok_rows, channels),
            grad_keys.astype(jnp.bfloat16),
            grad_values.astype(jnp.bfloat16),
        ),
        axis=2,
    ).reshape(tokens, 3 * channels)
    grad_joined_self = grad_dot(normed_self, grad_projected)
    unused, pull_norm = jax.vjp(layer_norm, stream_in, gain_self)
    grad_part, grad_gain_self = pull_norm(back_dot(grad_projected, joined_self))
    grad_stream = grad_stream + grad_part
    grad_stream_low = grad_stream.astype(jnp.bfloat16)
    grad_project_in = grad_dot(normed_block, grad_stream_low)
    grad_block = back_dot(grad_stream_low, project_in).reshape(
        images, row_count, col_count, channels
    )
    grad_resid_part, grad_gain_block = norm_backward(
        block_piece,
        resid,
        gain_block,
        first_block,
        second_block,
        grad_block,
        row_mask,
        spread_fn,
        pick_fn,
    )
    grad_resid = grad_output + grad_resid_part
    grad_second_low = grad_resid.astype(jnp.bfloat16)
    grad_conv_second = conv_weight_grad(padded_mid, grad_second_low)
    grad_act_mid = conv_rows(grads_halo(grad_second_low), flipped(conv_second))
    grad_mid, grad_gain_mid = norm_backward(
        res_piece,
        mid_in,
        gain_mid,
        first_mid,
        second_mid,
        grad_act_mid,
        row_mask,
        spread_fn,
        pick_fn,
    )
    grad_time = jnp.sum(grad_mid, axis=(1, 2))
    grad_time_weight = exact_grad_dot(time_act.astype(jnp.float32), grad_time)
    grad_first_low = grad_mid.astype(jnp.bfloat16)
    grad_conv_first = conv_weight_grad(padded_in, grad_first_low)
    grad_act_in = conv_rows(grads_halo(grad_first_low), flipped(conv_first))
    grad_in_part, grad_gain_in = norm_backward(
        res_piece, latents, gain_in, first_in, second_in, grad_act_in, row_mask, spread_fn, pick_fn
    )
    latent_grad = grad_resid + grad_in_part
    shares = (
        lax.psum_scatter(
            grad_gain_in.reshape(1, -1).astype(jnp.bfloat16), SEQ, scatter_dimension=1, tiled=True
        ).astype(jnp.float32),
        lax.psum_scatter(
            grad_conv_first.reshape(-1, channels).astype(jnp.bfloat16),
            SEQ,
            scatter_dimension=1,
            tiled=True,
        ).astype(jnp.float32),
        lax.psum_scatter(
            grad_time_weight.astype(jnp.bfloat16), SEQ, scatter_dimension=1, tiled=True
        ).astype(jnp.float32),
        lax.psum_scatter(
            grad_gain_mid.reshape(1, -1).astype(jnp.bfloat16),
            SEQ,
            scatter_dimension=1,
            tiled=True,
        ).astype(jnp.float32),
        lax.psum_scatter(
            grad_conv_second.reshape(-1, channels).astype(jnp.bfloat16),
            SEQ,
            scatter_dimension=1,
            tiled=True,
        ).astype(jnp.float32),
        lax.psum_scatter(
            grad_gain_block.reshape(1, -1).astype(jnp.bfloat16),
            SEQ,
            scatter_dimension=1,
            tiled=True,
        ).astype(jnp.float32),
        lax.psum_scatter(
            grad_project_in.astype(jnp.bfloat16), SEQ, scatter_dimension=1, tiled=True
        ).astype(jnp.float32),
        lax.psum_scatter(
            grad_gain_self.reshape(1, -1).astype(jnp.bfloat16),
            SEQ,
            scatter_dimension=1,
            tiled=True,
        ).astype(jnp.float32),
        lax.psum_scatter(
            grad_joined_self[:, :channels].astype(jnp.bfloat16),
            SEQ,
            scatter_dimension=1,
            tiled=True,
        ).astype(jnp.float32),
        lax.psum_scatter(
            grad_joined_self[:, channels : 2 * channels].astype(jnp.bfloat16),
            SEQ,
            scatter_dimension=1,
            tiled=True,
        ).astype(jnp.float32),
        lax.psum_scatter(
            grad_joined_self[:, 2 * channels :].astype(jnp.bfloat16),
            SEQ,
            scatter_dimension=1,
            tiled=True,
        ).astype(jnp.float32),
        lax.psum_scatter(
            grad_out_self.astype(jnp.bfloat16), SEQ, scatter_dimension=1, tiled=True
        ).astype(jnp.float32),
        lax.psum_scatter(
            grad_gain_cross.reshape(1, -1).astype(jnp.bfloat16),
            SEQ,
            scatter_dimension=1,
            tiled=True,
        ).astype(jnp.float32),
        lax.psum_scatter(
            grad_query_cross.astype(jnp.bfloat16), SEQ, scatter_dimension=1, tiled=True
        ).astype(jnp.float32),
        lax.psum_scatter(
            grad_key_cross.astype(jnp.bfloat16), SEQ, scatter_dimension=1, tiled=True
        ).astype(jnp.float32),
        lax.psum_scatter(
            grad_value_cross.astype(jnp.bfloat16), SEQ, scatter_dimension=1, tiled=True
        ).astype(jnp.float32),
        lax.psum_scatter(
            grad_out_cross.astype(jnp.bfloat16), SEQ, scatter_dimension=1, tiled=True
        ).astype(jnp.float32),
        lax.psum_scatter(
            grad_gain_feed.reshape(1, -1).astype(jnp.bfloat16),
            SEQ,
            scatter_dimension=1,
            tiled=True,
        ).astype(jnp.float32),
        lax.psum_scatter(
            grad_feed_up.astype(jnp.bfloat16), SEQ, scatter_dimension=1, tiled=True
        ).astype(jnp.float32),
        lax.psum_scatter(
            grad_feed_down.astype(jnp.bfloat16), SEQ, scatter_dimension=1, tiled=True
        ).astype(jnp.float32),
        lax.psum_scatter(
            grad_project_out.astype(jnp.bfloat16), SEQ, scatter_dimension=1, tiled=True
        ).astype(jnp.float32),
    )
    totals = (
        lax.psum(shares[0].astype(jnp.bfloat16), BATCH).astype(jnp.float32),
        lax.psum(shares[1].astype(jnp.bfloat16), BATCH).astype(jnp.float32),
        lax.psum(shares[2].astype(jnp.bfloat16), BATCH).astype(jnp.float32),
        lax.psum(shares[3].astype(jnp.bfloat16), BATCH).astype(jnp.float32),
        lax.psum(shares[4].astype(jnp.bfloat16), BATCH).astype(jnp.float32),
        lax.psum(shares[5].astype(jnp.bfloat16), BATCH).astype(jnp.float32),
        lax.psum(shares[6].astype(jnp.bfloat16), BATCH).astype(jnp.float32),
        lax.psum(shares[7].astype(jnp.bfloat16), BATCH).astype(jnp.float32),
        lax.psum(shares[8].astype(jnp.bfloat16), BATCH).astype(jnp.float32),
        lax.psum(shares[9].astype(jnp.bfloat16), BATCH).astype(jnp.float32),
        lax.psum(shares[10].astype(jnp.bfloat16), BATCH).astype(jnp.float32),
        lax.psum(shares[11].astype(jnp.bfloat16), BATCH).astype(jnp.float32),
        lax.psum(shares[12].astype(jnp.bfloat16), BATCH).astype(jnp.float32),
        lax.psum(shares[13].astype(jnp.bfloat16), BATCH).astype(jnp.float32),
        lax.psum(shares[14].astype(jnp.bfloat16), BATCH).astype(jnp.float32),
        lax.psum(shares[15].astype(jnp.bfloat16), BATCH).astype(jnp.float32),
        lax.psum(shares[16].astype(jnp.bfloat16), BATCH).astype(jnp.float32),
        lax.psum(shares[17].astype(jnp.bfloat16), BATCH).astype(jnp.float32),
        lax.psum(shares[18].astype(jnp.bfloat16), BATCH).astype(jnp.float32),
        lax.psum(shares[19].astype(jnp.bfloat16), BATCH).astype(jnp.float32),
        lax.psum(shares[20].astype(jnp.bfloat16), BATCH).astype(jnp.float32),
    )
    return (
        output,
        latent_grad,
        totals[0].reshape(-1),
        totals[1].reshape(3, 3, channels, -1),
        totals[2],
        totals[3].reshape(-1),
        totals[4].reshape(3, 3, channels, -1),
        totals[5].reshape(-1),
        totals[6],
        totals[7].reshape(-1),
        totals[8],
        totals[9],
        totals[10],
        totals[11],
        totals[12].reshape(-1),
        totals[13],
        totals[14],
        totals[15],
        totals[16],
        totals[17].reshape(-1),
        totals[18],
        totals[19],
        totals[20],
    )


def solution(mesh):
    in_specs = (
        P(BATCH, SEQ, None, None),
        P(BATCH),
        P(BATCH, None),
        P(BATCH, None, None),
        P(),
        P(),
        P(),
        P(),
        P(),
        P(),
        P(),
        P(),
        P(),
        P(),
        P(),
        P(),
        P(),
        P(),
        P(),
        P(),
        P(),
        P(),
        P(),
        P(),
        P(),
        P(BATCH, SEQ, None, None),
    )
    out_specs = (
        P(BATCH, SEQ, None, None),
        P(BATCH, SEQ, None, None),
        P(SEQ),
        P(None, None, None, SEQ),
        P(None, SEQ),
        P(SEQ),
        P(None, None, None, SEQ),
        P(SEQ),
        P(None, SEQ),
        P(SEQ),
        P(None, SEQ),
        P(None, SEQ),
        P(None, SEQ),
        P(None, SEQ),
        P(SEQ),
        P(None, SEQ),
        P(None, SEQ),
        P(None, SEQ),
        P(None, SEQ),
        P(SEQ),
        P(None, SEQ),
        P(None, SEQ),
        P(None, SEQ),
    )
    device_fn = fast_device if mesh.shape[SEQ] == HEADS else on_device
    return jax.shard_map(
        device_fn, mesh=mesh, in_specs=in_specs, out_specs=out_specs, check_vma=False
    )
```

```python
import types
import typing

import jax
import jax.numpy as jnp
from jax import lax
from jax.experimental import pallas as pl
from jax.experimental.pallas import tpu as pltpu
from jax.sharding import PartitionSpec as P

BATCH, SEQ = "batch", "seq"
HEADS = 8
HEAD = 40
GROUPS = 32


epsilon = 1e-05
layout = ("NHWC", "HWIO", "NHWC")


def extended(block, sides, width):
    for axis, dim in sides:
        count = lax.axis_size(axis)
        forward = [(i, i + 1) for i in range(count - 1)]
        backward = [(target, source) for source, target in forward]
        low = lax.ppermute(
            lax.slice_in_dim(block, block.shape[dim] - width, None, axis=dim), axis, forward
        )
        high = lax.ppermute(lax.slice_in_dim(block, 0, width, axis=dim), axis, backward)
        block = jnp.concatenate([low, block, high], axis=dim)
    return block


def layer_norm(values, norm_gain):
    centred = values - jnp.mean(values, axis=-1, keepdims=True)
    spread = jnp.mean(centred * centred, axis=-1, keepdims=True)
    return centred * lax.rsqrt(spread + epsilon) * norm_gain


def geglu(joined):
    half_width = joined.shape[-1] // 2
    return joined[:, :half_width] * jax.nn.gelu(joined[:, half_width:], approximate=False)


def back_dot(left_side, weight):
    return lax.dot_general(
        left_side, weight, (((1,), (1,)), ((), ())), preferred_element_type=jnp.float32
    )


def grad_dot(left_side, right_side):
    return lax.dot_general(
        left_side, right_side, (((0,), (0,)), ((), ())), preferred_element_type=jnp.float32
    )


def exact_grad_dot(left_side, right_side):
    return lax.dot_general(
        left_side,
        right_side,
        (((0,), (0,)), ((), ())),
        precision=lax.Precision.HIGHEST,
        preferred_element_type=jnp.float32,
    )


def conv_rows(padded, weight):
    return lax.conv_general_dilated(
        padded,
        weight,
        (1, 1),
        ((0, 0), (1, 1)),
        dimension_numbers=layout,
        preferred_element_type=jnp.float32,
    )


def conv_weight_grad(padded, grad_output):
    row_count = grad_output.shape[1]
    col_count = grad_output.shape[2]
    padded_cols = jnp.pad(padded, ((0, 0), (0, 0), (1, 1), (0, 0)))
    flat_grad = grad_output.reshape(-1, grad_output.shape[3])
    tap_rows = []
    for shift_row in range(3):
        tap_line = []
        for shift_col in range(3):
            patch_rows = padded_cols[
                :, shift_row : shift_row + row_count, shift_col : shift_col + col_count
            ].reshape(-1, padded.shape[3])
            tap_line.append(grad_dot(patch_rows, flat_grad))
        tap_rows.append(jnp.stack(tap_line))
    return jnp.stack(tap_rows)


def flipped(weight):
    return jnp.swapaxes(weight[::-1, ::-1], 2, 3)


def group_sums(values, row_mask):
    full_shape = values.shape
    grouped = values.reshape(
        full_shape[0], full_shape[1], full_shape[2], GROUPS, full_shape[3] // GROUPS
    )
    masked = grouped * row_mask[:, :, None, None, None]
    return (jnp.sum(masked, axis=(1, 2, 4)), jnp.sum(masked * grouped, axis=(1, 2, 4)))


def group_apply(values, norm_gain, sum_first, sum_second, cell_counts):
    full_shape = values.shape
    grouped = values.reshape(
        full_shape[0], full_shape[1], full_shape[2], GROUPS, full_shape[3] // GROUPS
    )
    group_mean = sum_first / cell_counts[:, None]
    spread = sum_second / cell_counts[:, None] - group_mean * group_mean
    inverse = lax.rsqrt(spread + epsilon)
    normed = (grouped - group_mean[:, None, None, :, None]) * inverse[:, None, None, :, None]
    return normed.reshape(full_shape) * norm_gain


def norm_stats(values, row_mask, spread_fn, pick_fn):
    sum_first, sum_second = group_sums(values, row_mask)
    total_first, total_second = lax.psum((spread_fn(sum_first), spread_fn(sum_second)), SEQ)
    return (pick_fn(total_first), pick_fn(total_second))


def norm_back(grad_first, grad_second, spread_fn, pick_fn):
    total_first, total_second = lax.psum((spread_fn(grad_first), spread_fn(grad_second)), SEQ)
    return (pick_fn(total_first), pick_fn(total_second))


def rows_halo(values):
    return extended(values, ((SEQ, 1),), 1)


def grads_halo(values):
    return extended(values, ((SEQ, 1),), 1)


def norm_backward(
    piece_fn, values, norm_gain, sum_first, sum_second, grad_output, row_mask, spread_fn, pick_fn
):
    unused, pull_piece = jax.vjp(piece_fn, values, norm_gain, sum_first, sum_second)
    grad_values, grad_gain, grad_first, grad_second = pull_piece(grad_output)
    total_first, total_second = norm_back(grad_first, grad_second, spread_fn, pick_fn)
    unused, pull_sums = jax.vjp(lambda inner_vals: group_sums(inner_vals, row_mask), values)
    extra_part = pull_sums((total_first, total_second))[0]
    return (grad_values + extra_part, grad_gain)


def masked_scores(queries, keys_all, key_mask, score_scale):
    row_count = queries.shape[0]
    key_count = keys_all.shape[0]
    raw_scores = (
        jnp.einsum(
            "qhd,khd->hqk",
            queries.reshape(row_count, HEADS, HEAD),
            keys_all.reshape(key_count, HEADS, HEAD),
            preferred_element_type=jnp.float32,
        )
        * score_scale
    )
    return jnp.where(key_mask[None, None, :] > 0, raw_scores, -1e30)


def self_forward(bundle, score_scale):
    queries, keys_all, values_all, key_mask = bundle
    row_count = queries.shape[0]
    scores = masked_scores(queries, keys_all, key_mask, score_scale)
    log_total = jax.nn.logsumexp(scores, axis=-1)
    attention = jnp.exp(scores - log_total[:, :, None]).astype(jnp.bfloat16)
    attn_mixed = jnp.einsum(
        "hqk,khd->qhd",
        attention,
        values_all.reshape(keys_all.shape[0], HEADS, HEAD),
        preferred_element_type=jnp.float32,
    )
    return (attn_mixed.astype(jnp.bfloat16).reshape(row_count, -1), log_total)


def query_side(bundle, score_scale):
    queries, grad_mixed, log_total, keys_all, values_all, key_mask = bundle
    row_count = queries.shape[0]
    key_count = keys_all.shape[0]
    scores = masked_scores(queries, keys_all, key_mask, score_scale)
    attention = jnp.exp(scores - log_total[:, :, None])
    grad_attn = jnp.einsum(
        "qhd,khd->hqk",
        grad_mixed.reshape(row_count, HEADS, HEAD),
        values_all.reshape(key_count, HEADS, HEAD),
        preferred_element_type=jnp.float32,
    )
    row_delta = jnp.sum(attention * grad_attn, axis=-1)
    grad_scores = (attention * (grad_attn - row_delta[:, :, None])).astype(jnp.bfloat16)
    grad_queries = (
        jnp.einsum(
            "hqk,khd->qhd",
            grad_scores,
            keys_all.reshape(key_count, HEADS, HEAD),
            preferred_element_type=jnp.float32,
        )
        * score_scale
    )
    return (
        grad_queries.astype(jnp.bfloat16).reshape(row_count, -1),
        attention.astype(jnp.bfloat16),
        grad_scores,
    )


LANES = 128
MESH = pl.DeviceIdType.MESH
LOW = jnp.bfloat16
F32 = jnp.float32
TILE = 64


def dot_nn(left, right):
    return jnp.dot(left, right, preferred_element_type=F32)


def dot_nt(left, right):
    return lax.dot_general(left, right, (((1,), (1,)), ((), ())), preferred_element_type=F32)


def dot_tn(left, right):
    return lax.dot_general(left, right, (((0,), (0,)), ((), ())), preferred_element_type=F32)


def iota(shape, dim):
    return lax.broadcasted_iota(jnp.int32, shape, dim)


def floor_div(values, by):
    return jnp.floor((values.astype(F32) + 0.5) * (1.0 / by)).astype(jnp.int32)


def split_three(values):
    high = values.astype(LOW).astype(F32)
    rest = values - high
    middle = rest.astype(LOW).astype(F32)
    return jnp.concatenate([high, middle, rest - middle], axis=0).astype(LOW)


def sum_three(values):
    rows = values.shape[0] // 3
    return values[:rows] + values[rows : 2 * rows] + values[2 * rows :]


def row_of(ref):
    return ref[...].reshape(1, -1)


def sigmoid(values):
    return 1.0 / (1.0 + jnp.exp(-values))


def col_sum(values):
    return jnp.sum(values, axis=0, keepdims=True)


ROUNDS = 6


class Packs(typing.NamedTuple):
    up: typing.Any
    down: typing.Any
    trio: typing.Any
    pair: typing.Any
    heads: typing.Any
    second: typing.Any
    first: typing.Any


class Sizes:
    def __init__(self, mesh_batch, mesh_seq, latents, time_vector, text_states, feed_down):
        self.batches = mesh_batch
        self.seqs = mesh_seq
        self.rows = latents.shape[1]
        self.width = latents.shape[2]
        self.channels = latents.shape[3]
        self.tokens = self.rows * self.width
        self.wide = self.tokens + 2 * self.width
        self.keys = self.tokens * mesh_seq
        self.emb = time_vector.shape[1]
        self.text = text_states.shape[1]
        self.text_pad = -(-self.text // 16) * 16
        self.context = text_states.shape[2]
        self.hidden = feed_down.shape[0]
        self.slot = 48
        self.packed = HEADS * LANES
        self.down_rows = 512
        channels = self.channels
        sizes = Packs(
            up=3 * channels,
            down=self.down_rows,
            trio=channels,
            pair=HEADS * self.slot,
            heads=channels,
            second=3 * channels,
            first=3 * channels,
        )
        starts = [sum(sizes[:place]) for place in range(len(sizes))]
        self.start = Packs(*starts)
        self.pack_rows = sum(sizes)
        self.sizes = sizes
        self.chunks = [
            (0, sizes.up + sizes.down + sizes.trio),
            (self.start.pair, sizes.pair + sizes.heads),
            (self.start.second, sizes.second),
            (self.start.first, 512),
            (self.start.first + 512, sizes.first - 512),
        ]


class Inputs(typing.NamedTuple):
    latents: typing.Any
    heights: typing.Any
    time_vector: typing.Any
    text_states: typing.Any
    gain_in: typing.Any
    conv_first: typing.Any
    time_weight: typing.Any
    gain_mid: typing.Any
    conv_second: typing.Any
    gain_block: typing.Any
    project_in: typing.Any
    gain_self: typing.Any
    query_self: typing.Any
    key_self: typing.Any
    value_self: typing.Any
    out_self: typing.Any
    gain_cross: typing.Any
    query_cross: typing.Any
    key_cross: typing.Any
    value_cross: typing.Any
    out_cross: typing.Any
    gain_feed: typing.Any
    feed_up: typing.Any
    feed_down: typing.Any
    project_out: typing.Any
    cotangent: typing.Any


class Fetched(typing.NamedTuple):
    query_self: typing.Any
    key_self: typing.Any
    value_self: typing.Any
    time_weight: typing.Any
    conv_first: typing.Any
    conv_second: typing.Any
    project_in: typing.Any
    key_cross: typing.Any
    value_cross: typing.Any
    out_self: typing.Any
    query_cross: typing.Any
    out_cross: typing.Any
    feed_up: typing.Any
    feed_down: typing.Any
    project_out: typing.Any


def buffers(sz):
    c, t, w, k = sz.channels, sz.tokens, sz.wide, sz.keys
    half = sz.seqs // 2
    others = sz.batches - 1
    return dict(
        lat6=((w, c), F32),
        cot6=((w, c), F32),
        mid6=((w, c), F32),
        res6=((w, c), F32),
        gblk6=((w, c), F32),
        gact6=((w, c), F32),
        shift_in=((3, w, c), LOW),
        shift_mid=((3, w, c), LOW),
        shift_grad=((3, w, c), LOW),
        stat_send=((ROUNDS, 8, LANES), F32),
        extra_send=((8, c), F32),
        extra_recv=((sz.seqs, 8, c), F32),
        stat_recv=((ROUNDS, sz.seqs, 8, LANES), F32),
        norms=((3, 8, c), F32),
        gain_parts=((8, c), F32),
        final_send=((8, c), F32),
        group=((c, c), LOW),
        place=((3, c, sz.packed), LOW),
        wqkv=((c, sz.packed), LOW),
        osp=((HEADS * sz.slot, c), LOW),
        time_send=((8, sz.emb), F32),
        normed_block=((t, c), LOW),
        stream_in=((t, c), F32),
        normed_self=((t, c), LOW),
        qkv_send=((t, sz.packed), LOW),
        qkv=((k, LANES), LOW),
        qh=((k, LANES), LOW),
        kh=((k, LANES), LOW),
        vh=((k, sz.slot), LOW),
        vt=((sz.slot, k), LOW),
        kt=((sz.slot, k), LOW),
        scores=((max(k, 2 * sz.hidden), t), F32),
        probs=((2, k, t), LOW),
        mixed_full=((sz.seqs, sz.slot, t), F32),
        inverse=((sz.seqs, 8, t), F32),
        mixed_send=((sz.seqs, sz.slot, t), LOW),
        mixed=((HEADS * sz.slot, t), LOW),
        stream=((t, c), F32),
        centred_cross=((t, c), F32),
        scale_cross=((t, LANES), F32),
        normed_cross=((t, c), LOW),
        query_text=((t, c), LOW),
        text_rows=((2, sz.text_pad, c), F32),
        text_key=((HEADS * sz.text_pad, c), LOW),
        text_value=((HEADS * sz.text_pad, c), LOW),
        cross=((HEADS * sz.text_pad, t), F32),
        cross_low=((HEADS * sz.text_pad, t), LOW),
        cross_scores=((HEADS * sz.text_pad, t), LOW),
        cross_mixed=((t, c), LOW),
        scale_feed=((t, LANES), F32),
        normed_feed=((t, c), LOW),
        gated=((t, sz.hidden), LOW),
        grad_gated=((t, 2 * LANES), F32),
        grad_joined=((t, 2 * sz.hidden), LOW),
        stream_low=((t, c), LOW),
        grad_branch=((t, c), LOW),
        grad=((t, c), F32),
        tmp=((t, c), F32),
        grad_feed_low=((t, c), LOW),
        grad_cross_low=((t, c), LOW),
        grad_cross_mixed=((t, c), LOW),
        grad_query_text=((t, c), LOW),
        grad_self_low=((t, c), LOW),
        grad_in_low=((t, c), LOW),
        text_send=((sz.text_pad, sz.packed), LOW),
        text_recv=((sz.seqs, sz.text_pad, LANES), LOW),
        gm_send=((HEADS * sz.slot, t), LOW),
        gm=((sz.seqs, sz.slot, t), LOW),
        dscores=((k, t), LOW),
        gp=((t, sz.packed), LOW),
        pack=((sz.seqs, sz.pack_rows, LANES), LOW),
        recv_core=((half, sz.pack_rows, LANES), LOW),
        recv_batch=((others, half, sz.pack_rows // sz.batches, LANES), LOW),
        recv_z=((half - 1, sz.pack_rows // sz.batches, LANES), LOW),
    )


class Halo:
    def __init__(self, seq, last, after, before):
        self.seq, self.last, self.after, self.before = seq, last, after, before

    def start(self):
        @pl.when(self.seq < self.last)
        def _():
            self.after.start()

        @pl.when(self.seq > 0)
        def _():
            self.before.start()

    def wait(self):
        @pl.when(self.seq < self.last)
        def _():
            self.after.wait_send()
            self.before.wait_recv()

        @pl.when(self.seq > 0)
        def _():
            self.before.wait_send()
            self.after.wait_recv()


class Fused:
    def __init__(self, sz, refs, local):
        self.sz = sz
        self.r = refs
        self.v = local
        self.used = 0
        self.batch = lax.axis_index(BATCH)
        self.seq = lax.axis_index(SEQ)
        self.z_pos = self.seq // 2
        self.core = lax.rem(self.seq, 2)
        self.partner = (self.batch, self.seq + 1 - 2 * self.core)
        self.seq_others = [lax.rem(self.seq + step, sz.seqs) for step in range(1, sz.seqs)]
        self.batch_others = [lax.rem(self.batch + step, sz.batches) for step in range(1, sz.batches)]
        half = sz.seqs // 2
        self.z_others = [lax.rem(self.z_pos + step, half) for step in range(1, half)]
        self.height = refs.heights[0]
        self.scale = HEAD ** (-0.5)

    def remote(self, source, target, device, index=None):
        if index is None:
            index = self.used
            self.used += 1
        return pltpu.make_async_remote_copy(
            src_ref=source,
            dst_ref=target,
            send_sem=self.r.sems.at[0, index],
            recv_sem=self.r.sems.at[1, index],
            device_id=device,
            device_id_type=MESH,
        )

    def to_seq(self, source, target):
        return [self.remote(source(other), target, (self.batch, other)) for other in self.seq_others]

    def to_batch(self, source, target):
        return [self.remote(source, target, (other, self.seq)) for other in self.batch_others]

    def start(self, copies):
        for one in copies:
            one.start()

    def wait(self, copies):
        for one in copies:
            one.wait()

    def entry(self):
        r = self.r
        barrier = pltpu.get_barrier_semaphore()
        for other in self.seq_others:
            pl.semaphore_signal(barrier, inc=1, device_id=(self.batch, other), device_id_type=MESH)
        for other in self.batch_others:
            pl.semaphore_signal(barrier, inc=1, device_id=(other, self.seq), device_id_type=MESH)
        self.local = {}
        self.named = {id(getattr(r, name)): name for name in Fetched._fields}
        for number, name in enumerate(Fetched._fields):
            self.local[name] = pltpu.make_async_copy(
                getattr(r, name), getattr(self.v, name), r.local_sems.at[number]
            )
            self.local[name].start()
        own = pl.ds(self.sz.width, self.sz.tokens)
        self.images = [
            pltpu.make_async_copy(source, target.at[own], r.local_sems.at[len(Fetched._fields) + place])
            for place, (source, target) in enumerate(((r.latents, r.lat6), (r.cotangent, r.cot6)))
        ]
        self.start(self.images)

    def joined(self):
        barrier = pltpu.get_barrier_semaphore()
        pl.semaphore_wait(barrier, self.sz.seqs - 1 + self.sz.batches - 1)

    def weight(self, ref):
        name = self.named[id(ref)]
        if name in self.local:
            self.local.pop(name).wait()
        return getattr(self.v, name)

    def wide_row(self, start, size):
        rows = floor_div(iota((size, 1), 0) + start, self.sz.width) - 1
        return rows + self.seq * self.sz.rows

    def wide_mask(self, start, size):
        rows = self.wide_row(start, size)
        return jnp.where((rows >= 0) & (rows < self.height), 1.0, 0.0)

    def inside_mask(self, start, size):
        rows = self.wide_row(start, size)
        return jnp.where((rows >= 0) & (rows < self.sz.rows * self.sz.seqs), 1.0, 0.0)

    def chunks(self, total):
        return [(start, TILE) for start in range(0, total, TILE)]

    def halo(self, ref):
        sz, width = self.sz, self.sz.width
        after = self.remote(
            ref.at[pl.ds(sz.tokens, width)],
            ref.at[pl.ds(0, width)],
            (self.batch, jnp.minimum(self.seq + 1, sz.seqs - 1)),
        )
        before = self.remote(
            ref.at[pl.ds(width, width)],
            ref.at[pl.ds(width + sz.tokens, width)],
            (self.batch, jnp.maximum(self.seq - 1, 0)),
        )
        return Halo(self.seq, sz.seqs - 1, after, before)

    def lane_tiles(self):
        channels = self.sz.channels
        return [(start, min(LANES, channels - start)) for start in range(0, channels, LANES)]

    def stats_store(self, number, rows):
        r = self.r
        r.stat_send[number] = jnp.zeros(r.stat_send.shape[1:], F32)
        tiles = self.lane_tiles()
        for which, row in enumerate(rows):
            for place, (start, size) in enumerate(tiles):
                at = which * len(tiles) + place
                r.stat_send[number, at : at + 1, 0:size] = row[:, start : start + size]
        r.stat_recv[number, self.seq] = r.stat_send[number]

    def stats_start(self, number):
        r = self.r
        copies = self.to_seq(lambda other: r.stat_send.at[number], r.stat_recv.at[number, self.seq])
        self.start(copies)
        return copies

    def stats_total(self, number):
        r = self.r
        total = r.stat_recv[number, 0]
        for place in range(1, self.sz.seqs):
            total = total + r.stat_recv[number, place]
        tiles = self.lane_tiles()
        rows = []
        for which in range(2):
            parts = [
                total[which * len(tiles) + place : which * len(tiles) + place + 1, 0:size]
                for place, (start, size) in enumerate(tiles)
            ]
            rows.append(jnp.concatenate(parts, axis=1))
        row = iota((8, 1), 0)
        return jnp.where(row == 0, rows[0], jnp.where(row == 1, rows[1], 0.0))

    def grouped(self, rows):
        return sum_three(dot_nn(split_three(rows), self.r.group[...]))

    def count(self):
        per_row = self.sz.width * (self.sz.channels // GROUPS)
        return (self.height * per_row).astype(F32)

    def set_norm(self, number, total):
        sums = self.grouped(total) / self.count()
        mean = sums[0:1]
        spread = sums[1:2] - mean * mean
        self.r.norms[number, 0:1] = mean
        self.r.norms[number, 1:2] = lax.rsqrt(spread + epsilon)

    def norm(self, number):
        return self.r.norms[number, 0:1], self.r.norms[number, 1:2]

    def value_sums(self, ref):
        r, sz = self.r, self.sz
        first = second = None
        for start, size in self.chunks(sz.tokens):
            start += sz.width
            values = ref[start : start + size]
            masked = values * self.wide_mask(start, size)
            one, two = col_sum(masked), col_sum(masked * values)
            first = one if first is None else first + one
            second = two if second is None else second + two
        return first, second

    def shifts(self, ref, start, size, values):
        column = lax.rem(iota((size, 1), 0), self.sz.width)
        ref[1, start : start + size] = values.astype(LOW)
        left = jnp.where(column == 0, 0.0, pltpu.roll(values, 1, 0))
        ref[0, start : start + size] = left.astype(LOW)
        right = jnp.where(column == self.sz.width - 1, 0.0, pltpu.roll(values, size - 1, 0))
        ref[2, start : start + size] = right.astype(LOW)

    def activate(self, source, number, gain, target):
        mean, inverse = self.norm(number)
        factor = inverse * row_of(gain)
        for start, size in self.chunks(self.sz.wide):
            normed = (source[start : start + size] - mean) * factor
            values = normed * sigmoid(normed) * self.wide_mask(start, size)
            self.shifts(target, start, size, values)

    def conv(self, ref, weight):
        sz = self.sz
        total = None
        for row in range(3):
            for col in range(3):
                part = dot_nn(ref[col, row * sz.width : row * sz.width + sz.tokens], weight[row, col])
                total = part if total is None else total + part
        return total

    def conv_back(self, ref, weight):
        sz = self.sz
        total = None
        for row in range(3):
            for col in range(3):
                part = dot_nt(
                    ref[col, row * sz.width : row * sz.width + sz.tokens], weight[2 - row, 2 - col]
                )
                total = part if total is None else total + part
        return total

    def constants(self):
        r, sz = self.r, self.sz
        channels = sz.channels
        size = channels // GROUPS
        r.group[...] = jnp.where(
            floor_div(iota((channels, 1), 0), size) == floor_div(iota((1, channels), 1), size), 1.0, 0.0
        ).astype(LOW)
        rows = iota((channels, 1), 0)
        target = rows + (LANES - HEAD) * floor_div(rows, HEAD)
        lanes = iota((1, sz.packed), 1)
        for number in range(3):
            r.place[number] = jnp.where(lanes == target + number * HEAD, 1.0, 0.0).astype(LOW)

    def residual(self):
        r, sz = self.r, self.sz
        width, tokens = sz.width, sz.tokens
        self.constants()
        self.wait(self.images)
        for ref in (r.lat6, r.cot6, r.mid6, r.res6, r.gblk6, r.gact6):

            @pl.when(self.seq == 0)
            def _():
                ref[0:width] = jnp.zeros((width, sz.channels), F32)

            @pl.when(self.seq == sz.seqs - 1)
            def _():
                ref[width + tokens :] = jnp.zeros((width, sz.channels), F32)

        self.stats_store(0, self.value_sums(r.lat6))
        self.joined()
        halo = self.halo(r.lat6)
        halo.start()
        stats = self.stats_start(0)
        late = [self.halo(r.cot6)]
        act = r.time_vector[...].astype(F32)
        act = (act * sigmoid(act)).astype(LOW)
        r.time_send[...] = jnp.zeros(r.time_send.shape, F32)
        r.time_send[0:1] = act.astype(F32)
        r.time_all[self.batch] = r.time_send[...]
        late += self.to_batch(r.time_send, r.time_all.at[self.batch])
        r.text_all[self.batch] = jnp.zeros(r.text_all.shape[1:], LOW)
        r.text_all[self.batch, 0 : sz.text] = r.text_states[...]
        late += self.to_batch(r.text_all.at[self.batch], r.text_all.at[self.batch])
        self.start(late)
        self.late = late
        time_weight = self.weight(self.r.time_weight)
        time_term = dot_nt(jnp.broadcast_to(act, (16, sz.emb)), time_weight[...])[0:1]
        wqkv = None
        for number, name in enumerate((r.query_self, r.key_self, r.value_self)):
            part = dot_nn(self.weight(name)[...], r.place[number])
            wqkv = part if wqkv is None else wqkv + part
        r.wqkv[...] = wqkv.astype(LOW)
        halo.wait()
        self.wait(stats)
        self.set_norm(0, self.stats_total(0))
        self.activate(r.lat6, 0, r.gain_in, r.shift_in)
        r.mid6[width : width + tokens] = self.conv(r.shift_in, self.weight(self.r.conv_first)) + time_term
        halo = self.halo(r.mid6)
        halo.start()
        self.stats_store(1, self.value_sums(r.mid6))
        stats = self.stats_start(1)
        self.weight(self.r.conv_second)
        halo.wait()
        self.wait(stats)
        self.set_norm(1, self.stats_total(1))
        self.activate(r.mid6, 1, r.gain_mid, r.shift_mid)
        r.res6[width : width + tokens] = r.lat6[width : width + tokens] + self.conv(
            r.shift_mid, self.v.conv_second
        )
        halo = self.halo(r.res6)
        self.stats_store(2, self.value_sums(r.res6))
        stats = self.stats_start(2)
        halo.start()
        self.late.append(halo)
        project_in = self.weight(self.r.project_in)
        self.wait(stats)
        self.set_norm(2, self.stats_total(2))
        mean, inverse = self.norm(2)
        factor = inverse * row_of(r.gain_block)
        for start, size in self.chunks(tokens):
            values = r.res6[width + start : width + start + size]
            r.normed_block[start : start + size] = ((values - mean) * factor).astype(LOW)
        r.stream_in[...] = dot_nn(r.normed_block[...], project_in[...])
        for start, size in self.chunks(tokens):
            values = r.stream_in[start : start + size]
            centred, scale = self.layer_parts(values)
            r.normed_self[start : start + size] = (centred * scale * row_of(r.gain_self)).astype(LOW)
        r.qkv_send[...] = dot_nn(r.normed_self[...], r.wqkv[...]).astype(LOW)
        rows = pl.ds(pl.multiple_of(self.seq * tokens, tokens), tokens)
        copies = [
            self.remote(
                r.qkv_send.at[:, pl.ds(pl.multiple_of(other * LANES, LANES), LANES)],
                r.qkv.at[rows],
                (self.batch, other),
            )
            for other in self.seq_others
        ]
        self.start(copies)
        r.qkv[rows] = r.qkv_send[:, pl.ds(pl.multiple_of(self.seq * LANES, LANES), LANES)]
        self.text_start()
        self.wait(copies)

    def layer_parts(self, values):
        centred = values - jnp.mean(values, axis=-1, keepdims=True)
        spread = jnp.mean(centred * centred, axis=-1, keepdims=True)
        return centred, lax.rsqrt(spread + epsilon)

    def layer_back(self, values, grad, gain):
        centred, scale = self.layer_parts(values)
        normed = centred * scale
        scaled = grad * gain
        first = jnp.mean(scaled, axis=-1, keepdims=True)
        second = jnp.mean(scaled * normed, axis=-1, keepdims=True)
        return scale * (scaled - first - normed * second), col_sum(grad * normed)

    def text_start(self):
        r, sz = self.r, self.sz
        r.text_rows[...] = jnp.zeros(r.text_rows.shape, F32)
        for number, (name, target) in enumerate(
            ((r.key_cross, r.text_key), (r.value_cross, r.text_value))
        ):
            r.text_rows[number, 0 : sz.text] = dot_nt(r.text_states[...], self.weight(name)[...])
            rows = r.text_rows[number]
            head = floor_div(iota((1, sz.channels), 1), HEAD)
            for one in range(HEADS):
                target[one * sz.text_pad : (one + 1) * sz.text_pad] = jnp.where(
                    head == one, rows, 0.0
                ).astype(LOW)
        spread = iota((HEADS * sz.slot, 1), 0)
        source = iota((1, sz.channels), 1)
        source = source + (sz.slot - HEAD) * floor_div(source, HEAD)
        one_hot = jnp.where(spread == source, 1.0, 0.0).astype(LOW)
        r.osp[...] = dot_nn(one_hot, self.weight(self.r.out_self)[...]).astype(LOW)

    def attention(self):
        r, sz = self.r, self.sz
        keys, tokens, slot = sz.keys, sz.tokens, sz.slot
        lane_in = iota((LANES, LANES), 0)
        lane_out = iota((LANES, LANES), 1)

        def shift(by):
            return jnp.where((lane_in == lane_out + by) & (lane_out < HEAD), 1.0, 0.0).astype(LOW)

        def shift_wide(by):
            source = iota((LANES, slot), 0)
            target = iota((LANES, slot), 1)
            return jnp.where((source == target + by) & (target < HEAD), 1.0, 0.0).astype(LOW)

        def shift_rows(by):
            source = iota((slot, LANES), 1)
            target = iota((slot, LANES), 0)
            return jnp.where((source == target + by) & (target < HEAD), 1.0, 0.0).astype(LOW)

        query_out = jnp.where((lane_in + HEAD == lane_out) & (lane_in < HEAD), 1.0, 0.0).astype(LOW)
        lane = iota((1, LANES), 1)
        for start in range(0, keys, 2 * tokens):
            rows = slice(start, start + 2 * tokens)
            block = r.qkv[rows]
            valid = iota((2 * tokens, 1), 0) + start < self.height * sz.width
            r.qh[rows] = jnp.where(
                lane < HEAD, block.astype(F32), jnp.where(lane == HEAD, 1.0, 0.0)
            ).astype(LOW)
            bias = jnp.where((lane == HEAD) & jnp.logical_not(valid), -1e30, 0.0)
            r.kh[rows] = (dot_nn(block, shift(HEAD)) + bias).astype(LOW)
            ones = jnp.where((iota((1, slot), 1) >= HEAD) & (iota((1, slot), 1) < HEAD + 3), 1.0, 0.0)
            r.vh[rows] = (dot_nn(block, shift_wide(2 * HEAD)) + ones).astype(LOW)
            one_row = jnp.where(iota((slot, 1), 0) == HEAD, 1.0, 0.0)
            r.vt[:, rows] = (dot_nt(shift_rows(2 * HEAD), block) + one_row).astype(LOW)
            r.kt[:, rows] = dot_nt(shift_rows(HEAD), block).astype(LOW)
            r.qkv[rows] = dot_nn(block, query_out).astype(LOW)
        factor = self.scale * 1.4426950408889634
        base = self.used
        self.used += sz.seqs

        def send(target, step):
            return self.remote(
                r.mixed_send.at[target],
                r.mixed.at[pl.ds(pl.multiple_of(self.seq * slot, 16), slot)],
                (self.batch, target),
                base + step,
            )

        def keep(step):
            return pltpu.make_async_copy(
                r.probs.at[lax.rem(step, 2)],
                r.kept_probs.at[lax.rem(self.seq + 1 + step, sz.seqs)],
                r.local_sems.at[len(Fetched._fields) + 2 + lax.rem(step, 2)],
            )

        def block(step, carry):
            target = lax.rem(self.seq + 1 + step, sz.seqs)
            slot_now = lax.rem(step, 2)

            @pl.when(step >= 2)
            def _():
                keep(step - 2).wait()

            queries = r.qh[pl.ds(pl.multiple_of(target * tokens, tokens), tokens)]
            top = None
            for start in range(0, keys, tokens):
                scores = dot_nt(r.kh[start : start + tokens], queries)
                r.scores[start : start + tokens] = scores
                part = jnp.max(scores.reshape(tokens // 8, 8, tokens), axis=0)
                top = part if top is None else jnp.maximum(top, part)
            offset = jnp.max(top, axis=0, keepdims=True) * factor
            for start in range(0, keys, LANES):
                powers = jnp.exp2(r.scores[start : start + LANES] * factor - offset)
                r.probs[slot_now, start : start + LANES] = powers.astype(LOW)
            keep(step).start()
            sums = dot_nn(r.vt[...], r.probs[slot_now])
            inverse = 1.0 / sums[HEAD : HEAD + 1]
            mixed = jnp.where(iota((slot, 1), 0) < HEAD, sums * inverse, 0.0)
            r.mixed_full[target] = mixed
            r.mixed_send[target] = mixed.astype(LOW)
            r.inverse[target] = jnp.broadcast_to(inverse, (8, tokens))

            @pl.when(step < sz.seqs - 1)
            def _():
                send(target, step).start()

            return carry

        lax.fori_loop(0, sz.seqs, block, 0)
        keep(sz.seqs - 2).wait()
        keep(sz.seqs - 1).wait()
        self.recall(0).start()
        r.mixed[pl.ds(pl.multiple_of(self.seq * slot, 16), slot)] = r.mixed_send[self.seq]
        for step in range(sz.seqs - 1):
            send(lax.rem(self.seq + 1 + step, sz.seqs), step).wait()

    def local_block(self):
        r, sz = self.r, self.sz
        tokens, channels = sz.tokens, sz.channels
        pad = sz.text_pad
        r.stream[...] = r.stream_in[...] + dot_tn(r.mixed[...], r.osp[...])
        for start, size in self.chunks(tokens):
            rows = slice(start, start + size)
            centred, scale = self.layer_parts(r.stream[rows])
            r.normed_cross[rows] = (centred * scale * row_of(r.gain_cross)).astype(LOW)
        r.query_text[...] = dot_nn(r.normed_cross[...], self.weight(self.r.query_cross)[...]).astype(LOW)
        r.cross[...] = dot_nt(r.text_key[...], r.query_text[...])
        for head in range(HEADS):
            rows = slice(head * pad, (head + 1) * pad)
            valid = iota((pad, 1), 0) < sz.text
            scores = jnp.where(valid, r.cross[rows] * self.scale, -1e30)
            powers = jnp.exp(scores - jnp.max(scores, axis=0, keepdims=True))
            attention = powers / jnp.sum(powers, axis=0, keepdims=True)
            r.cross[rows] = attention
            r.cross_low[rows] = attention.astype(LOW)
        r.cross_mixed[...] = dot_tn(r.cross_low[...], r.text_value[...]).astype(LOW)
        r.centred_cross[...] = r.stream[...]
        r.stream[...] = r.stream[...] + dot_nn(r.cross_mixed[...], self.weight(self.r.out_cross)[...])
        for start, size in self.chunks(tokens):
            rows = slice(start, start + size)
            centred, scale = self.layer_parts(r.stream[rows])
            r.normed_feed[rows] = (centred * scale * row_of(r.gain_feed)).astype(LOW)
        feed_up = self.weight(self.r.feed_up)
        joined = r.scores
        root = 0.7071067811865476
        block = 2 * LANES
        pieces = sz.hidden // block
        for piece in range(pieces):
            for place in (piece, piece + pieces):
                joined[place * tokens : (place + 1) * tokens] = dot_nn(
                    r.normed_feed[...], feed_up[:, place * block : (place + 1) * block]
                )
            for start, size in self.chunks(tokens):
                values = joined[piece * tokens + start : piece * tokens + start + size]
                gates_at = (piece + pieces) * tokens + start
                gates = joined[gates_at : gates_at + size]
                half = 0.5 * (1.0 + lax.erf(gates * root))
                slope = half + gates * (jnp.exp(-0.5 * gates * gates) * 0.3989422804014327)
                active = gates * half
                r.gated[start : start + size, piece * block : (piece + 1) * block] = (
                    values * active
                ).astype(LOW)
                joined[piece * tokens + start : piece * tokens + start + size] = active
                joined[gates_at : gates_at + size] = values * slope

        low = (
            r.stream[...] + dot_nt(r.gated[...], self.weight(self.r.feed_down)[...])
        ).astype(LOW)
        r.stream_low[...] = low
        project_out = self.weight(self.r.project_out)
        r.tmp[...] = dot_nn(r.stream_low[...], project_out[...])
        for start, size in self.chunks(tokens):
            rows = slice(start, start + size)
            wide = slice(start + sz.width, start + sz.width + size)
            mask = self.wide_mask(start + sz.width, size)
            r.output[rows] = (r.res6[wide] + r.tmp[rows]) * mask
            r.grad_branch[rows] = (r.cot6[wide] * mask).astype(LOW)
        r.grad[...] = dot_nt(r.grad_branch[...], project_out[...])
        r.grad_feed_low[...] = r.grad[...].astype(LOW)
        for piece in range(pieces):
            lanes = slice(piece * block, (piece + 1) * block)
            gate_lanes = slice(sz.hidden + piece * block, sz.hidden + (piece + 1) * block)
            r.grad_gated[...] = dot_nn(r.grad_feed_low[...], self.v.feed_down[:, lanes])
            for start, size in self.chunks(tokens):
                rows = slice(start, start + size)
                active = joined[piece * tokens + start : piece * tokens + start + size]
                gates_at = (piece + pieces) * tokens + start
                grads = r.grad_gated[rows]
                r.grad_joined[rows, lanes] = (grads * active).astype(LOW)
                r.grad_joined[rows, gate_lanes] = (grads * joined[gates_at : gates_at + size]).astype(LOW)
        r.tmp[...] = dot_nt(r.grad_joined[...], self.v.feed_up[...])
        self.layer_step(r.stream, r.gain_feed, 3, r.grad_cross_low)
        r.grad_cross_mixed[...] = dot_nt(r.grad_cross_low[...], self.v.out_cross[...]).astype(LOW)
        r.scores[0 : HEADS * pad] = dot_nt(r.text_value[...], r.grad_cross_mixed[...])
        for head in range(HEADS):
            rows = slice(head * pad, (head + 1) * pad)
            attention = r.cross[rows]
            grads = r.scores[rows]
            delta = jnp.sum(attention * grads, axis=0, keepdims=True)
            r.cross_scores[rows] = (attention * (grads - delta)).astype(LOW)
        r.grad_query_text[...] = (
            dot_tn(r.cross_scores[...], r.text_key[...]) * self.scale
        ).astype(LOW)
        r.tmp[...] = dot_nt(r.grad_query_text[...], self.v.query_cross[...])
        self.layer_step(r.centred_cross, r.gain_cross, 4, r.grad_self_low)
        r.gm_send[...] = dot_nt(r.osp[...], r.grad_self_low[...]).astype(LOW)
        slot = sz.slot
        copies = [
            self.remote(
                r.gm_send.at[pl.ds(pl.multiple_of(other * slot, 16), slot)],
                r.gm.at[self.seq],
                (self.batch, other),
            )
            for other in self.seq_others
        ]
        self.start(copies)
        self.gm_copies = copies
        r.gm[self.seq] = r.gm_send[pl.ds(pl.multiple_of(self.seq * slot, 16), slot)]

    def layer_step(self, source, gain, place, target):
        r = self.r
        gains = None
        for start, size in self.chunks(self.sz.tokens):
            rows = slice(start, start + size)
            part, gain_part = self.layer_back(source[rows], r.tmp[rows], row_of(gain))
            total = r.grad[rows] + part
            r.grad[rows] = total
            target[rows] = total.astype(LOW)
            gains = gain_part if gains is None else gains + gain_part
        r.gain_parts[place : place + 1] = gains

    def text_grads(self):
        r, sz = self.r, self.sz
        pad = sz.text_pad
        head_of = floor_div(iota((1, sz.channels), 1), HEAD)
        keys = dot_nn(r.cross_scores[...], r.query_text[...]) * self.scale
        values = dot_nn(r.cross_low[...], r.grad_cross_mixed[...])
        packed = None
        for number, grads in enumerate((keys, values)):
            total = None
            for head in range(HEADS):
                part = jnp.where(head_of == head, grads[head * pad : (head + 1) * pad], 0.0)
                total = part if total is None else total + part
            part = dot_nn(total.astype(LOW), r.place[number])
            packed = part if packed is None else packed + part
        r.text_send[...] = packed.astype(LOW)
        copies = [
            self.remote(
                r.text_send.at[:, pl.ds(pl.multiple_of(other * LANES, LANES), LANES)],
                r.text_recv.at[self.seq],
                (self.batch, other),
            )
            for other in self.seq_others
        ]
        self.start(copies)
        r.text_recv[self.seq] = r.text_send[
            :, pl.ds(pl.multiple_of(self.seq * LANES, LANES), LANES)
        ]
        self.text_copies = copies

    def text_second(self):
        r = self.r
        self.wait(self.text_copies)
        total = r.text_recv[0].astype(F32)
        for place in range(1, self.sz.seqs):
            total = total + r.text_recv[place].astype(F32)
        r.text_total[self.batch] = total
        copies = self.to_batch(r.text_total.at[self.batch], r.text_total.at[self.batch])
        self.start(copies)
        self.text_copies = copies

    def store_pack(self, start, rows, values):
        for shard in range(self.sz.seqs):
            self.r.pack[shard, start + rows.start : start + rows.stop] = values[
                :, shard * LANES : (shard + 1) * LANES
            ].astype(LOW)

    def early_grads(self):
        r, sz = self.r, self.sz
        channels = sz.channels
        rows = iota((2 * channels, 1), 0)
        target = jnp.where(rows >= channels, rows + (3 * LANES - channels), rows)
        spread = jnp.where(iota((1, 6 * LANES), 1) == target, 1.0, 0.0).astype(LOW)
        for z in range(sz.seqs // 2):
            wide = 2 * channels
            grads = dot_nn(r.grad_joined[:, z * wide : (z + 1) * wide], spread).astype(LOW)
            sums = dot_tn(r.normed_feed[...], grads)
            for tile in range(6):
                start = sz.start.up + (tile % 3) * channels
                r.pack[2 * z + tile // 3, start : start + channels] = sums[
                    :, tile * LANES : (tile + 1) * LANES
                ].astype(LOW)
        size = sz.down_rows
        tail = sz.hidden - 2 * size
        placed = [dot_nn(r.grad_feed_low[...], r.place[number]).astype(LOW) for number in range(3)]
        sums = dot_tn(r.gated[:, 0:size], placed[0]) + dot_tn(r.gated[:, size : 2 * size], placed[1])
        extra = dot_tn(r.gated[:, 2 * size :], placed[2])
        self.store_pack(sz.start.down, slice(0, tail), sums[0:tail] + extra)
        self.store_pack(sz.start.down, slice(tail, size), sums[tail:])
        sums = (
            dot_tn(r.stream_low[...], dot_nn(r.grad_branch[...], r.place[0]).astype(LOW))
            + dot_tn(r.cross_mixed[...], dot_nn(r.grad_cross_low[...], r.place[1]).astype(LOW))
            + dot_tn(r.normed_cross[...], dot_nn(r.grad_query_text[...], r.place[2]).astype(LOW))
        )
        self.store_pack(sz.start.trio, slice(0, channels), sums)

    def recall(self, step):
        r = self.r
        return pltpu.make_async_copy(
            r.kept_probs.at[lax.rem(self.seq + step, self.sz.seqs)],
            r.probs.at[lax.rem(step, 2)],
            r.local_sems.at[len(Fetched._fields) + 2 + lax.rem(step, 2)],
        )

    def attention_back(self):
        r, sz = self.r, self.sz
        keys, tokens, slot = sz.keys, sz.tokens, sz.slot
        self.wait(self.gm_copies)
        r.scores[0:keys, 0:LANES] = jnp.zeros((keys, LANES), F32)
        row = iota((slot, 1), 0)
        to_lanes = jnp.where(
            (iota((slot, LANES), 0) == iota((slot, LANES), 1)) & (iota((slot, LANES), 0) < HEAD), 1.0, 0.0
        ).astype(LOW)
        to_values = jnp.where(
            (iota((slot, LANES), 0) + 2 * HEAD == iota((slot, LANES), 1))
            & (iota((slot, LANES), 0) < HEAD),
            1.0,
            0.0,
        ).astype(LOW)

        def block(step, carry):
            source = lax.rem(self.seq + step, sz.seqs)
            slot_now = lax.rem(step, 2)
            self.recall(step).wait()

            @pl.when(step < sz.seqs - 1)
            def _():
                self.recall(step + 1).start()

            scaled = (r.gm[source].astype(F32) * r.inverse[source, 0:1]).astype(LOW).astype(F32)
            delta = -jnp.sum(r.mixed_full[source] * scaled, axis=0, keepdims=True)
            high = delta.astype(LOW).astype(F32)
            middle = (delta - high).astype(LOW).astype(F32)
            rest = delta - high - middle
            extended = jnp.where(row == HEAD, high, scaled)
            extended = jnp.where(row == HEAD + 1, middle, extended)
            extended = jnp.where(row == HEAD + 2, rest, extended).astype(LOW)
            for start in range(0, keys, tokens):
                rows = slice(start, start + tokens)
                grads = dot_nn(r.vh[rows], extended)
                r.dscores[rows] = (r.probs[slot_now, rows].astype(F32) * grads).astype(LOW)
            query_rows = pl.ds(pl.multiple_of(source * tokens, tokens), tokens)
            grad_query = (dot_nn(r.kt[...], r.dscores[...]) * self.scale).astype(LOW)
            r.kh[query_rows] = dot_tn(grad_query, to_lanes).astype(LOW)
            token_grads = dot_tn(scaled.astype(LOW), to_values).astype(LOW)
            queries = r.qkv[query_rows]
            for start in range(0, keys, tokens):
                rows = slice(start, start + tokens)
                r.scores[rows, 0:LANES] += dot_nn(r.dscores[rows], queries) + dot_nn(
                    r.probs[slot_now, rows], token_grads
                )
            return carry

        lax.fori_loop(0, sz.seqs // 2, block, 0)
        self.sums_batch(0)
        lax.fori_loop(sz.seqs // 2, sz.seqs, block, 0)
        factor = jnp.where(iota((1, LANES), 1) < 2 * HEAD, self.scale, 1.0)
        for place in range(sz.seqs):
            rows = slice(place * tokens, (place + 1) * tokens)
            grads = r.scores[rows, 0:LANES] * factor
            r.qh[rows] = (grads + r.kh[rows].astype(F32)).astype(LOW)
        lanes = pl.ds(pl.multiple_of(self.seq * LANES, LANES), LANES)
        copies = [
            self.remote(
                r.qh.at[pl.ds(pl.multiple_of(other * tokens, tokens), tokens)],
                r.gp.at[:, lanes],
                (self.batch, other),
            )
            for other in self.seq_others
        ]
        self.start(copies)
        r.gp[:, lanes] = r.qh[pl.ds(pl.multiple_of(self.seq * tokens, tokens), tokens)]
        self.gp_copies = copies

    def norm_sums(self, number, rows_of):
        first = second = None
        mean, inverse = self.norm(number)
        for start, size in self.chunks(self.sz.tokens):
            grads, values = rows_of(start, size)
            one, two = col_sum(grads), col_sum(grads * ((values - mean) * inverse))
            first = one if first is None else first + one
            second = two if second is None else second + two
        return first, second

    def norm_factors(self, number, gain, total):
        gains = row_of(gain)
        sums = self.grouped(total * gains) / self.count()
        mean, inverse = self.norm(number)
        return mean, inverse, gains * inverse, sums[0:1] * inverse, sums[1:2] * inverse

    def slope(self, source, number, gain, start, size):
        mean, inverse = self.norm(number)
        normed = (source[start : start + size] - mean) * inverse
        values = normed * row_of(gain)
        gate = sigmoid(values)
        return normed, gate * (1.0 + values * (1.0 - gate)) * self.wide_mask(start, size)

    def residual_back(self):
        r, sz = self.r, self.sz
        width, tokens, channels = sz.width, sz.tokens, sz.channels
        self.wait(self.gp_copies)
        r.tmp[...] = dot_nt(r.gp[...], r.wqkv[...])
        self.layer_step(r.stream_in, r.gain_self, 5, r.grad_in_low)
        r.gblk6[width : width + tokens] = dot_nt(r.grad_in_low[...], self.v.project_in[...])
        halo = self.halo(r.gblk6)
        halo.start()

        def block_rows(start, size):
            wide = slice(start + width, start + width + size)
            return r.gblk6[wide], r.res6[wide]

        self.stats_store(3, self.norm_sums(2, block_rows))
        stats = self.stats_start(3)
        self.wait(self.late)
        self.late = []
        self.middle_grads()
        self.sums_core(1)
        halo.wait()
        self.wait(stats)
        total = self.stats_total(3)
        r.gain_parts[2:3] = total[1:2]
        mean, inverse, factor, first, second = self.norm_factors(2, r.gain_block, total)
        for start, size in self.chunks(sz.wide):
            rows = slice(start, start + size)
            mask = self.wide_mask(start, size)
            normed = (r.res6[rows] - mean) * inverse
            grads = r.cot6[rows] * mask + r.gblk6[rows] * factor - mask * (first + normed * second)
            r.cot6[rows] = grads
            self.shifts(r.shift_grad, start, size, grads * self.inside_mask(start, size))
        r.gact6[width : width + tokens] = self.conv_back(r.shift_grad, self.v.conv_second)
        halo = self.halo(r.gact6)
        halo.start()

        def mid_rows(start, size):
            wide = slice(start + width, start + width + size)
            normed, slope = self.slope(r.mid6, 1, r.gain_mid, start + width, size)
            return r.gact6[wide] * slope, r.mid6[wide]

        self.stats_store(4, self.norm_sums(1, mid_rows))
        stats = self.stats_start(4)
        self.sums_z(0)
        self.sums_batch(1)
        self.conv_grads(sz.start.second, r.shift_mid, r.shift_grad)
        self.sums_core(2)
        halo.wait()
        self.wait(stats)
        total = self.stats_total(4)
        r.gain_parts[1:2] = total[1:2]
        mean, inverse, factor, first, second = self.norm_factors(1, r.gain_mid, total)
        time_total = None
        for start, size in self.chunks(sz.wide):
            rows = slice(start, start + size)
            normed, slope = self.slope(r.mid6, 1, r.gain_mid, start, size)
            grads = r.gact6[rows] * slope * factor - self.wide_mask(start, size) * (
                first + normed * second
            )
            self.shifts(r.shift_grad, start, size, grads)
            if width <= start < width + tokens:
                part = col_sum(grads)
                time_total = part if time_total is None else time_total + part
        self.conv_grads(sz.start.first, r.shift_in, r.shift_grad)
        self.sums_core(3)
        self.sums_core(4)
        self.sums_batch(2)
        r.gblk6[width : width + tokens] = self.conv_back(r.shift_grad, self.v.conv_first)

        def in_rows(start, size):
            wide = slice(start + width, start + width + size)
            normed, slope = self.slope(r.lat6, 0, r.gain_in, start + width, size)
            return r.gblk6[wide] * slope, r.lat6[wide]

        parts = r.gain_parts
        self.stats_store(5, self.norm_sums(0, in_rows))
        stats = self.stats_start(5)
        r.extra_send[...] = jnp.zeros(r.extra_send.shape, F32)
        r.extra_send[2:3] = time_total
        r.extra_send[3:6] = parts[3:6]
        r.extra_recv[self.seq] = r.extra_send[...]
        extras = self.to_seq(lambda other: r.extra_send, r.extra_recv.at[self.seq])
        self.start(extras)
        self.sums_batch(3)
        self.sums_batch(4)
        self.wait(stats)
        total = self.stats_total(5)
        mean, inverse, factor, first, second = self.norm_factors(0, r.gain_in, total)
        self.wait(extras)
        sums = r.extra_recv[0]
        for place in range(1, sz.seqs):
            sums = sums + r.extra_recv[place]
        r.final_send[...] = sums
        r.final_send[1:2] = total[1:2]
        r.final_send[0:1] = parts[1:2]
        r.final_send[6:7] = parts[2:3]
        r.final_recv[self.batch] = r.final_send[...]
        self.final_copies = self.to_batch(r.final_send, r.final_recv.at[self.batch])
        self.start(self.final_copies)
        for start, size in self.chunks(tokens):
            wide = slice(start + width, start + width + size)
            normed, slope = self.slope(r.lat6, 0, r.gain_in, start + width, size)
            r.latent_grad[start : start + size] = (
                r.cot6[wide]
                + r.gblk6[wide] * slope * factor
                - self.wide_mask(start + width, size) * (first + normed * second)
            )

    def middle_grads(self):
        r, sz = self.r, self.sz
        self.store_pack(sz.start.heads, slice(0, sz.channels), dot_tn(r.normed_self[...], r.gp[...]))
        outer = dot_nn(r.mixed[...], dot_nn(r.grad_self_low[...], r.place[0]).astype(LOW))
        inner = dot_tn(r.normed_block[...], dot_nn(r.grad_in_low[...], r.place[1]).astype(LOW))
        self.store_pack(sz.start.pair, slice(0, sz.channels), outer[0 : sz.channels] + inner)
        self.store_pack(sz.start.pair, slice(sz.channels, HEADS * sz.slot), outer[sz.channels :])

    def conv_grads(self, pack_start, shifted, grads):
        r, sz = self.r, self.sz
        own = grads[1, sz.width : sz.width + sz.tokens]
        placed = [dot_nn(own, r.place[number]).astype(LOW) for number in range(3)]
        for col in range(3):
            total = None
            for row in range(3):
                start = row * sz.width
                part = dot_tn(shifted[col, start : start + sz.tokens], placed[row])
                total = part if total is None else total + part
            self.store_pack(pack_start, slice(col * sz.channels, (col + 1) * sz.channels), total)

    def sums_setup(self):
        r, sz = self.r, self.sz
        half, batches = sz.seqs // 2, sz.batches
        self.stages = []
        for start, size in sz.chunks:
            rows = pl.ds(start, size)
            part = size // batches
            quarter = pl.ds(start // batches, part)
            one = [
                self.remote(r.pack.at[2 * z + 1 - self.core, rows], r.recv_core.at[z, rows], self.partner)
                for z in range(half)
            ]
            two = [
                self.remote(
                    r.recv_core.at[:, pl.ds(pl.multiple_of(start + other * part, 16), part)],
                    r.recv_batch.at[step, :, quarter],
                    (other, self.seq),
                )
                for step, other in enumerate(self.batch_others)
            ]
            three = [
                self.remote(
                    r.recv_batch.at[0, other, quarter],
                    r.recv_z.at[step, quarter],
                    (self.batch, other * 2 + self.core),
                )
                for step, other in enumerate(self.z_others)
            ]
            four = [
                self.remote(
                    r.gathered.at[pl.ds(pl.multiple_of(start + self.batch * part, 16), part)],
                    r.gathered.at[pl.ds(pl.multiple_of(start + self.batch * part, 16), part)],
                    (other, self.seq),
                )
                for other in self.batch_others
            ]
            self.stages.append((one, two, three, four))

    def sums_core(self, number):
        self.start(self.stages[number][0])

    def sums_batch(self, number):
        r, sz = self.r, self.sz
        start, size = sz.chunks[number]
        self.wait(self.stages[number][0])

        @pl.loop(0, sz.seqs // 2)
        def add(z):
            rows = pl.ds(start, size)
            r.recv_core[z, rows] = (
                r.pack[2 * z + self.core, rows].astype(F32) + r.recv_core[z, rows].astype(F32)
            ).astype(LOW)

        self.start(self.stages[number][1])

    def sums_z(self, number):
        r, sz = self.r, self.sz
        start, size = sz.chunks[number]
        part = size // sz.batches
        quarter = pl.ds(start // sz.batches, part)
        self.wait(self.stages[number][1])

        @pl.loop(0, sz.seqs // 2)
        def add(z):
            total = r.recv_core[z, pl.ds(pl.multiple_of(start + self.batch * part, 16), part)].astype(F32)
            for step in range(sz.batches - 1):
                total = total + r.recv_batch[step, z, quarter].astype(F32)
            r.recv_batch[0, z, quarter] = total.astype(LOW)

        self.start(self.stages[number][2])

    def sums_gather(self, number):
        r, sz = self.r, self.sz
        start, size = sz.chunks[number]
        quarter = pl.ds(start // sz.batches, size // sz.batches)
        self.wait(self.stages[number][2])
        total = r.recv_batch[0, self.z_pos, quarter].astype(F32)
        for step in range(sz.seqs // 2 - 1):
            total = total + r.recv_z[step, quarter].astype(F32)
        part = size // sz.batches
        own = pl.ds(pl.multiple_of(start + self.batch * part, 16), part)
        r.gathered[own] = total.astype(LOW)
        self.start(self.stages[number][3])

    def run(self):
        self.entry()
        self.sums_setup()
        self.residual()
        self.attention()
        self.local_block()
        self.text_grads()
        self.early_grads()
        self.sums_core(0)
        self.attention_back()
        self.text_second()
        self.residual_back()
        self.sums_gather(0)
        last = len(self.sz.chunks) - 1
        for number in range(1, last + 1):
            self.sums_z(number)
            if number > 1:
                self.sums_gather(number - 1)
        self.sums_gather(last)
        for stages in self.stages:
            self.wait(stages[3])
        self.wait(self.text_copies)
        self.wait(self.final_copies)


def fused_call(sz, operands):
    t, c = sz.tokens, sz.channels
    outs = dict(
        output=((t, c), F32),
        latent_grad=((t, c), F32),
        final_recv=((sz.batches, 8, c), F32),
        time_all=((sz.batches, 8, sz.emb), F32),
        text_all=((sz.batches, sz.text_pad, sz.context), LOW),
        text_total=((sz.batches, sz.text_pad, LANES), F32),
        gathered=((sz.pack_rows, LANES), LOW),
        kept_probs=((sz.seqs, sz.keys, t), LOW),
    )
    scratch = buffers(sz)
    vmem = pl.BlockSpec(memory_space=pltpu.VMEM)
    anywhere = pl.BlockSpec(memory_space=pl.ANY)
    fetched = [getattr(operands, name) for name in Fetched._fields]
    specs = operands._replace(**{name: vmem for name in Inputs._fields})
    specs = specs._replace(**{name: anywhere for name in Fetched._fields})
    specs = specs._replace(
        latents=anywhere, cotangent=anywhere, heights=pl.BlockSpec(memory_space=pltpu.SMEM)
    )
    names = list(Inputs._fields) + list(outs) + list(scratch)
    shapes = [pltpu.VMEM(shape, kind) for shape, kind in scratch.values()]
    shapes += [pltpu.VMEM(operand.shape, operand.dtype) for operand in fetched]
    shapes += [pltpu.SemaphoreType.DMA((2, 192)), pltpu.SemaphoreType.DMA((len(fetched) + 4,))]

    def body(*refs):
        count = len(names)
        named = types.SimpleNamespace(**dict(zip(names, refs[:count])))
        named.sems, named.local_sems = refs[-2:]
        Fused(sz, named, Fetched(*refs[count:-2])).run()

    return pl.pallas_call(
        body,
        out_shape=tuple(jax.ShapeDtypeStruct(shape, kind) for shape, kind in outs.values()),
        in_specs=list(specs),
        out_specs=(vmem,) * (len(outs) - 1) + (anywhere,),
        scratch_shapes=shapes,
        compiler_params=pltpu.CompilerParams(
            collective_id=5, has_side_effects=True, vmem_limit_bytes=63 << 20
        ),
    )(*operands)


class Outputs(typing.NamedTuple):
    output: typing.Any
    latent_grad: typing.Any
    gain_in: typing.Any
    conv_first: typing.Any
    time_weight: typing.Any
    gain_mid: typing.Any
    conv_second: typing.Any
    gain_block: typing.Any
    project_in: typing.Any
    gain_self: typing.Any
    query_self: typing.Any
    key_self: typing.Any
    value_self: typing.Any
    out_self: typing.Any
    gain_cross: typing.Any
    query_cross: typing.Any
    key_cross: typing.Any
    value_cross: typing.Any
    out_cross: typing.Any
    gain_feed: typing.Any
    feed_up: typing.Any
    feed_down: typing.Any
    project_out: typing.Any


def unpack_kernel(
    sz, output, latent_grad, final_recv, time_all, text_all, text_total, gathered, *out_refs
):
    outs = Outputs(*out_refs)
    channels = sz.channels
    outs.output[...] = output[...]
    outs.latent_grad[...] = latent_grad[...]
    eye = jnp.where(iota((LANES, LANES), 0) == iota((LANES, LANES), 1), 1.0, 0.0).astype(LOW)

    def turned(start, rows):
        return dot_nt(eye, gathered[start : start + rows])

    def three(values, *targets):
        for place, target in enumerate(targets):
            target[...] = values[place * HEAD : (place + 1) * HEAD]

    for tile in range(3):
        lanes = slice(tile * LANES, min((tile + 1) * LANES, outs.feed_up.shape[1]))
        start = sz.start.up + tile * channels
        outs.feed_up[:, lanes] = gathered[start : start + channels, : lanes.stop - lanes.start].astype(F32)
    values = turned(sz.start.down, sz.down_rows)
    for place in range(3):
        lanes = slice(place * sz.down_rows, min((place + 1) * sz.down_rows, sz.hidden))
        outs.feed_down[:, lanes] = values[
            place * HEAD : (place + 1) * HEAD, : lanes.stop - lanes.start
        ]
    three(turned(sz.start.trio, channels), outs.project_out, outs.out_cross, outs.query_cross)
    three(turned(sz.start.heads, channels), outs.query_self, outs.key_self, outs.value_self)
    outs.project_in[...] = turned(sz.start.pair, channels)[HEAD : 2 * HEAD]
    wide = turned(sz.start.pair, HEADS * sz.slot)[:HEAD].astype(LOW)
    source = iota((1, channels), 1)
    target = source + (sz.slot - HEAD) * floor_div(source, HEAD)
    squeeze = jnp.where(iota((HEADS * sz.slot, 1), 0) == target, 1.0, 0.0).astype(LOW)
    outs.out_self[...] = dot_nn(wide, squeeze)
    for start, out in ((sz.start.second, outs.conv_second), (sz.start.first, outs.conv_first)):
        for col in range(3):
            values = turned(start + col * channels, channels)
            for row in range(3):
                out[row, col] = values[row * HEAD : (row + 1) * HEAD]
    text = None
    for place in range(sz.batches):
        grads = text_total[place]
        high = grads.astype(LOW)
        rest = (grads - high.astype(F32)).astype(LOW)
        part = dot_tn(high, text_all[place]) + dot_tn(rest, text_all[place])
        text = part if text is None else text + part
    three(text, outs.key_cross, outs.value_cross)
    pick = jnp.where(
        (iota((channels, LANES), 0) == iota((channels, LANES), 1) + lax.axis_index(SEQ) * HEAD)
        & (iota((channels, LANES), 1) < HEAD),
        1.0,
        0.0,
    ).astype(LOW)
    total = time = None
    for place in range(sz.batches):
        rows = final_recv[place]
        total = rows if total is None else total + rows
        picked = dot_nn(split_three(jnp.where(iota((8, 1), 0) == 2, rows, 0.0)), pick)
        act = time_all[place]
        act = pltpu.roll(act, 2, 0)
        part = dot_tn(picked.astype(LOW), jnp.concatenate([act, act, act], axis=0).astype(LOW))
        time = part if time is None else time + part
    outs.time_weight[...] = time[:HEAD]
    gains = sum_three(dot_nn(split_three(total), pick))
    order = (
        outs.gain_mid,
        outs.gain_in,
        None,
        outs.gain_feed,
        outs.gain_cross,
        outs.gain_self,
        outs.gain_block,
    )
    for place, out in enumerate(order):
        if out is not None:
            out[...] = gains[place : place + 1, :HEAD]


def unpack_call(sz, results):
    channels, hidden = sz.channels, sz.hidden
    square = jax.ShapeDtypeStruct((HEAD, channels), F32)
    gain = jax.ShapeDtypeStruct((1, HEAD), F32)
    image = jax.ShapeDtypeStruct((sz.tokens, channels), F32)
    conv = jax.ShapeDtypeStruct((3, 3, HEAD, channels), F32)
    context = jax.ShapeDtypeStruct((HEAD, sz.context), F32)
    shapes = Outputs(*[square] * len(Outputs._fields))._replace(
        output=image,
        latent_grad=image,
        gain_in=gain,
        gain_mid=gain,
        gain_block=gain,
        gain_self=gain,
        gain_cross=gain,
        gain_feed=gain,
        conv_first=conv,
        conv_second=conv,
        time_weight=jax.ShapeDtypeStruct((HEAD, sz.emb), F32),
        key_cross=context,
        value_cross=context,
        feed_up=jax.ShapeDtypeStruct((channels, 2 * hidden // sz.seqs), F32),
        feed_down=jax.ShapeDtypeStruct((HEAD, hidden), F32),
    )
    vmem = pl.BlockSpec(memory_space=pltpu.VMEM)
    return Outputs(
        *pl.pallas_call(
            lambda *refs: unpack_kernel(sz, *refs),
            out_shape=tuple(shapes),
            in_specs=[vmem] * len(results),
            out_specs=(vmem,) * len(shapes),
            compiler_params=pltpu.CompilerParams(vmem_limit_bytes=60 << 20),
        )(*results)
    )


def fast_device(*arguments):
    given = Inputs(*arguments)
    latents = given.latents
    sz = Sizes(
        lax.axis_size(BATCH),
        lax.axis_size(SEQ),
        latents,
        given.time_vector,
        given.text_states,
        given.feed_down,
    )
    channels = sz.channels
    flat = given._replace(
        latents=latents.reshape(sz.tokens, channels),
        cotangent=given.cotangent.reshape(sz.tokens, channels),
        text_states=given.text_states.reshape(sz.text, sz.context),
        time_weight=given.time_weight.T,
        key_cross=given.key_cross.T,
        value_cross=given.value_cross.T,
        feed_down=given.feed_down.T,
    )
    results = fused_call(sz, flat)[:-1]
    outs = unpack_call(sz, results)
    shaped = outs._replace(
        output=outs.output.reshape(latents.shape), latent_grad=outs.latent_grad.reshape(latents.shape)
    )
    shaped = [jnp.swapaxes(one, -2, -1) if one.shape[-2] == HEAD else one for one in shaped]
    return tuple(one.reshape(-1) if one.shape[0] == 1 and one.ndim == 2 else one for one in shaped)


def on_device(
    latents,
    heights,
    time_vector,
    text_states,
    gain_in,
    conv_first,
    time_weight,
    gain_mid,
    conv_second,
    gain_block,
    project_in,
    gain_self,
    query_self,
    key_self,
    value_self,
    out_self,
    gain_cross,
    query_cross,
    key_cross,
    value_cross,
    out_cross,
    gain_feed,
    feed_up,
    feed_down,
    project_out,
    cotangent,
):
    images_in, rows_in, col_count, channels = latents.shape
    seq_size = lax.axis_size(SEQ)
    seq_index = lax.axis_index(SEQ)
    block_rows = rows_in * col_count
    keys_count = block_rows * seq_size
    score_scale = HEAD ** (-0.5)
    row_ids = seq_index * rows_in + jnp.arange(rows_in, dtype=jnp.int32)

    def spread_fn(values):
        return values

    def pick_fn(values):
        return values

    images, row_count = (latents.shape[0], latents.shape[1])
    tok_rows = row_count * col_count
    tokens = images * tok_rows
    row_valid = (row_ids[None, :] < heights[:, None]).astype(jnp.int32)
    row_mask = row_valid.astype(jnp.float32)
    cell_mask = row_mask[:, :, None, None]
    key_rows = jnp.arange(keys_count, dtype=jnp.int32) // col_count
    key_mask = (key_rows[None, :] < heights[:, None]).astype(jnp.int32)
    cell_counts = (heights * (col_count * (channels // GROUPS))).astype(jnp.float32)

    def res_piece(values, norm_gain, sum_first, sum_second):
        return (
            jax.nn.silu(group_apply(values, norm_gain, sum_first, sum_second, cell_counts))
            * cell_mask
        )

    def block_piece(values, norm_gain, sum_first, sum_second):
        return group_apply(values, norm_gain, sum_first, sum_second, cell_counts)

    first_in, second_in = norm_stats(latents, row_mask, spread_fn, pick_fn)
    act_in = res_piece(latents, gain_in, first_in, second_in).astype(jnp.bfloat16)
    padded_in = rows_halo(act_in)
    conv_out = conv_rows(padded_in, conv_first)
    time_act = jax.nn.silu(time_vector.astype(jnp.float32)).astype(jnp.bfloat16)
    time_term = jnp.dot(time_act, time_weight, preferred_element_type=jnp.float32)
    mid_in = conv_out + time_term[:, None, None, :]
    first_mid, second_mid = norm_stats(mid_in, row_mask, spread_fn, pick_fn)
    act_mid = res_piece(mid_in, gain_mid, first_mid, second_mid).astype(jnp.bfloat16)
    padded_mid = rows_halo(act_mid)
    resid = latents + conv_rows(padded_mid, conv_second)
    first_block, second_block = norm_stats(resid, row_mask, spread_fn, pick_fn)
    normed_block = (
        block_piece(resid, gain_block, first_block, second_block)
        .reshape(tokens, channels)
        .astype(jnp.bfloat16)
    )
    stream_in = jnp.dot(normed_block, project_in, preferred_element_type=jnp.float32)
    normed_self = layer_norm(stream_in, gain_self).astype(jnp.bfloat16)
    joined_self = jnp.concatenate((query_self, key_self, value_self), axis=1)
    projected = (
        jnp.dot(normed_self, joined_self, preferred_element_type=jnp.float32)
        .astype(jnp.bfloat16)
        .reshape(images, tok_rows, 3 * channels)
    )
    queries = projected[:, :, :channels]
    keys_local = projected[:, :, channels : 2 * channels]
    values_local = projected[:, :, 2 * channels :]
    keys_all = lax.all_gather(keys_local, SEQ, axis=1, tiled=True)
    values_all = lax.all_gather(values_local, SEQ, axis=1, tiled=True)

    def forward_image(bundle):
        image_queries, image_keys, image_values, image_mask = bundle
        query_blocks = image_queries.reshape(-1, block_rows, channels)
        return lax.map(
            lambda part: self_forward((part, image_keys, image_values, image_mask), score_scale),
            query_blocks,
        )

    attn_mixed, log_totals = lax.map(forward_image, (queries, keys_all, values_all, key_mask))
    mixed_flat = attn_mixed.reshape(tokens, channels)
    stream_self = stream_in + jnp.dot(mixed_flat, out_self, preferred_element_type=jnp.float32)
    normed_cross = layer_norm(stream_self, gain_cross).astype(jnp.bfloat16)
    query_text = (
        jnp.dot(normed_cross, query_cross, preferred_element_type=jnp.float32)
        .astype(jnp.bfloat16)
        .reshape(images, tok_rows, HEADS, HEAD)
    )
    text_flat = text_states.reshape(-1, text_states.shape[2])
    text_pairs = (
        jnp.dot(
            text_flat,
            jnp.concatenate((key_cross, value_cross), axis=1),
            preferred_element_type=jnp.float32,
        )
        .astype(jnp.bfloat16)
        .reshape(images, -1, 2, HEADS, HEAD)
    )
    text_keys = text_pairs[:, :, 0]
    text_values = text_pairs[:, :, 1]
    cross_scores = (
        jnp.einsum("iqhd,ikhd->ihqk", query_text, text_keys, preferred_element_type=jnp.float32)
        * score_scale
    )
    cross_attn = jnp.exp(cross_scores - jax.nn.logsumexp(cross_scores, axis=-1, keepdims=True))
    cross_low = cross_attn.astype(jnp.bfloat16)
    cross_mixed = (
        jnp.einsum("ihqk,ikhd->iqhd", cross_low, text_values, preferred_element_type=jnp.float32)
        .astype(jnp.bfloat16)
        .reshape(tokens, channels)
    )
    stream_cross = stream_self + jnp.dot(cross_mixed, out_cross, preferred_element_type=jnp.float32)
    normed_feed = layer_norm(stream_cross, gain_feed).astype(jnp.bfloat16)
    joined_feed = jnp.dot(normed_feed, feed_up, preferred_element_type=jnp.float32)
    gated = geglu(joined_feed).astype(jnp.bfloat16)
    stream_feed = stream_cross + jnp.dot(gated, feed_down, preferred_element_type=jnp.float32)
    stream_low = stream_feed.astype(jnp.bfloat16)
    branch_out = jnp.dot(stream_low, project_out, preferred_element_type=jnp.float32).reshape(
        images, row_count, col_count, channels
    )
    output = (resid + branch_out) * cell_mask
    grad_output = cotangent * cell_mask
    grad_branch = grad_output.reshape(tokens, channels).astype(jnp.bfloat16)
    grad_project_out = grad_dot(stream_low, grad_branch)
    grad_stream = back_dot(grad_branch, project_out)
    grad_feed_low = grad_stream.astype(jnp.bfloat16)
    grad_feed_down = grad_dot(gated, grad_feed_low)
    grad_gated = back_dot(grad_feed_low, feed_down)
    unused, pull_geglu = jax.vjp(geglu, joined_feed)
    grad_joined = pull_geglu(grad_gated)[0].astype(jnp.bfloat16)
    grad_feed_up = grad_dot(normed_feed, grad_joined)
    unused, pull_norm = jax.vjp(layer_norm, stream_cross, gain_feed)
    grad_part, grad_gain_feed = pull_norm(back_dot(grad_joined, feed_up))
    grad_stream = grad_stream + grad_part
    grad_cross_low = grad_stream.astype(jnp.bfloat16)
    grad_out_cross = grad_dot(cross_mixed, grad_cross_low)
    grad_cross_mixed = (
        back_dot(grad_cross_low, out_cross)
        .astype(jnp.bfloat16)
        .reshape(images, tok_rows, HEADS, HEAD)
    )
    grad_text_values = jnp.einsum(
        "ihqk,iqhd->ikhd", cross_low, grad_cross_mixed, preferred_element_type=jnp.float32
    )
    grad_cross_attn = jnp.einsum(
        "iqhd,ikhd->ihqk", grad_cross_mixed, text_values, preferred_element_type=jnp.float32
    )
    cross_delta = jnp.sum(cross_attn * grad_cross_attn, axis=-1, keepdims=True)
    grad_cross_scores = (cross_attn * (grad_cross_attn - cross_delta)).astype(jnp.bfloat16)
    grad_query_text = (
        (
            jnp.einsum(
                "ihqk,ikhd->iqhd", grad_cross_scores, text_keys, preferred_element_type=jnp.float32
            )
            * score_scale
        )
        .astype(jnp.bfloat16)
        .reshape(tokens, channels)
    )
    grad_text_keys = (
        jnp.einsum(
            "ihqk,iqhd->ikhd", grad_cross_scores, query_text, preferred_element_type=jnp.float32
        )
        * score_scale
    )
    text_wide = text_flat.astype(jnp.float32)
    grad_key_cross = exact_grad_dot(text_wide, grad_text_keys.reshape(-1, channels))
    grad_value_cross = exact_grad_dot(text_wide, grad_text_values.reshape(-1, channels))
    grad_query_cross = grad_dot(normed_cross, grad_query_text)
    unused, pull_norm = jax.vjp(layer_norm, stream_self, gain_cross)
    grad_part, grad_gain_cross = pull_norm(back_dot(grad_query_text, query_cross))
    grad_stream = grad_stream + grad_part
    grad_self_low = grad_stream.astype(jnp.bfloat16)
    grad_out_self = grad_dot(mixed_flat, grad_self_low)
    grad_mixed = (
        back_dot(grad_self_low, out_self).astype(jnp.bfloat16).reshape(images, tok_rows, channels)
    )

    def backward_image(bundle):
        image_queries, image_grads, image_totals, image_keys, image_values, image_mask = bundle
        query_blocks = image_queries.reshape(-1, block_rows, channels)
        grad_blocks = image_grads.reshape(-1, block_rows, channels)
        return lax.map(
            lambda part: query_side(
                (part[0], part[1], part[2], image_keys, image_values, image_mask), score_scale
            ),
            (query_blocks, grad_blocks, image_totals),
        )

    grad_queries, kept_attn, kept_grads = lax.map(
        backward_image, (queries, grad_mixed, log_totals, keys_all, values_all, key_mask)
    )
    grads_four = grad_mixed.reshape(images, -1, block_rows, HEADS, HEAD)
    queries_four = queries.reshape(images, -1, block_rows, HEADS, HEAD)
    row_total = tok_rows * lax.axis_size(SEQ)
    value_terms = jnp.einsum(
        "inhqk,inqhd->kihd", kept_attn, grads_four, preferred_element_type=jnp.float32
    )
    key_terms_part = (
        jnp.einsum(
            "inhqk,inqhd->kihd", kept_grads, queries_four, preferred_element_type=jnp.float32
        )
        * score_scale
    )
    summed = lax.psum_scatter(
        jnp.stack(
            (
                key_terms_part.reshape(row_total, images, -1),
                value_terms.reshape(row_total, images, -1),
            ),
            2,
        ).astype(jnp.bfloat16),
        SEQ,
        scatter_dimension=0,
        tiled=True,
    ).astype(jnp.float32)
    grad_keys = jnp.swapaxes(summed[:, :, 0], 0, 1)
    grad_values = jnp.swapaxes(summed[:, :, 1], 0, 1)
    grad_projected = jnp.concatenate(
        (
            grad_queries.reshape(images, tok_rows, channels),
            grad_keys.astype(jnp.bfloat16),
            grad_values.astype(jnp.bfloat16),
        ),
        axis=2,
    ).reshape(tokens, 3 * channels)
    grad_joined_self = grad_dot(normed_self, grad_projected)
    unused, pull_norm = jax.vjp(layer_norm, stream_in, gain_self)
    grad_part, grad_gain_self = pull_norm(back_dot(grad_projected, joined_self))
    grad_stream = grad_stream + grad_part
    grad_stream_low = grad_stream.astype(jnp.bfloat16)
    grad_project_in = grad_dot(normed_block, grad_stream_low)
    grad_block = back_dot(grad_stream_low, project_in).reshape(
        images, row_count, col_count, channels
    )
    grad_resid_part, grad_gain_block = norm_backward(
        block_piece,
        resid,
        gain_block,
        first_block,
        second_block,
        grad_block,
        row_mask,
        spread_fn,
        pick_fn,
    )
    grad_resid = grad_output + grad_resid_part
    grad_second_low = grad_resid.astype(jnp.bfloat16)
    grad_conv_second = conv_weight_grad(padded_mid, grad_second_low)
    grad_act_mid = conv_rows(grads_halo(grad_second_low), flipped(conv_second))
    grad_mid, grad_gain_mid = norm_backward(
        res_piece,
        mid_in,
        gain_mid,
        first_mid,
        second_mid,
        grad_act_mid,
        row_mask,
        spread_fn,
        pick_fn,
    )
    grad_time = jnp.sum(grad_mid, axis=(1, 2))
    grad_time_weight = exact_grad_dot(time_act.astype(jnp.float32), grad_time)
    grad_first_low = grad_mid.astype(jnp.bfloat16)
    grad_conv_first = conv_weight_grad(padded_in, grad_first_low)
    grad_act_in = conv_rows(grads_halo(grad_first_low), flipped(conv_first))
    grad_in_part, grad_gain_in = norm_backward(
        res_piece, latents, gain_in, first_in, second_in, grad_act_in, row_mask, spread_fn, pick_fn
    )
    latent_grad = grad_resid + grad_in_part
    shares = (
        lax.psum_scatter(
            grad_gain_in.reshape(1, -1).astype(jnp.bfloat16), SEQ, scatter_dimension=1, tiled=True
        ).astype(jnp.float32),
        lax.psum_scatter(
            grad_conv_first.reshape(-1, channels).astype(jnp.bfloat16),
            SEQ,
            scatter_dimension=1,
            tiled=True,
        ).astype(jnp.float32),
        lax.psum_scatter(
            grad_time_weight.astype(jnp.bfloat16), SEQ, scatter_dimension=1, tiled=True
        ).astype(jnp.float32),
        lax.psum_scatter(
            grad_gain_mid.reshape(1, -1).astype(jnp.bfloat16),
            SEQ,
            scatter_dimension=1,
            tiled=True,
        ).astype(jnp.float32),
        lax.psum_scatter(
            grad_conv_second.reshape(-1, channels).astype(jnp.bfloat16),
            SEQ,
            scatter_dimension=1,
            tiled=True,
        ).astype(jnp.float32),
        lax.psum_scatter(
            grad_gain_block.reshape(1, -1).astype(jnp.bfloat16),
            SEQ,
            scatter_dimension=1,
            tiled=True,
        ).astype(jnp.float32),
        lax.psum_scatter(
            grad_project_in.astype(jnp.bfloat16), SEQ, scatter_dimension=1, tiled=True
        ).astype(jnp.float32),
        lax.psum_scatter(
            grad_gain_self.reshape(1, -1).astype(jnp.bfloat16),
            SEQ,
            scatter_dimension=1,
            tiled=True,
        ).astype(jnp.float32),
        lax.psum_scatter(
            grad_joined_self[:, :channels].astype(jnp.bfloat16),
            SEQ,
            scatter_dimension=1,
            tiled=True,
        ).astype(jnp.float32),
        lax.psum_scatter(
            grad_joined_self[:, channels : 2 * channels].astype(jnp.bfloat16),
            SEQ,
            scatter_dimension=1,
            tiled=True,
        ).astype(jnp.float32),
        lax.psum_scatter(
            grad_joined_self[:, 2 * channels :].astype(jnp.bfloat16),
            SEQ,
            scatter_dimension=1,
            tiled=True,
        ).astype(jnp.float32),
        lax.psum_scatter(
            grad_out_self.astype(jnp.bfloat16), SEQ, scatter_dimension=1, tiled=True
        ).astype(jnp.float32),
        lax.psum_scatter(
            grad_gain_cross.reshape(1, -1).astype(jnp.bfloat16),
            SEQ,
            scatter_dimension=1,
            tiled=True,
        ).astype(jnp.float32),
        lax.psum_scatter(
            grad_query_cross.astype(jnp.bfloat16), SEQ, scatter_dimension=1, tiled=True
        ).astype(jnp.float32),
        lax.psum_scatter(
            grad_key_cross.astype(jnp.bfloat16), SEQ, scatter_dimension=1, tiled=True
        ).astype(jnp.float32),
        lax.psum_scatter(
            grad_value_cross.astype(jnp.bfloat16), SEQ, scatter_dimension=1, tiled=True
        ).astype(jnp.float32),
        lax.psum_scatter(
            grad_out_cross.astype(jnp.bfloat16), SEQ, scatter_dimension=1, tiled=True
        ).astype(jnp.float32),
        lax.psum_scatter(
            grad_gain_feed.reshape(1, -1).astype(jnp.bfloat16),
            SEQ,
            scatter_dimension=1,
            tiled=True,
        ).astype(jnp.float32),
        lax.psum_scatter(
            grad_feed_up.astype(jnp.bfloat16), SEQ, scatter_dimension=1, tiled=True
        ).astype(jnp.float32),
        lax.psum_scatter(
            grad_feed_down.astype(jnp.bfloat16), SEQ, scatter_dimension=1, tiled=True
        ).astype(jnp.float32),
        lax.psum_scatter(
            grad_project_out.astype(jnp.bfloat16), SEQ, scatter_dimension=1, tiled=True
        ).astype(jnp.float32),
    )
    totals = (
        lax.psum(shares[0].astype(jnp.bfloat16), BATCH).astype(jnp.float32),
        lax.psum(shares[1].astype(jnp.bfloat16), BATCH).astype(jnp.float32),
        lax.psum(shares[2].astype(jnp.bfloat16), BATCH).astype(jnp.float32),
        lax.psum(shares[3].astype(jnp.bfloat16), BATCH).astype(jnp.float32),
        lax.psum(shares[4].astype(jnp.bfloat16), BATCH).astype(jnp.float32),
        lax.psum(shares[5].astype(jnp.bfloat16), BATCH).astype(jnp.float32),
        lax.psum(shares[6].astype(jnp.bfloat16), BATCH).astype(jnp.float32),
        lax.psum(shares[7].astype(jnp.bfloat16), BATCH).astype(jnp.float32),
        lax.psum(shares[8].astype(jnp.bfloat16), BATCH).astype(jnp.float32),
        lax.psum(shares[9].astype(jnp.bfloat16), BATCH).astype(jnp.float32),
        lax.psum(shares[10].astype(jnp.bfloat16), BATCH).astype(jnp.float32),
        lax.psum(shares[11].astype(jnp.bfloat16), BATCH).astype(jnp.float32),
        lax.psum(shares[12].astype(jnp.bfloat16), BATCH).astype(jnp.float32),
        lax.psum(shares[13].astype(jnp.bfloat16), BATCH).astype(jnp.float32),
        lax.psum(shares[14].astype(jnp.bfloat16), BATCH).astype(jnp.float32),
        lax.psum(shares[15].astype(jnp.bfloat16), BATCH).astype(jnp.float32),
        lax.psum(shares[16].astype(jnp.bfloat16), BATCH).astype(jnp.float32),
        lax.psum(shares[17].astype(jnp.bfloat16), BATCH).astype(jnp.float32),
        lax.psum(shares[18].astype(jnp.bfloat16), BATCH).astype(jnp.float32),
        lax.psum(shares[19].astype(jnp.bfloat16), BATCH).astype(jnp.float32),
        lax.psum(shares[20].astype(jnp.bfloat16), BATCH).astype(jnp.float32),
    )
    return (
        output,
        latent_grad,
        totals[0].reshape(-1),
        totals[1].reshape(3, 3, channels, -1),
        totals[2],
        totals[3].reshape(-1),
        totals[4].reshape(3, 3, channels, -1),
        totals[5].reshape(-1),
        totals[6],
        totals[7].reshape(-1),
        totals[8],
        totals[9],
        totals[10],
        totals[11],
        totals[12].reshape(-1),
        totals[13],
        totals[14],
        totals[15],
        totals[16],
        totals[17].reshape(-1),
        totals[18],
        totals[19],
        totals[20],
    )


def solution(mesh):
    in_specs = (
        P(BATCH, SEQ, None, None),
        P(BATCH),
        P(BATCH, None),
        P(BATCH, None, None),
        P(),
        P(),
        P(),
        P(),
        P(),
        P(),
        P(),
        P(),
        P(),
        P(),
        P(),
        P(),
        P(),
        P(),
        P(),
        P(),
        P(),
        P(),
        P(),
        P(),
        P(),
        P(BATCH, SEQ, None, None),
    )
    out_specs = (
        P(BATCH, SEQ, None, None),
        P(BATCH, SEQ, None, None),
        P(SEQ),
        P(None, None, None, SEQ),
        P(None, SEQ),
        P(SEQ),
        P(None, None, None, SEQ),
        P(SEQ),
        P(None, SEQ),
        P(SEQ),
        P(None, SEQ),
        P(None, SEQ),
        P(None, SEQ),
        P(None, SEQ),
        P(SEQ),
        P(None, SEQ),
        P(None, SEQ),
        P(None, SEQ),
        P(None, SEQ),
        P(SEQ),
        P(None, SEQ),
        P(None, SEQ),
        P(None, SEQ),
    )
    device_fn = fast_device if mesh.shape[SEQ] == HEADS else on_device
    return jax.shard_map(
        device_fn, mesh=mesh, in_specs=in_specs, out_specs=out_specs, check_vma=False
    )
```

```python
import types
import typing

import jax
import jax.numpy as jnp
from jax import lax
from jax.experimental import pallas as pl
from jax.experimental.pallas import tpu as pltpu
from jax.sharding import PartitionSpec as P

BATCH, SEQ = "batch", "seq"
HEADS = 8
HEAD = 40
GROUPS = 32


epsilon = 1e-05
layout = ("NHWC", "HWIO", "NHWC")


def extended(block, sides, width):
    for axis, dim in sides:
        count = lax.axis_size(axis)
        forward = [(i, i + 1) for i in range(count - 1)]
        backward = [(target, source) for source, target in forward]
        low = lax.ppermute(
            lax.slice_in_dim(block, block.shape[dim] - width, None, axis=dim), axis, forward
        )
        high = lax.ppermute(lax.slice_in_dim(block, 0, width, axis=dim), axis, backward)
        block = jnp.concatenate([low, block, high], axis=dim)
    return block


def layer_norm(values, norm_gain):
    centred = values - jnp.mean(values, axis=-1, keepdims=True)
    spread = jnp.mean(centred * centred, axis=-1, keepdims=True)
    return centred * lax.rsqrt(spread + epsilon) * norm_gain


def geglu(joined):
    half_width = joined.shape[-1] // 2
    return joined[:, :half_width] * jax.nn.gelu(joined[:, half_width:], approximate=False)


def back_dot(left_side, weight):
    return lax.dot_general(
        left_side, weight, (((1,), (1,)), ((), ())), preferred_element_type=jnp.float32
    )


def grad_dot(left_side, right_side):
    return lax.dot_general(
        left_side, right_side, (((0,), (0,)), ((), ())), preferred_element_type=jnp.float32
    )


def exact_grad_dot(left_side, right_side):
    return lax.dot_general(
        left_side,
        right_side,
        (((0,), (0,)), ((), ())),
        precision=lax.Precision.HIGHEST,
        preferred_element_type=jnp.float32,
    )


def conv_rows(padded, weight):
    return lax.conv_general_dilated(
        padded,
        weight,
        (1, 1),
        ((0, 0), (1, 1)),
        dimension_numbers=layout,
        preferred_element_type=jnp.float32,
    )


def conv_weight_grad(padded, grad_output):
    row_count = grad_output.shape[1]
    col_count = grad_output.shape[2]
    padded_cols = jnp.pad(padded, ((0, 0), (0, 0), (1, 1), (0, 0)))
    flat_grad = grad_output.reshape(-1, grad_output.shape[3])
    tap_rows = []
    for shift_row in range(3):
        tap_line = []
        for shift_col in range(3):
            patch_rows = padded_cols[
                :, shift_row : shift_row + row_count, shift_col : shift_col + col_count
            ].reshape(-1, padded.shape[3])
            tap_line.append(grad_dot(patch_rows, flat_grad))
        tap_rows.append(jnp.stack(tap_line))
    return jnp.stack(tap_rows)


def flipped(weight):
    return jnp.swapaxes(weight[::-1, ::-1], 2, 3)


def group_sums(values, row_mask):
    full_shape = values.shape
    grouped = values.reshape(
        full_shape[0], full_shape[1], full_shape[2], GROUPS, full_shape[3] // GROUPS
    )
    masked = grouped * row_mask[:, :, None, None, None]
    return (jnp.sum(masked, axis=(1, 2, 4)), jnp.sum(masked * grouped, axis=(1, 2, 4)))


def group_apply(values, norm_gain, sum_first, sum_second, cell_counts):
    full_shape = values.shape
    grouped = values.reshape(
        full_shape[0], full_shape[1], full_shape[2], GROUPS, full_shape[3] // GROUPS
    )
    group_mean = sum_first / cell_counts[:, None]
    spread = sum_second / cell_counts[:, None] - group_mean * group_mean
    inverse = lax.rsqrt(spread + epsilon)
    normed = (grouped - group_mean[:, None, None, :, None]) * inverse[:, None, None, :, None]
    return normed.reshape(full_shape) * norm_gain


def norm_stats(values, row_mask, spread_fn, pick_fn):
    sum_first, sum_second = group_sums(values, row_mask)
    total_first, total_second = lax.psum((spread_fn(sum_first), spread_fn(sum_second)), SEQ)
    return (pick_fn(total_first), pick_fn(total_second))


def norm_back(grad_first, grad_second, spread_fn, pick_fn):
    total_first, total_second = lax.psum((spread_fn(grad_first), spread_fn(grad_second)), SEQ)
    return (pick_fn(total_first), pick_fn(total_second))


def rows_halo(values):
    return extended(values, ((SEQ, 1),), 1)


def grads_halo(values):
    return extended(values, ((SEQ, 1),), 1)


def norm_backward(
    piece_fn, values, norm_gain, sum_first, sum_second, grad_output, row_mask, spread_fn, pick_fn
):
    unused, pull_piece = jax.vjp(piece_fn, values, norm_gain, sum_first, sum_second)
    grad_values, grad_gain, grad_first, grad_second = pull_piece(grad_output)
    total_first, total_second = norm_back(grad_first, grad_second, spread_fn, pick_fn)
    unused, pull_sums = jax.vjp(lambda inner_vals: group_sums(inner_vals, row_mask), values)
    extra_part = pull_sums((total_first, total_second))[0]
    return (grad_values + extra_part, grad_gain)


def masked_scores(queries, keys_all, key_mask, score_scale):
    row_count = queries.shape[0]
    key_count = keys_all.shape[0]
    raw_scores = (
        jnp.einsum(
            "qhd,khd->hqk",
            queries.reshape(row_count, HEADS, HEAD),
            keys_all.reshape(key_count, HEADS, HEAD),
            preferred_element_type=jnp.float32,
        )
        * score_scale
    )
    return jnp.where(key_mask[None, None, :] > 0, raw_scores, -1e30)


def self_forward(bundle, score_scale):
    queries, keys_all, values_all, key_mask = bundle
    row_count = queries.shape[0]
    scores = masked_scores(queries, keys_all, key_mask, score_scale)
    log_total = jax.nn.logsumexp(scores, axis=-1)
    attention = jnp.exp(scores - log_total[:, :, None]).astype(jnp.bfloat16)
    attn_mixed = jnp.einsum(
        "hqk,khd->qhd",
        attention,
        values_all.reshape(keys_all.shape[0], HEADS, HEAD),
        preferred_element_type=jnp.float32,
    )
    return (attn_mixed.astype(jnp.bfloat16).reshape(row_count, -1), log_total)


def query_side(bundle, score_scale):
    queries, grad_mixed, log_total, keys_all, values_all, key_mask = bundle
    row_count = queries.shape[0]
    key_count = keys_all.shape[0]
    scores = masked_scores(queries, keys_all, key_mask, score_scale)
    attention = jnp.exp(scores - log_total[:, :, None])
    grad_attn = jnp.einsum(
        "qhd,khd->hqk",
        grad_mixed.reshape(row_count, HEADS, HEAD),
        values_all.reshape(key_count, HEADS, HEAD),
        preferred_element_type=jnp.float32,
    )
    row_delta = jnp.sum(attention * grad_attn, axis=-1)
    grad_scores = (attention * (grad_attn - row_delta[:, :, None])).astype(jnp.bfloat16)
    grad_queries = (
        jnp.einsum(
            "hqk,khd->qhd",
            grad_scores,
            keys_all.reshape(key_count, HEADS, HEAD),
            preferred_element_type=jnp.float32,
        )
        * score_scale
    )
    return (
        grad_queries.astype(jnp.bfloat16).reshape(row_count, -1),
        attention.astype(jnp.bfloat16),
        grad_scores,
    )


LANES = 128
MESH = pl.DeviceIdType.MESH
LOW = jnp.bfloat16
F32 = jnp.float32
TILE = 64


def dot_nn(left, right):
    return jnp.dot(left, right, preferred_element_type=F32)


def dot_nt(left, right):
    return lax.dot_general(left, right, (((1,), (1,)), ((), ())), preferred_element_type=F32)


def dot_tn(left, right):
    return lax.dot_general(left, right, (((0,), (0,)), ((), ())), preferred_element_type=F32)


def iota(shape, dim):
    return lax.broadcasted_iota(jnp.int32, shape, dim)


def floor_div(values, by):
    return jnp.floor((values.astype(F32) + 0.5) * (1.0 / by)).astype(jnp.int32)


def split_three(values):
    high = values.astype(LOW).astype(F32)
    rest = values - high
    middle = rest.astype(LOW).astype(F32)
    return jnp.concatenate([high, middle, rest - middle], axis=0).astype(LOW)


def sum_three(values):
    rows = values.shape[0] // 3
    return values[:rows] + values[rows : 2 * rows] + values[2 * rows :]


def row_of(ref):
    return ref[...].reshape(1, -1)


def sigmoid(values):
    return 1.0 / (1.0 + jnp.exp(-values))


def col_sum(values):
    return jnp.sum(values, axis=0, keepdims=True)


ROUNDS = 6
SEMAPHORES = 256


class Packs(typing.NamedTuple):
    up: typing.Any
    down: typing.Any
    trio: typing.Any
    pair: typing.Any
    heads: typing.Any
    second: typing.Any


class Sizes:
    def __init__(self, mesh_batch, mesh_seq, latents, time_vector, text_states, feed_down):
        self.batches = mesh_batch
        self.seqs = mesh_seq
        self.rows = latents.shape[1]
        self.width = latents.shape[2]
        self.channels = latents.shape[3]
        self.tokens = self.rows * self.width
        self.wide = self.tokens + 2 * self.width
        self.keys = self.tokens * mesh_seq
        self.emb = time_vector.shape[1]
        self.text = text_states.shape[1]
        self.text_pad = -(-self.text // 16) * 16
        self.context = text_states.shape[2]
        self.hidden = feed_down.shape[0]
        self.slot = 48
        self.packed = HEADS * LANES
        self.down_rows = 512
        self.conv_rows = -(-9 * self.slot // (16 * mesh_batch)) * 16 * mesh_batch
        channels = self.channels
        sizes = Packs(
            up=3 * channels,
            down=self.down_rows,
            trio=channels,
            pair=HEADS * self.slot,
            heads=channels,
            second=3 * channels,
        )
        starts = [sum(sizes[:place]) for place in range(len(sizes))]
        self.start = Packs(*starts)
        self.pack_rows = sum(sizes)
        self.sizes = sizes
        self.chunks = [
            (0, sizes.up),
            (self.start.down, sizes.down + sizes.trio),
            (self.start.pair, sizes.pair + sizes.heads),
            (self.start.second, sizes.second),
        ]


class Inputs(typing.NamedTuple):
    latents: typing.Any
    heights: typing.Any
    time_vector: typing.Any
    text_states: typing.Any
    gain_in: typing.Any
    conv_first: typing.Any
    time_weight: typing.Any
    gain_mid: typing.Any
    conv_second: typing.Any
    gain_block: typing.Any
    project_in: typing.Any
    gain_self: typing.Any
    query_self: typing.Any
    key_self: typing.Any
    value_self: typing.Any
    out_self: typing.Any
    gain_cross: typing.Any
    query_cross: typing.Any
    key_cross: typing.Any
    value_cross: typing.Any
    out_cross: typing.Any
    gain_feed: typing.Any
    feed_up: typing.Any
    feed_down: typing.Any
    project_out: typing.Any
    cotangent: typing.Any


class Fetched(typing.NamedTuple):
    query_self: typing.Any
    key_self: typing.Any
    value_self: typing.Any
    time_weight: typing.Any
    conv_first: typing.Any
    conv_second: typing.Any
    project_in: typing.Any
    key_cross: typing.Any
    value_cross: typing.Any
    out_self: typing.Any
    query_cross: typing.Any
    out_cross: typing.Any
    feed_up: typing.Any
    feed_down: typing.Any
    project_out: typing.Any


def buffers(sz):
    c, t, w, k = sz.channels, sz.tokens, sz.wide, sz.keys
    half = sz.seqs // 2
    return dict(
        lat6=((w, c), F32),
        cot6=((w, c), F32),
        mid6=((w, c), F32),
        res6=((w, c), F32),
        gblk6=((w, c), F32),
        gact6=((w, c), F32),
        shifted=((3, w, c), LOW),
        shift_grad=((3, w, c), LOW),
        act_in=((k + 2 * sz.width, c), LOW),
        widen=((HEADS * sz.slot, c), LOW),
        first_send=((HEADS * sz.slot, t), LOW),
        first_grads=((sz.slot, k), LOW),
        first_part=((sz.conv_rows, c), LOW),
        first_recv=((sz.batches - 1, sz.conv_rows // sz.batches, c), LOW),
        conv_stack=((3 * sz.slot, k), LOW),
        stat_send=((ROUNDS, 8, LANES), F32),
        extra_send=((8, c), F32),
        extra_recv=((sz.seqs, 8, c), F32),
        stat_recv=((ROUNDS, sz.seqs, 8, LANES), F32),
        norms=((3, 8, c), F32),
        gain_parts=((8, c), F32),
        final_send=((8, c), F32),
        group=((c, c), LOW),
        place=((3, c, sz.packed), LOW),
        wqkv=((c, sz.packed), LOW),
        osp=((HEADS * sz.slot, c), LOW),
        time_send=((8, sz.emb), F32),
        normed_block=((t, c), LOW),
        stream_in=((t, c), F32),
        normed_self=((t, c), LOW),
        qkv_send=((t, sz.packed), LOW),
        qkv=((k, LANES), LOW),
        qh=((k, LANES), LOW),
        kh=((k, LANES), LOW),
        vh=((k, sz.slot), LOW),
        vt=((sz.slot, k), LOW),
        kt=((sz.slot, k), LOW),
        scores=((max(k, 2 * sz.hidden), t), F32),
        scores_odd=((k, t), F32),
        tops=((2, 8, t), F32),
        probs=((2, k, t), LOW),
        mixed_full=((sz.seqs, sz.slot, t), F32),
        inverse=((sz.seqs, 8, t), F32),
        mixed_send=((sz.seqs, sz.slot, t), LOW),
        mixed=((HEADS * sz.slot, t), LOW),
        stream=((t, c), F32),
        centred_cross=((t, c), F32),
        scale_cross=((t, LANES), F32),
        normed_cross=((t, c), LOW),
        query_text=((t, c), LOW),
        text_rows=((2, sz.text_pad, c), F32),
        text_key=((HEADS * sz.text_pad, c), LOW),
        text_value=((HEADS * sz.text_pad, c), LOW),
        cross=((HEADS * sz.text_pad, t), F32),
        cross_low=((HEADS * sz.text_pad, t), LOW),
        cross_scores=((HEADS * sz.text_pad, t), LOW),
        cross_mixed=((t, c), LOW),
        scale_feed=((t, LANES), F32),
        normed_feed=((t, c), LOW),
        gated=((t, sz.hidden), LOW),
        grad_gated=((t, 2 * LANES), F32),
        grad_joined=((t, 2 * sz.hidden), LOW),
        stream_low=((t, c), LOW),
        grad_branch=((t, c), LOW),
        grad=((t, c), F32),
        tmp=((t, c), F32),
        grad_feed_low=((t, c), LOW),
        grad_cross_low=((t, c), LOW),
        grad_cross_mixed=((t, c), LOW),
        grad_query_text=((t, c), LOW),
        grad_self_low=((t, c), LOW),
        grad_in_low=((t, c), LOW),
        text_send=((sz.text_pad, sz.packed), LOW),
        text_recv=((sz.seqs, sz.text_pad, LANES), LOW),
        gm_send=((HEADS * sz.slot, t), LOW),
        gm=((sz.seqs, sz.slot, t), LOW),
        gp=((t, sz.packed), LOW),
        pack=((sz.seqs, sz.pack_rows, LANES), LOW),
        recv_core=((half, sz.pack_rows, LANES), LOW),
        recv_first=((2, half // 2, sz.pack_rows // 2, LANES), LOW),
        recv_second=((half, sz.pack_rows // sz.batches, LANES), LOW),
        recv_z=((half - 1, sz.pack_rows // sz.batches, LANES), LOW),
    )


class Halo:
    def __init__(self, seq, last, after, before):
        self.seq, self.last, self.after, self.before = seq, last, after, before

    def start(self):
        @pl.when(self.seq < self.last)
        def _():
            self.after.start()

        @pl.when(self.seq > 0)
        def _():
            self.before.start()

    def wait(self):
        @pl.when(self.seq < self.last)
        def _():
            self.after.wait_send()
            self.before.wait_recv()

        @pl.when(self.seq > 0)
        def _():
            self.before.wait_send()
            self.after.wait_recv()


class Fused:
    def __init__(self, sz, refs, local):
        self.sz = sz
        self.r = refs
        self.v = local
        self.used = 0
        self.batch = lax.axis_index(BATCH)
        self.seq = lax.axis_index(SEQ)
        self.z_pos = self.seq // 2
        self.core = lax.rem(self.seq, 2)
        self.batch_x = lax.rem(self.batch, 2)
        self.batch_y = self.batch // 2
        self.x_peer = (self.batch + 1 - 2 * self.batch_x, self.seq)
        self.y_peer = (self.batch + 2 - 4 * self.batch_y, self.seq)
        self.partner = (self.batch, self.seq + 1 - 2 * self.core)
        self.seq_others = [lax.rem(self.seq + step, sz.seqs) for step in range(1, sz.seqs)]
        self.batch_others = [lax.rem(self.batch + step, sz.batches) for step in range(1, sz.batches)]
        half = sz.seqs // 2
        self.z_others = [lax.rem(self.z_pos + step, half) for step in range(1, half)]
        self.height = refs.heights[0]
        self.scale = HEAD ** (-0.5)

    def remote(self, source, target, device, index=None):
        if index is None:
            index = self.used
            self.used += 1
        return pltpu.make_async_remote_copy(
            src_ref=source,
            dst_ref=target,
            send_sem=self.r.sems.at[0, index],
            recv_sem=self.r.sems.at[1, index],
            device_id=device,
            device_id_type=MESH,
        )

    def to_seq(self, source, target):
        return [self.remote(source(other), target, (self.batch, other)) for other in self.seq_others]

    def to_batch(self, source, target):
        return [self.remote(source, target, (other, self.seq)) for other in self.batch_others]

    def start(self, copies):
        for one in copies:
            one.start()

    def wait(self, copies):
        for one in copies:
            one.wait()

    def entry(self):
        r = self.r
        barrier = pltpu.get_barrier_semaphore()
        for other in self.seq_others:
            pl.semaphore_signal(barrier, inc=1, device_id=(self.batch, other), device_id_type=MESH)
        for other in self.batch_others:
            pl.semaphore_signal(barrier, inc=1, device_id=(other, self.seq), device_id_type=MESH)
        self.local = {}
        self.named = {id(getattr(r, name)): name for name in Fetched._fields}
        for number, name in enumerate(Fetched._fields):
            self.local[name] = pltpu.make_async_copy(
                getattr(r, name), getattr(self.v, name), r.local_sems.at[number]
            )
            self.local[name].start()
        own = pl.ds(self.sz.width, self.sz.tokens)
        self.images = [
            pltpu.make_async_copy(source, target.at[own], r.local_sems.at[len(Fetched._fields) + place])
            for place, (source, target) in enumerate(((r.latents, r.lat6), (r.cotangent, r.cot6)))
        ]
        self.start(self.images)

    def joined(self):
        barrier = pltpu.get_barrier_semaphore()
        pl.semaphore_wait(barrier, self.sz.seqs - 1 + self.sz.batches - 1)

    def weight(self, ref):
        name = self.named[id(ref)]
        if name in self.local:
            self.local.pop(name).wait()
        return getattr(self.v, name)

    def far_first(self, step):
        half = self.sz.seqs // 2
        offset = half + ((step + 1) // 2) * (1 - 2 * (step % 2))
        return lax.rem(self.seq + offset, self.sz.seqs)

    def wide_row(self, start, size):
        rows = floor_div(iota((size, 1), 0) + start, self.sz.width) - 1
        return rows + self.seq * self.sz.rows

    def wide_mask(self, start, size):
        rows = self.wide_row(start, size)
        return jnp.where((rows >= 0) & (rows < self.height), 1.0, 0.0)

    def inside_mask(self, start, size):
        rows = self.wide_row(start, size)
        return jnp.where((rows >= 0) & (rows < self.sz.rows * self.sz.seqs), 1.0, 0.0)

    def chunks(self, total):
        return [(start, TILE) for start in range(0, total, TILE)]

    def halo(self, ref):
        sz, width = self.sz, self.sz.width
        after = self.remote(
            ref.at[pl.ds(sz.tokens, width)],
            ref.at[pl.ds(0, width)],
            (self.batch, jnp.minimum(self.seq + 1, sz.seqs - 1)),
        )
        before = self.remote(
            ref.at[pl.ds(width, width)],
            ref.at[pl.ds(width + sz.tokens, width)],
            (self.batch, jnp.maximum(self.seq - 1, 0)),
        )
        return Halo(self.seq, sz.seqs - 1, after, before)

    def lane_tiles(self):
        channels = self.sz.channels
        return [(start, min(LANES, channels - start)) for start in range(0, channels, LANES)]

    def stats_store(self, number, rows):
        r = self.r
        r.stat_send[number] = jnp.zeros(r.stat_send.shape[1:], F32)
        tiles = self.lane_tiles()
        for which, row in enumerate(rows):
            for place, (start, size) in enumerate(tiles):
                at = which * len(tiles) + place
                r.stat_send[number, at : at + 1, 0:size] = row[:, start : start + size]
        r.stat_recv[number, self.seq] = r.stat_send[number]

    def stats_start(self, number):
        r = self.r
        copies = self.to_seq(lambda other: r.stat_send.at[number], r.stat_recv.at[number, self.seq])
        self.start(copies)
        return copies

    def stats_total(self, number):
        r = self.r
        total = r.stat_recv[number, 0]
        for place in range(1, self.sz.seqs):
            total = total + r.stat_recv[number, place]
        tiles = self.lane_tiles()
        rows = []
        for which in range(2):
            parts = [
                total[which * len(tiles) + place : which * len(tiles) + place + 1, 0:size]
                for place, (start, size) in enumerate(tiles)
            ]
            rows.append(jnp.concatenate(parts, axis=1))
        row = iota((8, 1), 0)
        return jnp.where(row == 0, rows[0], jnp.where(row == 1, rows[1], 0.0))

    def grouped(self, rows):
        return sum_three(dot_nn(split_three(rows), self.r.group[...]))

    def count(self):
        per_row = self.sz.width * (self.sz.channels // GROUPS)
        return (self.height * per_row).astype(F32)

    def set_norm(self, number, total):
        sums = self.grouped(total) / self.count()
        mean = sums[0:1]
        spread = sums[1:2] - mean * mean
        self.r.norms[number, 0:1] = mean
        self.r.norms[number, 1:2] = lax.rsqrt(spread + epsilon)

    def norm(self, number):
        return self.r.norms[number, 0:1], self.r.norms[number, 1:2]

    def value_sums(self, ref):
        r, sz = self.r, self.sz
        first = second = None
        for start, size in self.chunks(sz.tokens):
            start += sz.width
            values = ref[start : start + size]
            masked = values * self.wide_mask(start, size)
            one, two = col_sum(masked), col_sum(masked * values)
            first = one if first is None else first + one
            second = two if second is None else second + two
        return first, second

    def shifts(self, ref, start, size, values):
        column = lax.rem(iota((size, 1), 0), self.sz.width)
        ref[1, start : start + size] = values.astype(LOW)
        left = jnp.where(column == 0, 0.0, pltpu.roll(values, 1, 0))
        ref[0, start : start + size] = left.astype(LOW)
        right = jnp.where(column == self.sz.width - 1, 0.0, pltpu.roll(values, size - 1, 0))
        ref[2, start : start + size] = right.astype(LOW)

    def activate(self, source, number, gain, target, kept):
        mean, inverse = self.norm(number)
        factor = inverse * row_of(gain)
        for start, size in self.chunks(self.sz.wide):
            normed = (source[start : start + size] - mean) * factor
            values = normed * sigmoid(normed) * self.wide_mask(start, size)
            self.shifts(target, start, size, values)
        if kept is None:
            return
        width, tokens = self.sz.width, self.sz.tokens
        kept[self.own_rows()] = target[1, width : width + tokens]
        zeros = jnp.zeros((width, self.sz.channels), LOW)
        kept[0:width] = zeros
        kept[self.sz.keys + width :] = zeros

    def own_rows(self, seq=None):
        seq = self.seq if seq is None else seq
        width, tokens = self.sz.width, self.sz.tokens
        return pl.ds(pl.multiple_of(seq * tokens + width, width), tokens)

    def gather_piece(self, kept, pieces):
        width, tokens = self.sz.width, self.sz.tokens
        copies = []
        for piece in pieces:
            start = self.seq * tokens + width + piece * width
            rows = pl.ds(pl.multiple_of(start, width), width)
            copies += [
                self.remote(kept.at[rows], kept.at[rows], (self.batch, other * 2 + self.core))
                for other in self.z_others
            ]
        self.start(copies)
        return copies

    def gather_forward(self, kept, copies):
        rows = self.own_rows()
        more = [self.remote(kept.at[rows], kept.at[rows], self.partner)]
        self.start(more)
        self.wait(copies)
        half = self.sz.seqs // 2
        for step in range(1, half):
            rows = self.own_rows(lax.rem(self.z_pos + half - step, half) * 2 + self.core)
            more.append(self.remote(kept.at[rows], kept.at[rows], self.partner))
        self.start(more[1:])
        return more

    def conv_send(self, grads, send, target):
        sz, slot = self.sz, self.sz.slot
        send[...] = dot_nt(self.r.widen[...], grads[1, sz.width : sz.width + sz.tokens]).astype(LOW)
        lanes = pl.ds(pl.multiple_of(self.seq * sz.tokens, sz.tokens), sz.tokens)
        copies = [
            self.remote(
                send.at[pl.ds(pl.multiple_of(other * slot, 16), slot)],
                target.at[:, lanes],
                (self.batch, other),
            )
            for other in self.seq_others
        ]
        self.start(copies)
        target[:, lanes] = send[pl.ds(pl.multiple_of(self.seq * slot, 16), slot)]
        return copies

    def conv_grads(self, copies, gathered, grads, kept, part, received):
        r, sz = self.r, self.sz
        slot, keys, width = sz.slot, sz.keys, sz.width
        self.wait(copies)
        self.wait(gathered)
        values = grads[...].astype(F32)
        column = lax.rem(iota((1, keys), 1), width)
        r.conv_stack[slot : 2 * slot] = grads[...]
        left = jnp.where(column == width - 1, 0.0, pltpu.roll(values, keys - 1, 1))
        r.conv_stack[0:slot] = left.astype(LOW)
        right = jnp.where(column == 0, 0.0, pltpu.roll(values, 1, 1))
        r.conv_stack[2 * slot :] = right.astype(LOW)
        for row in range(3):
            rows = slice(row * 3 * slot, (row + 1) * 3 * slot)
            part[rows] = dot_nn(
                r.conv_stack[...], kept[row * width : row * width + keys]
            ).astype(LOW)
        if sz.conv_rows > 9 * slot:
            part[9 * slot :] = jnp.zeros((sz.conv_rows - 9 * slot, sz.channels), LOW)
        size = sz.conv_rows // sz.batches
        copies = [
            self.remote(
                part.at[pl.ds(pl.multiple_of(other * size, 16), size)],
                received.at[step],
                (other, self.seq),
            )
            for step, other in enumerate(self.batch_others)
        ]
        self.start(copies)
        return copies

    def conv_gather(self, copies, part, received, out):
        size = self.sz.conv_rows // self.sz.batches
        own = pl.ds(pl.multiple_of(self.batch * size, 16), size)
        self.wait(copies)
        total = part[own].astype(F32)
        for step in range(self.sz.batches - 1):
            total = total + received[step].astype(F32)
        out[own] = total.astype(LOW)
        copies = self.to_batch(out.at[own], out.at[own])
        self.start(copies)
        return copies

    def conv(self, ref, weight):
        sz = self.sz
        total = None
        for row in range(3):
            for col in range(3):
                part = dot_nn(ref[col, row * sz.width : row * sz.width + sz.tokens], weight[row, col])
                total = part if total is None else total + part
        return total

    def conv_back(self, ref, weight):
        sz = self.sz
        total = None
        for row in range(3):
            for col in range(3):
                part = dot_nt(
                    ref[col, row * sz.width : row * sz.width + sz.tokens], weight[2 - row, 2 - col]
                )
                total = part if total is None else total + part
        return total

    def constants(self):
        r, sz = self.r, self.sz
        channels = sz.channels
        size = channels // GROUPS
        r.group[...] = jnp.where(
            floor_div(iota((channels, 1), 0), size) == floor_div(iota((1, channels), 1), size), 1.0, 0.0
        ).astype(LOW)
        source = iota((1, channels), 1)
        source = source + (sz.slot - HEAD) * floor_div(source, HEAD)
        r.widen[...] = jnp.where(iota((HEADS * sz.slot, 1), 0) == source, 1.0, 0.0).astype(LOW)
        rows = iota((channels, 1), 0)
        target = rows + (LANES - HEAD) * floor_div(rows, HEAD)
        lanes = iota((1, sz.packed), 1)
        for number in range(3):
            r.place[number] = jnp.where(lanes == target + number * HEAD, 1.0, 0.0).astype(LOW)

    def residual(self):
        r, sz = self.r, self.sz
        width, tokens = sz.width, sz.tokens
        self.constants()
        self.wait(self.images)
        for ref in (r.lat6, r.cot6, r.mid6, r.res6, r.gblk6, r.gact6):

            @pl.when(self.seq == 0)
            def _():
                ref[0:width] = jnp.zeros((width, sz.channels), F32)

            @pl.when(self.seq == sz.seqs - 1)
            def _():
                ref[width + tokens :] = jnp.zeros((width, sz.channels), F32)

        self.stats_store(0, self.value_sums(r.lat6))
        self.joined()
        halo = self.halo(r.lat6)
        halo.start()
        stats = self.stats_start(0)
        late = [self.halo(r.cot6)]
        act = r.time_vector[...].astype(F32)
        act = (act * sigmoid(act)).astype(LOW)
        r.time_send[...] = jnp.zeros(r.time_send.shape, F32)
        r.time_send[0:1] = act.astype(F32)
        r.time_all[self.batch] = r.time_send[...]
        late += self.to_batch(r.time_send, r.time_all.at[self.batch])
        r.text_all[self.batch] = jnp.zeros(r.text_all.shape[1:], LOW)
        r.text_all[self.batch, 0 : sz.text] = r.text_states[...]
        late += self.to_batch(r.text_all.at[self.batch], r.text_all.at[self.batch])
        self.start(late)
        self.late = late
        time_weight = self.weight(self.r.time_weight)
        time_term = dot_nt(jnp.broadcast_to(act, (16, sz.emb)), time_weight[...])[0:1]
        wqkv = None
        for number, name in enumerate((r.query_self, r.key_self, r.value_self)):
            part = dot_nn(self.weight(name)[...], r.place[number])
            wqkv = part if wqkv is None else wqkv + part
        r.wqkv[...] = wqkv.astype(LOW)
        halo.wait()
        self.wait(stats)
        self.set_norm(0, self.stats_total(0))
        self.activate(r.lat6, 0, r.gain_in, r.shifted, r.act_in)
        r.mid6[width : width + tokens] = self.conv(r.shifted, self.weight(self.r.conv_first)) + time_term
        halo = self.halo(r.mid6)
        halo.start()
        self.stats_store(1, self.value_sums(r.mid6))
        stats = self.stats_start(1)
        self.weight(self.r.conv_second)
        halo.wait()
        self.wait(stats)
        self.set_norm(1, self.stats_total(1))
        self.activate(r.mid6, 1, r.gain_mid, r.shifted, None)
        r.res6[width : width + tokens] = r.lat6[width : width + tokens] + self.conv(
            r.shifted, self.v.conv_second
        )
        halo = self.halo(r.res6)
        self.stats_store(2, self.value_sums(r.res6))
        stats = self.stats_start(2)
        halo.start()
        self.late.append(halo)
        project_in = self.weight(self.r.project_in)
        self.wait(stats)
        self.set_norm(2, self.stats_total(2))
        mean, inverse = self.norm(2)
        factor = inverse * row_of(r.gain_block)
        for start, size in self.chunks(tokens):
            values = r.res6[width + start : width + start + size]
            r.normed_block[start : start + size] = ((values - mean) * factor).astype(LOW)
        r.stream_in[...] = dot_nn(r.normed_block[...], project_in[...])
        for start, size in self.chunks(tokens):
            values = r.stream_in[start : start + size]
            centred, scale = self.layer_parts(values)
            r.normed_self[start : start + size] = (centred * scale * row_of(r.gain_self)).astype(LOW)
        r.qkv_send[...] = dot_nn(r.normed_self[...], r.wqkv[...]).astype(LOW)
        rows = pl.ds(pl.multiple_of(self.seq * tokens, tokens), tokens)
        copies = [
            self.remote(
                r.qkv_send.at[:, pl.ds(pl.multiple_of(other * LANES, LANES), LANES)],
                r.qkv.at[rows],
                (self.batch, other),
            )
            for other in self.seq_others
        ]
        self.start(copies)
        r.qkv[rows] = r.qkv_send[:, pl.ds(pl.multiple_of(self.seq * LANES, LANES), LANES)]
        self.text_start()
        self.wait(copies)

    def layer_parts(self, values):
        centred = values - jnp.mean(values, axis=-1, keepdims=True)
        spread = jnp.mean(centred * centred, axis=-1, keepdims=True)
        return centred, lax.rsqrt(spread + epsilon)

    def layer_back(self, values, grad, gain):
        centred, scale = self.layer_parts(values)
        normed = centred * scale
        scaled = grad * gain
        first = jnp.mean(scaled, axis=-1, keepdims=True)
        second = jnp.mean(scaled * normed, axis=-1, keepdims=True)
        return scale * (scaled - first - normed * second), col_sum(grad * normed)

    def text_start(self):
        r, sz = self.r, self.sz
        r.text_rows[...] = jnp.zeros(r.text_rows.shape, F32)
        for number, (name, target) in enumerate(
            ((r.key_cross, r.text_key), (r.value_cross, r.text_value))
        ):
            r.text_rows[number, 0 : sz.text] = dot_nt(r.text_states[...], self.weight(name)[...])
            rows = r.text_rows[number]
            head = floor_div(iota((1, sz.channels), 1), HEAD)
            for one in range(HEADS):
                target[one * sz.text_pad : (one + 1) * sz.text_pad] = jnp.where(
                    head == one, rows, 0.0
                ).astype(LOW)
        r.osp[...] = dot_nn(r.widen[...], self.weight(self.r.out_self)[...]).astype(LOW)

    def attention(self):
        r, sz = self.r, self.sz
        keys, tokens, slot = sz.keys, sz.tokens, sz.slot
        self.in_pieces = self.gather_piece(r.act_in, range(1))
        lane_in = iota((LANES, LANES), 0)
        lane_out = iota((LANES, LANES), 1)

        def shift(by):
            return jnp.where((lane_in == lane_out + by) & (lane_out < HEAD), 1.0, 0.0).astype(LOW)

        def shift_wide(by):
            source = iota((LANES, slot), 0)
            target = iota((LANES, slot), 1)
            return jnp.where((source == target + by) & (target < HEAD), 1.0, 0.0).astype(LOW)

        def shift_rows(by):
            source = iota((slot, LANES), 1)
            target = iota((slot, LANES), 0)
            return jnp.where((source == target + by) & (target < HEAD), 1.0, 0.0).astype(LOW)

        query_out = jnp.where((lane_in + HEAD == lane_out) & (lane_in < HEAD), 1.0, 0.0).astype(LOW)
        lane = iota((1, LANES), 1)
        for start in range(0, keys, 2 * tokens):
            rows = slice(start, start + 2 * tokens)
            block = r.qkv[rows]
            valid = iota((2 * tokens, 1), 0) + start < self.height * sz.width
            r.qh[rows] = jnp.where(
                lane < HEAD, block.astype(F32), jnp.where(lane == HEAD, 1.0, 0.0)
            ).astype(LOW)
            bias = jnp.where((lane == HEAD) & jnp.logical_not(valid), -1e30, 0.0)
            r.kh[rows] = (dot_nn(block, shift(HEAD)) + bias).astype(LOW)
            ones = jnp.where((iota((1, slot), 1) >= HEAD) & (iota((1, slot), 1) < HEAD + 3), 1.0, 0.0)
            r.vh[rows] = (dot_nn(block, shift_wide(2 * HEAD)) + ones).astype(LOW)
            one_row = jnp.where(iota((slot, 1), 0) == HEAD, 1.0, 0.0)
            r.vt[:, rows] = (dot_nt(shift_rows(2 * HEAD), block) + one_row).astype(LOW)
            r.kt[:, rows] = dot_nt(shift_rows(HEAD), block).astype(LOW)
            r.qkv[rows] = dot_nn(block, query_out).astype(LOW)
        factor = self.scale * 1.4426950408889634
        base = self.used
        self.used += sz.seqs

        def send(target, step):
            return self.remote(
                r.mixed_send.at[target],
                r.mixed.at[pl.ds(pl.multiple_of(self.seq * slot, 16), slot)],
                (self.batch, target),
                base + step,
            )

        score_refs = (r.scores, r.scores_odd)

        def keep(step, parity):
            return pltpu.make_async_copy(
                r.probs.at[parity],
                r.kept_probs.at[self.far_first(step)],
                r.local_sems.at[len(Fetched._fields) + 2 + parity],
            )

        def own_scores(step, parity, start, top):
            target = self.far_first(step)
            queries = r.qh[pl.ds(pl.multiple_of(target * tokens, tokens), tokens)]
            scores = dot_nt(r.kh[start : start + tokens], queries)
            score_refs[parity][start : start + tokens] = scores
            part = jnp.max(scores.reshape(tokens // 8, 8, tokens), axis=0)
            top = part if top is None else jnp.maximum(top, part)
            if start + tokens == keys:
                r.tops[parity] = jnp.broadcast_to(jnp.max(top, axis=0, keepdims=True), (8, tokens))
            return top

        def finish(step, sums):
            target = self.far_first(step)
            inverse = 1.0 / sums[HEAD : HEAD + 1]
            mixed = jnp.where(iota((slot, 1), 0) < HEAD, sums * inverse, 0.0)
            r.mixed_full[target] = mixed
            r.mixed_send[target] = mixed.astype(LOW)
            r.inverse[target] = jnp.broadcast_to(inverse, (8, tokens))

        def half_step(step, parity, with_next, with_last, wait_kept):
            if wait_kept:
                keep(step - 2, parity).wait()
            offset = r.tops[parity, 0:1] * factor
            top = sums = None
            for start in range(0, keys, tokens):
                if with_next:
                    top = own_scores(step + 1, 1 - parity, start, top)
                for inner in range(start, start + tokens, LANES):
                    powers = jnp.exp2(score_refs[parity][inner : inner + LANES] * factor - offset)
                    r.probs[parity, inner : inner + LANES] = powers.astype(LOW)
                if with_last:
                    part = dot_nn(
                        r.vt[:, start : start + tokens], r.probs[1 - parity, start : start + tokens]
                    )
                    sums = part if sums is None else sums + part
            keep(step, parity).start()
            if with_last:
                finish(step - 1, sums)
                send(self.far_first(step - 1), step - 1).start()

        top = None
        for start in range(0, keys, tokens):
            top = own_scores(0, 0, start, top)
        half_step(0, 0, True, False, False)
        half_step(1, 1, True, True, False)

        def pair(number, carry):
            step = 2 + 2 * number
            half_step(step, 0, True, True, True)
            half_step(step + 1, 1, True, True, True)
            return carry

        lax.fori_loop(0, sz.seqs // 2 - 2, pair, 0)
        half_step(sz.seqs - 2, 0, True, True, True)
        half_step(sz.seqs - 1, 1, False, True, True)
        finish(sz.seqs - 1, dot_nn(r.vt[...], r.probs[1]))
        keep(sz.seqs - 2, 0).wait()
        keep(sz.seqs - 1, 1).wait()
        self.recall(0).start()
        r.mixed[pl.ds(pl.multiple_of(self.seq * slot, 16), slot)] = r.mixed_send[self.seq]
        for step in range(sz.seqs - 1):
            send(self.far_first(step), step).wait()

    def local_block(self):
        r, sz = self.r, self.sz
        tokens, channels = sz.tokens, sz.channels
        pad = sz.text_pad
        r.stream[...] = r.stream_in[...] + dot_tn(r.mixed[...], r.osp[...])
        for start, size in self.chunks(tokens):
            rows = slice(start, start + size)
            centred, scale = self.layer_parts(r.stream[rows])
            r.normed_cross[rows] = (centred * scale * row_of(r.gain_cross)).astype(LOW)
        r.query_text[...] = dot_nn(r.normed_cross[...], self.weight(self.r.query_cross)[...]).astype(LOW)
        r.cross[...] = dot_nt(r.text_key[...], r.query_text[...])
        for head in range(HEADS):
            rows = slice(head * pad, (head + 1) * pad)
            valid = iota((pad, 1), 0) < sz.text
            scores = jnp.where(valid, r.cross[rows] * self.scale, -1e30)
            powers = jnp.exp(scores - jnp.max(scores, axis=0, keepdims=True))
            attention = powers / jnp.sum(powers, axis=0, keepdims=True)
            r.cross[rows] = attention
            r.cross_low[rows] = attention.astype(LOW)
        r.cross_mixed[...] = dot_tn(r.cross_low[...], r.text_value[...]).astype(LOW)
        r.centred_cross[...] = r.stream[...]
        r.stream[...] = r.stream[...] + dot_nn(r.cross_mixed[...], self.weight(self.r.out_cross)[...])
        for start, size in self.chunks(tokens):
            rows = slice(start, start + size)
            centred, scale = self.layer_parts(r.stream[rows])
            r.normed_feed[rows] = (centred * scale * row_of(r.gain_feed)).astype(LOW)
        feed_up = self.weight(self.r.feed_up)
        joined = r.scores
        root = 0.7071067811865476
        block = 2 * LANES
        pieces = sz.hidden // block
        for piece in range(pieces):
            for place in (piece, piece + pieces):
                joined[place * tokens : (place + 1) * tokens] = dot_nn(
                    r.normed_feed[...], feed_up[:, place * block : (place + 1) * block]
                )
            for start, size in self.chunks(tokens):
                values = joined[piece * tokens + start : piece * tokens + start + size]
                gates_at = (piece + pieces) * tokens + start
                gates = joined[gates_at : gates_at + size]
                half = 0.5 * (1.0 + lax.erf(gates * root))
                slope = half + gates * (jnp.exp(-0.5 * gates * gates) * 0.3989422804014327)
                active = gates * half
                r.gated[start : start + size, piece * block : (piece + 1) * block] = (
                    values * active
                ).astype(LOW)
                joined[piece * tokens + start : piece * tokens + start + size] = active
                joined[gates_at : gates_at + size] = values * slope

        low = (
            r.stream[...] + dot_nt(r.gated[...], self.weight(self.r.feed_down)[...])
        ).astype(LOW)
        r.stream_low[...] = low
        project_out = self.weight(self.r.project_out)
        r.tmp[...] = dot_nn(r.stream_low[...], project_out[...])
        for start, size in self.chunks(tokens):
            rows = slice(start, start + size)
            wide = slice(start + sz.width, start + sz.width + size)
            mask = self.wide_mask(start + sz.width, size)
            r.output[rows] = (r.res6[wide] + r.tmp[rows]) * mask
            r.grad_branch[rows] = (r.cot6[wide] * mask).astype(LOW)
        r.grad[...] = dot_nt(r.grad_branch[...], project_out[...])
        r.grad_feed_low[...] = r.grad[...].astype(LOW)
        for piece in range(pieces):
            lanes = slice(piece * block, (piece + 1) * block)
            gate_lanes = slice(sz.hidden + piece * block, sz.hidden + (piece + 1) * block)
            r.grad_gated[...] = dot_nn(r.grad_feed_low[...], self.v.feed_down[:, lanes])
            for start, size in self.chunks(tokens):
                rows = slice(start, start + size)
                active = joined[piece * tokens + start : piece * tokens + start + size]
                gates_at = (piece + pieces) * tokens + start
                grads = r.grad_gated[rows]
                r.grad_joined[rows, lanes] = (grads * active).astype(LOW)
                r.grad_joined[rows, gate_lanes] = (grads * joined[gates_at : gates_at + size]).astype(LOW)
        r.tmp[...] = dot_nt(r.grad_joined[...], self.v.feed_up[...])
        self.layer_step(r.stream, r.gain_feed, 3, r.grad_cross_low)
        r.grad_cross_mixed[...] = dot_nt(r.grad_cross_low[...], self.v.out_cross[...]).astype(LOW)
        r.scores[0 : HEADS * pad] = dot_nt(r.text_value[...], r.grad_cross_mixed[...])
        for head in range(HEADS):
            rows = slice(head * pad, (head + 1) * pad)
            attention = r.cross[rows]
            grads = r.scores[rows]
            delta = jnp.sum(attention * grads, axis=0, keepdims=True)
            r.cross_scores[rows] = (attention * (grads - delta)).astype(LOW)
        r.grad_query_text[...] = (
            dot_tn(r.cross_scores[...], r.text_key[...]) * self.scale
        ).astype(LOW)
        r.tmp[...] = dot_nt(r.grad_query_text[...], self.v.query_cross[...])
        self.layer_step(r.centred_cross, r.gain_cross, 4, r.grad_self_low)
        r.gm_send[...] = dot_nt(r.osp[...], r.grad_self_low[...]).astype(LOW)
        slot = sz.slot
        copies = [
            self.remote(
                r.gm_send.at[pl.ds(pl.multiple_of(other * slot, 16), slot)],
                r.gm.at[self.seq],
                (self.batch, other),
            )
            for other in self.seq_others
        ]
        self.start(copies)
        self.gm_copies = copies
        r.gm[self.seq] = r.gm_send[pl.ds(pl.multiple_of(self.seq * slot, 16), slot)]

    def layer_step(self, source, gain, place, target):
        r = self.r
        gains = None
        for start, size in self.chunks(self.sz.tokens):
            rows = slice(start, start + size)
            part, gain_part = self.layer_back(source[rows], r.tmp[rows], row_of(gain))
            total = r.grad[rows] + part
            r.grad[rows] = total
            target[rows] = total.astype(LOW)
            gains = gain_part if gains is None else gains + gain_part
        r.gain_parts[place : place + 1] = gains

    def text_grads(self):
        r, sz = self.r, self.sz
        pad = sz.text_pad
        head_of = floor_div(iota((1, sz.channels), 1), HEAD)
        keys = dot_nn(r.cross_scores[...], r.query_text[...]) * self.scale
        values = dot_nn(r.cross_low[...], r.grad_cross_mixed[...])
        packed = None
        for number, grads in enumerate((keys, values)):
            total = None
            for head in range(HEADS):
                part = jnp.where(head_of == head, grads[head * pad : (head + 1) * pad], 0.0)
                total = part if total is None else total + part
            part = dot_nn(total.astype(LOW), r.place[number])
            packed = part if packed is None else packed + part
        r.text_send[...] = packed.astype(LOW)
        copies = [
            self.remote(
                r.text_send.at[:, pl.ds(pl.multiple_of(other * LANES, LANES), LANES)],
                r.text_recv.at[self.seq],
                (self.batch, other),
            )
            for other in self.seq_others
        ]
        self.start(copies)
        r.text_recv[self.seq] = r.text_send[
            :, pl.ds(pl.multiple_of(self.seq * LANES, LANES), LANES)
        ]
        self.text_copies = copies

    def text_second(self):
        r = self.r
        self.wait(self.text_copies)
        total = r.text_recv[0].astype(F32)
        for place in range(1, self.sz.seqs):
            total = total + r.text_recv[place].astype(F32)
        r.text_total[self.batch] = total
        copies = self.to_batch(r.text_total.at[self.batch], r.text_total.at[self.batch])
        self.start(copies)
        self.text_copies = copies

    def store_pack(self, start, rows, values):
        for shard in range(self.sz.seqs):
            self.r.pack[shard, start + rows.start : start + rows.stop] = values[
                :, shard * LANES : (shard + 1) * LANES
            ].astype(LOW)

    def early_grads(self):
        r, sz = self.r, self.sz
        channels = sz.channels
        rows = iota((2 * channels, 1), 0)
        target = jnp.where(rows >= channels, rows + (3 * LANES - channels), rows)
        spread = jnp.where(iota((1, 6 * LANES), 1) == target, 1.0, 0.0).astype(LOW)
        for z in range(sz.seqs // 2):
            wide = 2 * channels
            grads = dot_nn(r.grad_joined[:, z * wide : (z + 1) * wide], spread).astype(LOW)
            sums = dot_tn(r.normed_feed[...], grads)
            for tile in range(6):
                start = sz.start.up + (tile % 3) * channels
                r.pack[2 * z + tile // 3, start : start + channels] = sums[
                    :, tile * LANES : (tile + 1) * LANES
                ].astype(LOW)
        size = sz.down_rows
        tail = sz.hidden - 2 * size
        placed = [dot_nn(r.grad_feed_low[...], r.place[number]).astype(LOW) for number in range(3)]
        sums = dot_tn(r.gated[:, 0:size], placed[0]) + dot_tn(r.gated[:, size : 2 * size], placed[1])
        extra = dot_tn(r.gated[:, 2 * size :], placed[2])
        self.store_pack(sz.start.down, slice(0, tail), sums[0:tail] + extra)
        self.store_pack(sz.start.down, slice(tail, size), sums[tail:])
        sums = (
            dot_tn(r.stream_low[...], dot_nn(r.grad_branch[...], r.place[0]).astype(LOW))
            + dot_tn(r.cross_mixed[...], dot_nn(r.grad_cross_low[...], r.place[1]).astype(LOW))
            + dot_tn(r.normed_cross[...], dot_nn(r.grad_query_text[...], r.place[2]).astype(LOW))
        )
        self.store_pack(sz.start.trio, slice(0, channels), sums)

    def recall(self, step):
        r = self.r
        return pltpu.make_async_copy(
            r.kept_probs.at[lax.rem(self.seq + step, self.sz.seqs)],
            r.probs.at[lax.rem(step, 2)],
            r.local_sems.at[len(Fetched._fields) + 2 + lax.rem(step, 2)],
        )

    def attention_back(self):
        r, sz = self.r, self.sz
        keys, tokens, slot = sz.keys, sz.tokens, sz.slot
        self.wait(self.gm_copies)
        self.in_pieces += self.gather_piece(r.act_in, range(1, sz.rows))
        r.scores[0:keys, 0:LANES] = jnp.zeros((keys, LANES), F32)
        row = iota((slot, 1), 0)
        to_lanes = jnp.where(
            (iota((slot, LANES), 0) == iota((slot, LANES), 1)) & (iota((slot, LANES), 0) < HEAD), 1.0, 0.0
        ).astype(LOW)
        to_values = jnp.where(
            (iota((slot, LANES), 0) + 2 * HEAD == iota((slot, LANES), 1))
            & (iota((slot, LANES), 0) < HEAD),
            1.0,
            0.0,
        ).astype(LOW)

        def block(step, carry):
            source = lax.rem(self.seq + step, sz.seqs)
            slot_now = lax.rem(step, 2)
            self.recall(step).wait()

            @pl.when(step < sz.seqs - 1)
            def _():
                self.recall(step + 1).start()

            scaled = (r.gm[source].astype(F32) * r.inverse[source, 0:1]).astype(LOW).astype(F32)
            delta = -jnp.sum(r.mixed_full[source] * scaled, axis=0, keepdims=True)
            high = delta.astype(LOW).astype(F32)
            middle = (delta - high).astype(LOW).astype(F32)
            rest = delta - high - middle
            extended = jnp.where(row == HEAD, high, scaled)
            extended = jnp.where(row == HEAD + 1, middle, extended)
            extended = jnp.where(row == HEAD + 2, rest, extended).astype(LOW)
            query_rows = pl.ds(pl.multiple_of(source * tokens, tokens), tokens)
            token_grads = dot_tn(scaled.astype(LOW), to_values).astype(LOW)
            queries = r.qkv[query_rows]
            grad_query = None
            for start in range(0, keys, tokens):
                rows = slice(start, start + tokens)
                grads = dot_nn(r.vh[rows], extended)
                powers = r.probs[slot_now, rows]
                low = (powers.astype(F32) * grads).astype(LOW)
                r.scores[rows, 0:LANES] += dot_nn(low, queries) + dot_nn(powers, token_grads)
                part = dot_nn(r.kt[:, rows], low)
                grad_query = part if grad_query is None else grad_query + part
            r.kh[query_rows] = dot_tn((grad_query * self.scale).astype(LOW), to_lanes).astype(LOW)
            return carry

        lax.fori_loop(0, sz.seqs // 2, block, 0)
        self.sums_batch(0)
        self.sums_batch(1)
        lax.fori_loop(sz.seqs // 2, sz.seqs, block, 0)
        factor = jnp.where(iota((1, LANES), 1) < 2 * HEAD, self.scale, 1.0)
        for place in range(sz.seqs):
            rows = slice(place * tokens, (place + 1) * tokens)
            grads = r.scores[rows, 0:LANES] * factor
            r.qh[rows] = (grads + r.kh[rows].astype(F32)).astype(LOW)
        lanes = pl.ds(pl.multiple_of(self.seq * LANES, LANES), LANES)
        copies = [
            self.remote(
                r.qh.at[pl.ds(pl.multiple_of(other * tokens, tokens), tokens)],
                r.gp.at[:, lanes],
                (self.batch, other),
            )
            for other in self.seq_others
        ]
        self.start(copies)
        r.gp[:, lanes] = r.qh[pl.ds(pl.multiple_of(self.seq * tokens, tokens), tokens)]
        self.gp_copies = copies
        self.text_second()

    def norm_sums(self, number, rows_of):
        first = second = None
        mean, inverse = self.norm(number)
        for start, size in self.chunks(self.sz.tokens):
            grads, values = rows_of(start, size)
            one, two = col_sum(grads), col_sum(grads * ((values - mean) * inverse))
            first = one if first is None else first + one
            second = two if second is None else second + two
        return first, second

    def norm_factors(self, number, gain, total):
        gains = row_of(gain)
        sums = self.grouped(total * gains) / self.count()
        mean, inverse = self.norm(number)
        return mean, inverse, gains * inverse, sums[0:1] * inverse, sums[1:2] * inverse

    def slope(self, source, number, gain, start, size):
        mean, inverse = self.norm(number)
        normed = (source[start : start + size] - mean) * inverse
        values = normed * row_of(gain)
        gate = sigmoid(values)
        return normed, gate * (1.0 + values * (1.0 - gate)) * self.wide_mask(start, size)

    def residual_back(self):
        r, sz = self.r, self.sz
        width, tokens, channels = sz.width, sz.tokens, sz.channels
        self.wait(self.gp_copies)
        r.tmp[...] = dot_nt(r.gp[...], r.wqkv[...])
        self.layer_step(r.stream_in, r.gain_self, 5, r.grad_in_low)
        r.gblk6[width : width + tokens] = dot_nt(r.grad_in_low[...], self.v.project_in[...])
        halo = self.halo(r.gblk6)
        halo.start()

        def block_rows(start, size):
            wide = slice(start + width, start + width + size)
            return r.gblk6[wide], r.res6[wide]

        self.stats_store(3, self.norm_sums(2, block_rows))
        stats = self.stats_start(3)
        self.wait(self.late)
        self.late = []
        self.gather_in = self.gather_forward(r.act_in, self.in_pieces)
        self.sums_cross(0)
        self.sums_cross(1)
        self.middle_grads()
        self.sums_core(2)
        halo.wait()
        self.wait(stats)
        total = self.stats_total(3)
        r.gain_parts[2:3] = total[1:2]
        mean, inverse, factor, first, second = self.norm_factors(2, r.gain_block, total)
        for start, size in self.chunks(sz.wide):
            rows = slice(start, start + size)
            mask = self.wide_mask(start, size)
            normed = (r.res6[rows] - mean) * inverse
            grads = r.cot6[rows] * mask + r.gblk6[rows] * factor - mask * (first + normed * second)
            r.cot6[rows] = grads
            self.shifts(r.shift_grad, start, size, grads * self.inside_mask(start, size))
        r.gact6[width : width + tokens] = self.conv_back(r.shift_grad, self.v.conv_second)
        halo = self.halo(r.gact6)
        halo.start()

        def mid_rows(start, size):
            wide = slice(start + width, start + width + size)
            normed, slope = self.slope(r.mid6, 1, r.gain_mid, start + width, size)
            return r.gact6[wide] * slope, r.mid6[wide]

        self.stats_store(4, self.norm_sums(1, mid_rows))
        stats = self.stats_start(4)
        self.conv_pack(sz.start.second, r.shifted, r.shift_grad)
        self.sums_core(3)
        self.sums_batch(2)
        halo.wait()
        self.wait(stats)
        total = self.stats_total(4)
        r.gain_parts[1:2] = total[1:2]
        mean, inverse, factor, first, second = self.norm_factors(1, r.gain_mid, total)
        time_total = None
        for start, size in self.chunks(sz.wide):
            rows = slice(start, start + size)
            normed, slope = self.slope(r.mid6, 1, r.gain_mid, start, size)
            grads = r.gact6[rows] * slope * factor - self.wide_mask(start, size) * (
                first + normed * second
            )
            self.shifts(r.shift_grad, start, size, grads)
            if width <= start < width + tokens:
                part = col_sum(grads)
                time_total = part if time_total is None else time_total + part
        first_copies = self.conv_send(r.shift_grad, r.first_send, r.first_grads)
        r.gblk6[width : width + tokens] = self.conv_back(r.shift_grad, self.v.conv_first)

        def in_rows(start, size):
            wide = slice(start + width, start + width + size)
            normed, slope = self.slope(r.lat6, 0, r.gain_in, start + width, size)
            return r.gblk6[wide] * slope, r.lat6[wide]

        parts = r.gain_parts
        self.stats_store(5, self.norm_sums(0, in_rows))
        stats = self.stats_start(5)
        r.extra_send[...] = jnp.zeros(r.extra_send.shape, F32)
        r.extra_send[2:3] = time_total
        r.extra_send[3:6] = parts[3:6]
        r.extra_recv[self.seq] = r.extra_send[...]
        extras = self.to_seq(lambda other: r.extra_send, r.extra_recv.at[self.seq])
        self.start(extras)
        self.sums_batch(3)
        self.sums_z(0)
        first_copies = self.conv_grads(
            first_copies, self.gather_in, r.first_grads, r.act_in, r.first_part, r.first_recv
        )
        self.sums_cross(2)
        self.sums_cross(3)
        self.sums_z(1)
        self.wait(stats)
        total = self.stats_total(5)
        mean, inverse, factor, first, second = self.norm_factors(0, r.gain_in, total)
        self.wait(extras)
        sums = r.extra_recv[0]
        for place in range(1, sz.seqs):
            sums = sums + r.extra_recv[place]
        r.final_send[...] = sums
        r.final_send[1:2] = total[1:2]
        r.final_send[0:1] = parts[1:2]
        r.final_send[6:7] = parts[2:3]
        r.final_recv[self.batch] = r.final_send[...]
        self.final_copies = self.to_batch(r.final_send, r.final_recv.at[self.batch])
        self.start(self.final_copies)
        for start, size in self.chunks(tokens):
            wide = slice(start + width, start + width + size)
            normed, slope = self.slope(r.lat6, 0, r.gain_in, start + width, size)
            r.latent_grad[start : start + size] = (
                r.cot6[wide]
                + r.gblk6[wide] * slope * factor
                - self.wide_mask(start + width, size) * (first + normed * second)
            )
        first_copies = self.conv_gather(first_copies, r.first_part, r.first_recv, r.conv_first_sum)
        self.sums_z(2)
        self.sums_z(3)
        self.sums_gather(0)
        self.sums_gather(1)
        self.sums_gather(2)
        self.sums_gather(3)
        self.wait(first_copies)

    def middle_grads(self):
        r, sz = self.r, self.sz
        self.store_pack(sz.start.heads, slice(0, sz.channels), dot_tn(r.normed_self[...], r.gp[...]))
        outer = dot_nn(r.mixed[...], dot_nn(r.grad_self_low[...], r.place[0]).astype(LOW))
        inner = dot_tn(r.normed_block[...], dot_nn(r.grad_in_low[...], r.place[1]).astype(LOW))
        self.store_pack(sz.start.pair, slice(0, sz.channels), outer[0 : sz.channels] + inner)
        self.store_pack(sz.start.pair, slice(sz.channels, HEADS * sz.slot), outer[sz.channels :])

    def conv_pack(self, pack_start, shifted, grads):
        r, sz = self.r, self.sz
        own = grads[1, sz.width : sz.width + sz.tokens]
        placed = [dot_nn(own, r.place[number]).astype(LOW) for number in range(3)]
        for col in range(3):
            total = None
            for row in range(3):
                start = row * sz.width
                part = dot_tn(shifted[col, start : start + sz.tokens], placed[row])
                total = part if total is None else total + part
            self.store_pack(pack_start, slice(col * sz.channels, (col + 1) * sz.channels), total)

    def sums_setup(self):
        r, sz = self.r, self.sz
        half, batches = sz.seqs // 2, sz.batches
        self.stages = []
        for start, size in sz.chunks:
            rows = pl.ds(start, size)
            part = size // batches
            quarter = pl.ds(start // batches, part)
            one = [
                self.remote(r.pack.at[2 * z + 1 - self.core, rows], r.recv_core.at[z, rows], self.partner)
                for z in range(half)
            ]
            pair = half // 2
            x_rows = [
                pl.ds(pl.multiple_of(start + (2 * y + 1 - self.batch_x) * part, 16), part)
                for y in range(2)
            ]
            y_rows = pl.ds(pl.multiple_of(start + 2 * (1 - self.batch_y) * part, 16), 2 * part)
            two = [
                self.remote(
                    r.recv_core.at[pl.ds(0, pair), x_rows[y]],
                    r.recv_first.at[0, :, pl.ds(start // 2 + y * part, part)],
                    self.x_peer,
                )
                for y in range(2)
            ]
            two.append(
                self.remote(
                    r.recv_core.at[pl.ds(pair, pair), y_rows],
                    r.recv_first.at[1, :, pl.ds(start // 2, 2 * part)],
                    self.y_peer,
                )
            )
            far_y = 2 * (1 - self.batch_y) + self.batch_x
            far_x = 2 * self.batch_y + 1 - self.batch_x
            cross = [
                self.remote(
                    r.recv_core.at[
                        pl.ds(place * pair, pair), pl.ds(pl.multiple_of(start + far * part, 16), part)
                    ],
                    r.recv_second.at[pl.ds(place * pair, pair), quarter],
                    peer,
                )
                for place, (far, peer) in enumerate(((far_y, self.y_peer), (far_x, self.x_peer)))
            ]
            three = [
                self.remote(
                    r.recv_second.at[other, quarter],
                    r.recv_z.at[step, quarter],
                    (self.batch, other * 2 + self.core),
                )
                for step, other in enumerate(self.z_others)
            ]
            four = [
                self.remote(
                    r.gathered.at[pl.ds(pl.multiple_of(start + self.batch * part, 16), part)],
                    r.gathered.at[pl.ds(pl.multiple_of(start + self.batch * part, 16), part)],
                    (other, self.seq),
                )
                for other in self.batch_others
            ]
            self.stages.append((one, two, cross, three, four))

    def sums_core(self, number):
        self.start(self.stages[number][0])

    def sums_batch(self, number):
        r, sz = self.r, self.sz
        start, size = sz.chunks[number]
        self.wait(self.stages[number][0])

        @pl.loop(0, sz.seqs // 2)
        def add(z):
            rows = pl.ds(start, size)
            r.recv_core[z, rows] = (
                r.pack[2 * z + self.core, rows].astype(F32) + r.recv_core[z, rows].astype(F32)
            ).astype(LOW)

        self.start(self.stages[number][1])

    def sums_cross(self, number):
        r, sz = self.r, self.sz
        start, size = sz.chunks[number]
        part = size // sz.batches
        pair = sz.seqs // 4
        self.wait(self.stages[number][1])

        def add(target, source):
            r.recv_core[target] = (r.recv_core[target].astype(F32) + source.astype(F32)).astype(LOW)

        @pl.loop(0, pair)
        def sums(z):
            for y in range(2):
                rows = pl.ds(pl.multiple_of(start + (2 * y + self.batch_x) * part, 16), part)
                add((z, rows), r.recv_first[0, z, pl.ds(start // 2 + y * part, part)])
            rows = pl.ds(pl.multiple_of(start + 2 * self.batch_y * part, 16), 2 * part)
            add((z + pair, rows), r.recv_first[1, z, pl.ds(start // 2, 2 * part)])

        self.start(self.stages[number][2])

    def sums_z(self, number):
        r, sz = self.r, self.sz
        start, size = sz.chunks[number]
        part = size // sz.batches
        quarter = pl.ds(start // sz.batches, part)
        self.wait(self.stages[number][2])

        @pl.loop(0, sz.seqs // 2)
        def add(z):
            own = r.recv_core[z, pl.ds(pl.multiple_of(start + self.batch * part, 16), part)]
            r.recv_second[z, quarter] = (
                own.astype(F32) + r.recv_second[z, quarter].astype(F32)
            ).astype(LOW)

        self.start(self.stages[number][3])

    def sums_gather(self, number):
        r, sz = self.r, self.sz
        start, size = sz.chunks[number]
        part = size // sz.batches
        quarter = pl.ds(start // sz.batches, part)
        self.wait(self.stages[number][3])
        total = r.recv_second[self.z_pos, quarter].astype(F32)
        for step in range(sz.seqs // 2 - 1):
            total = total + r.recv_z[step, quarter].astype(F32)
        own = pl.ds(pl.multiple_of(start + self.batch * part, 16), part)
        r.gathered[own] = total.astype(LOW)
        self.start(self.stages[number][4])

    def run(self):
        self.entry()
        self.sums_setup()
        self.residual()
        self.attention()
        self.local_block()
        self.text_grads()
        self.early_grads()
        self.sums_core(0)
        self.sums_core(1)
        self.attention_back()
        self.residual_back()
        for stages in self.stages:
            self.wait(stages[4])
        self.wait(self.text_copies)
        self.wait(self.final_copies)
        assert self.used <= SEMAPHORES


def fused_call(sz, operands):
    t, c = sz.tokens, sz.channels
    outs = dict(
        output=((t, c), F32),
        latent_grad=((t, c), F32),
        final_recv=((sz.batches, 8, c), F32),
        time_all=((sz.batches, 8, sz.emb), F32),
        text_all=((sz.batches, sz.text_pad, sz.context), LOW),
        text_total=((sz.batches, sz.text_pad, LANES), F32),
        gathered=((sz.pack_rows, LANES), LOW),
        conv_first_sum=((sz.conv_rows, c), LOW),
        kept_probs=((sz.seqs, sz.keys, t), LOW),
    )
    scratch = buffers(sz)
    vmem = pl.BlockSpec(memory_space=pltpu.VMEM)
    anywhere = pl.BlockSpec(memory_space=pl.ANY)
    fetched = [getattr(operands, name) for name in Fetched._fields]
    specs = operands._replace(**{name: vmem for name in Inputs._fields})
    specs = specs._replace(**{name: anywhere for name in Fetched._fields})
    specs = specs._replace(
        latents=anywhere, cotangent=anywhere, heights=pl.BlockSpec(memory_space=pltpu.SMEM)
    )
    names = list(Inputs._fields) + list(outs) + list(scratch)
    shapes = [pltpu.VMEM(shape, kind) for shape, kind in scratch.values()]
    shapes += [pltpu.VMEM(operand.shape, operand.dtype) for operand in fetched]
    shapes += [pltpu.SemaphoreType.DMA((2, SEMAPHORES)), pltpu.SemaphoreType.DMA((len(fetched) + 4,))]

    def body(*refs):
        count = len(names)
        named = types.SimpleNamespace(**dict(zip(names, refs[:count])))
        named.sems, named.local_sems = refs[-2:]
        Fused(sz, named, Fetched(*refs[count:-2])).run()

    return pl.pallas_call(
        body,
        out_shape=tuple(jax.ShapeDtypeStruct(shape, kind) for shape, kind in outs.values()),
        in_specs=list(specs),
        out_specs=(vmem,) * (len(outs) - 1) + (anywhere,),
        scratch_shapes=shapes,
        compiler_params=pltpu.CompilerParams(
            collective_id=5, has_side_effects=True, vmem_limit_bytes=63 << 20
        ),
    )(*operands)


class Outputs(typing.NamedTuple):
    output: typing.Any
    latent_grad: typing.Any
    gain_in: typing.Any
    conv_first: typing.Any
    time_weight: typing.Any
    gain_mid: typing.Any
    conv_second: typing.Any
    gain_block: typing.Any
    project_in: typing.Any
    gain_self: typing.Any
    query_self: typing.Any
    key_self: typing.Any
    value_self: typing.Any
    out_self: typing.Any
    gain_cross: typing.Any
    query_cross: typing.Any
    key_cross: typing.Any
    value_cross: typing.Any
    out_cross: typing.Any
    gain_feed: typing.Any
    feed_up: typing.Any
    feed_down: typing.Any
    project_out: typing.Any


def unpack_kernel(
    sz,
    output,
    latent_grad,
    final_recv,
    time_all,
    text_all,
    text_total,
    gathered,
    first_sum,
    *out_refs,
):
    outs = Outputs(*out_refs)
    channels = sz.channels
    outs.output[...] = output[...]
    outs.latent_grad[...] = latent_grad[...]
    eye = jnp.where(iota((LANES, LANES), 0) == iota((LANES, LANES), 1), 1.0, 0.0).astype(LOW)

    def turned(start, rows):
        return dot_nt(eye, gathered[start : start + rows])

    def three(values, *targets):
        for place, target in enumerate(targets):
            target[...] = values[place * HEAD : (place + 1) * HEAD]

    for tile in range(3):
        lanes = slice(tile * LANES, min((tile + 1) * LANES, outs.feed_up.shape[1]))
        start = sz.start.up + tile * channels
        outs.feed_up[:, lanes] = gathered[start : start + channels, : lanes.stop - lanes.start].astype(F32)
    values = turned(sz.start.down, sz.down_rows)
    for place in range(3):
        lanes = slice(place * sz.down_rows, min((place + 1) * sz.down_rows, sz.hidden))
        outs.feed_down[:, lanes] = values[
            place * HEAD : (place + 1) * HEAD, : lanes.stop - lanes.start
        ]
    three(turned(sz.start.trio, channels), outs.project_out, outs.out_cross, outs.query_cross)
    three(turned(sz.start.heads, channels), outs.query_self, outs.key_self, outs.value_self)
    outs.project_in[...] = turned(sz.start.pair, channels)[HEAD : 2 * HEAD]
    wide = turned(sz.start.pair, HEADS * sz.slot)[:HEAD].astype(LOW)
    source = iota((1, channels), 1)
    target = source + (sz.slot - HEAD) * floor_div(source, HEAD)
    squeeze = jnp.where(iota((HEADS * sz.slot, 1), 0) == target, 1.0, 0.0).astype(LOW)
    outs.out_self[...] = dot_nn(wide, squeeze)
    for col in range(3):
        values = turned(sz.start.second + col * channels, channels)
        for row in range(3):
            outs.conv_second[row, col] = values[row * HEAD : (row + 1) * HEAD]
            at = (3 * row + col) * sz.slot
            outs.conv_first[row, col] = first_sum[at : at + sz.slot].astype(F32)[:HEAD]
    text = None
    for place in range(sz.batches):
        grads = text_total[place]
        high = grads.astype(LOW)
        rest = (grads - high.astype(F32)).astype(LOW)
        part = dot_tn(high, text_all[place]) + dot_tn(rest, text_all[place])
        text = part if text is None else text + part
    three(text, outs.key_cross, outs.value_cross)
    pick = jnp.where(
        (iota((channels, LANES), 0) == iota((channels, LANES), 1) + lax.axis_index(SEQ) * HEAD)
        & (iota((channels, LANES), 1) < HEAD),
        1.0,
        0.0,
    ).astype(LOW)
    total = time = None
    for place in range(sz.batches):
        rows = final_recv[place]
        total = rows if total is None else total + rows
        picked = dot_nn(split_three(jnp.where(iota((8, 1), 0) == 2, rows, 0.0)), pick)
        act = time_all[place]
        act = pltpu.roll(act, 2, 0)
        part = dot_tn(picked.astype(LOW), jnp.concatenate([act, act, act], axis=0).astype(LOW))
        time = part if time is None else time + part
    outs.time_weight[...] = time[:HEAD]
    gains = sum_three(dot_nn(split_three(total), pick))
    order = (
        outs.gain_mid,
        outs.gain_in,
        None,
        outs.gain_feed,
        outs.gain_cross,
        outs.gain_self,
        outs.gain_block,
    )
    for place, out in enumerate(order):
        if out is not None:
            out[...] = gains[place : place + 1, :HEAD]


def unpack_call(sz, results):
    channels, hidden = sz.channels, sz.hidden
    square = jax.ShapeDtypeStruct((HEAD, channels), F32)
    gain = jax.ShapeDtypeStruct((1, HEAD), F32)
    image = jax.ShapeDtypeStruct((sz.tokens, channels), F32)
    conv = jax.ShapeDtypeStruct((3, 3, HEAD, channels), F32)
    context = jax.ShapeDtypeStruct((HEAD, sz.context), F32)
    shapes = Outputs(*[square] * len(Outputs._fields))._replace(
        output=image,
        latent_grad=image,
        gain_in=gain,
        gain_mid=gain,
        gain_block=gain,
        gain_self=gain,
        gain_cross=gain,
        gain_feed=gain,
        conv_first=conv,
        conv_second=conv,
        time_weight=jax.ShapeDtypeStruct((HEAD, sz.emb), F32),
        key_cross=context,
        value_cross=context,
        feed_up=jax.ShapeDtypeStruct((channels, 2 * hidden // sz.seqs), F32),
        feed_down=jax.ShapeDtypeStruct((HEAD, hidden), F32),
    )
    vmem = pl.BlockSpec(memory_space=pltpu.VMEM)
    return Outputs(
        *pl.pallas_call(
            lambda *refs: unpack_kernel(sz, *refs),
            out_shape=tuple(shapes),
            in_specs=[vmem] * len(results),
            out_specs=(vmem,) * len(shapes),
            compiler_params=pltpu.CompilerParams(vmem_limit_bytes=60 << 20),
        )(*results)
    )


def fast_device(*arguments):
    given = Inputs(*arguments)
    latents = given.latents
    sz = Sizes(
        lax.axis_size(BATCH),
        lax.axis_size(SEQ),
        latents,
        given.time_vector,
        given.text_states,
        given.feed_down,
    )
    channels = sz.channels
    flat = given._replace(
        latents=latents.reshape(sz.tokens, channels),
        cotangent=given.cotangent.reshape(sz.tokens, channels),
        text_states=given.text_states.reshape(sz.text, sz.context),
        time_weight=given.time_weight.T,
        key_cross=given.key_cross.T,
        value_cross=given.value_cross.T,
        feed_down=given.feed_down.T,
    )
    results = fused_call(sz, flat)[:-1]
    outs = unpack_call(sz, results)
    shaped = outs._replace(
        output=outs.output.reshape(latents.shape), latent_grad=outs.latent_grad.reshape(latents.shape)
    )
    shaped = [jnp.swapaxes(one, -2, -1) if one.shape[-2] == HEAD else one for one in shaped]
    return tuple(one.reshape(-1) if one.shape[0] == 1 and one.ndim == 2 else one for one in shaped)


def on_device(
    latents,
    heights,
    time_vector,
    text_states,
    gain_in,
    conv_first,
    time_weight,
    gain_mid,
    conv_second,
    gain_block,
    project_in,
    gain_self,
    query_self,
    key_self,
    value_self,
    out_self,
    gain_cross,
    query_cross,
    key_cross,
    value_cross,
    out_cross,
    gain_feed,
    feed_up,
    feed_down,
    project_out,
    cotangent,
):
    images_in, rows_in, col_count, channels = latents.shape
    seq_size = lax.axis_size(SEQ)
    seq_index = lax.axis_index(SEQ)
    block_rows = rows_in * col_count
    keys_count = block_rows * seq_size
    score_scale = HEAD ** (-0.5)
    row_ids = seq_index * rows_in + jnp.arange(rows_in, dtype=jnp.int32)

    def spread_fn(values):
        return values

    def pick_fn(values):
        return values

    images, row_count = (latents.shape[0], latents.shape[1])
    tok_rows = row_count * col_count
    tokens = images * tok_rows
    row_valid = (row_ids[None, :] < heights[:, None]).astype(jnp.int32)
    row_mask = row_valid.astype(jnp.float32)
    cell_mask = row_mask[:, :, None, None]
    key_rows = jnp.arange(keys_count, dtype=jnp.int32) // col_count
    key_mask = (key_rows[None, :] < heights[:, None]).astype(jnp.int32)
    cell_counts = (heights * (col_count * (channels // GROUPS))).astype(jnp.float32)

    def res_piece(values, norm_gain, sum_first, sum_second):
        return (
            jax.nn.silu(group_apply(values, norm_gain, sum_first, sum_second, cell_counts))
            * cell_mask
        )

    def block_piece(values, norm_gain, sum_first, sum_second):
        return group_apply(values, norm_gain, sum_first, sum_second, cell_counts)

    first_in, second_in = norm_stats(latents, row_mask, spread_fn, pick_fn)
    act_in = res_piece(latents, gain_in, first_in, second_in).astype(jnp.bfloat16)
    padded_in = rows_halo(act_in)
    conv_out = conv_rows(padded_in, conv_first)
    time_act = jax.nn.silu(time_vector.astype(jnp.float32)).astype(jnp.bfloat16)
    time_term = jnp.dot(time_act, time_weight, preferred_element_type=jnp.float32)
    mid_in = conv_out + time_term[:, None, None, :]
    first_mid, second_mid = norm_stats(mid_in, row_mask, spread_fn, pick_fn)
    act_mid = res_piece(mid_in, gain_mid, first_mid, second_mid).astype(jnp.bfloat16)
    padded_mid = rows_halo(act_mid)
    resid = latents + conv_rows(padded_mid, conv_second)
    first_block, second_block = norm_stats(resid, row_mask, spread_fn, pick_fn)
    normed_block = (
        block_piece(resid, gain_block, first_block, second_block)
        .reshape(tokens, channels)
        .astype(jnp.bfloat16)
    )
    stream_in = jnp.dot(normed_block, project_in, preferred_element_type=jnp.float32)
    normed_self = layer_norm(stream_in, gain_self).astype(jnp.bfloat16)
    joined_self = jnp.concatenate((query_self, key_self, value_self), axis=1)
    projected = (
        jnp.dot(normed_self, joined_self, preferred_element_type=jnp.float32)
        .astype(jnp.bfloat16)
        .reshape(images, tok_rows, 3 * channels)
    )
    queries = projected[:, :, :channels]
    keys_local = projected[:, :, channels : 2 * channels]
    values_local = projected[:, :, 2 * channels :]
    keys_all = lax.all_gather(keys_local, SEQ, axis=1, tiled=True)
    values_all = lax.all_gather(values_local, SEQ, axis=1, tiled=True)

    def forward_image(bundle):
        image_queries, image_keys, image_values, image_mask = bundle
        query_blocks = image_queries.reshape(-1, block_rows, channels)
        return lax.map(
            lambda part: self_forward((part, image_keys, image_values, image_mask), score_scale),
            query_blocks,
        )

    attn_mixed, log_totals = lax.map(forward_image, (queries, keys_all, values_all, key_mask))
    mixed_flat = attn_mixed.reshape(tokens, channels)
    stream_self = stream_in + jnp.dot(mixed_flat, out_self, preferred_element_type=jnp.float32)
    normed_cross = layer_norm(stream_self, gain_cross).astype(jnp.bfloat16)
    query_text = (
        jnp.dot(normed_cross, query_cross, preferred_element_type=jnp.float32)
        .astype(jnp.bfloat16)
        .reshape(images, tok_rows, HEADS, HEAD)
    )
    text_flat = text_states.reshape(-1, text_states.shape[2])
    text_pairs = (
        jnp.dot(
            text_flat,
            jnp.concatenate((key_cross, value_cross), axis=1),
            preferred_element_type=jnp.float32,
        )
        .astype(jnp.bfloat16)
        .reshape(images, -1, 2, HEADS, HEAD)
    )
    text_keys = text_pairs[:, :, 0]
    text_values = text_pairs[:, :, 1]
    cross_scores = (
        jnp.einsum("iqhd,ikhd->ihqk", query_text, text_keys, preferred_element_type=jnp.float32)
        * score_scale
    )
    cross_attn = jnp.exp(cross_scores - jax.nn.logsumexp(cross_scores, axis=-1, keepdims=True))
    cross_low = cross_attn.astype(jnp.bfloat16)
    cross_mixed = (
        jnp.einsum("ihqk,ikhd->iqhd", cross_low, text_values, preferred_element_type=jnp.float32)
        .astype(jnp.bfloat16)
        .reshape(tokens, channels)
    )
    stream_cross = stream_self + jnp.dot(cross_mixed, out_cross, preferred_element_type=jnp.float32)
    normed_feed = layer_norm(stream_cross, gain_feed).astype(jnp.bfloat16)
    joined_feed = jnp.dot(normed_feed, feed_up, preferred_element_type=jnp.float32)
    gated = geglu(joined_feed).astype(jnp.bfloat16)
    stream_feed = stream_cross + jnp.dot(gated, feed_down, preferred_element_type=jnp.float32)
    stream_low = stream_feed.astype(jnp.bfloat16)
    branch_out = jnp.dot(stream_low, project_out, preferred_element_type=jnp.float32).reshape(
        images, row_count, col_count, channels
    )
    output = (resid + branch_out) * cell_mask
    grad_output = cotangent * cell_mask
    grad_branch = grad_output.reshape(tokens, channels).astype(jnp.bfloat16)
    grad_project_out = grad_dot(stream_low, grad_branch)
    grad_stream = back_dot(grad_branch, project_out)
    grad_feed_low = grad_stream.astype(jnp.bfloat16)
    grad_feed_down = grad_dot(gated, grad_feed_low)
    grad_gated = back_dot(grad_feed_low, feed_down)
    unused, pull_geglu = jax.vjp(geglu, joined_feed)
    grad_joined = pull_geglu(grad_gated)[0].astype(jnp.bfloat16)
    grad_feed_up = grad_dot(normed_feed, grad_joined)
    unused, pull_norm = jax.vjp(layer_norm, stream_cross, gain_feed)
    grad_part, grad_gain_feed = pull_norm(back_dot(grad_joined, feed_up))
    grad_stream = grad_stream + grad_part
    grad_cross_low = grad_stream.astype(jnp.bfloat16)
    grad_out_cross = grad_dot(cross_mixed, grad_cross_low)
    grad_cross_mixed = (
        back_dot(grad_cross_low, out_cross)
        .astype(jnp.bfloat16)
        .reshape(images, tok_rows, HEADS, HEAD)
    )
    grad_text_values = jnp.einsum(
        "ihqk,iqhd->ikhd", cross_low, grad_cross_mixed, preferred_element_type=jnp.float32
    )
    grad_cross_attn = jnp.einsum(
        "iqhd,ikhd->ihqk", grad_cross_mixed, text_values, preferred_element_type=jnp.float32
    )
    cross_delta = jnp.sum(cross_attn * grad_cross_attn, axis=-1, keepdims=True)
    grad_cross_scores = (cross_attn * (grad_cross_attn - cross_delta)).astype(jnp.bfloat16)
    grad_query_text = (
        (
            jnp.einsum(
                "ihqk,ikhd->iqhd", grad_cross_scores, text_keys, preferred_element_type=jnp.float32
            )
            * score_scale
        )
        .astype(jnp.bfloat16)
        .reshape(tokens, channels)
    )
    grad_text_keys = (
        jnp.einsum(
            "ihqk,iqhd->ikhd", grad_cross_scores, query_text, preferred_element_type=jnp.float32
        )
        * score_scale
    )
    text_wide = text_flat.astype(jnp.float32)
    grad_key_cross = exact_grad_dot(text_wide, grad_text_keys.reshape(-1, channels))
    grad_value_cross = exact_grad_dot(text_wide, grad_text_values.reshape(-1, channels))
    grad_query_cross = grad_dot(normed_cross, grad_query_text)
    unused, pull_norm = jax.vjp(layer_norm, stream_self, gain_cross)
    grad_part, grad_gain_cross = pull_norm(back_dot(grad_query_text, query_cross))
    grad_stream = grad_stream + grad_part
    grad_self_low = grad_stream.astype(jnp.bfloat16)
    grad_out_self = grad_dot(mixed_flat, grad_self_low)
    grad_mixed = (
        back_dot(grad_self_low, out_self).astype(jnp.bfloat16).reshape(images, tok_rows, channels)
    )

    def backward_image(bundle):
        image_queries, image_grads, image_totals, image_keys, image_values, image_mask = bundle
        query_blocks = image_queries.reshape(-1, block_rows, channels)
        grad_blocks = image_grads.reshape(-1, block_rows, channels)
        return lax.map(
            lambda part: query_side(
                (part[0], part[1], part[2], image_keys, image_values, image_mask), score_scale
            ),
            (query_blocks, grad_blocks, image_totals),
        )

    grad_queries, kept_attn, kept_grads = lax.map(
        backward_image, (queries, grad_mixed, log_totals, keys_all, values_all, key_mask)
    )
    grads_four = grad_mixed.reshape(images, -1, block_rows, HEADS, HEAD)
    queries_four = queries.reshape(images, -1, block_rows, HEADS, HEAD)
    row_total = tok_rows * lax.axis_size(SEQ)
    value_terms = jnp.einsum(
        "inhqk,inqhd->kihd", kept_attn, grads_four, preferred_element_type=jnp.float32
    )
    key_terms_part = (
        jnp.einsum(
            "inhqk,inqhd->kihd", kept_grads, queries_four, preferred_element_type=jnp.float32
        )
        * score_scale
    )
    summed = lax.psum_scatter(
        jnp.stack(
            (
                key_terms_part.reshape(row_total, images, -1),
                value_terms.reshape(row_total, images, -1),
            ),
            2,
        ).astype(jnp.bfloat16),
        SEQ,
        scatter_dimension=0,
        tiled=True,
    ).astype(jnp.float32)
    grad_keys = jnp.swapaxes(summed[:, :, 0], 0, 1)
    grad_values = jnp.swapaxes(summed[:, :, 1], 0, 1)
    grad_projected = jnp.concatenate(
        (
            grad_queries.reshape(images, tok_rows, channels),
            grad_keys.astype(jnp.bfloat16),
            grad_values.astype(jnp.bfloat16),
        ),
        axis=2,
    ).reshape(tokens, 3 * channels)
    grad_joined_self = grad_dot(normed_self, grad_projected)
    unused, pull_norm = jax.vjp(layer_norm, stream_in, gain_self)
    grad_part, grad_gain_self = pull_norm(back_dot(grad_projected, joined_self))
    grad_stream = grad_stream + grad_part
    grad_stream_low = grad_stream.astype(jnp.bfloat16)
    grad_project_in = grad_dot(normed_block, grad_stream_low)
    grad_block = back_dot(grad_stream_low, project_in).reshape(
        images, row_count, col_count, channels
    )
    grad_resid_part, grad_gain_block = norm_backward(
        block_piece,
        resid,
        gain_block,
        first_block,
        second_block,
        grad_block,
        row_mask,
        spread_fn,
        pick_fn,
    )
    grad_resid = grad_output + grad_resid_part
    grad_second_low = grad_resid.astype(jnp.bfloat16)
    grad_conv_second = conv_weight_grad(padded_mid, grad_second_low)
    grad_act_mid = conv_rows(grads_halo(grad_second_low), flipped(conv_second))
    grad_mid, grad_gain_mid = norm_backward(
        res_piece,
        mid_in,
        gain_mid,
        first_mid,
        second_mid,
        grad_act_mid,
        row_mask,
        spread_fn,
        pick_fn,
    )
    grad_time = jnp.sum(grad_mid, axis=(1, 2))
    grad_time_weight = exact_grad_dot(time_act.astype(jnp.float32), grad_time)
    grad_first_low = grad_mid.astype(jnp.bfloat16)
    grad_conv_first = conv_weight_grad(padded_in, grad_first_low)
    grad_act_in = conv_rows(grads_halo(grad_first_low), flipped(conv_first))
    grad_in_part, grad_gain_in = norm_backward(
        res_piece, latents, gain_in, first_in, second_in, grad_act_in, row_mask, spread_fn, pick_fn
    )
    latent_grad = grad_resid + grad_in_part
    shares = (
        lax.psum_scatter(
            grad_gain_in.reshape(1, -1).astype(jnp.bfloat16), SEQ, scatter_dimension=1, tiled=True
        ).astype(jnp.float32),
        lax.psum_scatter(
            grad_conv_first.reshape(-1, channels).astype(jnp.bfloat16),
            SEQ,
            scatter_dimension=1,
            tiled=True,
        ).astype(jnp.float32),
        lax.psum_scatter(
            grad_time_weight.astype(jnp.bfloat16), SEQ, scatter_dimension=1, tiled=True
        ).astype(jnp.float32),
        lax.psum_scatter(
            grad_gain_mid.reshape(1, -1).astype(jnp.bfloat16),
            SEQ,
            scatter_dimension=1,
            tiled=True,
        ).astype(jnp.float32),
        lax.psum_scatter(
            grad_conv_second.reshape(-1, channels).astype(jnp.bfloat16),
            SEQ,
            scatter_dimension=1,
            tiled=True,
        ).astype(jnp.float32),
        lax.psum_scatter(
            grad_gain_block.reshape(1, -1).astype(jnp.bfloat16),
            SEQ,
            scatter_dimension=1,
            tiled=True,
        ).astype(jnp.float32),
        lax.psum_scatter(
            grad_project_in.astype(jnp.bfloat16), SEQ, scatter_dimension=1, tiled=True
        ).astype(jnp.float32),
        lax.psum_scatter(
            grad_gain_self.reshape(1, -1).astype(jnp.bfloat16),
            SEQ,
            scatter_dimension=1,
            tiled=True,
        ).astype(jnp.float32),
        lax.psum_scatter(
            grad_joined_self[:, :channels].astype(jnp.bfloat16),
            SEQ,
            scatter_dimension=1,
            tiled=True,
        ).astype(jnp.float32),
        lax.psum_scatter(
            grad_joined_self[:, channels : 2 * channels].astype(jnp.bfloat16),
            SEQ,
            scatter_dimension=1,
            tiled=True,
        ).astype(jnp.float32),
        lax.psum_scatter(
            grad_joined_self[:, 2 * channels :].astype(jnp.bfloat16),
            SEQ,
            scatter_dimension=1,
            tiled=True,
        ).astype(jnp.float32),
        lax.psum_scatter(
            grad_out_self.astype(jnp.bfloat16), SEQ, scatter_dimension=1, tiled=True
        ).astype(jnp.float32),
        lax.psum_scatter(
            grad_gain_cross.reshape(1, -1).astype(jnp.bfloat16),
            SEQ,
            scatter_dimension=1,
            tiled=True,
        ).astype(jnp.float32),
        lax.psum_scatter(
            grad_query_cross.astype(jnp.bfloat16), SEQ, scatter_dimension=1, tiled=True
        ).astype(jnp.float32),
        lax.psum_scatter(
            grad_key_cross.astype(jnp.bfloat16), SEQ, scatter_dimension=1, tiled=True
        ).astype(jnp.float32),
        lax.psum_scatter(
            grad_value_cross.astype(jnp.bfloat16), SEQ, scatter_dimension=1, tiled=True
        ).astype(jnp.float32),
        lax.psum_scatter(
            grad_out_cross.astype(jnp.bfloat16), SEQ, scatter_dimension=1, tiled=True
        ).astype(jnp.float32),
        lax.psum_scatter(
            grad_gain_feed.reshape(1, -1).astype(jnp.bfloat16),
            SEQ,
            scatter_dimension=1,
            tiled=True,
        ).astype(jnp.float32),
        lax.psum_scatter(
            grad_feed_up.astype(jnp.bfloat16), SEQ, scatter_dimension=1, tiled=True
        ).astype(jnp.float32),
        lax.psum_scatter(
            grad_feed_down.astype(jnp.bfloat16), SEQ, scatter_dimension=1, tiled=True
        ).astype(jnp.float32),
        lax.psum_scatter(
            grad_project_out.astype(jnp.bfloat16), SEQ, scatter_dimension=1, tiled=True
        ).astype(jnp.float32),
    )
    totals = (
        lax.psum(shares[0].astype(jnp.bfloat16), BATCH).astype(jnp.float32),
        lax.psum(shares[1].astype(jnp.bfloat16), BATCH).astype(jnp.float32),
        lax.psum(shares[2].astype(jnp.bfloat16), BATCH).astype(jnp.float32),
        lax.psum(shares[3].astype(jnp.bfloat16), BATCH).astype(jnp.float32),
        lax.psum(shares[4].astype(jnp.bfloat16), BATCH).astype(jnp.float32),
        lax.psum(shares[5].astype(jnp.bfloat16), BATCH).astype(jnp.float32),
        lax.psum(shares[6].astype(jnp.bfloat16), BATCH).astype(jnp.float32),
        lax.psum(shares[7].astype(jnp.bfloat16), BATCH).astype(jnp.float32),
        lax.psum(shares[8].astype(jnp.bfloat16), BATCH).astype(jnp.float32),
        lax.psum(shares[9].astype(jnp.bfloat16), BATCH).astype(jnp.float32),
        lax.psum(shares[10].astype(jnp.bfloat16), BATCH).astype(jnp.float32),
        lax.psum(shares[11].astype(jnp.bfloat16), BATCH).astype(jnp.float32),
        lax.psum(shares[12].astype(jnp.bfloat16), BATCH).astype(jnp.float32),
        lax.psum(shares[13].astype(jnp.bfloat16), BATCH).astype(jnp.float32),
        lax.psum(shares[14].astype(jnp.bfloat16), BATCH).astype(jnp.float32),
        lax.psum(shares[15].astype(jnp.bfloat16), BATCH).astype(jnp.float32),
        lax.psum(shares[16].astype(jnp.bfloat16), BATCH).astype(jnp.float32),
        lax.psum(shares[17].astype(jnp.bfloat16), BATCH).astype(jnp.float32),
        lax.psum(shares[18].astype(jnp.bfloat16), BATCH).astype(jnp.float32),
        lax.psum(shares[19].astype(jnp.bfloat16), BATCH).astype(jnp.float32),
        lax.psum(shares[20].astype(jnp.bfloat16), BATCH).astype(jnp.float32),
    )
    return (
        output,
        latent_grad,
        totals[0].reshape(-1),
        totals[1].reshape(3, 3, channels, -1),
        totals[2],
        totals[3].reshape(-1),
        totals[4].reshape(3, 3, channels, -1),
        totals[5].reshape(-1),
        totals[6],
        totals[7].reshape(-1),
        totals[8],
        totals[9],
        totals[10],
        totals[11],
        totals[12].reshape(-1),
        totals[13],
        totals[14],
        totals[15],
        totals[16],
        totals[17].reshape(-1),
        totals[18],
        totals[19],
        totals[20],
    )


def solution(mesh):
    in_specs = (
        P(BATCH, SEQ, None, None),
        P(BATCH),
        P(BATCH, None),
        P(BATCH, None, None),
        P(),
        P(),
        P(),
        P(),
        P(),
        P(),
        P(),
        P(),
        P(),
        P(),
        P(),
        P(),
        P(),
        P(),
        P(),
        P(),
        P(),
        P(),
        P(),
        P(),
        P(),
        P(BATCH, SEQ, None, None),
    )
    out_specs = (
        P(BATCH, SEQ, None, None),
        P(BATCH, SEQ, None, None),
        P(SEQ),
        P(None, None, None, SEQ),
        P(None, SEQ),
        P(SEQ),
        P(None, None, None, SEQ),
        P(SEQ),
        P(None, SEQ),
        P(SEQ),
        P(None, SEQ),
        P(None, SEQ),
        P(None, SEQ),
        P(None, SEQ),
        P(SEQ),
        P(None, SEQ),
        P(None, SEQ),
        P(None, SEQ),
        P(None, SEQ),
        P(SEQ),
        P(None, SEQ),
        P(None, SEQ),
        P(None, SEQ),
    )
    device_fn = fast_device if mesh.shape[SEQ] == HEADS and mesh.shape[BATCH] == 4 else on_device
    return jax.shard_map(
        device_fn, mesh=mesh, in_specs=in_specs, out_specs=out_specs, check_vma=False
    )
```

```python
import types
import typing

import jax
import jax.numpy as jnp
from jax import lax
from jax.experimental import pallas as pl
from jax.experimental.pallas import tpu as pltpu
from jax.sharding import PartitionSpec as P

BATCH, SEQ = "batch", "seq"
HEADS = 8
HEAD = 40
GROUPS = 32


epsilon = 1e-05
layout = ("NHWC", "HWIO", "NHWC")


def extended(block, sides, width):
    for axis, dim in sides:
        count = lax.axis_size(axis)
        forward = [(i, i + 1) for i in range(count - 1)]
        backward = [(target, source) for source, target in forward]
        low = lax.ppermute(
            lax.slice_in_dim(block, block.shape[dim] - width, None, axis=dim), axis, forward
        )
        high = lax.ppermute(lax.slice_in_dim(block, 0, width, axis=dim), axis, backward)
        block = jnp.concatenate([low, block, high], axis=dim)
    return block


def layer_norm(values, norm_gain):
    centred = values - jnp.mean(values, axis=-1, keepdims=True)
    spread = jnp.mean(centred * centred, axis=-1, keepdims=True)
    return centred * lax.rsqrt(spread + epsilon) * norm_gain


def geglu(joined):
    half_width = joined.shape[-1] // 2
    return joined[:, :half_width] * jax.nn.gelu(joined[:, half_width:], approximate=False)


def back_dot(left_side, weight):
    return lax.dot_general(
        left_side, weight, (((1,), (1,)), ((), ())), preferred_element_type=jnp.float32
    )


def grad_dot(left_side, right_side):
    return lax.dot_general(
        left_side, right_side, (((0,), (0,)), ((), ())), preferred_element_type=jnp.float32
    )


def exact_grad_dot(left_side, right_side):
    return lax.dot_general(
        left_side,
        right_side,
        (((0,), (0,)), ((), ())),
        precision=lax.Precision.HIGHEST,
        preferred_element_type=jnp.float32,
    )


def conv_rows(padded, weight):
    return lax.conv_general_dilated(
        padded,
        weight,
        (1, 1),
        ((0, 0), (1, 1)),
        dimension_numbers=layout,
        preferred_element_type=jnp.float32,
    )


def conv_weight_grad(padded, grad_output):
    row_count = grad_output.shape[1]
    col_count = grad_output.shape[2]
    padded_cols = jnp.pad(padded, ((0, 0), (0, 0), (1, 1), (0, 0)))
    flat_grad = grad_output.reshape(-1, grad_output.shape[3])
    tap_rows = []
    for shift_row in range(3):
        tap_line = []
        for shift_col in range(3):
            patch_rows = padded_cols[
                :, shift_row : shift_row + row_count, shift_col : shift_col + col_count
            ].reshape(-1, padded.shape[3])
            tap_line.append(grad_dot(patch_rows, flat_grad))
        tap_rows.append(jnp.stack(tap_line))
    return jnp.stack(tap_rows)


def flipped(weight):
    return jnp.swapaxes(weight[::-1, ::-1], 2, 3)


def group_sums(values, row_mask):
    full_shape = values.shape
    grouped = values.reshape(
        full_shape[0], full_shape[1], full_shape[2], GROUPS, full_shape[3] // GROUPS
    )
    masked = grouped * row_mask[:, :, None, None, None]
    return (jnp.sum(masked, axis=(1, 2, 4)), jnp.sum(masked * grouped, axis=(1, 2, 4)))


def group_apply(values, norm_gain, sum_first, sum_second, cell_counts):
    full_shape = values.shape
    grouped = values.reshape(
        full_shape[0], full_shape[1], full_shape[2], GROUPS, full_shape[3] // GROUPS
    )
    group_mean = sum_first / cell_counts[:, None]
    spread = sum_second / cell_counts[:, None] - group_mean * group_mean
    inverse = lax.rsqrt(spread + epsilon)
    normed = (grouped - group_mean[:, None, None, :, None]) * inverse[:, None, None, :, None]
    return normed.reshape(full_shape) * norm_gain


def norm_stats(values, row_mask, spread_fn, pick_fn):
    sum_first, sum_second = group_sums(values, row_mask)
    total_first, total_second = lax.psum((spread_fn(sum_first), spread_fn(sum_second)), SEQ)
    return (pick_fn(total_first), pick_fn(total_second))


def norm_back(grad_first, grad_second, spread_fn, pick_fn):
    total_first, total_second = lax.psum((spread_fn(grad_first), spread_fn(grad_second)), SEQ)
    return (pick_fn(total_first), pick_fn(total_second))


def rows_halo(values):
    return extended(values, ((SEQ, 1),), 1)


def grads_halo(values):
    return extended(values, ((SEQ, 1),), 1)


def norm_backward(
    piece_fn, values, norm_gain, sum_first, sum_second, grad_output, row_mask, spread_fn, pick_fn
):
    unused, pull_piece = jax.vjp(piece_fn, values, norm_gain, sum_first, sum_second)
    grad_values, grad_gain, grad_first, grad_second = pull_piece(grad_output)
    total_first, total_second = norm_back(grad_first, grad_second, spread_fn, pick_fn)
    unused, pull_sums = jax.vjp(lambda inner_vals: group_sums(inner_vals, row_mask), values)
    extra_part = pull_sums((total_first, total_second))[0]
    return (grad_values + extra_part, grad_gain)


def masked_scores(queries, keys_all, key_mask, score_scale):
    row_count = queries.shape[0]
    key_count = keys_all.shape[0]
    raw_scores = (
        jnp.einsum(
            "qhd,khd->hqk",
            queries.reshape(row_count, HEADS, HEAD),
            keys_all.reshape(key_count, HEADS, HEAD),
            preferred_element_type=jnp.float32,
        )
        * score_scale
    )
    return jnp.where(key_mask[None, None, :] > 0, raw_scores, -1e30)


def self_forward(bundle, score_scale):
    queries, keys_all, values_all, key_mask = bundle
    row_count = queries.shape[0]
    scores = masked_scores(queries, keys_all, key_mask, score_scale)
    log_total = jax.nn.logsumexp(scores, axis=-1)
    attention = jnp.exp(scores - log_total[:, :, None]).astype(jnp.bfloat16)
    attn_mixed = jnp.einsum(
        "hqk,khd->qhd",
        attention,
        values_all.reshape(keys_all.shape[0], HEADS, HEAD),
        preferred_element_type=jnp.float32,
    )
    return (attn_mixed.astype(jnp.bfloat16).reshape(row_count, -1), log_total)


def query_side(bundle, score_scale):
    queries, grad_mixed, log_total, keys_all, values_all, key_mask = bundle
    row_count = queries.shape[0]
    key_count = keys_all.shape[0]
    scores = masked_scores(queries, keys_all, key_mask, score_scale)
    attention = jnp.exp(scores - log_total[:, :, None])
    grad_attn = jnp.einsum(
        "qhd,khd->hqk",
        grad_mixed.reshape(row_count, HEADS, HEAD),
        values_all.reshape(key_count, HEADS, HEAD),
        preferred_element_type=jnp.float32,
    )
    row_delta = jnp.sum(attention * grad_attn, axis=-1)
    grad_scores = (attention * (grad_attn - row_delta[:, :, None])).astype(jnp.bfloat16)
    grad_queries = (
        jnp.einsum(
            "hqk,khd->qhd",
            grad_scores,
            keys_all.reshape(key_count, HEADS, HEAD),
            preferred_element_type=jnp.float32,
        )
        * score_scale
    )
    return (
        grad_queries.astype(jnp.bfloat16).reshape(row_count, -1),
        attention.astype(jnp.bfloat16),
        grad_scores,
    )


LANES = 128
MESH = pl.DeviceIdType.MESH
LOW = jnp.bfloat16
F32 = jnp.float32
TILE = 64


def dot_nn(left, right):
    return jnp.dot(left, right, preferred_element_type=F32)


def dot_nt(left, right):
    return lax.dot_general(left, right, (((1,), (1,)), ((), ())), preferred_element_type=F32)


def dot_tn(left, right):
    return lax.dot_general(left, right, (((0,), (0,)), ((), ())), preferred_element_type=F32)


def iota(shape, dim):
    return lax.broadcasted_iota(jnp.int32, shape, dim)


def floor_div(values, by):
    return jnp.floor((values.astype(F32) + 0.5) * (1.0 / by)).astype(jnp.int32)


def split_three(values):
    high = values.astype(LOW).astype(F32)
    rest = values - high
    middle = rest.astype(LOW).astype(F32)
    return jnp.concatenate([high, middle, rest - middle], axis=0).astype(LOW)


def sum_three(values):
    rows = values.shape[0] // 3
    return values[:rows] + values[rows : 2 * rows] + values[2 * rows :]


def row_of(ref):
    return ref[...].reshape(1, -1)


def sigmoid(values):
    return 1.0 / (1.0 + jnp.exp(-values))


def col_sum(values):
    return jnp.sum(values, axis=0, keepdims=True)


ROUNDS = 6
SEMAPHORES = 256


class Packs(typing.NamedTuple):
    up: typing.Any
    down: typing.Any
    trio: typing.Any
    pair: typing.Any
    heads: typing.Any
    second: typing.Any


class Sizes:
    def __init__(self, mesh_batch, mesh_seq, latents, time_vector, text_states, feed_down):
        self.batches = mesh_batch
        self.seqs = mesh_seq
        self.rows = latents.shape[1]
        self.width = latents.shape[2]
        self.channels = latents.shape[3]
        self.tokens = self.rows * self.width
        self.wide = self.tokens + 2 * self.width
        self.keys = self.tokens * mesh_seq
        self.emb = time_vector.shape[1]
        self.text = text_states.shape[1]
        self.text_pad = -(-self.text // 16) * 16
        self.context = text_states.shape[2]
        self.hidden = feed_down.shape[0]
        self.slot = 48
        self.packed = HEADS * LANES
        self.down_rows = 512
        self.conv_rows = 3 * LANES
        channels = self.channels
        sizes = Packs(
            up=3 * channels,
            down=self.down_rows,
            trio=channels,
            pair=HEADS * self.slot,
            heads=-(-channels // LANES) * LANES,
            second=3 * channels,
        )
        starts = [sum(sizes[:place]) for place in range(len(sizes))]
        self.start = Packs(*starts)
        self.pack_rows = sum(sizes)
        self.sizes = sizes
        self.chunks = [
            (0, sizes.up),
            (self.start.down, sizes.down + sizes.trio),
            (self.start.pair, sizes.pair + sizes.heads),
            (self.start.second, sizes.second),
        ]


class Inputs(typing.NamedTuple):
    latents: typing.Any
    heights: typing.Any
    time_vector: typing.Any
    text_states: typing.Any
    gain_in: typing.Any
    conv_first: typing.Any
    time_weight: typing.Any
    gain_mid: typing.Any
    conv_second: typing.Any
    gain_block: typing.Any
    project_in: typing.Any
    gain_self: typing.Any
    query_self: typing.Any
    key_self: typing.Any
    value_self: typing.Any
    out_self: typing.Any
    gain_cross: typing.Any
    query_cross: typing.Any
    key_cross: typing.Any
    value_cross: typing.Any
    out_cross: typing.Any
    gain_feed: typing.Any
    feed_up: typing.Any
    feed_down: typing.Any
    project_out: typing.Any
    cotangent: typing.Any


class Fetched(typing.NamedTuple):
    query_self: typing.Any
    key_self: typing.Any
    value_self: typing.Any
    time_weight: typing.Any
    conv_first: typing.Any
    conv_second: typing.Any
    project_in: typing.Any
    key_cross: typing.Any
    value_cross: typing.Any
    out_self: typing.Any
    query_cross: typing.Any
    out_cross: typing.Any
    feed_up: typing.Any
    feed_down: typing.Any
    project_out: typing.Any


def buffers(sz):
    c, t, w, k = sz.channels, sz.tokens, sz.wide, sz.keys
    half = sz.seqs // 2
    return dict(
        lat6=((w, c), F32),
        cot6=((w, c), F32),
        mid6=((w, c), F32),
        res6=((w, c), F32),
        gblk6=((w, c), F32),
        gact6=((w, c), F32),
        shifted=((3, w, c), LOW),
        shift_grad=((3, w, c), LOW),
        act_in=((k + 2 * sz.width, c), LOW),
        widen=((HEADS * sz.slot, c), LOW),
        first_send=((HEADS * sz.slot, t), LOW),
        first_grads=((sz.slot, k), LOW),
        first_part=((sz.conv_rows, c), LOW),
        first_recv=((3, sz.batches - 1, LANES // sz.batches, c), LOW),
        conv_stack=((LANES, k), LOW),
        stat_send=((ROUNDS, 8, LANES), F32),
        extra_send=((8, c), F32),
        extra_recv=((sz.seqs, 8, c), F32),
        stat_recv=((ROUNDS, sz.seqs, 8, LANES), F32),
        norms=((3, 8, c), F32),
        gain_parts=((8, c), F32),
        final_send=((8, c), F32),
        group=((c, c), LOW),
        place=((3, c, sz.packed), LOW),
        wqkv=((c, sz.packed), LOW),
        osp=((HEADS * sz.slot, c), LOW),
        time_send=((8, sz.emb), F32),
        normed_block=((t, c), LOW),
        stream_in=((t, c), F32),
        normed_self=((t, c), LOW),
        qkv_send=((t, sz.packed), LOW),
        qkv=((k, LANES), LOW),
        qh=((k, LANES), LOW),
        kh=((k, LANES), LOW),
        vh=((k, sz.slot), LOW),
        vt=((sz.slot, k), LOW),
        kt=((sz.slot, k), LOW),
        scores=((max(k, 2 * sz.hidden), t), F32),
        scores_odd=((k, t), F32),
        tops=((2, 8, t), F32),
        probs=((2, k, t), LOW),
        mixed_full=((sz.seqs, sz.slot, t), F32),
        inverse=((sz.seqs, 8, t), F32),
        mixed_send=((sz.seqs, sz.slot, t), LOW),
        mixed=((HEADS * sz.slot, t), LOW),
        stream=((t, c), F32),
        centred_cross=((t, c), F32),
        scale_cross=((t, LANES), F32),
        normed_cross=((t, c), LOW),
        query_text=((t, c), LOW),
        text_rows=((2, sz.text_pad, c), F32),
        text_key=((HEADS * sz.text_pad, c), LOW),
        text_value=((HEADS * sz.text_pad, c), LOW),
        cross=((HEADS * sz.text_pad, t), F32),
        cross_low=((HEADS * sz.text_pad, t), LOW),
        cross_scores=((HEADS * sz.text_pad, t), LOW),
        cross_mixed=((t, c), LOW),
        scale_feed=((t, LANES), F32),
        normed_feed=((t, c), LOW),
        gated=((t, sz.hidden), LOW),
        grad_gated=((t, 2 * LANES), F32),
        grad_joined=((t, 2 * sz.hidden), LOW),
        stream_low=((t, c), LOW),
        grad_branch=((t, c), LOW),
        grad=((t, c), F32),
        tmp=((t, c), F32),
        grad_feed_low=((t, c), LOW),
        grad_cross_low=((t, c), LOW),
        grad_cross_mixed=((t, c), LOW),
        grad_query_text=((t, c), LOW),
        grad_self_low=((t, c), LOW),
        grad_in_low=((t, c), LOW),
        text_send=((sz.text_pad, sz.packed), LOW),
        text_recv=((sz.seqs, sz.text_pad, LANES), LOW),
        gm_send=((HEADS * sz.slot, t), LOW),
        gm=((sz.seqs, sz.slot, t), LOW),
        query_rows=((HEADS * sz.slot, c), LOW),
        value_rows=((HEADS * 2 * HEAD, c), LOW),
        dq_send=((sz.seqs, sz.slot, t), LOW),
        dq=((HEADS * sz.slot, t), LOW),
        dkv_send=((HEADS * 2 * HEAD, t), LOW),
        dkv=((HEADS * 2 * HEAD, t), LOW),
        pack=((2, half, sz.start.second, LANES), LOW),
        near_shifted=((3, w, c), LOW),
        near_grads=((t, c), LOW),
        place_half=((3, c, half * LANES), LOW),
        recv_core=((half, sz.pack_rows, LANES), LOW),
        recv_first=((2, half // 2, sz.pack_rows // 2, LANES), LOW),
        recv_second=((half, sz.pack_rows // sz.batches, LANES), LOW),
        recv_z=((half - 1, sz.pack_rows // sz.batches, LANES), LOW),
    )


class Halo:
    def __init__(self, seq, last, after, before):
        self.seq, self.last, self.after, self.before = seq, last, after, before

    def start(self):
        @pl.when(self.seq < self.last)
        def _():
            self.after.start()

        @pl.when(self.seq > 0)
        def _():
            self.before.start()

    def wait(self):
        @pl.when(self.seq < self.last)
        def _():
            self.after.wait_send()
            self.before.wait_recv()

        @pl.when(self.seq > 0)
        def _():
            self.before.wait_send()
            self.after.wait_recv()


class Fused:
    def __init__(self, sz, refs, local):
        self.sz = sz
        self.r = refs
        self.v = local
        self.used = 0
        self.batch = lax.axis_index(BATCH)
        self.seq = lax.axis_index(SEQ)
        self.z_pos = self.seq // 2
        self.core = lax.rem(self.seq, 2)
        self.batch_x = lax.rem(self.batch, 2)
        self.batch_y = self.batch // 2
        self.x_peer = (self.batch + 1 - 2 * self.batch_x, self.seq)
        self.y_peer = (self.batch + 2 - 4 * self.batch_y, self.seq)
        self.partner = (self.batch, self.seq + 1 - 2 * self.core)
        far = sorted(range(1, sz.seqs), key=lambda step: -min(step, sz.seqs - step))
        self.seq_others = [lax.rem(self.seq + step, sz.seqs) for step in far]
        self.batch_others = [lax.rem(self.batch + step, sz.batches) for step in range(1, sz.batches)]
        half = sz.seqs // 2
        self.z_others = [lax.rem(self.z_pos + step, half) for step in range(1, half)]
        self.height = refs.heights[0]
        self.scale = HEAD ** (-0.5)

    def remote(self, source, target, device, index=None):
        if index is None:
            index = self.used
            self.used += 1
        return pltpu.make_async_remote_copy(
            src_ref=source,
            dst_ref=target,
            send_sem=self.r.sems.at[0, index],
            recv_sem=self.r.sems.at[1, index],
            device_id=device,
            device_id_type=MESH,
        )

    def to_seq(self, source, target):
        return [self.remote(source(other), target, (self.batch, other)) for other in self.seq_others]

    def to_batch(self, source, target):
        return [self.remote(source, target, (other, self.seq)) for other in self.batch_others]

    def start(self, copies):
        for one in copies:
            one.start()

    def wait(self, copies):
        for one in copies:
            one.wait()

    def entry(self):
        r = self.r
        barrier = pltpu.get_barrier_semaphore()
        for other in self.seq_others:
            pl.semaphore_signal(barrier, inc=1, device_id=(self.batch, other), device_id_type=MESH)
        for other in self.batch_others:
            pl.semaphore_signal(barrier, inc=1, device_id=(other, self.seq), device_id_type=MESH)
        self.local = {}
        self.named = {id(getattr(r, name)): name for name in Fetched._fields}
        for number, name in enumerate(Fetched._fields):
            self.local[name] = pltpu.make_async_copy(
                getattr(r, name), getattr(self.v, name), r.local_sems.at[number]
            )
            self.local[name].start()
        own = pl.ds(self.sz.width, self.sz.tokens)
        self.images = [
            pltpu.make_async_copy(source, target.at[own], r.local_sems.at[len(Fetched._fields) + place])
            for place, (source, target) in enumerate(((r.latents, r.lat6), (r.cotangent, r.cot6)))
        ]
        self.start(self.images)

    def joined(self):
        barrier = pltpu.get_barrier_semaphore()
        pl.semaphore_wait(barrier, self.sz.seqs - 1 + self.sz.batches - 1)

    def weight(self, ref):
        name = self.named[id(ref)]
        if name in self.local:
            self.local.pop(name).wait()
        return getattr(self.v, name)

    def far_first(self, step):
        half = self.sz.seqs // 2
        offset = half + ((step + 1) // 2) * (1 - 2 * (step % 2))
        return lax.rem(self.seq + offset, self.sz.seqs)

    def wide_row(self, start, size):
        rows = floor_div(iota((size, 1), 0) + start, self.sz.width) - 1
        return rows + self.seq * self.sz.rows

    def wide_mask(self, start, size):
        rows = self.wide_row(start, size)
        return jnp.where((rows >= 0) & (rows < self.height), 1.0, 0.0)

    def inside_mask(self, start, size):
        rows = self.wide_row(start, size)
        return jnp.where((rows >= 0) & (rows < self.sz.rows * self.sz.seqs), 1.0, 0.0)

    def chunks(self, total):
        return [(start, TILE) for start in range(0, total, TILE)]

    def halo(self, ref):
        sz, width = self.sz, self.sz.width
        after = self.remote(
            ref.at[pl.ds(sz.tokens, width)],
            ref.at[pl.ds(0, width)],
            (self.batch, jnp.minimum(self.seq + 1, sz.seqs - 1)),
        )
        before = self.remote(
            ref.at[pl.ds(width, width)],
            ref.at[pl.ds(width + sz.tokens, width)],
            (self.batch, jnp.maximum(self.seq - 1, 0)),
        )
        return Halo(self.seq, sz.seqs - 1, after, before)

    def lane_tiles(self):
        channels = self.sz.channels
        return [(start, min(LANES, channels - start)) for start in range(0, channels, LANES)]

    def stats_store(self, number, rows):
        r = self.r
        r.stat_send[number] = jnp.zeros(r.stat_send.shape[1:], F32)
        tiles = self.lane_tiles()
        for which, row in enumerate(rows):
            for place, (start, size) in enumerate(tiles):
                at = which * len(tiles) + place
                r.stat_send[number, at : at + 1, 0:size] = row[:, start : start + size]
        r.stat_recv[number, self.seq] = r.stat_send[number]

    def stats_start(self, number):
        r = self.r
        copies = self.to_seq(lambda other: r.stat_send.at[number], r.stat_recv.at[number, self.seq])
        self.start(copies)
        return copies

    def stats_total(self, number):
        r = self.r
        total = r.stat_recv[number, 0]
        for place in range(1, self.sz.seqs):
            total = total + r.stat_recv[number, place]
        tiles = self.lane_tiles()
        rows = []
        for which in range(2):
            parts = [
                total[which * len(tiles) + place : which * len(tiles) + place + 1, 0:size]
                for place, (start, size) in enumerate(tiles)
            ]
            rows.append(jnp.concatenate(parts, axis=1))
        row = iota((8, 1), 0)
        return jnp.where(row == 0, rows[0], jnp.where(row == 1, rows[1], 0.0))

    def grouped(self, rows):
        return sum_three(dot_nn(split_three(rows), self.r.group[...]))

    def count(self):
        per_row = self.sz.width * (self.sz.channels // GROUPS)
        return (self.height * per_row).astype(F32)

    def set_norm(self, number, total):
        sums = self.grouped(total) / self.count()
        mean = sums[0:1]
        spread = sums[1:2] - mean * mean
        self.r.norms[number, 0:1] = mean
        self.r.norms[number, 1:2] = lax.rsqrt(spread + epsilon)

    def norm(self, number):
        return self.r.norms[number, 0:1], self.r.norms[number, 1:2]

    def value_sums(self, ref):
        r, sz = self.r, self.sz
        first = second = None
        for start, size in self.chunks(sz.tokens):
            start += sz.width
            values = ref[start : start + size]
            masked = values * self.wide_mask(start, size)
            one, two = col_sum(masked), col_sum(masked * values)
            first = one if first is None else first + one
            second = two if second is None else second + two
        return first, second

    def shifts(self, ref, start, size, values):
        column = lax.rem(iota((size, 1), 0), self.sz.width)
        ref[1, start : start + size] = values.astype(LOW)
        left = jnp.where(column == 0, 0.0, pltpu.roll(values, 1, 0))
        ref[0, start : start + size] = left.astype(LOW)
        right = jnp.where(column == self.sz.width - 1, 0.0, pltpu.roll(values, size - 1, 0))
        ref[2, start : start + size] = right.astype(LOW)

    def activate(self, source, number, gain, target, kept):
        mean, inverse = self.norm(number)
        factor = inverse * row_of(gain)
        for start, size in self.chunks(self.sz.wide):
            normed = (source[start : start + size] - mean) * factor
            values = normed * sigmoid(normed) * self.wide_mask(start, size)
            self.shifts(target, start, size, values)
        if kept is None:
            return
        width, tokens = self.sz.width, self.sz.tokens
        kept[self.own_rows()] = target[1, width : width + tokens]
        zeros = jnp.zeros((width, self.sz.channels), LOW)
        kept[0:width] = zeros
        kept[self.sz.keys + width :] = zeros

    def own_rows(self, seq=None):
        seq = self.seq if seq is None else seq
        width, tokens = self.sz.width, self.sz.tokens
        return pl.ds(pl.multiple_of(seq * tokens + width, width), tokens)

    def gather_rows(self, kept, first, last):
        width, tokens = self.sz.width, self.sz.tokens
        start = self.seq * tokens + (first + 1) * width
        rows = pl.ds(pl.multiple_of(start, width), (last - first) * width)
        copies = [
            self.remote(kept.at[rows], kept.at[rows], (self.batch, other * 2 + self.core))
            for other in self.z_others
        ]
        self.start(copies)
        return copies

    def gather_forward(self, kept, copies):
        rows = self.own_rows()
        more = [self.remote(kept.at[rows], kept.at[rows], self.partner)]
        self.start(more)
        self.wait(copies)
        half = self.sz.seqs // 2
        for step in range(1, half):
            rows = self.own_rows(lax.rem(self.z_pos + half - step, half) * 2 + self.core)
            more.append(self.remote(kept.at[rows], kept.at[rows], self.partner))
        self.start(more[1:])
        return more

    def conv_send(self, grads, send, target):
        sz, slot = self.sz, self.sz.slot
        send[...] = dot_nt(self.r.widen[...], grads[1, sz.width : sz.width + sz.tokens]).astype(LOW)
        lanes = pl.ds(pl.multiple_of(self.seq * sz.tokens, sz.tokens), sz.tokens)
        copies = [
            self.remote(
                send.at[pl.ds(pl.multiple_of(other * slot, 16), slot)],
                target.at[:, lanes],
                (self.batch, other),
            )
            for other in self.seq_others
        ]
        self.start(copies)
        target[:, lanes] = send[pl.ds(pl.multiple_of(self.seq * slot, 16), slot)]
        return copies

    def conv_grads(self, copies, gathered, grads, kept, part, received):
        r, sz = self.r, self.sz
        keys, width = sz.keys, sz.width
        self.wait(copies)
        self.wait(gathered)
        values = grads[0:HEAD].astype(F32)
        column = lax.rem(iota((1, keys), 1), width)
        left = jnp.where(column == width - 1, 0.0, pltpu.roll(values, keys - 1, 1))
        right = jnp.where(column == 0, 0.0, pltpu.roll(values, 1, 1))
        rest = jnp.zeros((LANES - 3 * HEAD, keys), F32)
        r.conv_stack[...] = jnp.concatenate([left, values, right, rest], axis=0).astype(LOW)
        size = LANES // sz.batches
        pieces = []
        for row in range(3):
            part[row * LANES : (row + 1) * LANES] = dot_nn(
                r.conv_stack[...], kept[row * width : row * width + keys]
            ).astype(LOW)
            copies = []
            for step, other in enumerate(self.batch_others):
                rows = pl.ds(pl.multiple_of(row * LANES + other * size, 16), size)
                copies.append(self.remote(part.at[rows], received.at[row, step], (other, self.seq)))
            self.start(copies)
            pieces.append(copies)
        return pieces

    def conv_gather(self, pieces, part, received, out):
        size = LANES // self.sz.batches
        sent = []
        for row, copies in enumerate(pieces):
            own = pl.ds(pl.multiple_of(row * LANES + self.batch * size, 16), size)
            self.wait(copies)
            total = part[own].astype(F32)
            for step in range(self.sz.batches - 1):
                total = total + received[row, step].astype(F32)
            out[own] = total.astype(LOW)
            copies = self.to_batch(out.at[own], out.at[own])
            self.start(copies)
            sent += copies
        return sent

    def conv(self, ref, weight):
        sz = self.sz
        total = None
        for row in range(3):
            for col in range(3):
                part = dot_nn(ref[col, row * sz.width : row * sz.width + sz.tokens], weight[row, col])
                total = part if total is None else total + part
        return total

    def conv_back(self, ref, weight):
        sz = self.sz
        total = None
        for row in range(3):
            for col in range(3):
                part = dot_nt(
                    ref[col, row * sz.width : row * sz.width + sz.tokens], weight[2 - row, 2 - col]
                )
                total = part if total is None else total + part
        return total

    def constants(self):
        r, sz = self.r, self.sz
        channels = sz.channels
        size = channels // GROUPS
        r.group[...] = jnp.where(
            floor_div(iota((channels, 1), 0), size) == floor_div(iota((1, channels), 1), size), 1.0, 0.0
        ).astype(LOW)
        source = iota((1, channels), 1)
        source = source + (sz.slot - HEAD) * floor_div(source, HEAD)
        r.widen[...] = jnp.where(iota((HEADS * sz.slot, 1), 0) == source, 1.0, 0.0).astype(LOW)
        rows = iota((channels, 1), 0)
        target = rows + (LANES - HEAD) * floor_div(rows, HEAD)
        lanes = iota((1, sz.packed), 1)
        for number in range(3):
            r.place[number] = jnp.where(lanes == target + number * HEAD, 1.0, 0.0).astype(LOW)
        head = floor_div(rows, HEAD)
        pair = floor_div(head, 2)
        target = jnp.where(head - 2 * pair == self.core, rows - head * HEAD + pair * LANES, -LANES)
        lanes = iota((1, r.place_half.shape[2]), 1)
        for number in range(3):
            r.place_half[number] = jnp.where(lanes == target + number * HEAD, 1.0, 0.0).astype(LOW)

    def residual(self):
        r, sz = self.r, self.sz
        width, tokens = sz.width, sz.tokens
        self.constants()
        self.wait(self.images)
        for ref in (r.lat6, r.cot6, r.mid6, r.res6, r.gblk6, r.gact6):

            @pl.when(self.seq == 0)
            def _():
                ref[0:width] = jnp.zeros((width, sz.channels), F32)

            @pl.when(self.seq == sz.seqs - 1)
            def _():
                ref[width + tokens :] = jnp.zeros((width, sz.channels), F32)

        self.stats_store(0, self.value_sums(r.lat6))
        self.joined()
        halo = self.halo(r.lat6)
        halo.start()
        stats = self.stats_start(0)
        late = [self.halo(r.cot6)]
        act = r.time_vector[...].astype(F32)
        act = (act * sigmoid(act)).astype(LOW)
        r.time_send[...] = jnp.zeros(r.time_send.shape, F32)
        r.time_send[0:1] = act.astype(F32)
        r.time_all[self.batch] = r.time_send[...]
        late += self.to_batch(r.time_send, r.time_all.at[self.batch])
        r.text_all[self.batch] = jnp.zeros(r.text_all.shape[1:], LOW)
        r.text_all[self.batch, 0 : sz.text] = r.text_states[...]
        late += self.to_batch(r.text_all.at[self.batch], r.text_all.at[self.batch])
        self.start(late)
        self.late = late
        time_weight = self.weight(self.r.time_weight)
        time_term = dot_nt(jnp.broadcast_to(act, (16, sz.emb)), time_weight[...])[0:1]
        wqkv = None
        for number, name in enumerate((r.query_self, r.key_self, r.value_self)):
            part = dot_nn(self.weight(name)[...], r.place[number])
            wqkv = part if wqkv is None else wqkv + part
        r.wqkv[...] = wqkv.astype(LOW)
        halo.wait()
        self.wait(stats)
        self.set_norm(0, self.stats_total(0))
        self.activate(r.lat6, 0, r.gain_in, r.shifted, r.act_in)
        r.mid6[width : width + tokens] = self.conv(r.shifted, self.weight(self.r.conv_first)) + time_term
        halo = self.halo(r.mid6)
        halo.start()
        self.stats_store(1, self.value_sums(r.mid6))
        stats = self.stats_start(1)
        self.weight(self.r.conv_second)
        halo.wait()
        self.wait(stats)
        self.set_norm(1, self.stats_total(1))
        self.activate(r.mid6, 1, r.gain_mid, r.shifted, None)
        r.res6[width : width + tokens] = r.lat6[width : width + tokens] + self.conv(
            r.shifted, self.v.conv_second
        )
        halo = self.halo(r.res6)
        self.stats_store(2, self.value_sums(r.res6))
        stats = self.stats_start(2)
        halo.start()
        self.late.append(halo)
        near = self.remote(r.shifted, r.near_shifted, self.partner)
        near.start()
        self.late.append(near)
        project_in = self.weight(self.r.project_in)
        self.wait(stats)
        self.set_norm(2, self.stats_total(2))
        mean, inverse = self.norm(2)
        factor = inverse * row_of(r.gain_block)
        for start, size in self.chunks(tokens):
            values = r.res6[width + start : width + start + size]
            r.normed_block[start : start + size] = ((values - mean) * factor).astype(LOW)
        r.stream_in[...] = dot_nn(r.normed_block[...], project_in[...])
        for start, size in self.chunks(tokens):
            values = r.stream_in[start : start + size]
            centred, scale = self.layer_parts(values)
            r.normed_self[start : start + size] = (centred * scale * row_of(r.gain_self)).astype(LOW)
        r.qkv_send[...] = dot_nn(r.normed_self[...], r.wqkv[...]).astype(LOW)
        rows = pl.ds(pl.multiple_of(self.seq * tokens, tokens), tokens)
        copies = [
            self.remote(
                r.qkv_send.at[:, pl.ds(pl.multiple_of(other * LANES, LANES), LANES)],
                r.qkv.at[rows],
                (self.batch, other),
            )
            for other in self.seq_others
        ]
        self.start(copies)
        r.qkv[rows] = r.qkv_send[:, pl.ds(pl.multiple_of(self.seq * LANES, LANES), LANES)]
        self.text_start()
        self.wait(copies)

    def layer_parts(self, values):
        centred = values - jnp.mean(values, axis=-1, keepdims=True)
        spread = jnp.mean(centred * centred, axis=-1, keepdims=True)
        return centred, lax.rsqrt(spread + epsilon)

    def layer_back(self, values, grad, gain):
        centred, scale = self.layer_parts(values)
        normed = centred * scale
        scaled = grad * gain
        first = jnp.mean(scaled, axis=-1, keepdims=True)
        second = jnp.mean(scaled * normed, axis=-1, keepdims=True)
        return scale * (scaled - first - normed * second), col_sum(grad * normed)

    def text_start(self):
        r, sz = self.r, self.sz
        r.text_rows[...] = jnp.zeros(r.text_rows.shape, F32)
        for number, (name, target) in enumerate(
            ((r.key_cross, r.text_key), (r.value_cross, r.text_value))
        ):
            r.text_rows[number, 0 : sz.text] = dot_nt(r.text_states[...], self.weight(name)[...])
            rows = r.text_rows[number]
            head = floor_div(iota((1, sz.channels), 1), HEAD)
            for one in range(HEADS):
                target[one * sz.text_pad : (one + 1) * sz.text_pad] = jnp.where(
                    head == one, rows, 0.0
                ).astype(LOW)
        r.query_rows[...] = dot_nt(r.widen[...], self.v.query_self[...]).astype(LOW)
        rows = iota((HEADS * 2 * HEAD, 1), 0)
        source = iota((1, sz.channels), 1)
        source = source + HEAD * floor_div(source, HEAD)
        r.value_rows[...] = (
            dot_nt(jnp.where(rows == source, 1.0, 0.0).astype(LOW), self.v.key_self[...])
            + dot_nt(jnp.where(rows == source + HEAD, 1.0, 0.0).astype(LOW), self.v.value_self[...])
        ).astype(LOW)
        r.osp[...] = dot_nn(r.widen[...], self.weight(self.r.out_self)[...]).astype(LOW)

    def attention(self):
        r, sz = self.r, self.sz
        keys, tokens, slot = sz.keys, sz.tokens, sz.slot
        self.in_pieces = self.gather_rows(r.act_in, 0, 1)
        lane_in = iota((LANES, LANES), 0)
        lane_out = iota((LANES, LANES), 1)

        def shift(by):
            return jnp.where((lane_in == lane_out + by) & (lane_out < HEAD), 1.0, 0.0).astype(LOW)

        def shift_wide(by):
            source = iota((LANES, slot), 0)
            target = iota((LANES, slot), 1)
            return jnp.where((source == target + by) & (target < HEAD), 1.0, 0.0).astype(LOW)

        def shift_rows(by):
            source = iota((slot, LANES), 1)
            target = iota((slot, LANES), 0)
            return jnp.where((source == target + by) & (target < HEAD), 1.0, 0.0).astype(LOW)

        query_out = jnp.where((lane_in + HEAD == lane_out) & (lane_in < HEAD), 1.0, 0.0).astype(LOW)
        lane = iota((1, LANES), 1)
        for start in range(0, keys, 2 * tokens):
            rows = slice(start, start + 2 * tokens)
            block = r.qkv[rows]
            valid = iota((2 * tokens, 1), 0) + start < self.height * sz.width
            r.qh[rows] = jnp.where(
                lane < HEAD, block.astype(F32), jnp.where(lane == HEAD, 1.0, 0.0)
            ).astype(LOW)
            bias = jnp.where((lane == HEAD) & jnp.logical_not(valid), -1e30, 0.0)
            r.kh[rows] = (dot_nn(block, shift(HEAD)) + bias).astype(LOW)
            ones = jnp.where((iota((1, slot), 1) >= HEAD) & (iota((1, slot), 1) < HEAD + 3), 1.0, 0.0)
            r.vh[rows] = (dot_nn(block, shift_wide(2 * HEAD)) + ones).astype(LOW)
            one_row = jnp.where(iota((slot, 1), 0) == HEAD, 1.0, 0.0)
            r.vt[:, rows] = (dot_nt(shift_rows(2 * HEAD), block) + one_row).astype(LOW)
            r.kt[:, rows] = dot_nt(shift_rows(HEAD), block).astype(LOW)
            r.qkv[rows] = dot_nn(block, query_out).astype(LOW)
        factor = self.scale * 1.4426950408889634
        base = self.used
        self.used += sz.seqs

        def send(target, step):
            return self.remote(
                r.mixed_send.at[target],
                r.mixed.at[pl.ds(pl.multiple_of(self.seq * slot, 16), slot)],
                (self.batch, target),
                base + step,
            )

        score_refs = (r.scores, r.scores_odd)

        def keep(step, parity):
            return pltpu.make_async_copy(
                r.probs.at[parity],
                r.kept_probs.at[self.far_first(step)],
                r.local_sems.at[len(Fetched._fields) + 2 + parity],
            )

        def own_scores(step, parity, start, top):
            target = self.far_first(step)
            queries = r.qh[pl.ds(pl.multiple_of(target * tokens, tokens), tokens)]
            scores = dot_nt(r.kh[start : start + tokens], queries)
            score_refs[parity][start : start + tokens] = scores
            part = jnp.max(scores.reshape(tokens // 8, 8, tokens), axis=0)
            top = part if top is None else jnp.maximum(top, part)
            if start + tokens == keys:
                r.tops[parity] = jnp.broadcast_to(jnp.max(top, axis=0, keepdims=True), (8, tokens))
            return top

        def finish(step, sums):
            target = self.far_first(step)
            inverse = 1.0 / sums[HEAD : HEAD + 1]
            mixed = jnp.where(iota((slot, 1), 0) < HEAD, sums * inverse, 0.0)
            r.mixed_full[target] = mixed
            r.mixed_send[target] = mixed.astype(LOW)
            r.inverse[target] = jnp.broadcast_to(inverse, (8, tokens))

        def half_step(step, parity, with_next, with_last, wait_kept):
            if wait_kept:
                keep(step - 2, parity).wait()
            offset = r.tops[parity, 0:1] * factor
            top = sums = None
            for start in range(0, keys, tokens):
                if with_next:
                    top = own_scores(step + 1, 1 - parity, start, top)
                for inner in range(start, start + tokens, LANES):
                    powers = jnp.exp2(score_refs[parity][inner : inner + LANES] * factor - offset)
                    r.probs[parity, inner : inner + LANES] = powers.astype(LOW)
                if with_last:
                    part = dot_nn(
                        r.vt[:, start : start + tokens], r.probs[1 - parity, start : start + tokens]
                    )
                    sums = part if sums is None else sums + part
            keep(step, parity).start()
            if with_last:
                finish(step - 1, sums)
                send(self.far_first(step - 1), step - 1).start()

        top = None
        for start in range(0, keys, tokens):
            top = own_scores(0, 0, start, top)
        half_step(0, 0, True, False, False)
        half_step(1, 1, True, True, False)

        def pair(number, carry):
            step = 2 + 2 * number
            half_step(step, 0, True, True, True)
            half_step(step + 1, 1, True, True, True)
            return carry

        lax.fori_loop(0, sz.seqs // 2 - 2, pair, 0)
        half_step(sz.seqs - 2, 0, True, True, True)
        half_step(sz.seqs - 1, 1, False, True, True)
        finish(sz.seqs - 1, dot_nn(r.vt[...], r.probs[1]))
        keep(sz.seqs - 2, 0).wait()
        keep(sz.seqs - 1, 1).wait()
        self.recall(0).start()
        r.mixed[pl.ds(pl.multiple_of(self.seq * slot, 16), slot)] = r.mixed_send[self.seq]
        for step in range(sz.seqs - 1):
            send(self.far_first(step), step).wait()

    def local_block(self):
        r, sz = self.r, self.sz
        tokens, channels = sz.tokens, sz.channels
        pad = sz.text_pad
        r.stream[...] = r.stream_in[...] + dot_tn(r.mixed[...], r.osp[...])
        for start, size in self.chunks(tokens):
            rows = slice(start, start + size)
            centred, scale = self.layer_parts(r.stream[rows])
            r.normed_cross[rows] = (centred * scale * row_of(r.gain_cross)).astype(LOW)
        r.query_text[...] = dot_nn(r.normed_cross[...], self.weight(self.r.query_cross)[...]).astype(LOW)
        r.cross[...] = dot_nt(r.text_key[...], r.query_text[...])
        for head in range(HEADS):
            rows = slice(head * pad, (head + 1) * pad)
            valid = iota((pad, 1), 0) < sz.text
            scores = jnp.where(valid, r.cross[rows] * self.scale, -1e30)
            powers = jnp.exp(scores - jnp.max(scores, axis=0, keepdims=True))
            attention = powers / jnp.sum(powers, axis=0, keepdims=True)
            r.cross[rows] = attention
            r.cross_low[rows] = attention.astype(LOW)
        r.cross_mixed[...] = dot_tn(r.cross_low[...], r.text_value[...]).astype(LOW)
        r.centred_cross[...] = r.stream[...]
        r.stream[...] = r.stream[...] + dot_nn(r.cross_mixed[...], self.weight(self.r.out_cross)[...])
        for start, size in self.chunks(tokens):
            rows = slice(start, start + size)
            centred, scale = self.layer_parts(r.stream[rows])
            r.normed_feed[rows] = (centred * scale * row_of(r.gain_feed)).astype(LOW)
        feed_up = self.weight(self.r.feed_up)
        joined = r.scores
        root = 0.7071067811865476
        block = 2 * LANES
        pieces = sz.hidden // block
        for piece in range(pieces):
            for place in (piece, piece + pieces):
                joined[place * tokens : (place + 1) * tokens] = dot_nn(
                    r.normed_feed[...], feed_up[:, place * block : (place + 1) * block]
                )
            for start, size in self.chunks(tokens):
                values = joined[piece * tokens + start : piece * tokens + start + size]
                gates_at = (piece + pieces) * tokens + start
                gates = joined[gates_at : gates_at + size]
                half = 0.5 * (1.0 + lax.erf(gates * root))
                slope = half + gates * (jnp.exp(-0.5 * gates * gates) * 0.3989422804014327)
                active = gates * half
                r.gated[start : start + size, piece * block : (piece + 1) * block] = (
                    values * active
                ).astype(LOW)
                joined[piece * tokens + start : piece * tokens + start + size] = active
                joined[gates_at : gates_at + size] = values * slope

        low = (
            r.stream[...] + dot_nt(r.gated[...], self.weight(self.r.feed_down)[...])
        ).astype(LOW)
        r.stream_low[...] = low
        project_out = self.weight(self.r.project_out)
        r.tmp[...] = dot_nn(r.stream_low[...], project_out[...])
        for start, size in self.chunks(tokens):
            rows = slice(start, start + size)
            wide = slice(start + sz.width, start + sz.width + size)
            mask = self.wide_mask(start + sz.width, size)
            r.output[rows] = (r.res6[wide] + r.tmp[rows]) * mask
            r.grad_branch[rows] = (r.cot6[wide] * mask).astype(LOW)
        r.grad[...] = dot_nt(r.grad_branch[...], project_out[...])
        r.grad_feed_low[...] = r.grad[...].astype(LOW)
        for piece in range(pieces):
            lanes = slice(piece * block, (piece + 1) * block)
            gate_lanes = slice(sz.hidden + piece * block, sz.hidden + (piece + 1) * block)
            r.grad_gated[...] = dot_nn(r.grad_feed_low[...], self.v.feed_down[:, lanes])
            for start, size in self.chunks(tokens):
                rows = slice(start, start + size)
                active = joined[piece * tokens + start : piece * tokens + start + size]
                gates_at = (piece + pieces) * tokens + start
                grads = r.grad_gated[rows]
                r.grad_joined[rows, lanes] = (grads * active).astype(LOW)
                r.grad_joined[rows, gate_lanes] = (grads * joined[gates_at : gates_at + size]).astype(LOW)
        r.tmp[...] = dot_nt(r.grad_joined[...], self.v.feed_up[...])
        self.layer_step(r.stream, r.gain_feed, 3, r.grad_cross_low)
        r.grad_cross_mixed[...] = dot_nt(r.grad_cross_low[...], self.v.out_cross[...]).astype(LOW)
        r.scores[0 : HEADS * pad] = dot_nt(r.text_value[...], r.grad_cross_mixed[...])
        for head in range(HEADS):
            rows = slice(head * pad, (head + 1) * pad)
            attention = r.cross[rows]
            grads = r.scores[rows]
            delta = jnp.sum(attention * grads, axis=0, keepdims=True)
            r.cross_scores[rows] = (attention * (grads - delta)).astype(LOW)
        r.grad_query_text[...] = (
            dot_tn(r.cross_scores[...], r.text_key[...]) * self.scale
        ).astype(LOW)
        r.tmp[...] = dot_nt(r.grad_query_text[...], self.v.query_cross[...])
        self.layer_step(r.centred_cross, r.gain_cross, 4, r.grad_self_low)
        r.gm_send[...] = dot_nt(r.osp[...], r.grad_self_low[...]).astype(LOW)
        slot = sz.slot
        copies = [
            self.remote(
                r.gm_send.at[pl.ds(pl.multiple_of(other * slot, 16), slot)],
                r.gm.at[self.seq],
                (self.batch, other),
            )
            for other in self.seq_others
        ]
        self.start(copies)
        self.gm_copies = copies
        r.gm[self.seq] = r.gm_send[pl.ds(pl.multiple_of(self.seq * slot, 16), slot)]

    def layer_step(self, source, gain, place, target):
        r = self.r
        gains = None
        for start, size in self.chunks(self.sz.tokens):
            rows = slice(start, start + size)
            part, gain_part = self.layer_back(source[rows], r.tmp[rows], row_of(gain))
            total = r.grad[rows] + part
            r.grad[rows] = total
            target[rows] = total.astype(LOW)
            gains = gain_part if gains is None else gains + gain_part
        r.gain_parts[place : place + 1] = gains

    def text_grads(self):
        r, sz = self.r, self.sz
        pad = sz.text_pad
        head_of = floor_div(iota((1, sz.channels), 1), HEAD)
        keys = dot_nn(r.cross_scores[...], r.query_text[...]) * self.scale
        values = dot_nn(r.cross_low[...], r.grad_cross_mixed[...])
        packed = None
        for number, grads in enumerate((keys, values)):
            total = None
            for head in range(HEADS):
                part = jnp.where(head_of == head, grads[head * pad : (head + 1) * pad], 0.0)
                total = part if total is None else total + part
            part = dot_nn(total.astype(LOW), r.place[number])
            packed = part if packed is None else packed + part
        r.text_send[...] = packed.astype(LOW)
        copies = [
            self.remote(
                r.text_send.at[:, pl.ds(pl.multiple_of(other * LANES, LANES), LANES)],
                r.text_recv.at[self.seq],
                (self.batch, other),
            )
            for other in self.seq_others
        ]
        self.start(copies)
        r.text_recv[self.seq] = r.text_send[
            :, pl.ds(pl.multiple_of(self.seq * LANES, LANES), LANES)
        ]
        self.text_copies = copies

    def text_second(self):
        r = self.r
        self.wait(self.text_copies)
        total = r.text_recv[0].astype(F32)
        for place in range(1, self.sz.seqs):
            total = total + r.text_recv[place].astype(F32)
        r.text_total[self.batch] = total
        copies = self.to_batch(r.text_total.at[self.batch], r.text_total.at[self.batch])
        self.start(copies)
        self.text_copies = copies

    def store_pack(self, start, rows, values):
        for shard in range(self.sz.seqs):
            self.r.pack[shard % 2, shard // 2, start + rows.start : start + rows.stop] = values[
                :, shard * LANES : (shard + 1) * LANES
            ].astype(LOW)

    def early_grads(self):
        r, sz = self.r, self.sz
        channels = sz.channels
        rows = iota((2 * channels, 1), 0)
        target = jnp.where(rows >= channels, rows + (3 * LANES - channels), rows)
        spread = jnp.where(iota((1, 6 * LANES), 1) == target, 1.0, 0.0).astype(LOW)
        for z in range(sz.seqs // 2):
            wide = 2 * channels
            grads = dot_nn(r.grad_joined[:, z * wide : (z + 1) * wide], spread).astype(LOW)
            sums = dot_tn(r.normed_feed[...], grads)
            for tile in range(6):
                start = sz.start.up + (tile % 3) * channels
                r.pack[tile // 3, z, start : start + channels] = sums[
                    :, tile * LANES : (tile + 1) * LANES
                ].astype(LOW)
        size = sz.down_rows
        tail = sz.hidden - 2 * size
        placed = [dot_nn(r.grad_feed_low[...], r.place[number]).astype(LOW) for number in range(3)]
        sums = dot_tn(r.gated[:, 0:size], placed[0]) + dot_tn(r.gated[:, size : 2 * size], placed[1])
        extra = dot_tn(r.gated[:, 2 * size :], placed[2])
        self.store_pack(sz.start.down, slice(0, tail), sums[0:tail] + extra)
        self.store_pack(sz.start.down, slice(tail, size), sums[tail:])
        sums = (
            dot_tn(r.stream_low[...], dot_nn(r.grad_branch[...], r.place[0]).astype(LOW))
            + dot_tn(r.cross_mixed[...], dot_nn(r.grad_cross_low[...], r.place[1]).astype(LOW))
            + dot_tn(r.normed_cross[...], dot_nn(r.grad_query_text[...], r.place[2]).astype(LOW))
        )
        self.store_pack(sz.start.trio, slice(0, channels), sums)

    def recall(self, step):
        r = self.r
        return pltpu.make_async_copy(
            r.kept_probs.at[lax.rem(self.seq + step, self.sz.seqs)],
            r.probs.at[lax.rem(step, 2)],
            r.local_sems.at[len(Fetched._fields) + 2 + lax.rem(step, 2)],
        )

    def attention_back(self):
        r, sz = self.r, self.sz
        keys, tokens, slot = sz.keys, sz.tokens, sz.slot
        self.wait(self.gm_copies)
        base = self.used
        self.used += sz.seqs
        own_slot = pl.ds(pl.multiple_of(self.seq * slot, 16), slot)

        def send(step):
            target = lax.rem(self.seq + step, sz.seqs)
            return self.remote(
                r.dq_send.at[target], r.dq.at[own_slot], (self.batch, target), base + step
            )

        self.in_pieces += self.gather_rows(r.act_in, 1, sz.rows)
        r.scores[0:keys, 0:LANES] = jnp.zeros((keys, LANES), F32)
        row = iota((slot, 1), 0)
        to_values = jnp.where(
            (iota((slot, LANES), 0) + 2 * HEAD == iota((slot, LANES), 1))
            & (iota((slot, LANES), 0) < HEAD),
            1.0,
            0.0,
        ).astype(LOW)

        def block(step, carry):
            source = lax.rem(self.seq + step, sz.seqs)
            slot_now = lax.rem(step, 2)
            self.recall(step).wait()

            @pl.when(step < sz.seqs - 1)
            def _():
                self.recall(step + 1).start()

            scaled = (r.gm[source].astype(F32) * r.inverse[source, 0:1]).astype(LOW).astype(F32)
            delta = -jnp.sum(r.mixed_full[source] * scaled, axis=0, keepdims=True)
            high = delta.astype(LOW).astype(F32)
            middle = (delta - high).astype(LOW).astype(F32)
            rest = delta - high - middle
            extended = jnp.where(row == HEAD, high, scaled)
            extended = jnp.where(row == HEAD + 1, middle, extended)
            extended = jnp.where(row == HEAD + 2, rest, extended).astype(LOW)
            query_rows = pl.ds(pl.multiple_of(source * tokens, tokens), tokens)
            token_grads = dot_tn(scaled.astype(LOW), to_values).astype(LOW)
            queries = r.qkv[query_rows]
            grad_query = None
            for start in range(0, keys, tokens):
                rows = slice(start, start + tokens)
                grads = dot_nn(r.vh[rows], extended)
                powers = r.probs[slot_now, rows]
                low = (powers.astype(F32) * grads).astype(LOW)
                r.scores[rows, 0:LANES] += dot_nn(low, queries) + dot_nn(powers, token_grads)
                part = dot_nn(r.kt[:, rows], low)
                grad_query = part if grad_query is None else grad_query + part
            r.dq_send[source] = (grad_query * self.scale).astype(LOW)

            @pl.when(step > 0)
            def _():
                send(step).start()

            return carry

        lax.fori_loop(0, sz.seqs // 2, block, 0)
        self.sums_batch(0)
        self.sums_batch(1)
        lax.fori_loop(sz.seqs // 2, sz.seqs, block, 0)
        factor = jnp.where(iota((1, LANES), 1) < 2 * HEAD, self.scale, 1.0)
        pick = jnp.where(
            iota((2 * HEAD, LANES), 1) == iota((2 * HEAD, LANES), 0) + HEAD, 1.0, 0.0
        ).astype(LOW)
        wide = 2 * HEAD
        for place in range(sz.seqs):
            rows = slice(place * tokens, (place + 1) * tokens)
            grads = (r.scores[rows, 0:LANES] * factor).astype(LOW)
            r.dkv_send[place * wide : (place + 1) * wide] = dot_nt(pick, grads).astype(LOW)
        own_wide = pl.ds(pl.multiple_of(self.seq * wide, 16), wide)
        copies = [
            self.remote(
                r.dkv_send.at[pl.ds(pl.multiple_of(other * wide, 16), wide)],
                r.dkv.at[own_wide],
                (self.batch, other),
            )
            for other in self.seq_others
        ]
        self.start(copies)
        r.dkv[own_wide] = r.dkv_send[own_wide]
        r.dq[own_slot] = r.dq_send[self.seq]
        self.gp_copies = copies + [send(step) for step in range(1, sz.seqs)]
        self.text_second()

    def norm_sums(self, number, rows_of):
        first = second = None
        mean, inverse = self.norm(number)
        for start, size in self.chunks(self.sz.tokens):
            grads, values = rows_of(start, size)
            one, two = col_sum(grads), col_sum(grads * ((values - mean) * inverse))
            first = one if first is None else first + one
            second = two if second is None else second + two
        return first, second

    def norm_factors(self, number, gain, total):
        gains = row_of(gain)
        sums = self.grouped(total * gains) / self.count()
        mean, inverse = self.norm(number)
        return mean, inverse, gains * inverse, sums[0:1] * inverse, sums[1:2] * inverse

    def slope(self, source, number, gain, start, size):
        mean, inverse = self.norm(number)
        normed = (source[start : start + size] - mean) * inverse
        values = normed * row_of(gain)
        gate = sigmoid(values)
        return normed, gate * (1.0 + values * (1.0 - gate)) * self.wide_mask(start, size)

    def residual_back(self):
        r, sz = self.r, self.sz
        width, tokens, channels = sz.width, sz.tokens, sz.channels
        self.wait(self.gp_copies)
        r.tmp[...] = dot_tn(r.dq[...], r.query_rows[...]) + dot_tn(r.dkv[...], r.value_rows[...])
        self.layer_step(r.stream_in, r.gain_self, 5, r.grad_in_low)
        r.gblk6[width : width + tokens] = dot_nt(r.grad_in_low[...], self.v.project_in[...])
        halo = self.halo(r.gblk6)
        halo.start()

        def block_rows(start, size):
            wide = slice(start + width, start + width + size)
            return r.gblk6[wide], r.res6[wide]

        self.stats_store(3, self.norm_sums(2, block_rows))
        stats = self.stats_start(3)
        self.wait(self.late)
        self.late = []
        self.gather_in = self.gather_forward(r.act_in, self.in_pieces)
        self.sums_cross(0)
        self.sums_cross(1)
        self.middle_grads()
        self.sums_core(2)
        halo.wait()
        self.wait(stats)
        total = self.stats_total(3)
        r.gain_parts[2:3] = total[1:2]
        mean, inverse, factor, first, second = self.norm_factors(2, r.gain_block, total)
        for start, size in self.chunks(sz.wide):
            rows = slice(start, start + size)
            mask = self.wide_mask(start, size)
            normed = (r.res6[rows] - mean) * inverse
            grads = r.cot6[rows] * mask + r.gblk6[rows] * factor - mask * (first + normed * second)
            r.cot6[rows] = grads
            self.shifts(r.shift_grad, start, size, grads * self.inside_mask(start, size))
        near = [self.remote(r.shift_grad.at[1, pl.ds(width, tokens)], r.near_grads, self.partner)]
        self.start(near)
        r.gact6[width : width + tokens] = self.conv_back(r.shift_grad, self.v.conv_second)
        halo = self.halo(r.gact6)
        halo.start()

        def mid_rows(start, size):
            wide = slice(start + width, start + width + size)
            normed, slope = self.slope(r.mid6, 1, r.gain_mid, start + width, size)
            return r.gact6[wide] * slope, r.mid6[wide]

        self.stats_store(4, self.norm_sums(1, mid_rows))
        stats = self.stats_start(4)
        self.sums_batch(2)
        self.sums_z(0)
        self.wait(near)
        self.conv_pack(sz.start.second)
        self.start(self.stages[3][1])
        halo.wait()
        self.wait(stats)
        total = self.stats_total(4)
        r.gain_parts[1:2] = total[1:2]
        mean, inverse, factor, first, second = self.norm_factors(1, r.gain_mid, total)
        time_total = None
        for start, size in self.chunks(sz.wide):
            rows = slice(start, start + size)
            normed, slope = self.slope(r.mid6, 1, r.gain_mid, start, size)
            grads = r.gact6[rows] * slope * factor - self.wide_mask(start, size) * (
                first + normed * second
            )
            self.shifts(r.shift_grad, start, size, grads)
            if width <= start < width + tokens:
                part = col_sum(grads)
                time_total = part if time_total is None else time_total + part
        first_copies = self.conv_send(r.shift_grad, r.first_send, r.first_grads)
        r.gblk6[width : width + tokens] = self.conv_back(r.shift_grad, self.v.conv_first)

        def in_rows(start, size):
            wide = slice(start + width, start + width + size)
            normed, slope = self.slope(r.lat6, 0, r.gain_in, start + width, size)
            return r.gblk6[wide] * slope, r.lat6[wide]

        parts = r.gain_parts
        self.stats_store(5, self.norm_sums(0, in_rows))
        stats = self.stats_start(5)
        r.extra_send[...] = jnp.zeros(r.extra_send.shape, F32)
        r.extra_send[2:3] = time_total
        r.extra_send[3:6] = parts[3:6]
        r.extra_recv[self.seq] = r.extra_send[...]
        extras = self.to_seq(lambda other: r.extra_send, r.extra_recv.at[self.seq])
        self.start(extras)
        self.sums_gather(0)
        self.sums_cross(2)
        self.sums_z(1)
        self.sums_cross(3)
        self.sums_z(2)
        first_copies = self.conv_grads(
            first_copies, self.gather_in, r.first_grads, r.act_in, r.first_part, r.first_recv
        )
        self.wait(stats)
        total = self.stats_total(5)
        mean, inverse, factor, first, second = self.norm_factors(0, r.gain_in, total)
        self.wait(extras)
        sums = r.extra_recv[0]
        for place in range(1, sz.seqs):
            sums = sums + r.extra_recv[place]
        r.final_send[...] = sums
        r.final_send[1:2] = total[1:2]
        r.final_send[0:1] = parts[1:2]
        r.final_send[6:7] = parts[2:3]
        r.final_recv[self.batch] = r.final_send[...]
        self.final_copies = self.to_batch(r.final_send, r.final_recv.at[self.batch])
        self.start(self.final_copies)
        for start, size in self.chunks(tokens):
            wide = slice(start + width, start + width + size)
            normed, slope = self.slope(r.lat6, 0, r.gain_in, start + width, size)
            r.latent_grad[start : start + size] = (
                r.cot6[wide]
                + r.gblk6[wide] * slope * factor
                - self.wide_mask(start + width, size) * (first + normed * second)
            )
        self.sums_gather(1)
        self.sums_z(3)
        first_copies = self.conv_gather(first_copies, r.first_part, r.first_recv, r.conv_first_sum)
        self.sums_gather(2)
        self.sums_gather(3)
        self.wait(first_copies)

    def middle_grads(self):
        r, sz = self.r, self.sz
        queries = dot_nn(r.dq[...], r.normed_self[...]).astype(LOW)
        values = dot_nn(r.dkv[...], r.normed_self[...]).astype(LOW)
        slot, wide = sz.slot, 2 * HEAD
        for shard in range(sz.seqs):
            for tile, (start, size) in enumerate(self.lane_tiles()):
                target = r.pack.at[shard % 2, shard // 2]
                at = sz.start.heads + tile * LANES
                if size < LANES:
                    target[at : at + LANES] = jnp.zeros((LANES, LANES), LOW)
                lanes = slice(start, start + size)
                target[at : at + slot, 0:size] = queries[shard * slot : (shard + 1) * slot, lanes]
                target[at + slot : at + LANES, 0:size] = values[shard * wide : (shard + 1) * wide, lanes]
        outer = dot_nn(r.mixed[...], dot_nn(r.grad_self_low[...], r.place[0]).astype(LOW))
        inner = dot_tn(r.normed_block[...], dot_nn(r.grad_in_low[...], r.place[1]).astype(LOW))
        self.store_pack(sz.start.pair, slice(0, sz.channels), outer[0 : sz.channels] + inner)
        self.store_pack(sz.start.pair, slice(sz.channels, HEADS * sz.slot), outer[sz.channels :])

    def conv_pack(self, start):
        r, sz = self.r, self.sz
        own = r.shift_grad[1, sz.width : sz.width + sz.tokens]
        placed = [dot_nn(own, r.place_half[number]).astype(LOW) for number in range(3)]
        near = [dot_nn(r.near_grads[...], r.place_half[number]).astype(LOW) for number in range(3)]
        for col in range(3):
            total = None
            for row in range(3):
                rows = slice(row * sz.width, row * sz.width + sz.tokens)
                part = dot_tn(r.shifted[col, rows], placed[row])
                part = part + dot_tn(r.near_shifted[col, rows], near[row])
                total = part if total is None else total + part
            at = start + col * sz.channels
            for z in range(sz.seqs // 2):
                r.recv_core[z, at : at + sz.channels] = total[:, z * LANES : (z + 1) * LANES].astype(LOW)

    def sums_setup(self):
        r, sz = self.r, self.sz
        half, batches = sz.seqs // 2, sz.batches
        self.stages = []
        for start, size in sz.chunks:
            rows = pl.ds(start, size)
            part = size // batches
            quarter = pl.ds(start // batches, part)
            one = []
            if start < sz.start.second:
                one.append(
                    self.remote(r.pack.at[1 - self.core, :, rows], r.recv_core.at[:, rows], self.partner)
                )
            pair = half // 2
            x_rows = pl.ds(pl.multiple_of(start + 2 * (1 - self.batch_x) * part, 16), 2 * part)
            y_rows = pl.ds(pl.multiple_of(start + 2 * (1 - self.batch_y) * part, 16), 2 * part)
            two = [
                self.remote(
                    r.recv_core.at[pl.ds(place * pair, pair), far_rows],
                    r.recv_first.at[place, :, pl.ds(start // 2, 2 * part)],
                    peer,
                )
                for place, (far_rows, peer) in enumerate(((x_rows, self.x_peer), (y_rows, self.y_peer)))
            ]
            far_y = 2 * self.batch_x + 1 - self.batch_y
            far_x = 2 * self.batch_y + 1 - self.batch_x
            cross = [
                self.remote(
                    r.recv_core.at[
                        pl.ds(place * pair, pair), pl.ds(pl.multiple_of(start + far * part, 16), part)
                    ],
                    r.recv_second.at[pl.ds(place * pair, pair), quarter],
                    peer,
                )
                for place, (far, peer) in enumerate(((far_y, self.y_peer), (far_x, self.x_peer)))
            ]
            three = [
                self.remote(
                    r.recv_second.at[other, quarter],
                    r.recv_z.at[step, quarter],
                    (self.batch, other * 2 + self.core),
                )
                for step, other in enumerate(self.z_others)
            ]
            four = [
                self.remote(
                    r.gathered.at[pl.ds(pl.multiple_of(start + self.quarter_of(self.z_pos) * part, 16), part)],
                    r.gathered.at[pl.ds(pl.multiple_of(start + self.quarter_of(self.z_pos) * part, 16), part)],
                    (other, self.seq),
                )
                for other in self.batch_others
            ]
            self.stages.append((one, two, cross, three, four))

    def quarter_of(self, z):
        second = z // (self.sz.seqs // 4)
        x, y = self.batch_x, self.batch_y
        return (1 - second) * (2 * x + y) + second * (2 * y + x)

    def sums_core(self, number):
        self.start(self.stages[number][0])

    def sums_batch(self, number):
        r, sz = self.r, self.sz
        start, size = sz.chunks[number]
        self.wait(self.stages[number][0])

        @pl.loop(0, sz.seqs // 2)
        def add(z):
            rows = pl.ds(start, size)
            r.recv_core[z, rows] = (
                r.pack[self.core, z, rows].astype(F32) + r.recv_core[z, rows].astype(F32)
            ).astype(LOW)

        self.start(self.stages[number][1])

    def sums_cross(self, number):
        r, sz = self.r, self.sz
        start, size = sz.chunks[number]
        part = size // sz.batches
        pair = sz.seqs // 4
        self.wait(self.stages[number][1])

        def add(target, source):
            r.recv_core[target] = (r.recv_core[target].astype(F32) + source.astype(F32)).astype(LOW)

        @pl.loop(0, pair)
        def sums(z):
            for place, near in enumerate((self.batch_x, self.batch_y)):
                rows = pl.ds(pl.multiple_of(start + 2 * near * part, 16), 2 * part)
                add((z + place * pair, rows), r.recv_first[place, z, pl.ds(start // 2, 2 * part)])

        self.start(self.stages[number][2])

    def sums_z(self, number):
        r, sz = self.r, self.sz
        start, size = sz.chunks[number]
        part = size // sz.batches
        quarter = pl.ds(start // sz.batches, part)
        self.wait(self.stages[number][2])

        @pl.loop(0, sz.seqs // 2)
        def add(z):
            own = r.recv_core[z, pl.ds(pl.multiple_of(start + self.quarter_of(z) * part, 16), part)]
            r.recv_second[z, quarter] = (
                own.astype(F32) + r.recv_second[z, quarter].astype(F32)
            ).astype(LOW)

        self.start(self.stages[number][3])

    def sums_gather(self, number):
        r, sz = self.r, self.sz
        start, size = sz.chunks[number]
        part = size // sz.batches
        quarter = pl.ds(start // sz.batches, part)
        self.wait(self.stages[number][3])
        total = r.recv_second[self.z_pos, quarter].astype(F32)
        for step in range(sz.seqs // 2 - 1):
            total = total + r.recv_z[step, quarter].astype(F32)
        own = pl.ds(pl.multiple_of(start + self.quarter_of(self.z_pos) * part, 16), part)
        r.gathered[own] = total.astype(LOW)
        self.start(self.stages[number][4])

    def run(self):
        self.entry()
        self.sums_setup()
        self.residual()
        self.attention()
        self.local_block()
        self.text_grads()
        self.early_grads()
        self.sums_core(0)
        self.sums_core(1)
        self.attention_back()
        self.residual_back()
        for stages in self.stages:
            self.wait(stages[4])
        self.wait(self.text_copies)
        self.wait(self.final_copies)
        assert self.used <= SEMAPHORES


def fused_call(sz, operands):
    t, c = sz.tokens, sz.channels
    outs = dict(
        output=((t, c), F32),
        latent_grad=((t, c), F32),
        final_recv=((sz.batches, 8, c), F32),
        time_all=((sz.batches, 8, sz.emb), F32),
        text_all=((sz.batches, sz.text_pad, sz.context), LOW),
        text_total=((sz.batches, sz.text_pad, LANES), F32),
        gathered=((sz.pack_rows, LANES), LOW),
        conv_first_sum=((sz.conv_rows, c), LOW),
        kept_probs=((sz.seqs, sz.keys, t), LOW),
    )
    scratch = buffers(sz)
    vmem = pl.BlockSpec(memory_space=pltpu.VMEM)
    anywhere = pl.BlockSpec(memory_space=pl.ANY)
    fetched = [getattr(operands, name) for name in Fetched._fields]
    specs = operands._replace(**{name: vmem for name in Inputs._fields})
    specs = specs._replace(**{name: anywhere for name in Fetched._fields})
    specs = specs._replace(
        latents=anywhere, cotangent=anywhere, heights=pl.BlockSpec(memory_space=pltpu.SMEM)
    )
    names = list(Inputs._fields) + list(outs) + list(scratch)
    shapes = [pltpu.VMEM(shape, kind) for shape, kind in scratch.values()]
    shapes += [pltpu.VMEM(operand.shape, operand.dtype) for operand in fetched]
    shapes += [pltpu.SemaphoreType.DMA((2, SEMAPHORES)), pltpu.SemaphoreType.DMA((len(fetched) + 4,))]

    def body(*refs):
        count = len(names)
        named = types.SimpleNamespace(**dict(zip(names, refs[:count])))
        named.sems, named.local_sems = refs[-2:]
        Fused(sz, named, Fetched(*refs[count:-2])).run()

    return pl.pallas_call(
        body,
        out_shape=tuple(jax.ShapeDtypeStruct(shape, kind) for shape, kind in outs.values()),
        in_specs=list(specs),
        out_specs=(vmem,) * (len(outs) - 1) + (anywhere,),
        scratch_shapes=shapes,
        compiler_params=pltpu.CompilerParams(
            collective_id=5, has_side_effects=True, vmem_limit_bytes=63 << 20
        ),
    )(*operands)


class Outputs(typing.NamedTuple):
    output: typing.Any
    latent_grad: typing.Any
    gain_in: typing.Any
    conv_first: typing.Any
    time_weight: typing.Any
    gain_mid: typing.Any
    conv_second: typing.Any
    gain_block: typing.Any
    project_in: typing.Any
    gain_self: typing.Any
    query_self: typing.Any
    key_self: typing.Any
    value_self: typing.Any
    out_self: typing.Any
    gain_cross: typing.Any
    query_cross: typing.Any
    key_cross: typing.Any
    value_cross: typing.Any
    out_cross: typing.Any
    gain_feed: typing.Any
    feed_up: typing.Any
    feed_down: typing.Any
    project_out: typing.Any


def unpack_kernel(
    sz,
    output,
    latent_grad,
    final_recv,
    time_all,
    text_all,
    text_total,
    gathered,
    first_sum,
    *out_refs,
):
    outs = Outputs(*out_refs)
    channels = sz.channels
    outs.output[...] = output[...]
    outs.latent_grad[...] = latent_grad[...]
    eye = jnp.where(iota((LANES, LANES), 0) == iota((LANES, LANES), 1), 1.0, 0.0).astype(LOW)

    def turned(start, rows):
        return dot_nt(eye, gathered[start : start + rows])

    def three(values, *targets):
        for place, target in enumerate(targets):
            target[...] = values[place * HEAD : (place + 1) * HEAD]

    for tile in range(3):
        lanes = slice(tile * LANES, min((tile + 1) * LANES, outs.feed_up.shape[1]))
        start = sz.start.up + tile * channels
        outs.feed_up[:, lanes] = gathered[start : start + channels, : lanes.stop - lanes.start].astype(F32)
    values = turned(sz.start.down, sz.down_rows)
    for place in range(3):
        lanes = slice(place * sz.down_rows, min((place + 1) * sz.down_rows, sz.hidden))
        outs.feed_down[:, lanes] = values[
            place * HEAD : (place + 1) * HEAD, : lanes.stop - lanes.start
        ]
    three(turned(sz.start.trio, channels), outs.project_out, outs.out_cross, outs.query_cross)
    for tile in range(sz.sizes.heads // LANES):
        lanes = slice(tile * LANES, min((tile + 1) * LANES, channels))
        start = sz.start.heads + tile * LANES
        values = gathered[start : start + LANES].astype(F32)[:, : lanes.stop - lanes.start]
        outs.query_self[:, lanes] = values[:HEAD]
        outs.key_self[:, lanes] = values[sz.slot : sz.slot + HEAD]
        outs.value_self[:, lanes] = values[sz.slot + HEAD :]
    outs.project_in[...] = turned(sz.start.pair, channels)[HEAD : 2 * HEAD]
    wide = turned(sz.start.pair, HEADS * sz.slot)[:HEAD].astype(LOW)
    source = iota((1, channels), 1)
    target = source + (sz.slot - HEAD) * floor_div(source, HEAD)
    squeeze = jnp.where(iota((HEADS * sz.slot, 1), 0) == target, 1.0, 0.0).astype(LOW)
    outs.out_self[...] = dot_nn(wide, squeeze)
    for col in range(3):
        values = turned(sz.start.second + col * channels, channels)
        for row in range(3):
            outs.conv_second[row, col] = values[row * HEAD : (row + 1) * HEAD]
    for row in range(3):
        values = first_sum[row * LANES : (row + 1) * LANES].astype(F32)
        for col in range(3):
            outs.conv_first[row, col] = values[col * HEAD : (col + 1) * HEAD]
    text = None
    for place in range(sz.batches):
        grads = text_total[place]
        high = grads.astype(LOW)
        rest = (grads - high.astype(F32)).astype(LOW)
        part = dot_tn(high, text_all[place]) + dot_tn(rest, text_all[place])
        text = part if text is None else text + part
    three(text, outs.key_cross, outs.value_cross)
    pick = jnp.where(
        (iota((channels, LANES), 0) == iota((channels, LANES), 1) + lax.axis_index(SEQ) * HEAD)
        & (iota((channels, LANES), 1) < HEAD),
        1.0,
        0.0,
    ).astype(LOW)
    total = time = None
    for place in range(sz.batches):
        rows = final_recv[place]
        total = rows if total is None else total + rows
        picked = dot_nn(split_three(jnp.where(iota((8, 1), 0) == 2, rows, 0.0)), pick)
        act = time_all[place]
        act = pltpu.roll(act, 2, 0)
        part = dot_tn(picked.astype(LOW), jnp.concatenate([act, act, act], axis=0).astype(LOW))
        time = part if time is None else time + part
    outs.time_weight[...] = time[:HEAD]
    gains = sum_three(dot_nn(split_three(total), pick))
    order = (
        outs.gain_mid,
        outs.gain_in,
        None,
        outs.gain_feed,
        outs.gain_cross,
        outs.gain_self,
        outs.gain_block,
    )
    for place, out in enumerate(order):
        if out is not None:
            out[...] = gains[place : place + 1, :HEAD]


def unpack_call(sz, results):
    channels, hidden = sz.channels, sz.hidden
    square = jax.ShapeDtypeStruct((HEAD, channels), F32)
    gain = jax.ShapeDtypeStruct((1, HEAD), F32)
    image = jax.ShapeDtypeStruct((sz.tokens, channels), F32)
    conv = jax.ShapeDtypeStruct((3, 3, HEAD, channels), F32)
    context = jax.ShapeDtypeStruct((HEAD, sz.context), F32)
    shapes = Outputs(*[square] * len(Outputs._fields))._replace(
        output=image,
        latent_grad=image,
        gain_in=gain,
        gain_mid=gain,
        gain_block=gain,
        gain_self=gain,
        gain_cross=gain,
        gain_feed=gain,
        conv_first=conv,
        conv_second=conv,
        time_weight=jax.ShapeDtypeStruct((HEAD, sz.emb), F32),
        key_cross=context,
        value_cross=context,
        feed_up=jax.ShapeDtypeStruct((channels, 2 * hidden // sz.seqs), F32),
        feed_down=jax.ShapeDtypeStruct((HEAD, hidden), F32),
    )
    vmem = pl.BlockSpec(memory_space=pltpu.VMEM)
    return Outputs(
        *pl.pallas_call(
            lambda *refs: unpack_kernel(sz, *refs),
            out_shape=tuple(shapes),
            in_specs=[vmem] * len(results),
            out_specs=(vmem,) * len(shapes),
            compiler_params=pltpu.CompilerParams(vmem_limit_bytes=60 << 20),
        )(*results)
    )


def fast_device(*arguments):
    given = Inputs(*arguments)
    latents = given.latents
    sz = Sizes(
        lax.axis_size(BATCH),
        lax.axis_size(SEQ),
        latents,
        given.time_vector,
        given.text_states,
        given.feed_down,
    )
    channels = sz.channels
    flat = given._replace(
        latents=latents.reshape(sz.tokens, channels),
        cotangent=given.cotangent.reshape(sz.tokens, channels),
        text_states=given.text_states.reshape(sz.text, sz.context),
        time_weight=given.time_weight.T,
        key_cross=given.key_cross.T,
        value_cross=given.value_cross.T,
        feed_down=given.feed_down.T,
    )
    results = fused_call(sz, flat)[:-1]
    outs = unpack_call(sz, results)
    shaped = outs._replace(
        output=outs.output.reshape(latents.shape), latent_grad=outs.latent_grad.reshape(latents.shape)
    )
    shaped = [jnp.swapaxes(one, -2, -1) if one.shape[-2] == HEAD else one for one in shaped]
    return tuple(one.reshape(-1) if one.shape[0] == 1 and one.ndim == 2 else one for one in shaped)


def on_device(
    latents,
    heights,
    time_vector,
    text_states,
    gain_in,
    conv_first,
    time_weight,
    gain_mid,
    conv_second,
    gain_block,
    project_in,
    gain_self,
    query_self,
    key_self,
    value_self,
    out_self,
    gain_cross,
    query_cross,
    key_cross,
    value_cross,
    out_cross,
    gain_feed,
    feed_up,
    feed_down,
    project_out,
    cotangent,
):
    images_in, rows_in, col_count, channels = latents.shape
    seq_size = lax.axis_size(SEQ)
    seq_index = lax.axis_index(SEQ)
    block_rows = rows_in * col_count
    keys_count = block_rows * seq_size
    score_scale = HEAD ** (-0.5)
    row_ids = seq_index * rows_in + jnp.arange(rows_in, dtype=jnp.int32)

    def spread_fn(values):
        return values

    def pick_fn(values):
        return values

    images, row_count = (latents.shape[0], latents.shape[1])
    tok_rows = row_count * col_count
    tokens = images * tok_rows
    row_valid = (row_ids[None, :] < heights[:, None]).astype(jnp.int32)
    row_mask = row_valid.astype(jnp.float32)
    cell_mask = row_mask[:, :, None, None]
    key_rows = jnp.arange(keys_count, dtype=jnp.int32) // col_count
    key_mask = (key_rows[None, :] < heights[:, None]).astype(jnp.int32)
    cell_counts = (heights * (col_count * (channels // GROUPS))).astype(jnp.float32)

    def res_piece(values, norm_gain, sum_first, sum_second):
        return (
            jax.nn.silu(group_apply(values, norm_gain, sum_first, sum_second, cell_counts))
            * cell_mask
        )

    def block_piece(values, norm_gain, sum_first, sum_second):
        return group_apply(values, norm_gain, sum_first, sum_second, cell_counts)

    first_in, second_in = norm_stats(latents, row_mask, spread_fn, pick_fn)
    act_in = res_piece(latents, gain_in, first_in, second_in).astype(jnp.bfloat16)
    padded_in = rows_halo(act_in)
    conv_out = conv_rows(padded_in, conv_first)
    time_act = jax.nn.silu(time_vector.astype(jnp.float32)).astype(jnp.bfloat16)
    time_term = jnp.dot(time_act, time_weight, preferred_element_type=jnp.float32)
    mid_in = conv_out + time_term[:, None, None, :]
    first_mid, second_mid = norm_stats(mid_in, row_mask, spread_fn, pick_fn)
    act_mid = res_piece(mid_in, gain_mid, first_mid, second_mid).astype(jnp.bfloat16)
    padded_mid = rows_halo(act_mid)
    resid = latents + conv_rows(padded_mid, conv_second)
    first_block, second_block = norm_stats(resid, row_mask, spread_fn, pick_fn)
    normed_block = (
        block_piece(resid, gain_block, first_block, second_block)
        .reshape(tokens, channels)
        .astype(jnp.bfloat16)
    )
    stream_in = jnp.dot(normed_block, project_in, preferred_element_type=jnp.float32)
    normed_self = layer_norm(stream_in, gain_self).astype(jnp.bfloat16)
    joined_self = jnp.concatenate((query_self, key_self, value_self), axis=1)
    projected = (
        jnp.dot(normed_self, joined_self, preferred_element_type=jnp.float32)
        .astype(jnp.bfloat16)
        .reshape(images, tok_rows, 3 * channels)
    )
    queries = projected[:, :, :channels]
    keys_local = projected[:, :, channels : 2 * channels]
    values_local = projected[:, :, 2 * channels :]
    keys_all = lax.all_gather(keys_local, SEQ, axis=1, tiled=True)
    values_all = lax.all_gather(values_local, SEQ, axis=1, tiled=True)

    def forward_image(bundle):
        image_queries, image_keys, image_values, image_mask = bundle
        query_blocks = image_queries.reshape(-1, block_rows, channels)
        return lax.map(
            lambda part: self_forward((part, image_keys, image_values, image_mask), score_scale),
            query_blocks,
        )

    attn_mixed, log_totals = lax.map(forward_image, (queries, keys_all, values_all, key_mask))
    mixed_flat = attn_mixed.reshape(tokens, channels)
    stream_self = stream_in + jnp.dot(mixed_flat, out_self, preferred_element_type=jnp.float32)
    normed_cross = layer_norm(stream_self, gain_cross).astype(jnp.bfloat16)
    query_text = (
        jnp.dot(normed_cross, query_cross, preferred_element_type=jnp.float32)
        .astype(jnp.bfloat16)
        .reshape(images, tok_rows, HEADS, HEAD)
    )
    text_flat = text_states.reshape(-1, text_states.shape[2])
    text_pairs = (
        jnp.dot(
            text_flat,
            jnp.concatenate((key_cross, value_cross), axis=1),
            preferred_element_type=jnp.float32,
        )
        .astype(jnp.bfloat16)
        .reshape(images, -1, 2, HEADS, HEAD)
    )
    text_keys = text_pairs[:, :, 0]
    text_values = text_pairs[:, :, 1]
    cross_scores = (
        jnp.einsum("iqhd,ikhd->ihqk", query_text, text_keys, preferred_element_type=jnp.float32)
        * score_scale
    )
    cross_attn = jnp.exp(cross_scores - jax.nn.logsumexp(cross_scores, axis=-1, keepdims=True))
    cross_low = cross_attn.astype(jnp.bfloat16)
    cross_mixed = (
        jnp.einsum("ihqk,ikhd->iqhd", cross_low, text_values, preferred_element_type=jnp.float32)
        .astype(jnp.bfloat16)
        .reshape(tokens, channels)
    )
    stream_cross = stream_self + jnp.dot(cross_mixed, out_cross, preferred_element_type=jnp.float32)
    normed_feed = layer_norm(stream_cross, gain_feed).astype(jnp.bfloat16)
    joined_feed = jnp.dot(normed_feed, feed_up, preferred_element_type=jnp.float32)
    gated = geglu(joined_feed).astype(jnp.bfloat16)
    stream_feed = stream_cross + jnp.dot(gated, feed_down, preferred_element_type=jnp.float32)
    stream_low = stream_feed.astype(jnp.bfloat16)
    branch_out = jnp.dot(stream_low, project_out, preferred_element_type=jnp.float32).reshape(
        images, row_count, col_count, channels
    )
    output = (resid + branch_out) * cell_mask
    grad_output = cotangent * cell_mask
    grad_branch = grad_output.reshape(tokens, channels).astype(jnp.bfloat16)
    grad_project_out = grad_dot(stream_low, grad_branch)
    grad_stream = back_dot(grad_branch, project_out)
    grad_feed_low = grad_stream.astype(jnp.bfloat16)
    grad_feed_down = grad_dot(gated, grad_feed_low)
    grad_gated = back_dot(grad_feed_low, feed_down)
    unused, pull_geglu = jax.vjp(geglu, joined_feed)
    grad_joined = pull_geglu(grad_gated)[0].astype(jnp.bfloat16)
    grad_feed_up = grad_dot(normed_feed, grad_joined)
    unused, pull_norm = jax.vjp(layer_norm, stream_cross, gain_feed)
    grad_part, grad_gain_feed = pull_norm(back_dot(grad_joined, feed_up))
    grad_stream = grad_stream + grad_part
    grad_cross_low = grad_stream.astype(jnp.bfloat16)
    grad_out_cross = grad_dot(cross_mixed, grad_cross_low)
    grad_cross_mixed = (
        back_dot(grad_cross_low, out_cross)
        .astype(jnp.bfloat16)
        .reshape(images, tok_rows, HEADS, HEAD)
    )
    grad_text_values = jnp.einsum(
        "ihqk,iqhd->ikhd", cross_low, grad_cross_mixed, preferred_element_type=jnp.float32
    )
    grad_cross_attn = jnp.einsum(
        "iqhd,ikhd->ihqk", grad_cross_mixed, text_values, preferred_element_type=jnp.float32
    )
    cross_delta = jnp.sum(cross_attn * grad_cross_attn, axis=-1, keepdims=True)
    grad_cross_scores = (cross_attn * (grad_cross_attn - cross_delta)).astype(jnp.bfloat16)
    grad_query_text = (
        (
            jnp.einsum(
                "ihqk,ikhd->iqhd", grad_cross_scores, text_keys, preferred_element_type=jnp.float32
            )
            * score_scale
        )
        .astype(jnp.bfloat16)
        .reshape(tokens, channels)
    )
    grad_text_keys = (
        jnp.einsum(
            "ihqk,iqhd->ikhd", grad_cross_scores, query_text, preferred_element_type=jnp.float32
        )
        * score_scale
    )
    text_wide = text_flat.astype(jnp.float32)
    grad_key_cross = exact_grad_dot(text_wide, grad_text_keys.reshape(-1, channels))
    grad_value_cross = exact_grad_dot(text_wide, grad_text_values.reshape(-1, channels))
    grad_query_cross = grad_dot(normed_cross, grad_query_text)
    unused, pull_norm = jax.vjp(layer_norm, stream_self, gain_cross)
    grad_part, grad_gain_cross = pull_norm(back_dot(grad_query_text, query_cross))
    grad_stream = grad_stream + grad_part
    grad_self_low = grad_stream.astype(jnp.bfloat16)
    grad_out_self = grad_dot(mixed_flat, grad_self_low)
    grad_mixed = (
        back_dot(grad_self_low, out_self).astype(jnp.bfloat16).reshape(images, tok_rows, channels)
    )

    def backward_image(bundle):
        image_queries, image_grads, image_totals, image_keys, image_values, image_mask = bundle
        query_blocks = image_queries.reshape(-1, block_rows, channels)
        grad_blocks = image_grads.reshape(-1, block_rows, channels)
        return lax.map(
            lambda part: query_side(
                (part[0], part[1], part[2], image_keys, image_values, image_mask), score_scale
            ),
            (query_blocks, grad_blocks, image_totals),
        )

    grad_queries, kept_attn, kept_grads = lax.map(
        backward_image, (queries, grad_mixed, log_totals, keys_all, values_all, key_mask)
    )
    grads_four = grad_mixed.reshape(images, -1, block_rows, HEADS, HEAD)
    queries_four = queries.reshape(images, -1, block_rows, HEADS, HEAD)
    row_total = tok_rows * lax.axis_size(SEQ)
    value_terms = jnp.einsum(
        "inhqk,inqhd->kihd", kept_attn, grads_four, preferred_element_type=jnp.float32
    )
    key_terms_part = (
        jnp.einsum(
            "inhqk,inqhd->kihd", kept_grads, queries_four, preferred_element_type=jnp.float32
        )
        * score_scale
    )
    summed = lax.psum_scatter(
        jnp.stack(
            (
                key_terms_part.reshape(row_total, images, -1),
                value_terms.reshape(row_total, images, -1),
            ),
            2,
        ).astype(jnp.bfloat16),
        SEQ,
        scatter_dimension=0,
        tiled=True,
    ).astype(jnp.float32)
    grad_keys = jnp.swapaxes(summed[:, :, 0], 0, 1)
    grad_values = jnp.swapaxes(summed[:, :, 1], 0, 1)
    grad_projected = jnp.concatenate(
        (
            grad_queries.reshape(images, tok_rows, channels),
            grad_keys.astype(jnp.bfloat16),
            grad_values.astype(jnp.bfloat16),
        ),
        axis=2,
    ).reshape(tokens, 3 * channels)
    grad_joined_self = grad_dot(normed_self, grad_projected)
    unused, pull_norm = jax.vjp(layer_norm, stream_in, gain_self)
    grad_part, grad_gain_self = pull_norm(back_dot(grad_projected, joined_self))
    grad_stream = grad_stream + grad_part
    grad_stream_low = grad_stream.astype(jnp.bfloat16)
    grad_project_in = grad_dot(normed_block, grad_stream_low)
    grad_block = back_dot(grad_stream_low, project_in).reshape(
        images, row_count, col_count, channels
    )
    grad_resid_part, grad_gain_block = norm_backward(
        block_piece,
        resid,
        gain_block,
        first_block,
        second_block,
        grad_block,
        row_mask,
        spread_fn,
        pick_fn,
    )
    grad_resid = grad_output + grad_resid_part
    grad_second_low = grad_resid.astype(jnp.bfloat16)
    grad_conv_second = conv_weight_grad(padded_mid, grad_second_low)
    grad_act_mid = conv_rows(grads_halo(grad_second_low), flipped(conv_second))
    grad_mid, grad_gain_mid = norm_backward(
        res_piece,
        mid_in,
        gain_mid,
        first_mid,
        second_mid,
        grad_act_mid,
        row_mask,
        spread_fn,
        pick_fn,
    )
    grad_time = jnp.sum(grad_mid, axis=(1, 2))
    grad_time_weight = exact_grad_dot(time_act.astype(jnp.float32), grad_time)
    grad_first_low = grad_mid.astype(jnp.bfloat16)
    grad_conv_first = conv_weight_grad(padded_in, grad_first_low)
    grad_act_in = conv_rows(grads_halo(grad_first_low), flipped(conv_first))
    grad_in_part, grad_gain_in = norm_backward(
        res_piece, latents, gain_in, first_in, second_in, grad_act_in, row_mask, spread_fn, pick_fn
    )
    latent_grad = grad_resid + grad_in_part
    shares = (
        lax.psum_scatter(
            grad_gain_in.reshape(1, -1).astype(jnp.bfloat16), SEQ, scatter_dimension=1, tiled=True
        ).astype(jnp.float32),
        lax.psum_scatter(
            grad_conv_first.reshape(-1, channels).astype(jnp.bfloat16),
            SEQ,
            scatter_dimension=1,
            tiled=True,
        ).astype(jnp.float32),
        lax.psum_scatter(
            grad_time_weight.astype(jnp.bfloat16), SEQ, scatter_dimension=1, tiled=True
        ).astype(jnp.float32),
        lax.psum_scatter(
            grad_gain_mid.reshape(1, -1).astype(jnp.bfloat16),
            SEQ,
            scatter_dimension=1,
            tiled=True,
        ).astype(jnp.float32),
        lax.psum_scatter(
            grad_conv_second.reshape(-1, channels).astype(jnp.bfloat16),
            SEQ,
            scatter_dimension=1,
            tiled=True,
        ).astype(jnp.float32),
        lax.psum_scatter(
            grad_gain_block.reshape(1, -1).astype(jnp.bfloat16),
            SEQ,
            scatter_dimension=1,
            tiled=True,
        ).astype(jnp.float32),
        lax.psum_scatter(
            grad_project_in.astype(jnp.bfloat16), SEQ, scatter_dimension=1, tiled=True
        ).astype(jnp.float32),
        lax.psum_scatter(
            grad_gain_self.reshape(1, -1).astype(jnp.bfloat16),
            SEQ,
            scatter_dimension=1,
            tiled=True,
        ).astype(jnp.float32),
        lax.psum_scatter(
            grad_joined_self[:, :channels].astype(jnp.bfloat16),
            SEQ,
            scatter_dimension=1,
            tiled=True,
        ).astype(jnp.float32),
        lax.psum_scatter(
            grad_joined_self[:, channels : 2 * channels].astype(jnp.bfloat16),
            SEQ,
            scatter_dimension=1,
            tiled=True,
        ).astype(jnp.float32),
        lax.psum_scatter(
            grad_joined_self[:, 2 * channels :].astype(jnp.bfloat16),
            SEQ,
            scatter_dimension=1,
            tiled=True,
        ).astype(jnp.float32),
        lax.psum_scatter(
            grad_out_self.astype(jnp.bfloat16), SEQ, scatter_dimension=1, tiled=True
        ).astype(jnp.float32),
        lax.psum_scatter(
            grad_gain_cross.reshape(1, -1).astype(jnp.bfloat16),
            SEQ,
            scatter_dimension=1,
            tiled=True,
        ).astype(jnp.float32),
        lax.psum_scatter(
            grad_query_cross.astype(jnp.bfloat16), SEQ, scatter_dimension=1, tiled=True
        ).astype(jnp.float32),
        lax.psum_scatter(
            grad_key_cross.astype(jnp.bfloat16), SEQ, scatter_dimension=1, tiled=True
        ).astype(jnp.float32),
        lax.psum_scatter(
            grad_value_cross.astype(jnp.bfloat16), SEQ, scatter_dimension=1, tiled=True
        ).astype(jnp.float32),
        lax.psum_scatter(
            grad_out_cross.astype(jnp.bfloat16), SEQ, scatter_dimension=1, tiled=True
        ).astype(jnp.float32),
        lax.psum_scatter(
            grad_gain_feed.reshape(1, -1).astype(jnp.bfloat16),
            SEQ,
            scatter_dimension=1,
            tiled=True,
        ).astype(jnp.float32),
        lax.psum_scatter(
            grad_feed_up.astype(jnp.bfloat16), SEQ, scatter_dimension=1, tiled=True
        ).astype(jnp.float32),
        lax.psum_scatter(
            grad_feed_down.astype(jnp.bfloat16), SEQ, scatter_dimension=1, tiled=True
        ).astype(jnp.float32),
        lax.psum_scatter(
            grad_project_out.astype(jnp.bfloat16), SEQ, scatter_dimension=1, tiled=True
        ).astype(jnp.float32),
    )
    totals = (
        lax.psum(shares[0].astype(jnp.bfloat16), BATCH).astype(jnp.float32),
        lax.psum(shares[1].astype(jnp.bfloat16), BATCH).astype(jnp.float32),
        lax.psum(shares[2].astype(jnp.bfloat16), BATCH).astype(jnp.float32),
        lax.psum(shares[3].astype(jnp.bfloat16), BATCH).astype(jnp.float32),
        lax.psum(shares[4].astype(jnp.bfloat16), BATCH).astype(jnp.float32),
        lax.psum(shares[5].astype(jnp.bfloat16), BATCH).astype(jnp.float32),
        lax.psum(shares[6].astype(jnp.bfloat16), BATCH).astype(jnp.float32),
        lax.psum(shares[7].astype(jnp.bfloat16), BATCH).astype(jnp.float32),
        lax.psum(shares[8].astype(jnp.bfloat16), BATCH).astype(jnp.float32),
        lax.psum(shares[9].astype(jnp.bfloat16), BATCH).astype(jnp.float32),
        lax.psum(shares[10].astype(jnp.bfloat16), BATCH).astype(jnp.float32),
        lax.psum(shares[11].astype(jnp.bfloat16), BATCH).astype(jnp.float32),
        lax.psum(shares[12].astype(jnp.bfloat16), BATCH).astype(jnp.float32),
        lax.psum(shares[13].astype(jnp.bfloat16), BATCH).astype(jnp.float32),
        lax.psum(shares[14].astype(jnp.bfloat16), BATCH).astype(jnp.float32),
        lax.psum(shares[15].astype(jnp.bfloat16), BATCH).astype(jnp.float32),
        lax.psum(shares[16].astype(jnp.bfloat16), BATCH).astype(jnp.float32),
        lax.psum(shares[17].astype(jnp.bfloat16), BATCH).astype(jnp.float32),
        lax.psum(shares[18].astype(jnp.bfloat16), BATCH).astype(jnp.float32),
        lax.psum(shares[19].astype(jnp.bfloat16), BATCH).astype(jnp.float32),
        lax.psum(shares[20].astype(jnp.bfloat16), BATCH).astype(jnp.float32),
    )
    return (
        output,
        latent_grad,
        totals[0].reshape(-1),
        totals[1].reshape(3, 3, channels, -1),
        totals[2],
        totals[3].reshape(-1),
        totals[4].reshape(3, 3, channels, -1),
        totals[5].reshape(-1),
        totals[6],
        totals[7].reshape(-1),
        totals[8],
        totals[9],
        totals[10],
        totals[11],
        totals[12].reshape(-1),
        totals[13],
        totals[14],
        totals[15],
        totals[16],
        totals[17].reshape(-1),
        totals[18],
        totals[19],
        totals[20],
    )


def solution(mesh):
    in_specs = (
        P(BATCH, SEQ, None, None),
        P(BATCH),
        P(BATCH, None),
        P(BATCH, None, None),
        P(),
        P(),
        P(),
        P(),
        P(),
        P(),
        P(),
        P(),
        P(),
        P(),
        P(),
        P(),
        P(),
        P(),
        P(),
        P(),
        P(),
        P(),
        P(),
        P(),
        P(),
        P(BATCH, SEQ, None, None),
    )
    out_specs = (
        P(BATCH, SEQ, None, None),
        P(BATCH, SEQ, None, None),
        P(SEQ),
        P(None, None, None, SEQ),
        P(None, SEQ),
        P(SEQ),
        P(None, None, None, SEQ),
        P(SEQ),
        P(None, SEQ),
        P(SEQ),
        P(None, SEQ),
        P(None, SEQ),
        P(None, SEQ),
        P(None, SEQ),
        P(SEQ),
        P(None, SEQ),
        P(None, SEQ),
        P(None, SEQ),
        P(None, SEQ),
        P(SEQ),
        P(None, SEQ),
        P(None, SEQ),
        P(None, SEQ),
    )
    device_fn = fast_device if mesh.shape[SEQ] == HEADS and mesh.shape[BATCH] == 4 else on_device
    return jax.shard_map(
        device_fn, mesh=mesh, in_specs=in_specs, out_specs=out_specs, check_vma=False
    )
```

```python
import types
import typing

import jax
import jax.numpy as jnp
from jax import lax
from jax.experimental import pallas as pl
from jax.experimental.pallas import tpu as pltpu
from jax.sharding import PartitionSpec as P

BATCH, SEQ = "batch", "seq"
HEADS = 8
HEAD = 40
GROUPS = 32


epsilon = 1e-05
layout = ("NHWC", "HWIO", "NHWC")


def extended(block, sides, width):
    for axis, dim in sides:
        count = lax.axis_size(axis)
        forward = [(i, i + 1) for i in range(count - 1)]
        backward = [(target, source) for source, target in forward]
        low = lax.ppermute(
            lax.slice_in_dim(block, block.shape[dim] - width, None, axis=dim), axis, forward
        )
        high = lax.ppermute(lax.slice_in_dim(block, 0, width, axis=dim), axis, backward)
        block = jnp.concatenate([low, block, high], axis=dim)
    return block


def layer_norm(values, norm_gain):
    centred = values - jnp.mean(values, axis=-1, keepdims=True)
    spread = jnp.mean(centred * centred, axis=-1, keepdims=True)
    return centred * lax.rsqrt(spread + epsilon) * norm_gain


def geglu(joined):
    half_width = joined.shape[-1] // 2
    return joined[:, :half_width] * jax.nn.gelu(joined[:, half_width:], approximate=False)


def back_dot(left_side, weight):
    return lax.dot_general(
        left_side, weight, (((1,), (1,)), ((), ())), preferred_element_type=jnp.float32
    )


def grad_dot(left_side, right_side):
    return lax.dot_general(
        left_side, right_side, (((0,), (0,)), ((), ())), preferred_element_type=jnp.float32
    )


def exact_grad_dot(left_side, right_side):
    return lax.dot_general(
        left_side,
        right_side,
        (((0,), (0,)), ((), ())),
        precision=lax.Precision.HIGHEST,
        preferred_element_type=jnp.float32,
    )


def conv_rows(padded, weight):
    return lax.conv_general_dilated(
        padded,
        weight,
        (1, 1),
        ((0, 0), (1, 1)),
        dimension_numbers=layout,
        preferred_element_type=jnp.float32,
    )


def conv_weight_grad(padded, grad_output):
    row_count = grad_output.shape[1]
    col_count = grad_output.shape[2]
    padded_cols = jnp.pad(padded, ((0, 0), (0, 0), (1, 1), (0, 0)))
    flat_grad = grad_output.reshape(-1, grad_output.shape[3])
    tap_rows = []
    for shift_row in range(3):
        tap_line = []
        for shift_col in range(3):
            patch_rows = padded_cols[
                :, shift_row : shift_row + row_count, shift_col : shift_col + col_count
            ].reshape(-1, padded.shape[3])
            tap_line.append(grad_dot(patch_rows, flat_grad))
        tap_rows.append(jnp.stack(tap_line))
    return jnp.stack(tap_rows)


def flipped(weight):
    return jnp.swapaxes(weight[::-1, ::-1], 2, 3)


def group_sums(values, row_mask):
    full_shape = values.shape
    grouped = values.reshape(
        full_shape[0], full_shape[1], full_shape[2], GROUPS, full_shape[3] // GROUPS
    )
    masked = grouped * row_mask[:, :, None, None, None]
    return (jnp.sum(masked, axis=(1, 2, 4)), jnp.sum(masked * grouped, axis=(1, 2, 4)))


def group_apply(values, norm_gain, sum_first, sum_second, cell_counts):
    full_shape = values.shape
    grouped = values.reshape(
        full_shape[0], full_shape[1], full_shape[2], GROUPS, full_shape[3] // GROUPS
    )
    group_mean = sum_first / cell_counts[:, None]
    spread = sum_second / cell_counts[:, None] - group_mean * group_mean
    inverse = lax.rsqrt(spread + epsilon)
    normed = (grouped - group_mean[:, None, None, :, None]) * inverse[:, None, None, :, None]
    return normed.reshape(full_shape) * norm_gain


def norm_stats(values, row_mask, spread_fn, pick_fn):
    sum_first, sum_second = group_sums(values, row_mask)
    total_first, total_second = lax.psum((spread_fn(sum_first), spread_fn(sum_second)), SEQ)
    return (pick_fn(total_first), pick_fn(total_second))


def norm_back(grad_first, grad_second, spread_fn, pick_fn):
    total_first, total_second = lax.psum((spread_fn(grad_first), spread_fn(grad_second)), SEQ)
    return (pick_fn(total_first), pick_fn(total_second))


def rows_halo(values):
    return extended(values, ((SEQ, 1),), 1)


def grads_halo(values):
    return extended(values, ((SEQ, 1),), 1)


def norm_backward(
    piece_fn, values, norm_gain, sum_first, sum_second, grad_output, row_mask, spread_fn, pick_fn
):
    unused, pull_piece = jax.vjp(piece_fn, values, norm_gain, sum_first, sum_second)
    grad_values, grad_gain, grad_first, grad_second = pull_piece(grad_output)
    total_first, total_second = norm_back(grad_first, grad_second, spread_fn, pick_fn)
    unused, pull_sums = jax.vjp(lambda inner_vals: group_sums(inner_vals, row_mask), values)
    extra_part = pull_sums((total_first, total_second))[0]
    return (grad_values + extra_part, grad_gain)


def masked_scores(queries, keys_all, key_mask, score_scale):
    row_count = queries.shape[0]
    key_count = keys_all.shape[0]
    raw_scores = (
        jnp.einsum(
            "qhd,khd->hqk",
            queries.reshape(row_count, HEADS, HEAD),
            keys_all.reshape(key_count, HEADS, HEAD),
            preferred_element_type=jnp.float32,
        )
        * score_scale
    )
    return jnp.where(key_mask[None, None, :] > 0, raw_scores, -1e30)


def self_forward(bundle, score_scale):
    queries, keys_all, values_all, key_mask = bundle
    row_count = queries.shape[0]
    scores = masked_scores(queries, keys_all, key_mask, score_scale)
    log_total = jax.nn.logsumexp(scores, axis=-1)
    attention = jnp.exp(scores - log_total[:, :, None]).astype(jnp.bfloat16)
    attn_mixed = jnp.einsum(
        "hqk,khd->qhd",
        attention,
        values_all.reshape(keys_all.shape[0], HEADS, HEAD),
        preferred_element_type=jnp.float32,
    )
    return (attn_mixed.astype(jnp.bfloat16).reshape(row_count, -1), log_total)


def query_side(bundle, score_scale):
    queries, grad_mixed, log_total, keys_all, values_all, key_mask = bundle
    row_count = queries.shape[0]
    key_count = keys_all.shape[0]
    scores = masked_scores(queries, keys_all, key_mask, score_scale)
    attention = jnp.exp(scores - log_total[:, :, None])
    grad_attn = jnp.einsum(
        "qhd,khd->hqk",
        grad_mixed.reshape(row_count, HEADS, HEAD),
        values_all.reshape(key_count, HEADS, HEAD),
        preferred_element_type=jnp.float32,
    )
    row_delta = jnp.sum(attention * grad_attn, axis=-1)
    grad_scores = (attention * (grad_attn - row_delta[:, :, None])).astype(jnp.bfloat16)
    grad_queries = (
        jnp.einsum(
            "hqk,khd->qhd",
            grad_scores,
            keys_all.reshape(key_count, HEADS, HEAD),
            preferred_element_type=jnp.float32,
        )
        * score_scale
    )
    return (
        grad_queries.astype(jnp.bfloat16).reshape(row_count, -1),
        attention.astype(jnp.bfloat16),
        grad_scores,
    )


LANES = 128
MESH = pl.DeviceIdType.MESH
LOW = jnp.bfloat16
F32 = jnp.float32
TILE = 64


def dot_nn(left, right):
    return jnp.dot(left, right, preferred_element_type=F32)


def dot_nt(left, right):
    return lax.dot_general(left, right, (((1,), (1,)), ((), ())), preferred_element_type=F32)


def dot_tn(left, right):
    return lax.dot_general(left, right, (((0,), (0,)), ((), ())), preferred_element_type=F32)


def iota(shape, dim):
    return lax.broadcasted_iota(jnp.int32, shape, dim)


def floor_div(values, by):
    return jnp.floor((values.astype(F32) + 0.5) * (1.0 / by)).astype(jnp.int32)


def split_three(values):
    high = values.astype(LOW).astype(F32)
    rest = values - high
    middle = rest.astype(LOW).astype(F32)
    return jnp.concatenate([high, middle, rest - middle], axis=0).astype(LOW)


def sum_three(values):
    rows = values.shape[0] // 3
    return values[:rows] + values[rows : 2 * rows] + values[2 * rows :]


def row_of(ref):
    return ref[...].reshape(1, -1)


def sigmoid(values):
    return 1.0 / (1.0 + jnp.exp(-values))


def col_sum(values):
    return jnp.sum(values, axis=0, keepdims=True)


ROUNDS = 6
SEMAPHORES = 256


class Packs(typing.NamedTuple):
    up: typing.Any
    down: typing.Any
    trio: typing.Any
    pair: typing.Any
    heads: typing.Any
    second: typing.Any


class Sizes:
    def __init__(self, mesh_batch, mesh_seq, latents, time_vector, text_states, feed_down):
        self.batches = mesh_batch
        self.seqs = mesh_seq
        self.rows = latents.shape[1]
        self.width = latents.shape[2]
        self.channels = latents.shape[3]
        self.tokens = self.rows * self.width
        self.wide = self.tokens + 2 * self.width
        self.keys = self.tokens * mesh_seq
        self.emb = time_vector.shape[1]
        self.text = text_states.shape[1]
        self.text_pad = -(-self.text // 16) * 16
        self.context = text_states.shape[2]
        self.hidden = feed_down.shape[0]
        self.slot = 48
        self.packed = HEADS * LANES
        self.down_rows = 512
        self.conv_rows = 3 * LANES
        channels = self.channels
        sizes = Packs(
            up=3 * channels,
            down=self.down_rows,
            trio=channels,
            pair=HEADS * self.slot,
            heads=-(-channels // LANES) * LANES,
            second=3 * channels,
        )
        starts = [sum(sizes[:place]) for place in range(len(sizes))]
        self.start = Packs(*starts)
        self.pack_rows = sum(sizes)
        self.sizes = sizes
        self.chunks = [
            (0, sizes.up),
            (self.start.down, sizes.down + sizes.trio),
            (self.start.pair, sizes.pair + sizes.heads),
            (self.start.second, sizes.second),
        ]


class Inputs(typing.NamedTuple):
    latents: typing.Any
    heights: typing.Any
    time_vector: typing.Any
    text_states: typing.Any
    gain_in: typing.Any
    conv_first: typing.Any
    time_weight: typing.Any
    gain_mid: typing.Any
    conv_second: typing.Any
    gain_block: typing.Any
    project_in: typing.Any
    gain_self: typing.Any
    query_self: typing.Any
    key_self: typing.Any
    value_self: typing.Any
    out_self: typing.Any
    gain_cross: typing.Any
    query_cross: typing.Any
    key_cross: typing.Any
    value_cross: typing.Any
    out_cross: typing.Any
    gain_feed: typing.Any
    feed_up: typing.Any
    feed_down: typing.Any
    project_out: typing.Any
    cotangent: typing.Any


class Fetched(typing.NamedTuple):
    query_self: typing.Any
    key_self: typing.Any
    value_self: typing.Any
    time_weight: typing.Any
    conv_first: typing.Any
    conv_second: typing.Any
    project_in: typing.Any
    key_cross: typing.Any
    value_cross: typing.Any
    out_self: typing.Any
    query_cross: typing.Any
    out_cross: typing.Any
    feed_up: typing.Any
    feed_down: typing.Any
    project_out: typing.Any


def buffers(sz):
    c, t, w, k = sz.channels, sz.tokens, sz.wide, sz.keys
    half = sz.seqs // 2
    return dict(
        lat6=((w, c), F32),
        cot6=((w, c), F32),
        mid6=((w, c), F32),
        res6=((w, c), F32),
        gblk6=((w, c), F32),
        gact6=((w, c), F32),
        slope_mid=((w, c), F32),
        normed_mid=((w, c), F32),
        shifted=((3, w, c), LOW),
        shift_grad=((3, w, c), LOW),
        act_in=((k + 2 * sz.width, c), LOW),
        widen=((HEADS * sz.slot, c), LOW),
        first_send=((HEADS * sz.slot, t), LOW),
        first_grads=((sz.slot, k), LOW),
        first_part=((sz.conv_rows, c), LOW),
        first_recv=((3, sz.batches - 1, LANES // sz.batches, c), LOW),
        conv_stack=((LANES, k), LOW),
        stat_send=((ROUNDS, 8, LANES), F32),
        extra_send=((8, c), F32),
        extra_recv=((sz.seqs, 8, c), F32),
        stat_recv=((ROUNDS, sz.seqs, 8, LANES), F32),
        norms=((3, 8, c), F32),
        gain_parts=((8, c), F32),
        final_send=((8, c), F32),
        group=((c, c), LOW),
        place=((3, c, sz.packed), LOW),
        wqkv=((c, sz.packed), LOW),
        osp=((HEADS * sz.slot, c), LOW),
        time_send=((8, sz.emb), F32),
        normed_block=((t, c), LOW),
        stream_in=((t, c), F32),
        normed_self=((t, c), LOW),
        qkv_send=((t, sz.packed), LOW),
        qkv=((k, LANES), LOW),
        qh=((k, LANES), LOW),
        kh=((k, LANES), LOW),
        vh=((k, sz.slot), LOW),
        vt=((sz.slot, k), LOW),
        kt=((sz.slot, k), LOW),
        scores=((max(k, 2 * sz.hidden), t), F32),
        scores_odd=((k, t), F32),
        tops=((2, 8, t), F32),
        probs=((2, k, t), LOW),
        mixed_full=((sz.seqs, sz.slot, t), F32),
        inverse=((sz.seqs, 8, t), F32),
        mixed_send=((sz.seqs, sz.slot, t), LOW),
        mixed=((HEADS * sz.slot, t), LOW),
        stream=((t, c), F32),
        hat_self=((t, c), F32),
        scale_self=((t, LANES), F32),
        hat_cross=((t, c), F32),
        scale_cross=((t, LANES), F32),
        hat_feed=((t, c), F32),
        normed_cross=((t, c), LOW),
        query_text=((t, c), LOW),
        text_rows=((2, sz.text_pad, c), F32),
        text_key=((HEADS * sz.text_pad, c), LOW),
        text_value=((HEADS * sz.text_pad, c), LOW),
        cross=((HEADS * sz.text_pad, t), F32),
        cross_low=((HEADS * sz.text_pad, t), LOW),
        cross_scores=((HEADS * sz.text_pad, t), LOW),
        cross_mixed=((t, c), LOW),
        scale_feed=((t, LANES), F32),
        normed_feed=((t, c), LOW),
        gated=((t, sz.hidden), LOW),
        grad_gated=((t, 2 * LANES), F32),
        grad_joined=((t, 2 * sz.hidden), LOW),
        stream_low=((t, c), LOW),
        grad_branch=((t, c), LOW),
        grad=((t, c), F32),
        tmp=((t, c), F32),
        grad_feed_low=((t, c), LOW),
        grad_cross_low=((t, c), LOW),
        grad_cross_mixed=((t, c), LOW),
        grad_query_text=((t, c), LOW),
        grad_self_low=((t, c), LOW),
        grad_in_low=((t, c), LOW),
        text_send=((sz.text_pad, sz.packed), LOW),
        text_recv=((sz.seqs, sz.text_pad, LANES), LOW),
        gm_send=((HEADS * sz.slot, t), LOW),
        gm=((sz.seqs, sz.slot, t), LOW),
        query_rows=((HEADS * sz.slot, c), LOW),
        value_rows=((HEADS * 2 * HEAD, c), LOW),
        dq_send=((sz.seqs, sz.slot, t), LOW),
        dq=((HEADS * sz.slot, t), LOW),
        dkv_send=((HEADS * 2 * HEAD, t), LOW),
        dkv=((HEADS * 2 * HEAD, t), LOW),
        pack=((2, half, sz.start.second, LANES), LOW),
        near_shifted=((3, w, c), LOW),
        output_own=((t, c), F32),
        latent_own=((t, c), F32),
        text_own=((sz.text_pad, sz.context), LOW),
        text_sum=((sz.text_pad, LANES), F32),
        sum_own=((sz.pack_rows // sz.batches, LANES), LOW),
        first_own=((3, LANES // sz.batches, c), LOW),
        near_grads=((t, c), LOW),
        place_half=((3, c, half * LANES), LOW),
        recv_core=((half, sz.pack_rows, LANES), LOW),
        recv_first=((2, half // 2, sz.pack_rows // 2, LANES), LOW),
        recv_second=((half, sz.pack_rows // sz.batches, LANES), LOW),
        recv_z=((half - 1, sz.pack_rows // sz.batches, LANES), LOW),
    )


class Halo:
    def __init__(self, seq, last, after, before):
        self.seq, self.last, self.after, self.before = seq, last, after, before

    def start(self):
        @pl.when(self.seq < self.last)
        def _():
            self.after.start()

        @pl.when(self.seq > 0)
        def _():
            self.before.start()

    def wait(self):
        @pl.when(self.seq < self.last)
        def _():
            self.after.wait_send()
            self.before.wait_recv()

        @pl.when(self.seq > 0)
        def _():
            self.before.wait_send()
            self.after.wait_recv()


class Fused:
    def __init__(self, sz, refs, local):
        self.sz = sz
        self.r = refs
        self.v = local
        self.used = 0
        self.puts = []
        self.batch = lax.axis_index(BATCH)
        self.seq = lax.axis_index(SEQ)
        self.z_pos = self.seq // 2
        self.core = lax.rem(self.seq, 2)
        self.batch_x = lax.rem(self.batch, 2)
        self.batch_y = self.batch // 2
        self.x_peer = (self.batch + 1 - 2 * self.batch_x, self.seq)
        self.y_peer = (self.batch + 2 - 4 * self.batch_y, self.seq)
        self.partner = (self.batch, self.seq + 1 - 2 * self.core)
        far = sorted(range(1, sz.seqs), key=lambda step: -min(step, sz.seqs - step))
        self.seq_others = [lax.rem(self.seq + step, sz.seqs) for step in far]
        self.batch_others = [lax.rem(self.batch + step, sz.batches) for step in range(1, sz.batches)]
        half = sz.seqs // 2
        self.z_others = [lax.rem(self.z_pos + step, half) for step in range(1, half)]
        self.height = refs.heights[0]
        self.scale = HEAD ** (-0.5)

    def remote(self, source, target, device, index=None):
        if index is None:
            index = self.used
            self.used += 1
        return pltpu.make_async_remote_copy(
            src_ref=source,
            dst_ref=target,
            send_sem=self.r.sems.at[0, index],
            recv_sem=self.r.sems.at[1, index],
            device_id=device,
            device_id_type=MESH,
        )

    def to_seq(self, source, target):
        return [self.remote(source(other), target, (self.batch, other)) for other in self.seq_others]

    def to_batch(self, source, target):
        return [self.remote(source, target, (other, self.seq)) for other in self.batch_others]

    def put(self, source, target):
        index = len(Fetched._fields) + 4 + len(self.puts)
        self.puts.append(pltpu.make_async_copy(source, target, self.r.local_sems.at[index]))
        self.puts[-1].start()

    def start(self, copies):
        for one in copies:
            one.start()

    def wait(self, copies):
        for one in copies:
            one.wait()

    def entry(self):
        r = self.r
        barrier = pltpu.get_barrier_semaphore()
        for other in self.seq_others:
            pl.semaphore_signal(barrier, inc=1, device_id=(self.batch, other), device_id_type=MESH)
        for other in self.batch_others:
            pl.semaphore_signal(barrier, inc=1, device_id=(other, self.seq), device_id_type=MESH)
        self.local = {}
        self.named = {id(getattr(r, name)): name for name in Fetched._fields}
        for number, name in enumerate(Fetched._fields):
            self.local[name] = pltpu.make_async_copy(
                getattr(r, name), getattr(self.v, name), r.local_sems.at[number]
            )
            self.local[name].start()
        own = pl.ds(self.sz.width, self.sz.tokens)
        self.images = [
            pltpu.make_async_copy(source, target.at[own], r.local_sems.at[len(Fetched._fields) + place])
            for place, (source, target) in enumerate(((r.latents, r.lat6), (r.cotangent, r.cot6)))
        ]
        self.start(self.images)

    def joined(self):
        barrier = pltpu.get_barrier_semaphore()
        pl.semaphore_wait(barrier, self.sz.seqs - 1 + self.sz.batches - 1)

    def weight(self, ref):
        name = self.named[id(ref)]
        if name in self.local:
            self.local.pop(name).wait()
        return getattr(self.v, name)

    def far_first(self, step):
        half = self.sz.seqs // 2
        offset = half + ((step + 1) // 2) * (1 - 2 * (step % 2))
        return lax.rem(self.seq + offset, self.sz.seqs)

    def wide_row(self, start, size):
        rows = floor_div(iota((size, 1), 0) + start, self.sz.width) - 1
        return rows + self.seq * self.sz.rows

    def wide_mask(self, start, size):
        rows = self.wide_row(start, size)
        return jnp.where((rows >= 0) & (rows < self.height), 1.0, 0.0)

    def inside_mask(self, start, size):
        rows = self.wide_row(start, size)
        return jnp.where((rows >= 0) & (rows < self.sz.rows * self.sz.seqs), 1.0, 0.0)

    def chunks(self, total):
        return [(start, TILE) for start in range(0, total, TILE)]

    def halo(self, ref):
        sz, width = self.sz, self.sz.width
        after = self.remote(
            ref.at[pl.ds(sz.tokens, width)],
            ref.at[pl.ds(0, width)],
            (self.batch, jnp.minimum(self.seq + 1, sz.seqs - 1)),
        )
        before = self.remote(
            ref.at[pl.ds(width, width)],
            ref.at[pl.ds(width + sz.tokens, width)],
            (self.batch, jnp.maximum(self.seq - 1, 0)),
        )
        return Halo(self.seq, sz.seqs - 1, after, before)

    def lane_tiles(self):
        channels = self.sz.channels
        return [(start, min(LANES, channels - start)) for start in range(0, channels, LANES)]

    def stats_store(self, number, rows):
        r = self.r
        r.stat_send[number] = jnp.zeros(r.stat_send.shape[1:], F32)
        tiles = self.lane_tiles()
        for which, row in enumerate(rows):
            for place, (start, size) in enumerate(tiles):
                at = which * len(tiles) + place
                r.stat_send[number, at : at + 1, 0:size] = row[:, start : start + size]
        r.stat_recv[number, self.seq] = r.stat_send[number]

    def stats_start(self, number):
        r = self.r
        copies = self.to_seq(lambda other: r.stat_send.at[number], r.stat_recv.at[number, self.seq])
        self.start(copies)
        return copies

    def stats_total(self, number):
        r = self.r
        total = r.stat_recv[number, 0]
        for place in range(1, self.sz.seqs):
            total = total + r.stat_recv[number, place]
        tiles = self.lane_tiles()
        rows = []
        for which in range(2):
            parts = [
                total[which * len(tiles) + place : which * len(tiles) + place + 1, 0:size]
                for place, (start, size) in enumerate(tiles)
            ]
            rows.append(jnp.concatenate(parts, axis=1))
        row = iota((8, 1), 0)
        return jnp.where(row == 0, rows[0], jnp.where(row == 1, rows[1], 0.0))

    def grouped(self, rows):
        return sum_three(dot_nn(split_three(rows), self.r.group[...]))

    def count(self):
        per_row = self.sz.width * (self.sz.channels // GROUPS)
        return (self.height * per_row).astype(F32)

    def set_norm(self, number, total):
        sums = self.grouped(total) / self.count()
        mean = sums[0:1]
        spread = sums[1:2] - mean * mean
        self.r.norms[number, 0:1] = mean
        self.r.norms[number, 1:2] = lax.rsqrt(spread + epsilon)

    def norm(self, number):
        return self.r.norms[number, 0:1], self.r.norms[number, 1:2]

    def value_sums(self, ref):
        r, sz = self.r, self.sz
        first = second = None
        for start, size in self.chunks(sz.tokens):
            start += sz.width
            values = ref[start : start + size]
            masked = values * self.wide_mask(start, size)
            one, two = col_sum(masked), col_sum(masked * values)
            first = one if first is None else first + one
            second = two if second is None else second + two
        return first, second

    def shifts(self, ref, start, size, values):
        column = lax.rem(iota((size, 1), 0), self.sz.width)
        ref[1, start : start + size] = values.astype(LOW)
        left = jnp.where(column == 0, 0.0, pltpu.roll(values, 1, 0))
        ref[0, start : start + size] = left.astype(LOW)
        right = jnp.where(column == self.sz.width - 1, 0.0, pltpu.roll(values, size - 1, 0))
        ref[2, start : start + size] = right.astype(LOW)

    def activate(self, source, number, gain, target, kept):
        mean, inverse = self.norm(number)
        factor = inverse * row_of(gain)
        for start, size in self.chunks(self.sz.wide):
            normed = (source[start : start + size] - mean) * factor
            values = normed * sigmoid(normed) * self.wide_mask(start, size)
            self.shifts(target, start, size, values)
        if kept is None:
            return
        width, tokens = self.sz.width, self.sz.tokens
        kept[self.own_rows()] = target[1, width : width + tokens]
        zeros = jnp.zeros((width, self.sz.channels), LOW)
        kept[0:width] = zeros
        kept[self.sz.keys + width :] = zeros

    def own_rows(self, seq=None):
        seq = self.seq if seq is None else seq
        width, tokens = self.sz.width, self.sz.tokens
        return pl.ds(pl.multiple_of(seq * tokens + width, width), tokens)

    def gather_rows(self, kept, first, last):
        width, tokens = self.sz.width, self.sz.tokens
        start = self.seq * tokens + (first + 1) * width
        rows = pl.ds(pl.multiple_of(start, width), (last - first) * width)
        copies = [
            self.remote(kept.at[rows], kept.at[rows], (self.batch, other * 2 + self.core))
            for other in self.z_others
        ]
        self.start(copies)
        return copies

    def gather_forward(self, kept, copies):
        rows = self.own_rows()
        more = [self.remote(kept.at[rows], kept.at[rows], self.partner)]
        self.start(more)
        self.wait(copies)
        half = self.sz.seqs // 2
        for step in range(1, half):
            rows = self.own_rows(lax.rem(self.z_pos + half - step, half) * 2 + self.core)
            more.append(self.remote(kept.at[rows], kept.at[rows], self.partner))
        self.start(more[1:])
        return more

    def conv_send(self, grads, send, target):
        sz, slot = self.sz, self.sz.slot
        send[...] = dot_nt(self.r.widen[...], grads[1, sz.width : sz.width + sz.tokens]).astype(LOW)
        lanes = pl.ds(pl.multiple_of(self.seq * sz.tokens, sz.tokens), sz.tokens)
        copies = [
            self.remote(
                send.at[pl.ds(pl.multiple_of(other * slot, 16), slot)],
                target.at[:, lanes],
                (self.batch, other),
            )
            for other in self.seq_others
        ]
        self.start(copies)
        target[:, lanes] = send[pl.ds(pl.multiple_of(self.seq * slot, 16), slot)]
        return copies

    def conv_grads(self, copies, gathered, grads, kept, part, received):
        r, sz = self.r, self.sz
        keys, width = sz.keys, sz.width
        self.wait(copies)
        self.wait(gathered)
        values = grads[0:HEAD].astype(F32)
        column = lax.rem(iota((1, keys), 1), width)
        left = jnp.where(column == width - 1, 0.0, pltpu.roll(values, keys - 1, 1))
        right = jnp.where(column == 0, 0.0, pltpu.roll(values, 1, 1))
        rest = jnp.zeros((LANES - 3 * HEAD, keys), F32)
        r.conv_stack[...] = jnp.concatenate([left, values, right, rest], axis=0).astype(LOW)
        size = LANES // sz.batches
        pieces = []
        for row in range(3):
            part[row * LANES : (row + 1) * LANES] = dot_nn(
                r.conv_stack[...], kept[row * width : row * width + keys]
            ).astype(LOW)
            copies = []
            for step, other in enumerate(self.batch_others):
                rows = pl.ds(pl.multiple_of(row * LANES + other * size, 16), size)
                copies.append(self.remote(part.at[rows], received.at[row, step], (other, self.seq)))
            self.start(copies)
            pieces.append(copies)
        return pieces

    def conv_gather(self, pieces, part, received, out):
        size = LANES // self.sz.batches
        sent = []
        for row, copies in enumerate(pieces):
            own = pl.ds(pl.multiple_of(row * LANES + self.batch * size, 16), size)
            self.wait(copies)
            total = part[own].astype(F32)
            for step in range(self.sz.batches - 1):
                total = total + received[row, step].astype(F32)
            self.r.first_own[row] = total.astype(LOW)
            self.put(self.r.first_own.at[row], out.at[own])
            copies = self.to_batch(self.r.first_own.at[row], out.at[own])
            self.start(copies)
            sent += copies
        return sent

    def conv(self, ref, weight):
        sz = self.sz
        total = None
        for row in range(3):
            for col in range(3):
                part = dot_nn(ref[col, row * sz.width : row * sz.width + sz.tokens], weight[row, col])
                total = part if total is None else total + part
        return total

    def conv_back(self, ref, weight):
        sz = self.sz
        total = None
        for row in range(3):
            for col in range(3):
                part = dot_nt(
                    ref[col, row * sz.width : row * sz.width + sz.tokens], weight[2 - row, 2 - col]
                )
                total = part if total is None else total + part
        return total

    def constants(self):
        r, sz = self.r, self.sz
        channels = sz.channels
        size = channels // GROUPS
        r.group[...] = jnp.where(
            floor_div(iota((channels, 1), 0), size) == floor_div(iota((1, channels), 1), size), 1.0, 0.0
        ).astype(LOW)
        source = iota((1, channels), 1)
        source = source + (sz.slot - HEAD) * floor_div(source, HEAD)
        r.widen[...] = jnp.where(iota((HEADS * sz.slot, 1), 0) == source, 1.0, 0.0).astype(LOW)
        rows = iota((channels, 1), 0)
        target = rows + (LANES - HEAD) * floor_div(rows, HEAD)
        lanes = iota((1, sz.packed), 1)
        for number in range(3):
            r.place[number] = jnp.where(lanes == target + number * HEAD, 1.0, 0.0).astype(LOW)
        head = floor_div(rows, HEAD)
        pair = floor_div(head, 2)
        target = jnp.where(head - 2 * pair == self.core, rows - head * HEAD + pair * LANES, -LANES)
        lanes = iota((1, r.place_half.shape[2]), 1)
        for number in range(3):
            r.place_half[number] = jnp.where(lanes == target + number * HEAD, 1.0, 0.0).astype(LOW)

    def residual(self):
        r, sz = self.r, self.sz
        width, tokens = sz.width, sz.tokens
        self.constants()
        self.wait(self.images)
        for ref in (r.lat6, r.cot6, r.mid6, r.res6, r.gblk6, r.gact6):

            @pl.when(self.seq == 0)
            def _():
                ref[0:width] = jnp.zeros((width, sz.channels), F32)

            @pl.when(self.seq == sz.seqs - 1)
            def _():
                ref[width + tokens :] = jnp.zeros((width, sz.channels), F32)

        self.stats_store(0, self.value_sums(r.lat6))
        self.joined()
        halo = self.halo(r.lat6)
        halo.start()
        stats = self.stats_start(0)
        late = [self.halo(r.cot6)]
        act = r.time_vector[...].astype(F32)
        act = (act * sigmoid(act)).astype(LOW)
        r.time_send[...] = jnp.zeros(r.time_send.shape, F32)
        r.time_send[0:1] = act.astype(F32)
        self.put(r.time_send, r.time_all.at[self.batch])
        late += self.to_batch(r.time_send, r.time_all.at[self.batch])
        r.text_own[...] = jnp.zeros(r.text_own.shape, LOW)
        r.text_own[0 : sz.text] = r.text_states[...]
        self.put(r.text_own, r.text_all.at[self.batch])
        late += self.to_batch(r.text_own, r.text_all.at[self.batch])
        self.start(late)
        self.late = late
        time_weight = self.weight(self.r.time_weight)
        time_term = dot_nt(jnp.broadcast_to(act, (16, sz.emb)), time_weight[...])[0:1]
        wqkv = None
        for number, name in enumerate((r.query_self, r.key_self, r.value_self)):
            part = dot_nn(self.weight(name)[...], r.place[number])
            wqkv = part if wqkv is None else wqkv + part
        r.wqkv[...] = wqkv.astype(LOW)
        halo.wait()
        self.wait(stats)
        self.set_norm(0, self.stats_total(0))
        self.activate(r.lat6, 0, r.gain_in, r.shifted, r.act_in)
        r.mid6[width : width + tokens] = self.conv(r.shifted, self.weight(self.r.conv_first)) + time_term
        halo = self.halo(r.mid6)
        halo.start()
        self.stats_store(1, self.value_sums(r.mid6))
        stats = self.stats_start(1)
        self.weight(self.r.conv_second)
        halo.wait()
        self.wait(stats)
        self.set_norm(1, self.stats_total(1))
        self.activate(r.mid6, 1, r.gain_mid, r.shifted, None)
        r.res6[width : width + tokens] = r.lat6[width : width + tokens] + self.conv(
            r.shifted, self.v.conv_second
        )
        halo = self.halo(r.res6)
        self.stats_store(2, self.value_sums(r.res6))
        stats = self.stats_start(2)
        halo.start()
        self.late.append(halo)
        near = self.remote(r.shifted, r.near_shifted, self.partner)
        near.start()
        self.late.append(near)
        project_in = self.weight(self.r.project_in)
        self.wait(stats)
        self.set_norm(2, self.stats_total(2))
        mean, inverse = self.norm(2)
        factor = inverse * row_of(r.gain_block)
        for start, size in self.chunks(tokens):
            values = r.res6[width + start : width + start + size]
            r.normed_block[start : start + size] = ((values - mean) * factor).astype(LOW)
        r.stream_in[...] = dot_nn(r.normed_block[...], project_in[...])
        for start, size in self.chunks(tokens):
            rows = slice(start, start + size)
            self.layer_norm(r.stream_in[rows], r.gain_self, rows, r.normed_self, r.hat_self, r.scale_self)
        r.qkv_send[...] = dot_nn(r.normed_self[...], r.wqkv[...]).astype(LOW)
        rows = pl.ds(pl.multiple_of(self.seq * tokens, tokens), tokens)
        copies = [
            self.remote(
                r.qkv_send.at[:, pl.ds(pl.multiple_of(other * LANES, LANES), LANES)],
                r.qkv.at[rows],
                (self.batch, other),
            )
            for other in self.seq_others
        ]
        self.start(copies)
        r.qkv[rows] = r.qkv_send[:, pl.ds(pl.multiple_of(self.seq * LANES, LANES), LANES)]
        self.text_start()
        self.wait(copies)

    def layer_parts(self, values):
        centred = values - jnp.mean(values, axis=-1, keepdims=True)
        spread = jnp.mean(centred * centred, axis=-1, keepdims=True)
        return centred, lax.rsqrt(spread + epsilon)

    def layer_norm(self, values, gain, rows, target, hat, kept_scale):
        centred, scale = self.layer_parts(values)
        normed = centred * scale
        hat[rows] = normed
        kept_scale[rows] = jnp.broadcast_to(scale, (values.shape[0], LANES))
        target[rows] = (normed * row_of(gain)).astype(LOW)

    def layer_back(self, normed, scale, grad, gain):
        scaled = grad * gain
        first = jnp.mean(scaled, axis=-1, keepdims=True)
        second = jnp.mean(scaled * normed, axis=-1, keepdims=True)
        return scale * (scaled - first - normed * second), col_sum(grad * normed)

    def text_start(self):
        r, sz = self.r, self.sz
        r.text_rows[...] = jnp.zeros(r.text_rows.shape, F32)
        for number, (name, target) in enumerate(
            ((r.key_cross, r.text_key), (r.value_cross, r.text_value))
        ):
            r.text_rows[number, 0 : sz.text] = dot_nt(r.text_states[...], self.weight(name)[...])
            rows = r.text_rows[number]
            head = floor_div(iota((1, sz.channels), 1), HEAD)
            for one in range(HEADS):
                target[one * sz.text_pad : (one + 1) * sz.text_pad] = jnp.where(
                    head == one, rows, 0.0
                ).astype(LOW)
        r.query_rows[...] = dot_nt(r.widen[...], self.v.query_self[...]).astype(LOW)
        rows = iota((HEADS * 2 * HEAD, 1), 0)
        source = iota((1, sz.channels), 1)
        source = source + HEAD * floor_div(source, HEAD)
        r.value_rows[...] = (
            dot_nt(jnp.where(rows == source, 1.0, 0.0).astype(LOW), self.v.key_self[...])
            + dot_nt(jnp.where(rows == source + HEAD, 1.0, 0.0).astype(LOW), self.v.value_self[...])
        ).astype(LOW)
        r.osp[...] = dot_nn(r.widen[...], self.weight(self.r.out_self)[...]).astype(LOW)

    def attention(self):
        r, sz = self.r, self.sz
        keys, tokens, slot = sz.keys, sz.tokens, sz.slot
        self.in_pieces = self.gather_rows(r.act_in, 0, 1)
        lane_in = iota((LANES, LANES), 0)
        lane_out = iota((LANES, LANES), 1)

        def shift(by):
            return jnp.where((lane_in == lane_out + by) & (lane_out < HEAD), 1.0, 0.0).astype(LOW)

        def shift_wide(by):
            source = iota((LANES, slot), 0)
            target = iota((LANES, slot), 1)
            return jnp.where((source == target + by) & (target < HEAD), 1.0, 0.0).astype(LOW)

        def shift_rows(by):
            source = iota((slot, LANES), 1)
            target = iota((slot, LANES), 0)
            return jnp.where((source == target + by) & (target < HEAD), 1.0, 0.0).astype(LOW)

        query_out = jnp.where((lane_in + HEAD == lane_out) & (lane_in < HEAD), 1.0, 0.0).astype(LOW)
        lane = iota((1, LANES), 1)
        for start in range(0, keys, 2 * tokens):
            rows = slice(start, start + 2 * tokens)
            block = r.qkv[rows]
            valid = iota((2 * tokens, 1), 0) + start < self.height * sz.width
            r.qh[rows] = jnp.where(
                lane < HEAD, block.astype(F32), jnp.where(lane == HEAD, 1.0, 0.0)
            ).astype(LOW)
            bias = jnp.where((lane == HEAD) & jnp.logical_not(valid), -1e30, 0.0)
            r.kh[rows] = (dot_nn(block, shift(HEAD)) + bias).astype(LOW)
            ones = jnp.where((iota((1, slot), 1) >= HEAD) & (iota((1, slot), 1) < HEAD + 3), 1.0, 0.0)
            r.vh[rows] = (dot_nn(block, shift_wide(2 * HEAD)) + ones).astype(LOW)
            one_row = jnp.where(iota((slot, 1), 0) == HEAD, 1.0, 0.0)
            r.vt[:, rows] = (dot_nt(shift_rows(2 * HEAD), block) + one_row).astype(LOW)
            r.kt[:, rows] = dot_nt(shift_rows(HEAD), block).astype(LOW)
            r.qkv[rows] = dot_nn(block, query_out).astype(LOW)
        factor = self.scale * 1.4426950408889634
        base = self.used
        self.used += sz.seqs

        def send(target, step):
            return self.remote(
                r.mixed_send.at[target],
                r.mixed.at[pl.ds(pl.multiple_of(self.seq * slot, 16), slot)],
                (self.batch, target),
                base + step,
            )

        score_refs = (r.scores, r.scores_odd)

        def keep(step, parity):
            return pltpu.make_async_copy(
                r.probs.at[parity],
                r.kept_probs.at[self.far_first(step)],
                r.local_sems.at[len(Fetched._fields) + 2 + parity],
            )

        def own_scores(step, parity, start, top):
            target = self.far_first(step)
            queries = r.qh[pl.ds(pl.multiple_of(target * tokens, tokens), tokens)]
            scores = dot_nt(r.kh[start : start + tokens], queries)
            score_refs[parity][start : start + tokens] = scores
            part = jnp.max(scores.reshape(tokens // 8, 8, tokens), axis=0)
            top = part if top is None else jnp.maximum(top, part)
            if start + tokens == keys:
                r.tops[parity] = jnp.broadcast_to(jnp.max(top, axis=0, keepdims=True), (8, tokens))
            return top

        def finish(step, sums):
            target = self.far_first(step)
            inverse = 1.0 / sums[HEAD : HEAD + 1]
            mixed = jnp.where(iota((slot, 1), 0) < HEAD, sums * inverse, 0.0)
            r.mixed_full[target] = mixed
            r.mixed_send[target] = mixed.astype(LOW)
            r.inverse[target] = jnp.broadcast_to(inverse, (8, tokens))

        def half_step(step, parity, with_next, with_last, wait_kept):
            if wait_kept:
                keep(step - 2, parity).wait()
            offset = r.tops[parity, 0:1] * factor
            top = sums = None
            for start in range(0, keys, tokens):
                if with_next:
                    top = own_scores(step + 1, 1 - parity, start, top)
                for inner in range(start, start + tokens, LANES):
                    powers = jnp.exp2(score_refs[parity][inner : inner + LANES] * factor - offset)
                    r.probs[parity, inner : inner + LANES] = powers.astype(LOW)
                if with_last:
                    part = dot_nn(
                        r.vt[:, start : start + tokens], r.probs[1 - parity, start : start + tokens]
                    )
                    sums = part if sums is None else sums + part
            keep(step, parity).start()
            if with_last:
                finish(step - 1, sums)
                send(self.far_first(step - 1), step - 1).start()

        top = None
        for start in range(0, keys, tokens):
            top = own_scores(0, 0, start, top)
        half_step(0, 0, True, False, False)
        half_step(1, 1, True, True, False)

        def pair(number, carry):
            step = 2 + 2 * number
            half_step(step, 0, True, True, True)
            half_step(step + 1, 1, True, True, True)
            return carry

        lax.fori_loop(0, sz.seqs // 2 - 2, pair, 0)
        half_step(sz.seqs - 2, 0, True, True, True)
        half_step(sz.seqs - 1, 1, False, True, True)
        finish(sz.seqs - 1, dot_nn(r.vt[...], r.probs[1]))
        keep(sz.seqs - 2, 0).wait()
        keep(sz.seqs - 1, 1).wait()
        self.recall(0).start()
        r.mixed[pl.ds(pl.multiple_of(self.seq * slot, 16), slot)] = r.mixed_send[self.seq]
        for step in range(sz.seqs - 1):
            send(self.far_first(step), step).wait()

    def local_block(self):
        r, sz = self.r, self.sz
        tokens, channels = sz.tokens, sz.channels
        pad = sz.text_pad
        r.stream[...] = r.stream_in[...] + dot_tn(r.mixed[...], r.osp[...])
        for start, size in self.chunks(tokens):
            rows = slice(start, start + size)
            self.layer_norm(r.stream[rows], r.gain_cross, rows, r.normed_cross, r.hat_cross, r.scale_cross)
        r.query_text[...] = dot_nn(r.normed_cross[...], self.weight(self.r.query_cross)[...]).astype(LOW)
        r.cross[...] = dot_nt(r.text_key[...], r.query_text[...])
        for head in range(HEADS):
            rows = slice(head * pad, (head + 1) * pad)
            valid = iota((pad, 1), 0) < sz.text
            scores = jnp.where(valid, r.cross[rows] * self.scale, -1e30)
            powers = jnp.exp(scores - jnp.max(scores, axis=0, keepdims=True))
            attention = powers / jnp.sum(powers, axis=0, keepdims=True)
            r.cross[rows] = attention
            r.cross_low[rows] = attention.astype(LOW)
        r.cross_mixed[...] = dot_tn(r.cross_low[...], r.text_value[...]).astype(LOW)
        r.stream[...] = r.stream[...] + dot_nn(r.cross_mixed[...], self.weight(self.r.out_cross)[...])
        for start, size in self.chunks(tokens):
            rows = slice(start, start + size)
            self.layer_norm(r.stream[rows], r.gain_feed, rows, r.normed_feed, r.hat_feed, r.scale_feed)
        feed_up = self.weight(self.r.feed_up)
        joined = r.scores
        root = 0.7071067811865476
        block = 2 * LANES
        pieces = sz.hidden // block
        for piece in range(pieces):
            for place in (piece, piece + pieces):
                joined[place * tokens : (place + 1) * tokens] = dot_nn(
                    r.normed_feed[...], feed_up[:, place * block : (place + 1) * block]
                )
            for start, size in self.chunks(tokens):
                values = joined[piece * tokens + start : piece * tokens + start + size]
                gates_at = (piece + pieces) * tokens + start
                gates = joined[gates_at : gates_at + size]
                half = 0.5 * (1.0 + lax.erf(gates * root))
                slope = half + gates * (jnp.exp(-0.5 * gates * gates) * 0.3989422804014327)
                active = gates * half
                r.gated[start : start + size, piece * block : (piece + 1) * block] = (
                    values * active
                ).astype(LOW)
                joined[piece * tokens + start : piece * tokens + start + size] = active
                joined[gates_at : gates_at + size] = values * slope

        low = (
            r.stream[...] + dot_nt(r.gated[...], self.weight(self.r.feed_down)[...])
        ).astype(LOW)
        r.stream_low[...] = low
        project_out = self.weight(self.r.project_out)
        r.tmp[...] = dot_nn(r.stream_low[...], project_out[...])
        for start, size in self.chunks(tokens):
            rows = slice(start, start + size)
            wide = slice(start + sz.width, start + sz.width + size)
            mask = self.wide_mask(start + sz.width, size)
            r.output_own[rows] = (r.res6[wide] + r.tmp[rows]) * mask
            r.grad_branch[rows] = (r.cot6[wide] * mask).astype(LOW)
        self.put(r.output_own, r.output)
        r.grad[...] = dot_nt(r.grad_branch[...], project_out[...])
        r.grad_feed_low[...] = r.grad[...].astype(LOW)
        for piece in range(pieces):
            lanes = slice(piece * block, (piece + 1) * block)
            gate_lanes = slice(sz.hidden + piece * block, sz.hidden + (piece + 1) * block)
            r.grad_gated[...] = dot_nn(r.grad_feed_low[...], self.v.feed_down[:, lanes])
            for start, size in self.chunks(tokens):
                rows = slice(start, start + size)
                active = joined[piece * tokens + start : piece * tokens + start + size]
                gates_at = (piece + pieces) * tokens + start
                grads = r.grad_gated[rows]
                r.grad_joined[rows, lanes] = (grads * active).astype(LOW)
                r.grad_joined[rows, gate_lanes] = (grads * joined[gates_at : gates_at + size]).astype(LOW)
        r.tmp[...] = dot_nt(r.grad_joined[...], self.v.feed_up[...])
        self.layer_step(r.hat_feed, r.scale_feed, r.gain_feed, 3, r.grad_cross_low)
        r.grad_cross_mixed[...] = dot_nt(r.grad_cross_low[...], self.v.out_cross[...]).astype(LOW)
        r.scores[0 : HEADS * pad] = dot_nt(r.text_value[...], r.grad_cross_mixed[...])
        for head in range(HEADS):
            rows = slice(head * pad, (head + 1) * pad)
            attention = r.cross[rows]
            grads = r.scores[rows]
            delta = jnp.sum(attention * grads, axis=0, keepdims=True)
            r.cross_scores[rows] = (attention * (grads - delta)).astype(LOW)
        r.grad_query_text[...] = (
            dot_tn(r.cross_scores[...], r.text_key[...]) * self.scale
        ).astype(LOW)
        r.tmp[...] = dot_nt(r.grad_query_text[...], self.v.query_cross[...])
        self.layer_step(r.hat_cross, r.scale_cross, r.gain_cross, 4, r.grad_self_low)
        r.gm_send[...] = dot_nt(r.osp[...], r.grad_self_low[...]).astype(LOW)
        slot = sz.slot
        copies = [
            self.remote(
                r.gm_send.at[pl.ds(pl.multiple_of(other * slot, 16), slot)],
                r.gm.at[self.seq],
                (self.batch, other),
            )
            for other in self.seq_others
        ]
        self.start(copies)
        self.gm_copies = copies
        r.gm[self.seq] = r.gm_send[pl.ds(pl.multiple_of(self.seq * slot, 16), slot)]

    def layer_step(self, hat, scale, gain, place, target):
        r = self.r
        gains = None
        for start, size in self.chunks(self.sz.tokens):
            rows = slice(start, start + size)
            part, gain_part = self.layer_back(hat[rows], scale[rows, 0:1], r.tmp[rows], row_of(gain))
            total = r.grad[rows] + part
            r.grad[rows] = total
            target[rows] = total.astype(LOW)
            gains = gain_part if gains is None else gains + gain_part
        r.gain_parts[place : place + 1] = gains

    def text_grads(self):
        r, sz = self.r, self.sz
        pad = sz.text_pad
        head_of = floor_div(iota((1, sz.channels), 1), HEAD)
        keys = dot_nn(r.cross_scores[...], r.query_text[...]) * self.scale
        values = dot_nn(r.cross_low[...], r.grad_cross_mixed[...])
        packed = None
        for number, grads in enumerate((keys, values)):
            total = None
            for head in range(HEADS):
                part = jnp.where(head_of == head, grads[head * pad : (head + 1) * pad], 0.0)
                total = part if total is None else total + part
            part = dot_nn(total.astype(LOW), r.place[number])
            packed = part if packed is None else packed + part
        r.text_send[...] = packed.astype(LOW)
        copies = [
            self.remote(
                r.text_send.at[:, pl.ds(pl.multiple_of(other * LANES, LANES), LANES)],
                r.text_recv.at[self.seq],
                (self.batch, other),
            )
            for other in self.seq_others
        ]
        self.start(copies)
        r.text_recv[self.seq] = r.text_send[
            :, pl.ds(pl.multiple_of(self.seq * LANES, LANES), LANES)
        ]
        self.text_copies = copies

    def text_second(self):
        r = self.r
        self.wait(self.text_copies)
        total = r.text_recv[0].astype(F32)
        for place in range(1, self.sz.seqs):
            total = total + r.text_recv[place].astype(F32)
        r.text_sum[...] = total
        self.put(r.text_sum, r.text_total.at[self.batch])
        copies = self.to_batch(r.text_sum, r.text_total.at[self.batch])
        self.start(copies)
        self.text_copies = copies

    def store_pack(self, start, rows, values):
        for shard in range(self.sz.seqs):
            self.r.pack[shard % 2, shard // 2, start + rows.start : start + rows.stop] = values[
                :, shard * LANES : (shard + 1) * LANES
            ].astype(LOW)

    def early_grads(self):
        r, sz = self.r, self.sz
        channels = sz.channels
        rows = iota((2 * channels, 1), 0)
        target = jnp.where(rows >= channels, rows + (3 * LANES - channels), rows)
        spread = jnp.where(iota((1, 6 * LANES), 1) == target, 1.0, 0.0).astype(LOW)
        for z in range(sz.seqs // 2):
            wide = 2 * channels
            grads = dot_nn(r.grad_joined[:, z * wide : (z + 1) * wide], spread).astype(LOW)
            sums = dot_tn(r.normed_feed[...], grads)
            for tile in range(6):
                start = sz.start.up + (tile % 3) * channels
                r.pack[tile // 3, z, start : start + channels] = sums[
                    :, tile * LANES : (tile + 1) * LANES
                ].astype(LOW)
        size = sz.down_rows
        tail = sz.hidden - 2 * size
        placed = [dot_nn(r.grad_feed_low[...], r.place[number]).astype(LOW) for number in range(3)]
        sums = dot_tn(r.gated[:, 0:size], placed[0]) + dot_tn(r.gated[:, size : 2 * size], placed[1])
        extra = dot_tn(r.gated[:, 2 * size :], placed[2])
        self.store_pack(sz.start.down, slice(0, tail), sums[0:tail] + extra)
        self.store_pack(sz.start.down, slice(tail, size), sums[tail:])
        sums = (
            dot_tn(r.stream_low[...], dot_nn(r.grad_branch[...], r.place[0]).astype(LOW))
            + dot_tn(r.cross_mixed[...], dot_nn(r.grad_cross_low[...], r.place[1]).astype(LOW))
            + dot_tn(r.normed_cross[...], dot_nn(r.grad_query_text[...], r.place[2]).astype(LOW))
        )
        self.store_pack(sz.start.trio, slice(0, channels), sums)

    def recall(self, step):
        r = self.r
        return pltpu.make_async_copy(
            r.kept_probs.at[lax.rem(self.seq + step, self.sz.seqs)],
            r.probs.at[lax.rem(step, 2)],
            r.local_sems.at[len(Fetched._fields) + 2 + lax.rem(step, 2)],
        )

    def attention_back(self):
        r, sz = self.r, self.sz
        keys, tokens, slot = sz.keys, sz.tokens, sz.slot
        self.wait(self.gm_copies)
        base = self.used
        self.used += sz.seqs
        own_slot = pl.ds(pl.multiple_of(self.seq * slot, 16), slot)

        def send(step):
            target = lax.rem(self.seq + step, sz.seqs)
            return self.remote(
                r.dq_send.at[target], r.dq.at[own_slot], (self.batch, target), base + step
            )

        self.in_pieces += self.gather_rows(r.act_in, 2, sz.rows)
        r.scores[0:keys, 0:LANES] = jnp.zeros((keys, LANES), F32)
        row = iota((slot, 1), 0)
        to_values = jnp.where(
            (iota((slot, LANES), 0) + 2 * HEAD == iota((slot, LANES), 1))
            & (iota((slot, LANES), 0) < HEAD),
            1.0,
            0.0,
        ).astype(LOW)

        def block(step, carry):
            source = lax.rem(self.seq + step, sz.seqs)
            slot_now = lax.rem(step, 2)
            self.recall(step).wait()

            @pl.when(step < sz.seqs - 1)
            def _():
                self.recall(step + 1).start()

            scaled = (r.gm[source].astype(F32) * r.inverse[source, 0:1]).astype(LOW).astype(F32)
            delta = -jnp.sum(r.mixed_full[source] * scaled, axis=0, keepdims=True)
            high = delta.astype(LOW).astype(F32)
            middle = (delta - high).astype(LOW).astype(F32)
            rest = delta - high - middle
            extended = jnp.where(row == HEAD, high, scaled)
            extended = jnp.where(row == HEAD + 1, middle, extended)
            extended = jnp.where(row == HEAD + 2, rest, extended).astype(LOW)
            query_rows = pl.ds(pl.multiple_of(source * tokens, tokens), tokens)
            token_grads = dot_tn(scaled.astype(LOW), to_values).astype(LOW)
            queries = r.qkv[query_rows]
            grad_query = None
            for start in range(0, keys, tokens):
                rows = slice(start, start + tokens)
                grads = dot_nn(r.vh[rows], extended)
                powers = r.probs[slot_now, rows]
                low = (powers.astype(F32) * grads).astype(LOW)
                r.scores[rows, 0:LANES] += dot_nn(low, queries) + dot_nn(powers, token_grads)
                part = dot_nn(r.kt[:, rows], low)
                grad_query = part if grad_query is None else grad_query + part
            r.dq_send[source] = (grad_query * self.scale).astype(LOW)

            @pl.when(step > 0)
            def _():
                send(step).start()

            return carry

        lax.fori_loop(0, sz.seqs // 2, block, 0)
        self.sums_batch(0)
        self.sums_batch(1)
        lax.fori_loop(sz.seqs // 2, sz.seqs, block, 0)
        factor = jnp.where(iota((1, LANES), 1) < 2 * HEAD, self.scale, 1.0)
        pick = jnp.where(
            iota((2 * HEAD, LANES), 1) == iota((2 * HEAD, LANES), 0) + HEAD, 1.0, 0.0
        ).astype(LOW)
        wide = 2 * HEAD
        for place in range(sz.seqs):
            rows = slice(place * tokens, (place + 1) * tokens)
            grads = (r.scores[rows, 0:LANES] * factor).astype(LOW)
            r.dkv_send[place * wide : (place + 1) * wide] = dot_nt(pick, grads).astype(LOW)
        own_wide = pl.ds(pl.multiple_of(self.seq * wide, 16), wide)
        copies = [
            self.remote(
                r.dkv_send.at[pl.ds(pl.multiple_of(other * wide, 16), wide)],
                r.dkv.at[own_wide],
                (self.batch, other),
            )
            for other in self.seq_others
        ]
        self.start(copies)
        r.dkv[own_wide] = r.dkv_send[own_wide]
        r.dq[own_slot] = r.dq_send[self.seq]
        self.gp_copies = copies + [send(step) for step in range(1, sz.seqs)]
        self.text_second()

    def norm_sums(self, number, rows_of):
        first = second = None
        mean, inverse = self.norm(number)
        for start, size in self.chunks(self.sz.tokens):
            grads, values = rows_of(start, size)
            one, two = col_sum(grads), col_sum(grads * ((values - mean) * inverse))
            first = one if first is None else first + one
            second = two if second is None else second + two
        return first, second

    def norm_factors(self, number, gain, total):
        gains = row_of(gain)
        sums = self.grouped(total * gains) / self.count()
        mean, inverse = self.norm(number)
        return mean, inverse, gains * inverse, sums[0:1] * inverse, sums[1:2] * inverse

    def slope(self, source, number, gain, start, size):
        mean, inverse = self.norm(number)
        normed = (source[start : start + size] - mean) * inverse
        values = normed * row_of(gain)
        gate = sigmoid(values)
        return normed, gate * (1.0 + values * (1.0 - gate)) * self.wide_mask(start, size)

    def residual_back(self):
        r, sz = self.r, self.sz
        width, tokens, channels = sz.width, sz.tokens, sz.channels
        self.wait(self.gp_copies)
        r.tmp[...] = dot_tn(r.dq[...], r.query_rows[...]) + dot_tn(r.dkv[...], r.value_rows[...])
        self.layer_step(r.hat_self, r.scale_self, r.gain_self, 5, r.grad_in_low)
        r.gblk6[width : width + tokens] = dot_nt(r.grad_in_low[...], self.v.project_in[...])
        halo = self.halo(r.gblk6)
        halo.start()

        def block_rows(start, size):
            wide = slice(start + width, start + width + size)
            return r.gblk6[wide], r.res6[wide]

        self.stats_store(3, self.norm_sums(2, block_rows))
        stats = self.stats_start(3)
        self.wait(self.late)
        self.late = []
        self.gather_in = self.gather_forward(r.act_in, self.in_pieces)
        self.sums_cross(0)
        self.sums_cross(1)
        for start, size in self.chunks(sz.wide):
            rows = slice(start, start + size)
            r.normed_mid[rows], r.slope_mid[rows] = self.slope(r.mid6, 1, r.gain_mid, start, size)
        self.middle_grads()
        self.sums_core(2)
        halo.wait()
        self.wait(stats)
        total = self.stats_total(3)
        r.gain_parts[2:3] = total[1:2]
        mean, inverse, factor, first, second = self.norm_factors(2, r.gain_block, total)
        for start, size in self.chunks(sz.wide):
            rows = slice(start, start + size)
            mask = self.wide_mask(start, size)
            normed = (r.res6[rows] - mean) * inverse
            grads = r.cot6[rows] * mask + r.gblk6[rows] * factor - mask * (first + normed * second)
            r.cot6[rows] = grads
            self.shifts(r.shift_grad, start, size, grads * self.inside_mask(start, size))
        near = [self.remote(r.shift_grad.at[1, pl.ds(width, tokens)], r.near_grads, self.partner)]
        self.start(near)
        r.gact6[width : width + tokens] = self.conv_back(r.shift_grad, self.v.conv_second)
        halo = self.halo(r.gact6)
        halo.start()

        def mid_rows(start, size):
            wide = slice(start + width, start + width + size)
            return r.gact6[wide] * r.slope_mid[wide], r.mid6[wide]

        self.stats_store(4, self.norm_sums(1, mid_rows))
        stats = self.stats_start(4)
        self.sums_batch(2)
        self.sums_z(0)
        self.wait(near)
        self.conv_pack(sz.start.second)
        self.start(self.stages[3][1])
        halo.wait()
        self.wait(stats)
        total = self.stats_total(4)
        r.gain_parts[1:2] = total[1:2]
        mean, inverse, factor, first, second = self.norm_factors(1, r.gain_mid, total)
        time_total = None
        for start, size in self.chunks(sz.wide):
            rows = slice(start, start + size)
            grads = r.gact6[rows] * r.slope_mid[rows] * factor - self.wide_mask(start, size) * (
                first + r.normed_mid[rows] * second
            )
            self.shifts(r.shift_grad, start, size, grads)
            if width <= start < width + tokens:
                part = col_sum(grads)
                time_total = part if time_total is None else time_total + part
        first_copies = self.conv_send(r.shift_grad, r.first_send, r.first_grads)
        r.gblk6[width : width + tokens] = self.conv_back(r.shift_grad, self.v.conv_first)

        def in_rows(start, size):
            wide = slice(start + width, start + width + size)
            normed, slope = self.slope(r.lat6, 0, r.gain_in, start + width, size)
            return r.gblk6[wide] * slope, r.lat6[wide]

        parts = r.gain_parts
        self.stats_store(5, self.norm_sums(0, in_rows))
        stats = self.stats_start(5)
        r.extra_send[...] = jnp.zeros(r.extra_send.shape, F32)
        r.extra_send[2:3] = time_total
        r.extra_send[3:6] = parts[3:6]
        r.extra_recv[self.seq] = r.extra_send[...]
        extras = self.to_seq(lambda other: r.extra_send, r.extra_recv.at[self.seq])
        self.start(extras)
        self.sums_gather(0)
        self.sums_cross(2)
        self.sums_z(1)
        self.sums_cross(3)
        self.sums_z(2)
        first_copies = self.conv_grads(
            first_copies, self.gather_in, r.first_grads, r.act_in, r.first_part, r.first_recv
        )
        self.wait(stats)
        total = self.stats_total(5)
        mean, inverse, factor, first, second = self.norm_factors(0, r.gain_in, total)
        self.wait(extras)
        sums = r.extra_recv[0]
        for place in range(1, sz.seqs):
            sums = sums + r.extra_recv[place]
        r.final_send[...] = sums
        r.final_send[1:2] = total[1:2]
        r.final_send[0:1] = parts[1:2]
        r.final_send[6:7] = parts[2:3]
        self.put(r.final_send, r.final_recv.at[self.batch])
        self.final_copies = self.to_batch(r.final_send, r.final_recv.at[self.batch])
        self.start(self.final_copies)
        for start, size in self.chunks(tokens):
            wide = slice(start + width, start + width + size)
            normed, slope = self.slope(r.lat6, 0, r.gain_in, start + width, size)
            r.latent_own[start : start + size] = (
                r.cot6[wide]
                + r.gblk6[wide] * slope * factor
                - self.wide_mask(start + width, size) * (first + normed * second)
            )
        self.put(r.latent_own, r.latent_grad)
        self.sums_gather(1)
        self.sums_z(3)
        first_copies = self.conv_gather(first_copies, r.first_part, r.first_recv, r.conv_first_sum)
        self.sums_gather(2)
        self.sums_gather(3)
        self.wait(first_copies)

    def middle_grads(self):
        r, sz = self.r, self.sz
        queries = dot_nn(r.dq[...], r.normed_self[...]).astype(LOW)
        values = dot_nn(r.dkv[...], r.normed_self[...]).astype(LOW)
        slot, wide = sz.slot, 2 * HEAD
        for shard in range(sz.seqs):
            for tile, (start, size) in enumerate(self.lane_tiles()):
                target = r.pack.at[shard % 2, shard // 2]
                at = sz.start.heads + tile * LANES
                if size < LANES:
                    target[at : at + LANES] = jnp.zeros((LANES, LANES), LOW)
                lanes = slice(start, start + size)
                target[at : at + slot, 0:size] = queries[shard * slot : (shard + 1) * slot, lanes]
                target[at + slot : at + LANES, 0:size] = values[shard * wide : (shard + 1) * wide, lanes]
        outer = dot_nn(r.mixed[...], dot_nn(r.grad_self_low[...], r.place[0]).astype(LOW))
        inner = dot_tn(r.normed_block[...], dot_nn(r.grad_in_low[...], r.place[1]).astype(LOW))
        self.store_pack(sz.start.pair, slice(0, sz.channels), outer[0 : sz.channels] + inner)
        self.store_pack(sz.start.pair, slice(sz.channels, HEADS * sz.slot), outer[sz.channels :])

    def conv_pack(self, start):
        r, sz = self.r, self.sz
        own = r.shift_grad[1, sz.width : sz.width + sz.tokens]
        placed = [dot_nn(own, r.place_half[number]).astype(LOW) for number in range(3)]
        near = [dot_nn(r.near_grads[...], r.place_half[number]).astype(LOW) for number in range(3)]
        for col in range(3):
            total = None
            for row in range(3):
                rows = slice(row * sz.width, row * sz.width + sz.tokens)
                part = dot_tn(r.shifted[col, rows], placed[row])
                part = part + dot_tn(r.near_shifted[col, rows], near[row])
                total = part if total is None else total + part
            at = start + col * sz.channels
            for z in range(sz.seqs // 2):
                r.recv_core[z, at : at + sz.channels] = total[:, z * LANES : (z + 1) * LANES].astype(LOW)

    def sums_setup(self):
        r, sz = self.r, self.sz
        half, batches = sz.seqs // 2, sz.batches
        self.stages = []
        for start, size in sz.chunks:
            rows = pl.ds(start, size)
            part = size // batches
            quarter = pl.ds(start // batches, part)
            one = []
            if start < sz.start.second:
                one.append(
                    self.remote(r.pack.at[1 - self.core, :, rows], r.recv_core.at[:, rows], self.partner)
                )
            pair = half // 2
            x_rows = pl.ds(pl.multiple_of(start + 2 * (1 - self.batch_x) * part, 16), 2 * part)
            y_rows = pl.ds(pl.multiple_of(start + 2 * (1 - self.batch_y) * part, 16), 2 * part)
            two = [
                self.remote(
                    r.recv_core.at[pl.ds(place * pair, pair), far_rows],
                    r.recv_first.at[place, :, pl.ds(start // 2, 2 * part)],
                    peer,
                )
                for place, (far_rows, peer) in enumerate(((x_rows, self.x_peer), (y_rows, self.y_peer)))
            ]
            far_y = 2 * self.batch_x + 1 - self.batch_y
            far_x = 2 * self.batch_y + 1 - self.batch_x
            cross = [
                self.remote(
                    r.recv_core.at[
                        pl.ds(place * pair, pair), pl.ds(pl.multiple_of(start + far * part, 16), part)
                    ],
                    r.recv_second.at[pl.ds(place * pair, pair), quarter],
                    peer,
                )
                for place, (far, peer) in enumerate(((far_y, self.y_peer), (far_x, self.x_peer)))
            ]
            three = [
                self.remote(
                    r.recv_second.at[other, quarter],
                    r.recv_z.at[step, quarter],
                    (self.batch, other * 2 + self.core),
                )
                for step, other in enumerate(self.z_others)
            ]
            own = pl.ds(pl.multiple_of(start + self.quarter_of(self.z_pos) * part, 16), part)
            four = self.to_batch(r.sum_own.at[quarter], r.gathered.at[own])
            self.stages.append((one, two, cross, three, four))

    def quarter_of(self, z):
        second = z // (self.sz.seqs // 4)
        x, y = self.batch_x, self.batch_y
        return (1 - second) * (2 * x + y) + second * (2 * y + x)

    def sums_core(self, number):
        self.start(self.stages[number][0])

    def sums_batch(self, number):
        r, sz = self.r, self.sz
        start, size = sz.chunks[number]
        self.wait(self.stages[number][0])

        @pl.loop(0, sz.seqs // 2)
        def add(z):
            rows = pl.ds(start, size)
            r.recv_core[z, rows] = (
                r.pack[self.core, z, rows].astype(F32) + r.recv_core[z, rows].astype(F32)
            ).astype(LOW)

        self.start(self.stages[number][1])

    def sums_cross(self, number):
        r, sz = self.r, self.sz
        start, size = sz.chunks[number]
        part = size // sz.batches
        pair = sz.seqs // 4
        self.wait(self.stages[number][1])

        def add(target, source):
            r.recv_core[target] = (r.recv_core[target].astype(F32) + source.astype(F32)).astype(LOW)

        @pl.loop(0, pair)
        def sums(z):
            for place, near in enumerate((self.batch_x, self.batch_y)):
                rows = pl.ds(pl.multiple_of(start + 2 * near * part, 16), 2 * part)
                add((z + place * pair, rows), r.recv_first[place, z, pl.ds(start // 2, 2 * part)])

        self.start(self.stages[number][2])

    def sums_z(self, number):
        r, sz = self.r, self.sz
        start, size = sz.chunks[number]
        part = size // sz.batches
        quarter = pl.ds(start // sz.batches, part)
        self.wait(self.stages[number][2])

        @pl.loop(0, sz.seqs // 2)
        def add(z):
            own = r.recv_core[z, pl.ds(pl.multiple_of(start + self.quarter_of(z) * part, 16), part)]
            r.recv_second[z, quarter] = (
                own.astype(F32) + r.recv_second[z, quarter].astype(F32)
            ).astype(LOW)

        self.start(self.stages[number][3])

    def sums_gather(self, number):
        r, sz = self.r, self.sz
        start, size = sz.chunks[number]
        part = size // sz.batches
        quarter = pl.ds(start // sz.batches, part)
        self.wait(self.stages[number][3])
        total = r.recv_second[self.z_pos, quarter].astype(F32)
        for step in range(sz.seqs // 2 - 1):
            total = total + r.recv_z[step, quarter].astype(F32)
        own = pl.ds(pl.multiple_of(start + self.quarter_of(self.z_pos) * part, 16), part)
        r.sum_own[quarter] = total.astype(LOW)
        self.put(r.sum_own.at[quarter], r.gathered.at[own])
        self.start(self.stages[number][4])

    def run(self):
        self.entry()
        self.sums_setup()
        self.residual()
        self.attention()
        self.in_pieces += self.gather_rows(self.r.act_in, 1, 2)
        self.local_block()
        self.text_grads()
        self.early_grads()
        self.sums_core(0)
        self.sums_core(1)
        self.attention_back()
        self.residual_back()
        for stages in self.stages:
            self.wait(stages[4])
        self.wait(self.text_copies)
        self.wait(self.final_copies)
        self.wait(self.puts)
        assert self.used <= SEMAPHORES


def fused_call(sz, operands):
    t, c = sz.tokens, sz.channels
    outs = dict(
        output=((t, c), F32),
        latent_grad=((t, c), F32),
        final_recv=((sz.batches, 8, c), F32),
        time_all=((sz.batches, 8, sz.emb), F32),
        text_all=((sz.batches, sz.text_pad, sz.context), LOW),
        text_total=((sz.batches, sz.text_pad, LANES), F32),
        gathered=((sz.pack_rows, LANES), LOW),
        conv_first_sum=((sz.conv_rows, c), LOW),
        kept_probs=((sz.seqs, sz.keys, t), LOW),
    )
    scratch = buffers(sz)
    vmem = pl.BlockSpec(memory_space=pltpu.VMEM)
    anywhere = pl.BlockSpec(memory_space=pl.ANY)
    fetched = [getattr(operands, name) for name in Fetched._fields]
    specs = operands._replace(**{name: vmem for name in Inputs._fields})
    specs = specs._replace(**{name: anywhere for name in Fetched._fields})
    specs = specs._replace(
        latents=anywhere, cotangent=anywhere, heights=pl.BlockSpec(memory_space=pltpu.SMEM)
    )
    names = list(Inputs._fields) + list(outs) + list(scratch)
    shapes = [pltpu.VMEM(shape, kind) for shape, kind in scratch.values()]
    shapes += [pltpu.VMEM(operand.shape, operand.dtype) for operand in fetched]
    shapes += [pltpu.SemaphoreType.DMA((2, SEMAPHORES)), pltpu.SemaphoreType.DMA((len(fetched) + 24,))]

    def body(*refs):
        count = len(names)
        named = types.SimpleNamespace(**dict(zip(names, refs[:count])))
        named.sems, named.local_sems = refs[-2:]
        Fused(sz, named, Fetched(*refs[count:-2])).run()

    return pl.pallas_call(
        body,
        out_shape=tuple(jax.ShapeDtypeStruct(shape, kind) for shape, kind in outs.values()),
        in_specs=list(specs),
        out_specs=(anywhere,) * len(outs),
        scratch_shapes=shapes,
        compiler_params=pltpu.CompilerParams(
            collective_id=5, has_side_effects=True, vmem_limit_bytes=63 << 20
        ),
    )(*operands)


class Outputs(typing.NamedTuple):
    output: typing.Any
    latent_grad: typing.Any
    gain_in: typing.Any
    conv_first: typing.Any
    time_weight: typing.Any
    gain_mid: typing.Any
    conv_second: typing.Any
    gain_block: typing.Any
    project_in: typing.Any
    gain_self: typing.Any
    query_self: typing.Any
    key_self: typing.Any
    value_self: typing.Any
    out_self: typing.Any
    gain_cross: typing.Any
    query_cross: typing.Any
    key_cross: typing.Any
    value_cross: typing.Any
    out_cross: typing.Any
    gain_feed: typing.Any
    feed_up: typing.Any
    feed_down: typing.Any
    project_out: typing.Any


class Large(typing.NamedTuple):
    feed_up: typing.Any
    feed_down: typing.Any
    conv_second: typing.Any
    conv_first: typing.Any
    key_cross: typing.Any
    value_cross: typing.Any
    time_weight: typing.Any


LARGE = Large._fields


def unpack_kernel(sz, count, *refs):
    given = refs[:count]
    outs = Outputs(*refs[count : count + len(Outputs._fields)])
    held = refs[count + len(Outputs._fields) : -1]
    sems = refs[-1]
    channels = sz.channels
    pending = []

    def move(source, target):
        pending.append(pltpu.make_async_copy(source, target, sems.at[len(pending)]))
        pending[-1].start()
        return pending[-1]

    order = (6, 7, 0, 1, 2, 3, 4, 5)
    loads = {place: move(given[place], held[place]) for place in order}
    output, latent_grad, final_recv, time_all, text_all, text_total, gathered, first_sum = held[:count]
    finals = outs
    outs = outs._replace(**dict(zip(LARGE, held[count:])))
    moves = []
    loads[6].wait()
    eye = jnp.where(iota((LANES, LANES), 0) == iota((LANES, LANES), 1), 1.0, 0.0).astype(LOW)

    def turned(start, rows):
        return dot_nt(eye, gathered[start : start + rows])

    def three(values, *targets):
        for place, target in enumerate(targets):
            target[...] = values[place * HEAD : (place + 1) * HEAD]

    for tile in range(3):
        lanes = slice(tile * LANES, min((tile + 1) * LANES, outs.feed_up.shape[1]))
        start = sz.start.up + tile * channels
        outs.feed_up[:, lanes] = gathered[start : start + channels, : lanes.stop - lanes.start].astype(F32)
    values = turned(sz.start.down, sz.down_rows)
    for place in range(3):
        lanes = slice(place * sz.down_rows, min((place + 1) * sz.down_rows, sz.hidden))
        outs.feed_down[:, lanes] = values[
            place * HEAD : (place + 1) * HEAD, : lanes.stop - lanes.start
        ]
    moves.append(move(outs.feed_up, finals.feed_up))
    moves.append(move(outs.feed_down, finals.feed_down))
    three(turned(sz.start.trio, channels), outs.project_out, outs.out_cross, outs.query_cross)
    for tile in range(sz.sizes.heads // LANES):
        lanes = slice(tile * LANES, min((tile + 1) * LANES, channels))
        start = sz.start.heads + tile * LANES
        values = gathered[start : start + LANES].astype(F32)[:, : lanes.stop - lanes.start]
        outs.query_self[:, lanes] = values[:HEAD]
        outs.key_self[:, lanes] = values[sz.slot : sz.slot + HEAD]
        outs.value_self[:, lanes] = values[sz.slot + HEAD :]
    outs.project_in[...] = turned(sz.start.pair, channels)[HEAD : 2 * HEAD]
    wide = turned(sz.start.pair, HEADS * sz.slot)[:HEAD].astype(LOW)
    source = iota((1, channels), 1)
    target = source + (sz.slot - HEAD) * floor_div(source, HEAD)
    squeeze = jnp.where(iota((HEADS * sz.slot, 1), 0) == target, 1.0, 0.0).astype(LOW)
    outs.out_self[...] = dot_nn(wide, squeeze)
    for col in range(3):
        values = turned(sz.start.second + col * channels, channels)
        for row in range(3):
            outs.conv_second[row, col] = values[row * HEAD : (row + 1) * HEAD]
    moves.append(move(outs.conv_second, finals.conv_second))
    loads[0].wait()
    moves.append(move(output, finals.output))
    loads[1].wait()
    moves.append(move(latent_grad, finals.latent_grad))
    loads[7].wait()
    for row in range(3):
        values = first_sum[row * LANES : (row + 1) * LANES].astype(F32)
        for col in range(3):
            outs.conv_first[row, col] = values[col * HEAD : (col + 1) * HEAD]
    moves.append(move(outs.conv_first, finals.conv_first))
    for place in range(2, 6):
        loads[place].wait()
    text = None
    for place in range(sz.batches):
        grads = text_total[place]
        high = grads.astype(LOW)
        rest = (grads - high.astype(F32)).astype(LOW)
        part = dot_tn(high, text_all[place]) + dot_tn(rest, text_all[place])
        text = part if text is None else text + part
    three(text, outs.key_cross, outs.value_cross)
    moves.append(move(outs.key_cross, finals.key_cross))
    moves.append(move(outs.value_cross, finals.value_cross))
    pick = jnp.where(
        (iota((channels, LANES), 0) == iota((channels, LANES), 1) + lax.axis_index(SEQ) * HEAD)
        & (iota((channels, LANES), 1) < HEAD),
        1.0,
        0.0,
    ).astype(LOW)
    total = time = None
    for place in range(sz.batches):
        rows = final_recv[place]
        total = rows if total is None else total + rows
        picked = dot_nn(split_three(jnp.where(iota((8, 1), 0) == 2, rows, 0.0)), pick)
        act = time_all[place]
        act = pltpu.roll(act, 2, 0)
        part = dot_tn(picked.astype(LOW), jnp.concatenate([act, act, act], axis=0).astype(LOW))
        time = part if time is None else time + part
    outs.time_weight[...] = time[:HEAD]
    moves.append(move(outs.time_weight, finals.time_weight))
    gains = sum_three(dot_nn(split_three(total), pick))
    order = (
        outs.gain_mid,
        outs.gain_in,
        None,
        outs.gain_feed,
        outs.gain_cross,
        outs.gain_self,
        outs.gain_block,
    )
    for place, out in enumerate(order):
        if out is not None:
            out[...] = gains[place : place + 1, :HEAD]
    for one in moves:
        one.wait()


def unpack_call(sz, results):
    channels, hidden = sz.channels, sz.hidden
    square = jax.ShapeDtypeStruct((HEAD, channels), F32)
    gain = jax.ShapeDtypeStruct((1, HEAD), F32)
    image = jax.ShapeDtypeStruct((sz.tokens, channels), F32)
    conv = jax.ShapeDtypeStruct((3, 3, HEAD, channels), F32)
    context = jax.ShapeDtypeStruct((HEAD, sz.context), F32)
    shapes = Outputs(*[square] * len(Outputs._fields))._replace(
        output=image,
        latent_grad=image,
        gain_in=gain,
        gain_mid=gain,
        gain_block=gain,
        gain_self=gain,
        gain_cross=gain,
        gain_feed=gain,
        conv_first=conv,
        conv_second=conv,
        time_weight=jax.ShapeDtypeStruct((HEAD, sz.emb), F32),
        key_cross=context,
        value_cross=context,
        feed_up=jax.ShapeDtypeStruct((channels, 2 * hidden // sz.seqs), F32),
        feed_down=jax.ShapeDtypeStruct((HEAD, hidden), F32),
    )
    vmem = pl.BlockSpec(memory_space=pltpu.VMEM)
    anywhere = pl.BlockSpec(memory_space=pl.ANY)
    specs = Outputs(*[vmem] * len(shapes))._replace(**{name: anywhere for name in LARGE})
    specs = specs._replace(output=anywhere, latent_grad=anywhere)
    held = list(results) + [getattr(shapes, name) for name in LARGE]
    return Outputs(
        *pl.pallas_call(
            lambda *refs: unpack_kernel(sz, len(results), *refs),
            out_shape=tuple(shapes),
            in_specs=[anywhere] * len(results),
            out_specs=tuple(specs),
            scratch_shapes=[pltpu.VMEM(one.shape, one.dtype) for one in held]
            + [pltpu.SemaphoreType.DMA((len(results) + len(LARGE) + 2,))],
            compiler_params=pltpu.CompilerParams(vmem_limit_bytes=60 << 20),
        )(*results)
    )


def fast_device(*arguments):
    given = Inputs(*arguments)
    latents = given.latents
    sz = Sizes(
        lax.axis_size(BATCH),
        lax.axis_size(SEQ),
        latents,
        given.time_vector,
        given.text_states,
        given.feed_down,
    )
    channels = sz.channels
    flat = given._replace(
        latents=latents.reshape(sz.tokens, channels),
        cotangent=given.cotangent.reshape(sz.tokens, channels),
        text_states=given.text_states.reshape(sz.text, sz.context),
        time_weight=given.time_weight.T,
        key_cross=given.key_cross.T,
        value_cross=given.value_cross.T,
        feed_down=given.feed_down.T,
    )
    results = fused_call(sz, flat)[:-1]
    outs = unpack_call(sz, results)
    shaped = outs._replace(
        output=outs.output.reshape(latents.shape), latent_grad=outs.latent_grad.reshape(latents.shape)
    )
    shaped = [jnp.swapaxes(one, -2, -1) if one.shape[-2] == HEAD else one for one in shaped]
    return tuple(one.reshape(-1) if one.shape[0] == 1 and one.ndim == 2 else one for one in shaped)


def on_device(
    latents,
    heights,
    time_vector,
    text_states,
    gain_in,
    conv_first,
    time_weight,
    gain_mid,
    conv_second,
    gain_block,
    project_in,
    gain_self,
    query_self,
    key_self,
    value_self,
    out_self,
    gain_cross,
    query_cross,
    key_cross,
    value_cross,
    out_cross,
    gain_feed,
    feed_up,
    feed_down,
    project_out,
    cotangent,
):
    images_in, rows_in, col_count, channels = latents.shape
    seq_size = lax.axis_size(SEQ)
    seq_index = lax.axis_index(SEQ)
    block_rows = rows_in * col_count
    keys_count = block_rows * seq_size
    score_scale = HEAD ** (-0.5)
    row_ids = seq_index * rows_in + jnp.arange(rows_in, dtype=jnp.int32)

    def spread_fn(values):
        return values

    def pick_fn(values):
        return values

    images, row_count = (latents.shape[0], latents.shape[1])
    tok_rows = row_count * col_count
    tokens = images * tok_rows
    row_valid = (row_ids[None, :] < heights[:, None]).astype(jnp.int32)
    row_mask = row_valid.astype(jnp.float32)
    cell_mask = row_mask[:, :, None, None]
    key_rows = jnp.arange(keys_count, dtype=jnp.int32) // col_count
    key_mask = (key_rows[None, :] < heights[:, None]).astype(jnp.int32)
    cell_counts = (heights * (col_count * (channels // GROUPS))).astype(jnp.float32)

    def res_piece(values, norm_gain, sum_first, sum_second):
        return (
            jax.nn.silu(group_apply(values, norm_gain, sum_first, sum_second, cell_counts))
            * cell_mask
        )

    def block_piece(values, norm_gain, sum_first, sum_second):
        return group_apply(values, norm_gain, sum_first, sum_second, cell_counts)

    first_in, second_in = norm_stats(latents, row_mask, spread_fn, pick_fn)
    act_in = res_piece(latents, gain_in, first_in, second_in).astype(jnp.bfloat16)
    padded_in = rows_halo(act_in)
    conv_out = conv_rows(padded_in, conv_first)
    time_act = jax.nn.silu(time_vector.astype(jnp.float32)).astype(jnp.bfloat16)
    time_term = jnp.dot(time_act, time_weight, preferred_element_type=jnp.float32)
    mid_in = conv_out + time_term[:, None, None, :]
    first_mid, second_mid = norm_stats(mid_in, row_mask, spread_fn, pick_fn)
    act_mid = res_piece(mid_in, gain_mid, first_mid, second_mid).astype(jnp.bfloat16)
    padded_mid = rows_halo(act_mid)
    resid = latents + conv_rows(padded_mid, conv_second)
    first_block, second_block = norm_stats(resid, row_mask, spread_fn, pick_fn)
    normed_block = (
        block_piece(resid, gain_block, first_block, second_block)
        .reshape(tokens, channels)
        .astype(jnp.bfloat16)
    )
    stream_in = jnp.dot(normed_block, project_in, preferred_element_type=jnp.float32)
    normed_self = layer_norm(stream_in, gain_self).astype(jnp.bfloat16)
    joined_self = jnp.concatenate((query_self, key_self, value_self), axis=1)
    projected = (
        jnp.dot(normed_self, joined_self, preferred_element_type=jnp.float32)
        .astype(jnp.bfloat16)
        .reshape(images, tok_rows, 3 * channels)
    )
    queries = projected[:, :, :channels]
    keys_local = projected[:, :, channels : 2 * channels]
    values_local = projected[:, :, 2 * channels :]
    keys_all = lax.all_gather(keys_local, SEQ, axis=1, tiled=True)
    values_all = lax.all_gather(values_local, SEQ, axis=1, tiled=True)

    def forward_image(bundle):
        image_queries, image_keys, image_values, image_mask = bundle
        query_blocks = image_queries.reshape(-1, block_rows, channels)
        return lax.map(
            lambda part: self_forward((part, image_keys, image_values, image_mask), score_scale),
            query_blocks,
        )

    attn_mixed, log_totals = lax.map(forward_image, (queries, keys_all, values_all, key_mask))
    mixed_flat = attn_mixed.reshape(tokens, channels)
    stream_self = stream_in + jnp.dot(mixed_flat, out_self, preferred_element_type=jnp.float32)
    normed_cross = layer_norm(stream_self, gain_cross).astype(jnp.bfloat16)
    query_text = (
        jnp.dot(normed_cross, query_cross, preferred_element_type=jnp.float32)
        .astype(jnp.bfloat16)
        .reshape(images, tok_rows, HEADS, HEAD)
    )
    text_flat = text_states.reshape(-1, text_states.shape[2])
    text_pairs = (
        jnp.dot(
            text_flat,
            jnp.concatenate((key_cross, value_cross), axis=1),
            preferred_element_type=jnp.float32,
        )
        .astype(jnp.bfloat16)
        .reshape(images, -1, 2, HEADS, HEAD)
    )
    text_keys = text_pairs[:, :, 0]
    text_values = text_pairs[:, :, 1]
    cross_scores = (
        jnp.einsum("iqhd,ikhd->ihqk", query_text, text_keys, preferred_element_type=jnp.float32)
        * score_scale
    )
    cross_attn = jnp.exp(cross_scores - jax.nn.logsumexp(cross_scores, axis=-1, keepdims=True))
    cross_low = cross_attn.astype(jnp.bfloat16)
    cross_mixed = (
        jnp.einsum("ihqk,ikhd->iqhd", cross_low, text_values, preferred_element_type=jnp.float32)
        .astype(jnp.bfloat16)
        .reshape(tokens, channels)
    )
    stream_cross = stream_self + jnp.dot(cross_mixed, out_cross, preferred_element_type=jnp.float32)
    normed_feed = layer_norm(stream_cross, gain_feed).astype(jnp.bfloat16)
    joined_feed = jnp.dot(normed_feed, feed_up, preferred_element_type=jnp.float32)
    gated = geglu(joined_feed).astype(jnp.bfloat16)
    stream_feed = stream_cross + jnp.dot(gated, feed_down, preferred_element_type=jnp.float32)
    stream_low = stream_feed.astype(jnp.bfloat16)
    branch_out = jnp.dot(stream_low, project_out, preferred_element_type=jnp.float32).reshape(
        images, row_count, col_count, channels
    )
    output = (resid + branch_out) * cell_mask
    grad_output = cotangent * cell_mask
    grad_branch = grad_output.reshape(tokens, channels).astype(jnp.bfloat16)
    grad_project_out = grad_dot(stream_low, grad_branch)
    grad_stream = back_dot(grad_branch, project_out)
    grad_feed_low = grad_stream.astype(jnp.bfloat16)
    grad_feed_down = grad_dot(gated, grad_feed_low)
    grad_gated = back_dot(grad_feed_low, feed_down)
    unused, pull_geglu = jax.vjp(geglu, joined_feed)
    grad_joined = pull_geglu(grad_gated)[0].astype(jnp.bfloat16)
    grad_feed_up = grad_dot(normed_feed, grad_joined)
    unused, pull_norm = jax.vjp(layer_norm, stream_cross, gain_feed)
    grad_part, grad_gain_feed = pull_norm(back_dot(grad_joined, feed_up))
    grad_stream = grad_stream + grad_part
    grad_cross_low = grad_stream.astype(jnp.bfloat16)
    grad_out_cross = grad_dot(cross_mixed, grad_cross_low)
    grad_cross_mixed = (
        back_dot(grad_cross_low, out_cross)
        .astype(jnp.bfloat16)
        .reshape(images, tok_rows, HEADS, HEAD)
    )
    grad_text_values = jnp.einsum(
        "ihqk,iqhd->ikhd", cross_low, grad_cross_mixed, preferred_element_type=jnp.float32
    )
    grad_cross_attn = jnp.einsum(
        "iqhd,ikhd->ihqk", grad_cross_mixed, text_values, preferred_element_type=jnp.float32
    )
    cross_delta = jnp.sum(cross_attn * grad_cross_attn, axis=-1, keepdims=True)
    grad_cross_scores = (cross_attn * (grad_cross_attn - cross_delta)).astype(jnp.bfloat16)
    grad_query_text = (
        (
            jnp.einsum(
                "ihqk,ikhd->iqhd", grad_cross_scores, text_keys, preferred_element_type=jnp.float32
            )
            * score_scale
        )
        .astype(jnp.bfloat16)
        .reshape(tokens, channels)
    )
    grad_text_keys = (
        jnp.einsum(
            "ihqk,iqhd->ikhd", grad_cross_scores, query_text, preferred_element_type=jnp.float32
        )
        * score_scale
    )
    text_wide = text_flat.astype(jnp.float32)
    grad_key_cross = exact_grad_dot(text_wide, grad_text_keys.reshape(-1, channels))
    grad_value_cross = exact_grad_dot(text_wide, grad_text_values.reshape(-1, channels))
    grad_query_cross = grad_dot(normed_cross, grad_query_text)
    unused, pull_norm = jax.vjp(layer_norm, stream_self, gain_cross)
    grad_part, grad_gain_cross = pull_norm(back_dot(grad_query_text, query_cross))
    grad_stream = grad_stream + grad_part
    grad_self_low = grad_stream.astype(jnp.bfloat16)
    grad_out_self = grad_dot(mixed_flat, grad_self_low)
    grad_mixed = (
        back_dot(grad_self_low, out_self).astype(jnp.bfloat16).reshape(images, tok_rows, channels)
    )

    def backward_image(bundle):
        image_queries, image_grads, image_totals, image_keys, image_values, image_mask = bundle
        query_blocks = image_queries.reshape(-1, block_rows, channels)
        grad_blocks = image_grads.reshape(-1, block_rows, channels)
        return lax.map(
            lambda part: query_side(
                (part[0], part[1], part[2], image_keys, image_values, image_mask), score_scale
            ),
            (query_blocks, grad_blocks, image_totals),
        )

    grad_queries, kept_attn, kept_grads = lax.map(
        backward_image, (queries, grad_mixed, log_totals, keys_all, values_all, key_mask)
    )
    grads_four = grad_mixed.reshape(images, -1, block_rows, HEADS, HEAD)
    queries_four = queries.reshape(images, -1, block_rows, HEADS, HEAD)
    row_total = tok_rows * lax.axis_size(SEQ)
    value_terms = jnp.einsum(
        "inhqk,inqhd->kihd", kept_attn, grads_four, preferred_element_type=jnp.float32
    )
    key_terms_part = (
        jnp.einsum(
            "inhqk,inqhd->kihd", kept_grads, queries_four, preferred_element_type=jnp.float32
        )
        * score_scale
    )
    summed = lax.psum_scatter(
        jnp.stack(
            (
                key_terms_part.reshape(row_total, images, -1),
                value_terms.reshape(row_total, images, -1),
            ),
            2,
        ).astype(jnp.bfloat16),
        SEQ,
        scatter_dimension=0,
        tiled=True,
    ).astype(jnp.float32)
    grad_keys = jnp.swapaxes(summed[:, :, 0], 0, 1)
    grad_values = jnp.swapaxes(summed[:, :, 1], 0, 1)
    grad_projected = jnp.concatenate(
        (
            grad_queries.reshape(images, tok_rows, channels),
            grad_keys.astype(jnp.bfloat16),
            grad_values.astype(jnp.bfloat16),
        ),
        axis=2,
    ).reshape(tokens, 3 * channels)
    grad_joined_self = grad_dot(normed_self, grad_projected)
    unused, pull_norm = jax.vjp(layer_norm, stream_in, gain_self)
    grad_part, grad_gain_self = pull_norm(back_dot(grad_projected, joined_self))
    grad_stream = grad_stream + grad_part
    grad_stream_low = grad_stream.astype(jnp.bfloat16)
    grad_project_in = grad_dot(normed_block, grad_stream_low)
    grad_block = back_dot(grad_stream_low, project_in).reshape(
        images, row_count, col_count, channels
    )
    grad_resid_part, grad_gain_block = norm_backward(
        block_piece,
        resid,
        gain_block,
        first_block,
        second_block,
        grad_block,
        row_mask,
        spread_fn,
        pick_fn,
    )
    grad_resid = grad_output + grad_resid_part
    grad_second_low = grad_resid.astype(jnp.bfloat16)
    grad_conv_second = conv_weight_grad(padded_mid, grad_second_low)
    grad_act_mid = conv_rows(grads_halo(grad_second_low), flipped(conv_second))
    grad_mid, grad_gain_mid = norm_backward(
        res_piece,
        mid_in,
        gain_mid,
        first_mid,
        second_mid,
        grad_act_mid,
        row_mask,
        spread_fn,
        pick_fn,
    )
    grad_time = jnp.sum(grad_mid, axis=(1, 2))
    grad_time_weight = exact_grad_dot(time_act.astype(jnp.float32), grad_time)
    grad_first_low = grad_mid.astype(jnp.bfloat16)
    grad_conv_first = conv_weight_grad(padded_in, grad_first_low)
    grad_act_in = conv_rows(grads_halo(grad_first_low), flipped(conv_first))
    grad_in_part, grad_gain_in = norm_backward(
        res_piece, latents, gain_in, first_in, second_in, grad_act_in, row_mask, spread_fn, pick_fn
    )
    latent_grad = grad_resid + grad_in_part
    shares = (
        lax.psum_scatter(
            grad_gain_in.reshape(1, -1).astype(jnp.bfloat16), SEQ, scatter_dimension=1, tiled=True
        ).astype(jnp.float32),
        lax.psum_scatter(
            grad_conv_first.reshape(-1, channels).astype(jnp.bfloat16),
            SEQ,
            scatter_dimension=1,
            tiled=True,
        ).astype(jnp.float32),
        lax.psum_scatter(
            grad_time_weight.astype(jnp.bfloat16), SEQ, scatter_dimension=1, tiled=True
        ).astype(jnp.float32),
        lax.psum_scatter(
            grad_gain_mid.reshape(1, -1).astype(jnp.bfloat16),
            SEQ,
            scatter_dimension=1,
            tiled=True,
        ).astype(jnp.float32),
        lax.psum_scatter(
            grad_conv_second.reshape(-1, channels).astype(jnp.bfloat16),
            SEQ,
            scatter_dimension=1,
            tiled=True,
        ).astype(jnp.float32),
        lax.psum_scatter(
            grad_gain_block.reshape(1, -1).astype(jnp.bfloat16),
            SEQ,
            scatter_dimension=1,
            tiled=True,
        ).astype(jnp.float32),
        lax.psum_scatter(
            grad_project_in.astype(jnp.bfloat16), SEQ, scatter_dimension=1, tiled=True
        ).astype(jnp.float32),
        lax.psum_scatter(
            grad_gain_self.reshape(1, -1).astype(jnp.bfloat16),
            SEQ,
            scatter_dimension=1,
            tiled=True,
        ).astype(jnp.float32),
        lax.psum_scatter(
            grad_joined_self[:, :channels].astype(jnp.bfloat16),
            SEQ,
            scatter_dimension=1,
            tiled=True,
        ).astype(jnp.float32),
        lax.psum_scatter(
            grad_joined_self[:, channels : 2 * channels].astype(jnp.bfloat16),
            SEQ,
            scatter_dimension=1,
            tiled=True,
        ).astype(jnp.float32),
        lax.psum_scatter(
            grad_joined_self[:, 2 * channels :].astype(jnp.bfloat16),
            SEQ,
            scatter_dimension=1,
            tiled=True,
        ).astype(jnp.float32),
        lax.psum_scatter(
            grad_out_self.astype(jnp.bfloat16), SEQ, scatter_dimension=1, tiled=True
        ).astype(jnp.float32),
        lax.psum_scatter(
            grad_gain_cross.reshape(1, -1).astype(jnp.bfloat16),
            SEQ,
            scatter_dimension=1,
            tiled=True,
        ).astype(jnp.float32),
        lax.psum_scatter(
            grad_query_cross.astype(jnp.bfloat16), SEQ, scatter_dimension=1, tiled=True
        ).astype(jnp.float32),
        lax.psum_scatter(
            grad_key_cross.astype(jnp.bfloat16), SEQ, scatter_dimension=1, tiled=True
        ).astype(jnp.float32),
        lax.psum_scatter(
            grad_value_cross.astype(jnp.bfloat16), SEQ, scatter_dimension=1, tiled=True
        ).astype(jnp.float32),
        lax.psum_scatter(
            grad_out_cross.astype(jnp.bfloat16), SEQ, scatter_dimension=1, tiled=True
        ).astype(jnp.float32),
        lax.psum_scatter(
            grad_gain_feed.reshape(1, -1).astype(jnp.bfloat16),
            SEQ,
            scatter_dimension=1,
            tiled=True,
        ).astype(jnp.float32),
        lax.psum_scatter(
            grad_feed_up.astype(jnp.bfloat16), SEQ, scatter_dimension=1, tiled=True
        ).astype(jnp.float32),
        lax.psum_scatter(
            grad_feed_down.astype(jnp.bfloat16), SEQ, scatter_dimension=1, tiled=True
        ).astype(jnp.float32),
        lax.psum_scatter(
            grad_project_out.astype(jnp.bfloat16), SEQ, scatter_dimension=1, tiled=True
        ).astype(jnp.float32),
    )
    totals = (
        lax.psum(shares[0].astype(jnp.bfloat16), BATCH).astype(jnp.float32),
        lax.psum(shares[1].astype(jnp.bfloat16), BATCH).astype(jnp.float32),
        lax.psum(shares[2].astype(jnp.bfloat16), BATCH).astype(jnp.float32),
        lax.psum(shares[3].astype(jnp.bfloat16), BATCH).astype(jnp.float32),
        lax.psum(shares[4].astype(jnp.bfloat16), BATCH).astype(jnp.float32),
        lax.psum(shares[5].astype(jnp.bfloat16), BATCH).astype(jnp.float32),
        lax.psum(shares[6].astype(jnp.bfloat16), BATCH).astype(jnp.float32),
        lax.psum(shares[7].astype(jnp.bfloat16), BATCH).astype(jnp.float32),
        lax.psum(shares[8].astype(jnp.bfloat16), BATCH).astype(jnp.float32),
        lax.psum(shares[9].astype(jnp.bfloat16), BATCH).astype(jnp.float32),
        lax.psum(shares[10].astype(jnp.bfloat16), BATCH).astype(jnp.float32),
        lax.psum(shares[11].astype(jnp.bfloat16), BATCH).astype(jnp.float32),
        lax.psum(shares[12].astype(jnp.bfloat16), BATCH).astype(jnp.float32),
        lax.psum(shares[13].astype(jnp.bfloat16), BATCH).astype(jnp.float32),
        lax.psum(shares[14].astype(jnp.bfloat16), BATCH).astype(jnp.float32),
        lax.psum(shares[15].astype(jnp.bfloat16), BATCH).astype(jnp.float32),
        lax.psum(shares[16].astype(jnp.bfloat16), BATCH).astype(jnp.float32),
        lax.psum(shares[17].astype(jnp.bfloat16), BATCH).astype(jnp.float32),
        lax.psum(shares[18].astype(jnp.bfloat16), BATCH).astype(jnp.float32),
        lax.psum(shares[19].astype(jnp.bfloat16), BATCH).astype(jnp.float32),
        lax.psum(shares[20].astype(jnp.bfloat16), BATCH).astype(jnp.float32),
    )
    return (
        output,
        latent_grad,
        totals[0].reshape(-1),
        totals[1].reshape(3, 3, channels, -1),
        totals[2],
        totals[3].reshape(-1),
        totals[4].reshape(3, 3, channels, -1),
        totals[5].reshape(-1),
        totals[6],
        totals[7].reshape(-1),
        totals[8],
        totals[9],
        totals[10],
        totals[11],
        totals[12].reshape(-1),
        totals[13],
        totals[14],
        totals[15],
        totals[16],
        totals[17].reshape(-1),
        totals[18],
        totals[19],
        totals[20],
    )


def solution(mesh):
    in_specs = (
        P(BATCH, SEQ, None, None),
        P(BATCH),
        P(BATCH, None),
        P(BATCH, None, None),
        P(),
        P(),
        P(),
        P(),
        P(),
        P(),
        P(),
        P(),
        P(),
        P(),
        P(),
        P(),
        P(),
        P(),
        P(),
        P(),
        P(),
        P(),
        P(),
        P(),
        P(),
        P(BATCH, SEQ, None, None),
    )
    out_specs = (
        P(BATCH, SEQ, None, None),
        P(BATCH, SEQ, None, None),
        P(SEQ),
        P(None, None, None, SEQ),
        P(None, SEQ),
        P(SEQ),
        P(None, None, None, SEQ),
        P(SEQ),
        P(None, SEQ),
        P(SEQ),
        P(None, SEQ),
        P(None, SEQ),
        P(None, SEQ),
        P(None, SEQ),
        P(SEQ),
        P(None, SEQ),
        P(None, SEQ),
        P(None, SEQ),
        P(None, SEQ),
        P(SEQ),
        P(None, SEQ),
        P(None, SEQ),
        P(None, SEQ),
    )
    device_fn = fast_device if mesh.shape[SEQ] == HEADS and mesh.shape[BATCH] == 4 else on_device
    return jax.shard_map(
        device_fn, mesh=mesh, in_specs=in_specs, out_specs=out_specs, check_vma=False
    )
```

```python
import types
import typing

import jax
import jax.numpy as jnp
from jax import lax
from jax.experimental import pallas as pl
from jax.experimental.pallas import tpu as pltpu
from jax.sharding import PartitionSpec as P

BATCH, SEQ = "batch", "seq"
HEADS = 8
HEAD = 40
GROUPS = 32


epsilon = 1e-05
layout = ("NHWC", "HWIO", "NHWC")


def extended(block, sides, width):
    for axis, dim in sides:
        count = lax.axis_size(axis)
        forward = [(i, i + 1) for i in range(count - 1)]
        backward = [(target, source) for source, target in forward]
        low = lax.ppermute(
            lax.slice_in_dim(block, block.shape[dim] - width, None, axis=dim), axis, forward
        )
        high = lax.ppermute(lax.slice_in_dim(block, 0, width, axis=dim), axis, backward)
        block = jnp.concatenate([low, block, high], axis=dim)
    return block


def layer_norm(values, norm_gain):
    centred = values - jnp.mean(values, axis=-1, keepdims=True)
    spread = jnp.mean(centred * centred, axis=-1, keepdims=True)
    return centred * lax.rsqrt(spread + epsilon) * norm_gain


def geglu(joined):
    half_width = joined.shape[-1] // 2
    return joined[:, :half_width] * jax.nn.gelu(joined[:, half_width:], approximate=False)


def back_dot(left_side, weight):
    return lax.dot_general(
        left_side, weight, (((1,), (1,)), ((), ())), preferred_element_type=jnp.float32
    )


def grad_dot(left_side, right_side):
    return lax.dot_general(
        left_side, right_side, (((0,), (0,)), ((), ())), preferred_element_type=jnp.float32
    )


def exact_grad_dot(left_side, right_side):
    return lax.dot_general(
        left_side,
        right_side,
        (((0,), (0,)), ((), ())),
        precision=lax.Precision.HIGHEST,
        preferred_element_type=jnp.float32,
    )


def conv_rows(padded, weight):
    return lax.conv_general_dilated(
        padded,
        weight,
        (1, 1),
        ((0, 0), (1, 1)),
        dimension_numbers=layout,
        preferred_element_type=jnp.float32,
    )


def conv_weight_grad(padded, grad_output):
    row_count = grad_output.shape[1]
    col_count = grad_output.shape[2]
    padded_cols = jnp.pad(padded, ((0, 0), (0, 0), (1, 1), (0, 0)))
    flat_grad = grad_output.reshape(-1, grad_output.shape[3])
    tap_rows = []
    for shift_row in range(3):
        tap_line = []
        for shift_col in range(3):
            patch_rows = padded_cols[
                :, shift_row : shift_row + row_count, shift_col : shift_col + col_count
            ].reshape(-1, padded.shape[3])
            tap_line.append(grad_dot(patch_rows, flat_grad))
        tap_rows.append(jnp.stack(tap_line))
    return jnp.stack(tap_rows)


def flipped(weight):
    return jnp.swapaxes(weight[::-1, ::-1], 2, 3)


def group_sums(values, row_mask):
    full_shape = values.shape
    grouped = values.reshape(
        full_shape[0], full_shape[1], full_shape[2], GROUPS, full_shape[3] // GROUPS
    )
    masked = grouped * row_mask[:, :, None, None, None]
    return (jnp.sum(masked, axis=(1, 2, 4)), jnp.sum(masked * grouped, axis=(1, 2, 4)))


def group_apply(values, norm_gain, sum_first, sum_second, cell_counts):
    full_shape = values.shape
    grouped = values.reshape(
        full_shape[0], full_shape[1], full_shape[2], GROUPS, full_shape[3] // GROUPS
    )
    group_mean = sum_first / cell_counts[:, None]
    spread = sum_second / cell_counts[:, None] - group_mean * group_mean
    inverse = lax.rsqrt(spread + epsilon)
    normed = (grouped - group_mean[:, None, None, :, None]) * inverse[:, None, None, :, None]
    return normed.reshape(full_shape) * norm_gain


def norm_stats(values, row_mask, spread_fn, pick_fn):
    sum_first, sum_second = group_sums(values, row_mask)
    total_first, total_second = lax.psum((spread_fn(sum_first), spread_fn(sum_second)), SEQ)
    return (pick_fn(total_first), pick_fn(total_second))


def norm_back(grad_first, grad_second, spread_fn, pick_fn):
    total_first, total_second = lax.psum((spread_fn(grad_first), spread_fn(grad_second)), SEQ)
    return (pick_fn(total_first), pick_fn(total_second))


def rows_halo(values):
    return extended(values, ((SEQ, 1),), 1)


def grads_halo(values):
    return extended(values, ((SEQ, 1),), 1)


def norm_backward(
    piece_fn, values, norm_gain, sum_first, sum_second, grad_output, row_mask, spread_fn, pick_fn
):
    unused, pull_piece = jax.vjp(piece_fn, values, norm_gain, sum_first, sum_second)
    grad_values, grad_gain, grad_first, grad_second = pull_piece(grad_output)
    total_first, total_second = norm_back(grad_first, grad_second, spread_fn, pick_fn)
    unused, pull_sums = jax.vjp(lambda inner_vals: group_sums(inner_vals, row_mask), values)
    extra_part = pull_sums((total_first, total_second))[0]
    return (grad_values + extra_part, grad_gain)


def masked_scores(queries, keys_all, key_mask, score_scale):
    row_count = queries.shape[0]
    key_count = keys_all.shape[0]
    raw_scores = (
        jnp.einsum(
            "qhd,khd->hqk",
            queries.reshape(row_count, HEADS, HEAD),
            keys_all.reshape(key_count, HEADS, HEAD),
            preferred_element_type=jnp.float32,
        )
        * score_scale
    )
    return jnp.where(key_mask[None, None, :] > 0, raw_scores, -1e30)


def self_forward(bundle, score_scale):
    queries, keys_all, values_all, key_mask = bundle
    row_count = queries.shape[0]
    scores = masked_scores(queries, keys_all, key_mask, score_scale)
    log_total = jax.nn.logsumexp(scores, axis=-1)
    attention = jnp.exp(scores - log_total[:, :, None]).astype(jnp.bfloat16)
    attn_mixed = jnp.einsum(
        "hqk,khd->qhd",
        attention,
        values_all.reshape(keys_all.shape[0], HEADS, HEAD),
        preferred_element_type=jnp.float32,
    )
    return (attn_mixed.astype(jnp.bfloat16).reshape(row_count, -1), log_total)


def query_side(bundle, score_scale):
    queries, grad_mixed, log_total, keys_all, values_all, key_mask = bundle
    row_count = queries.shape[0]
    key_count = keys_all.shape[0]
    scores = masked_scores(queries, keys_all, key_mask, score_scale)
    attention = jnp.exp(scores - log_total[:, :, None])
    grad_attn = jnp.einsum(
        "qhd,khd->hqk",
        grad_mixed.reshape(row_count, HEADS, HEAD),
        values_all.reshape(key_count, HEADS, HEAD),
        preferred_element_type=jnp.float32,
    )
    row_delta = jnp.sum(attention * grad_attn, axis=-1)
    grad_scores = (attention * (grad_attn - row_delta[:, :, None])).astype(jnp.bfloat16)
    grad_queries = (
        jnp.einsum(
            "hqk,khd->qhd",
            grad_scores,
            keys_all.reshape(key_count, HEADS, HEAD),
            preferred_element_type=jnp.float32,
        )
        * score_scale
    )
    return (
        grad_queries.astype(jnp.bfloat16).reshape(row_count, -1),
        attention.astype(jnp.bfloat16),
        grad_scores,
    )


LANES = 128
MESH = pl.DeviceIdType.MESH
LOW = jnp.bfloat16
F32 = jnp.float32
TILE = 64


def dot_nn(left, right):
    return jnp.dot(left, right, preferred_element_type=F32)


def dot_nt(left, right):
    return lax.dot_general(left, right, (((1,), (1,)), ((), ())), preferred_element_type=F32)


def dot_tn(left, right):
    return lax.dot_general(left, right, (((0,), (0,)), ((), ())), preferred_element_type=F32)


def iota(shape, dim):
    return lax.broadcasted_iota(jnp.int32, shape, dim)


def floor_div(values, by):
    return jnp.floor((values.astype(F32) + 0.5) * (1.0 / by)).astype(jnp.int32)


def split_three(values):
    high = values.astype(LOW).astype(F32)
    rest = values - high
    middle = rest.astype(LOW).astype(F32)
    return jnp.concatenate([high, middle, rest - middle], axis=0).astype(LOW)


def sum_three(values):
    rows = values.shape[0] // 3
    return values[:rows] + values[rows : 2 * rows] + values[2 * rows :]


def row_of(ref):
    return ref[...].reshape(1, -1)


def sigmoid(values):
    return 1.0 / (1.0 + jnp.exp(-values))


def col_sum(values):
    return jnp.sum(values, axis=0, keepdims=True)


ROUNDS = 6
SEMAPHORES = 256


class Packs(typing.NamedTuple):
    up: typing.Any
    down: typing.Any
    trio: typing.Any
    pair: typing.Any
    heads: typing.Any
    second: typing.Any


class Sizes:
    def __init__(self, mesh_batch, mesh_seq, latents, time_vector, text_states, feed_down):
        self.batches = mesh_batch
        self.seqs = mesh_seq
        self.rows = latents.shape[1]
        self.width = latents.shape[2]
        self.channels = latents.shape[3]
        self.tokens = self.rows * self.width
        self.wide = self.tokens + 2 * self.width
        self.keys = self.tokens * mesh_seq
        self.emb = time_vector.shape[1]
        self.text = text_states.shape[1]
        self.text_pad = -(-self.text // 16) * 16
        self.context = text_states.shape[2]
        self.hidden = feed_down.shape[0]
        self.slot = 48
        self.packed = HEADS * LANES
        self.down_rows = 512
        self.conv_rows = 3 * LANES
        channels = self.channels
        sizes = Packs(
            up=3 * channels,
            down=self.down_rows,
            trio=channels,
            pair=HEADS * self.slot,
            heads=-(-channels // LANES) * LANES,
            second=3 * channels,
        )
        starts = [sum(sizes[:place]) for place in range(len(sizes))]
        self.start = Packs(*starts)
        self.pack_rows = sum(sizes)
        self.sizes = sizes
        self.chunks = [
            (0, sizes.up),
            (self.start.down, sizes.down + sizes.trio),
            (self.start.pair, sizes.pair + sizes.heads),
            (self.start.second, sizes.second),
        ]


class Inputs(typing.NamedTuple):
    latents: typing.Any
    heights: typing.Any
    time_vector: typing.Any
    text_states: typing.Any
    gain_in: typing.Any
    conv_first: typing.Any
    time_weight: typing.Any
    gain_mid: typing.Any
    conv_second: typing.Any
    gain_block: typing.Any
    project_in: typing.Any
    gain_self: typing.Any
    query_self: typing.Any
    key_self: typing.Any
    value_self: typing.Any
    out_self: typing.Any
    gain_cross: typing.Any
    query_cross: typing.Any
    key_cross: typing.Any
    value_cross: typing.Any
    out_cross: typing.Any
    gain_feed: typing.Any
    feed_up: typing.Any
    feed_down: typing.Any
    project_out: typing.Any
    cotangent: typing.Any


class Fetched(typing.NamedTuple):
    query_self: typing.Any
    key_self: typing.Any
    value_self: typing.Any
    time_weight: typing.Any
    conv_first: typing.Any
    conv_second: typing.Any
    project_in: typing.Any
    key_cross: typing.Any
    value_cross: typing.Any
    out_self: typing.Any
    query_cross: typing.Any
    out_cross: typing.Any
    feed_up: typing.Any
    feed_down: typing.Any
    project_out: typing.Any


def buffers(sz):
    c, t, w, k = sz.channels, sz.tokens, sz.wide, sz.keys
    half = sz.seqs // 2
    return dict(
        lat6=((w, c), F32),
        cot6=((w, c), F32),
        mid6=((w, c), F32),
        res6=((w, c), F32),
        gblk6=((w, c), F32),
        gact6=((w, c), F32),
        slope_mid=((w, c), F32),
        normed_mid=((w, c), F32),
        shifted=((3, w, c), LOW),
        shift_grad=((3, w, c), LOW),
        act_in=((k + 2 * sz.width, c), LOW),
        widen=((HEADS * sz.slot, c), LOW),
        first_send=((HEADS * sz.slot, t), LOW),
        first_grads=((sz.slot, k), LOW),
        first_part=((sz.conv_rows, c), LOW),
        first_recv=((3, sz.batches - 1, LANES // sz.batches, c), LOW),
        conv_stack=((LANES, k), LOW),
        stat_send=((ROUNDS, 8, LANES), F32),
        extra_send=((8, c), F32),
        extra_recv=((sz.seqs, 8, c), F32),
        stat_recv=((ROUNDS, sz.seqs, 8, LANES), F32),
        norms=((3, 8, c), F32),
        gain_parts=((8, c), F32),
        final_send=((8, c), F32),
        group=((c, c), LOW),
        place=((3, c, sz.packed), LOW),
        wqkv=((c, sz.packed), LOW),
        osp=((HEADS * sz.slot, c), LOW),
        time_send=((8, sz.emb), F32),
        normed_block=((t, c), LOW),
        stream_in=((t, c), F32),
        normed_self=((t, c), LOW),
        qkv_send=((t, sz.packed), LOW),
        qkv=((k, LANES), LOW),
        qh=((k, LANES), LOW),
        kh=((k, LANES), LOW),
        vh=((k, sz.slot), LOW),
        vt=((sz.slot, k), LOW),
        kt=((sz.slot, k), LOW),
        scores=((max(k, 2 * sz.hidden), t), F32),
        scores_odd=((k, t), F32),
        tops=((2, 8, t), F32),
        probs=((2, k, t), LOW),
        mixed_full=((sz.seqs, sz.slot, t), F32),
        inverse=((sz.seqs, 8, t), F32),
        mixed_send=((sz.seqs, sz.slot, t), LOW),
        mixed=((HEADS * sz.slot, t), LOW),
        stream=((t, c), F32),
        hat_self=((t, c), F32),
        scale_self=((t, LANES), F32),
        hat_cross=((t, c), F32),
        scale_cross=((t, LANES), F32),
        hat_feed=((t, c), F32),
        normed_cross=((t, c), LOW),
        query_text=((t, c), LOW),
        text_rows=((2, sz.text_pad, c), F32),
        text_key=((HEADS * sz.text_pad, c), LOW),
        text_value=((HEADS * sz.text_pad, c), LOW),
        cross=((HEADS * sz.text_pad, t), F32),
        cross_low=((HEADS * sz.text_pad, t), LOW),
        cross_scores=((HEADS * sz.text_pad, t), LOW),
        cross_mixed=((t, c), LOW),
        scale_feed=((t, LANES), F32),
        normed_feed=((t, c), LOW),
        gated=((t, sz.hidden), LOW),
        grad_gated=((t, 2 * LANES), F32),
        grad_joined=((t, 2 * sz.hidden), LOW),
        stream_low=((t, c), LOW),
        grad_branch=((t, c), LOW),
        grad=((t, c), F32),
        tmp=((t, c), F32),
        grad_feed_low=((t, c), LOW),
        grad_cross_low=((t, c), LOW),
        grad_cross_mixed=((t, c), LOW),
        grad_query_text=((t, c), LOW),
        grad_self_low=((t, c), LOW),
        grad_in_low=((t, c), LOW),
        text_send=((sz.text_pad, sz.packed), LOW),
        text_recv=((sz.seqs, sz.text_pad, LANES), LOW),
        gm_send=((HEADS * sz.slot, t), LOW),
        gm=((sz.seqs, sz.slot, t), LOW),
        query_rows=((HEADS * sz.slot, c), LOW),
        value_rows=((HEADS * 2 * HEAD, c), LOW),
        dq_send=((sz.seqs, sz.slot, t), LOW),
        dq=((HEADS * sz.slot, t), LOW),
        dkv_send=((HEADS * 2 * HEAD, t), LOW),
        dkv=((HEADS * 2 * HEAD, t), LOW),
        pack=((2, half, sz.start.second, LANES), LOW),
        near_shifted=((3, w, c), LOW),
        output_own=((t, c), F32),
        latent_own=((t, c), F32),
        text_own=((sz.text_pad, sz.context), LOW),
        text_sum=((sz.text_pad, LANES), F32),
        sum_own=((sz.pack_rows // sz.batches, LANES), LOW),
        first_own=((3, LANES // sz.batches, c), LOW),
        near_grads=((t, c), LOW),
        place_half=((3, c, half * LANES), LOW),
        recv_core=((half, sz.pack_rows, LANES), LOW),
        recv_first=((2, half // 2, sz.pack_rows // 2, LANES), LOW),
        recv_second=((half, sz.pack_rows // sz.batches, LANES), LOW),
        recv_z=((half - 1, sz.pack_rows // sz.batches, LANES), LOW),
    )


class Halo:
    def __init__(self, seq, last, after, before):
        self.seq, self.last, self.after, self.before = seq, last, after, before

    def start(self):
        @pl.when(self.seq < self.last)
        def _():
            self.after.start()

        @pl.when(self.seq > 0)
        def _():
            self.before.start()

    def wait(self):
        @pl.when(self.seq < self.last)
        def _():
            self.after.wait_send()
            self.before.wait_recv()

        @pl.when(self.seq > 0)
        def _():
            self.before.wait_send()
            self.after.wait_recv()


class Fused:
    def __init__(self, sz, refs, local):
        self.sz = sz
        self.r = refs
        self.v = local
        self.used = 0
        self.puts = []
        self.batch = lax.axis_index(BATCH)
        self.seq = lax.axis_index(SEQ)
        self.z_pos = self.seq // 2
        self.core = lax.rem(self.seq, 2)
        self.batch_x = lax.rem(self.batch, 2)
        self.batch_y = self.batch // 2
        self.x_peer = (self.batch + 1 - 2 * self.batch_x, self.seq)
        self.y_peer = (self.batch + 2 - 4 * self.batch_y, self.seq)
        self.partner = (self.batch, self.seq + 1 - 2 * self.core)
        far = sorted(range(1, sz.seqs), key=lambda step: -min(step, sz.seqs - step))
        self.seq_others = [lax.rem(self.seq + step, sz.seqs) for step in far]
        self.batch_others = [lax.rem(self.batch + step, sz.batches) for step in range(1, sz.batches)]
        half = sz.seqs // 2
        self.z_others = [lax.rem(self.z_pos + step, half) for step in range(1, half)]
        self.height = refs.heights[0]
        self.scale = HEAD ** (-0.5)

    def remote(self, source, target, device, index=None):
        if index is None:
            index = self.used
            self.used += 1
        return pltpu.make_async_remote_copy(
            src_ref=source,
            dst_ref=target,
            send_sem=self.r.sems.at[0, index],
            recv_sem=self.r.sems.at[1, index],
            device_id=device,
            device_id_type=MESH,
        )

    def to_seq(self, source, target):
        return [self.remote(source(other), target, (self.batch, other)) for other in self.seq_others]

    def to_batch(self, source, target):
        return [self.remote(source, target, (other, self.seq)) for other in self.batch_others]

    def put(self, source, target):
        index = len(Fetched._fields) + 4 + len(self.puts)
        self.puts.append(pltpu.make_async_copy(source, target, self.r.local_sems.at[index]))
        self.puts[-1].start()

    def start(self, copies):
        for one in copies:
            one.start()

    def wait(self, copies):
        for one in copies:
            one.wait()

    def entry(self):
        r = self.r
        barrier = pltpu.get_barrier_semaphore()
        for other in self.seq_others:
            pl.semaphore_signal(barrier, inc=1, device_id=(self.batch, other), device_id_type=MESH)
        for other in self.batch_others:
            pl.semaphore_signal(barrier, inc=1, device_id=(other, self.seq), device_id_type=MESH)
        self.local = {}
        self.named = {id(getattr(r, name)): name for name in Fetched._fields}
        for number, name in enumerate(Fetched._fields):
            self.local[name] = pltpu.make_async_copy(
                getattr(r, name), getattr(self.v, name), r.local_sems.at[number]
            )
            self.local[name].start()
        own = pl.ds(self.sz.width, self.sz.tokens)
        self.images = [
            pltpu.make_async_copy(source, target.at[own], r.local_sems.at[len(Fetched._fields) + place])
            for place, (source, target) in enumerate(((r.latents, r.lat6), (r.cotangent, r.cot6)))
        ]
        self.start(self.images)

    def joined(self):
        barrier = pltpu.get_barrier_semaphore()
        pl.semaphore_wait(barrier, self.sz.seqs - 1 + self.sz.batches - 1)

    def weight(self, ref):
        name = self.named[id(ref)]
        if name in self.local:
            self.local.pop(name).wait()
        return getattr(self.v, name)

    def far_first(self, step):
        half = self.sz.seqs // 2
        offset = half + ((step + 1) // 2) * (1 - 2 * (step % 2))
        return lax.rem(self.seq + offset, self.sz.seqs)

    def wide_row(self, start, size):
        rows = floor_div(iota((size, 1), 0) + start, self.sz.width) - 1
        return rows + self.seq * self.sz.rows

    def wide_mask(self, start, size):
        rows = self.wide_row(start, size)
        return jnp.where((rows >= 0) & (rows < self.height), 1.0, 0.0)

    def inside_mask(self, start, size):
        rows = self.wide_row(start, size)
        return jnp.where((rows >= 0) & (rows < self.sz.rows * self.sz.seqs), 1.0, 0.0)

    def chunks(self, total):
        return [(start, TILE) for start in range(0, total, TILE)]

    def halo(self, ref):
        sz, width = self.sz, self.sz.width
        after = self.remote(
            ref.at[pl.ds(sz.tokens, width)],
            ref.at[pl.ds(0, width)],
            (self.batch, jnp.minimum(self.seq + 1, sz.seqs - 1)),
        )
        before = self.remote(
            ref.at[pl.ds(width, width)],
            ref.at[pl.ds(width + sz.tokens, width)],
            (self.batch, jnp.maximum(self.seq - 1, 0)),
        )
        return Halo(self.seq, sz.seqs - 1, after, before)

    def lane_tiles(self):
        channels = self.sz.channels
        return [(start, min(LANES, channels - start)) for start in range(0, channels, LANES)]

    def stats_store(self, number, rows):
        r = self.r
        r.stat_send[number] = jnp.zeros(r.stat_send.shape[1:], F32)
        tiles = self.lane_tiles()
        for which, row in enumerate(rows):
            for place, (start, size) in enumerate(tiles):
                at = which * len(tiles) + place
                r.stat_send[number, at : at + 1, 0:size] = row[:, start : start + size]
        r.stat_recv[number, self.seq] = r.stat_send[number]

    def stats_start(self, number):
        r = self.r
        copies = self.to_seq(lambda other: r.stat_send.at[number], r.stat_recv.at[number, self.seq])
        self.start(copies)
        return copies

    def stats_total(self, number):
        r = self.r
        total = r.stat_recv[number, 0]
        for place in range(1, self.sz.seqs):
            total = total + r.stat_recv[number, place]
        tiles = self.lane_tiles()
        rows = []
        for which in range(2):
            parts = [
                total[which * len(tiles) + place : which * len(tiles) + place + 1, 0:size]
                for place, (start, size) in enumerate(tiles)
            ]
            rows.append(jnp.concatenate(parts, axis=1))
        row = iota((8, 1), 0)
        return jnp.where(row == 0, rows[0], jnp.where(row == 1, rows[1], 0.0))

    def grouped(self, rows):
        return sum_three(dot_nn(split_three(rows), self.r.group[...]))

    def count(self):
        per_row = self.sz.width * (self.sz.channels // GROUPS)
        return (self.height * per_row).astype(F32)

    def set_norm(self, number, total):
        sums = self.grouped(total) / self.count()
        mean = sums[0:1]
        spread = sums[1:2] - mean * mean
        self.r.norms[number, 0:1] = mean
        self.r.norms[number, 1:2] = lax.rsqrt(spread + epsilon)

    def norm(self, number):
        return self.r.norms[number, 0:1], self.r.norms[number, 1:2]

    def value_sums(self, ref):
        r, sz = self.r, self.sz
        first = second = None
        for start, size in self.chunks(sz.tokens):
            start += sz.width
            values = ref[start : start + size]
            masked = values * self.wide_mask(start, size)
            one, two = col_sum(masked), col_sum(masked * values)
            first = one if first is None else first + one
            second = two if second is None else second + two
        return first, second

    def shifts(self, ref, start, size, values):
        column = lax.rem(iota((size, 1), 0), self.sz.width)
        ref[1, start : start + size] = values.astype(LOW)
        left = jnp.where(column == 0, 0.0, pltpu.roll(values, 1, 0))
        ref[0, start : start + size] = left.astype(LOW)
        right = jnp.where(column == self.sz.width - 1, 0.0, pltpu.roll(values, size - 1, 0))
        ref[2, start : start + size] = right.astype(LOW)

    def activate(self, source, number, gain, target, kept):
        mean, inverse = self.norm(number)
        factor = inverse * row_of(gain)
        for start, size in self.chunks(self.sz.wide):
            normed = (source[start : start + size] - mean) * factor
            values = normed * sigmoid(normed) * self.wide_mask(start, size)
            self.shifts(target, start, size, values)
        if kept is None:
            return
        width, tokens = self.sz.width, self.sz.tokens
        kept[self.own_rows()] = target[1, width : width + tokens]
        zeros = jnp.zeros((width, self.sz.channels), LOW)
        kept[0:width] = zeros
        kept[self.sz.keys + width :] = zeros

    def own_rows(self, seq=None):
        seq = self.seq if seq is None else seq
        width, tokens = self.sz.width, self.sz.tokens
        return pl.ds(pl.multiple_of(seq * tokens + width, width), tokens)

    def gather_rows(self, kept, first, last):
        width, tokens = self.sz.width, self.sz.tokens
        start = self.seq * tokens + (first + 1) * width
        rows = pl.ds(pl.multiple_of(start, width), (last - first) * width)
        copies = [
            self.remote(kept.at[rows], kept.at[rows], (self.batch, other * 2 + self.core))
            for other in self.z_others
        ]
        self.start(copies)
        return copies

    def gather_forward(self, kept, copies):
        rows = self.own_rows()
        more = [self.remote(kept.at[rows], kept.at[rows], self.partner)]
        self.start(more)
        self.wait(copies)
        half = self.sz.seqs // 2
        for step in range(1, half):
            rows = self.own_rows(lax.rem(self.z_pos + half - step, half) * 2 + self.core)
            more.append(self.remote(kept.at[rows], kept.at[rows], self.partner))
        self.start(more[1:])
        return more

    def conv_send(self, grads, send, target):
        sz, slot = self.sz, self.sz.slot
        send[...] = dot_nt(self.r.widen[...], grads[1, sz.width : sz.width + sz.tokens]).astype(LOW)
        lanes = pl.ds(pl.multiple_of(self.seq * sz.tokens, sz.tokens), sz.tokens)
        copies = [
            self.remote(
                send.at[pl.ds(pl.multiple_of(other * slot, 16), slot)],
                target.at[:, lanes],
                (self.batch, other),
            )
            for other in self.seq_others
        ]
        self.start(copies)
        target[:, lanes] = send[pl.ds(pl.multiple_of(self.seq * slot, 16), slot)]
        return copies

    def conv_grads(self, copies, gathered, grads, kept, part, received):
        r, sz = self.r, self.sz
        keys, width = sz.keys, sz.width
        self.wait(copies)
        self.wait(gathered)
        values = grads[0:HEAD].astype(F32)
        column = lax.rem(iota((1, keys), 1), width)
        left = jnp.where(column == width - 1, 0.0, pltpu.roll(values, keys - 1, 1))
        right = jnp.where(column == 0, 0.0, pltpu.roll(values, 1, 1))
        rest = jnp.zeros((LANES - 3 * HEAD, keys), F32)
        r.conv_stack[...] = jnp.concatenate([left, values, right, rest], axis=0).astype(LOW)
        size = LANES // sz.batches
        pieces = []
        for row in range(3):
            part[row * LANES : (row + 1) * LANES] = dot_nn(
                r.conv_stack[...], kept[row * width : row * width + keys]
            ).astype(LOW)
            copies = []
            for step, other in enumerate(self.batch_others):
                rows = pl.ds(pl.multiple_of(row * LANES + other * size, 16), size)
                copies.append(self.remote(part.at[rows], received.at[row, step], (other, self.seq)))
            self.start(copies)
            pieces.append(copies)
        return pieces

    def conv_gather(self, pieces, part, received, out):
        size = LANES // self.sz.batches
        sent = []
        for row, copies in enumerate(pieces):
            own = pl.ds(pl.multiple_of(row * LANES + self.batch * size, 16), size)
            self.wait(copies)
            total = part[own].astype(F32)
            for step in range(self.sz.batches - 1):
                total = total + received[row, step].astype(F32)
            self.r.first_own[row] = total.astype(LOW)
            self.put(self.r.first_own.at[row], out.at[own])
            copies = self.to_batch(self.r.first_own.at[row], out.at[own])
            self.start(copies)
            sent += copies
        return sent

    def conv(self, ref, weight):
        sz = self.sz
        total = None
        for row in range(3):
            for col in range(3):
                part = dot_nn(ref[col, row * sz.width : row * sz.width + sz.tokens], weight[row, col])
                total = part if total is None else total + part
        return total

    def conv_back(self, ref, weight):
        sz = self.sz
        total = None
        for row in range(3):
            for col in range(3):
                part = dot_nt(
                    ref[col, row * sz.width : row * sz.width + sz.tokens], weight[2 - row, 2 - col]
                )
                total = part if total is None else total + part
        return total

    def constants(self):
        r, sz = self.r, self.sz
        channels = sz.channels
        size = channels // GROUPS
        r.group[...] = jnp.where(
            floor_div(iota((channels, 1), 0), size) == floor_div(iota((1, channels), 1), size), 1.0, 0.0
        ).astype(LOW)
        source = iota((1, channels), 1)
        source = source + (sz.slot - HEAD) * floor_div(source, HEAD)
        r.widen[...] = jnp.where(iota((HEADS * sz.slot, 1), 0) == source, 1.0, 0.0).astype(LOW)
        rows = iota((channels, 1), 0)
        target = rows + (LANES - HEAD) * floor_div(rows, HEAD)
        lanes = iota((1, sz.packed), 1)
        for number in range(3):
            r.place[number] = jnp.where(lanes == target + number * HEAD, 1.0, 0.0).astype(LOW)
        head = floor_div(rows, HEAD)
        pair = floor_div(head, 2)
        target = jnp.where(head - 2 * pair == self.core, rows - head * HEAD + pair * LANES, -LANES)
        lanes = iota((1, r.place_half.shape[2]), 1)
        for number in range(3):
            r.place_half[number] = jnp.where(lanes == target + number * HEAD, 1.0, 0.0).astype(LOW)

    def residual(self):
        r, sz = self.r, self.sz
        width, tokens = sz.width, sz.tokens
        self.constants()
        self.wait(self.images)
        for ref in (r.lat6, r.cot6, r.mid6, r.res6, r.gblk6, r.gact6):

            @pl.when(self.seq == 0)
            def _():
                ref[0:width] = jnp.zeros((width, sz.channels), F32)

            @pl.when(self.seq == sz.seqs - 1)
            def _():
                ref[width + tokens :] = jnp.zeros((width, sz.channels), F32)

        self.stats_store(0, self.value_sums(r.lat6))
        self.joined()
        halo = self.halo(r.lat6)
        halo.start()
        stats = self.stats_start(0)
        late = [self.halo(r.cot6)]
        act = r.time_vector[...].astype(F32)
        act = (act * sigmoid(act)).astype(LOW)
        r.time_send[...] = jnp.zeros(r.time_send.shape, F32)
        r.time_send[0:1] = act.astype(F32)
        self.put(r.time_send, r.time_all.at[self.batch])
        late += self.to_batch(r.time_send, r.time_all.at[self.batch])
        r.text_own[...] = jnp.zeros(r.text_own.shape, LOW)
        r.text_own[0 : sz.text] = r.text_states[...]
        self.put(r.text_own, r.text_all.at[self.batch])
        late += self.to_batch(r.text_own, r.text_all.at[self.batch])
        self.start(late)
        self.late = late
        time_weight = self.weight(self.r.time_weight)
        time_term = dot_nt(jnp.broadcast_to(act, (16, sz.emb)), time_weight[...])[0:1]
        wqkv = None
        for number, name in enumerate((r.query_self, r.key_self, r.value_self)):
            part = dot_nn(self.weight(name)[...], r.place[number])
            wqkv = part if wqkv is None else wqkv + part
        r.wqkv[...] = wqkv.astype(LOW)
        halo.wait()
        self.wait(stats)
        self.set_norm(0, self.stats_total(0))
        self.activate(r.lat6, 0, r.gain_in, r.shifted, r.act_in)
        r.mid6[width : width + tokens] = self.conv(r.shifted, self.weight(self.r.conv_first)) + time_term
        halo = self.halo(r.mid6)
        halo.start()
        self.stats_store(1, self.value_sums(r.mid6))
        stats = self.stats_start(1)
        self.weight(self.r.conv_second)
        halo.wait()
        self.wait(stats)
        self.set_norm(1, self.stats_total(1))
        self.activate(r.mid6, 1, r.gain_mid, r.shifted, None)
        r.res6[width : width + tokens] = r.lat6[width : width + tokens] + self.conv(
            r.shifted, self.v.conv_second
        )
        halo = self.halo(r.res6)
        self.stats_store(2, self.value_sums(r.res6))
        stats = self.stats_start(2)
        halo.start()
        self.late.append(halo)
        near = self.remote(r.shifted, r.near_shifted, self.partner)
        near.start()
        self.late.append(near)
        project_in = self.weight(self.r.project_in)
        self.wait(stats)
        self.set_norm(2, self.stats_total(2))
        mean, inverse = self.norm(2)
        factor = inverse * row_of(r.gain_block)
        for start, size in self.chunks(tokens):
            values = r.res6[width + start : width + start + size]
            r.normed_block[start : start + size] = ((values - mean) * factor).astype(LOW)
        r.stream_in[...] = dot_nn(r.normed_block[...], project_in[...])
        for start, size in self.chunks(tokens):
            rows = slice(start, start + size)
            self.layer_norm(r.stream_in[rows], r.gain_self, rows, r.normed_self, r.hat_self, r.scale_self)
        r.qkv_send[...] = dot_nn(r.normed_self[...], r.wqkv[...]).astype(LOW)
        rows = pl.ds(pl.multiple_of(self.seq * tokens, tokens), tokens)
        copies = [
            self.remote(
                r.qkv_send.at[:, pl.ds(pl.multiple_of(other * LANES, LANES), LANES)],
                r.qkv.at[rows],
                (self.batch, other),
            )
            for other in self.seq_others
        ]
        self.start(copies)
        r.qkv[rows] = r.qkv_send[:, pl.ds(pl.multiple_of(self.seq * LANES, LANES), LANES)]
        self.text_start()
        self.wait(copies)

    def layer_parts(self, values):
        centred = values - jnp.mean(values, axis=-1, keepdims=True)
        spread = jnp.mean(centred * centred, axis=-1, keepdims=True)
        return centred, lax.rsqrt(spread + epsilon)

    def layer_norm(self, values, gain, rows, target, hat, kept_scale):
        centred, scale = self.layer_parts(values)
        normed = centred * scale
        hat[rows] = normed
        kept_scale[rows] = jnp.broadcast_to(scale, (values.shape[0], LANES))
        target[rows] = (normed * row_of(gain)).astype(LOW)

    def layer_back(self, normed, scale, grad, gain):
        scaled = grad * gain
        first = jnp.mean(scaled, axis=-1, keepdims=True)
        second = jnp.mean(scaled * normed, axis=-1, keepdims=True)
        return scale * (scaled - first - normed * second), col_sum(grad * normed)

    def text_start(self):
        r, sz = self.r, self.sz
        r.text_rows[...] = jnp.zeros(r.text_rows.shape, F32)
        for number, (name, target) in enumerate(
            ((r.key_cross, r.text_key), (r.value_cross, r.text_value))
        ):
            r.text_rows[number, 0 : sz.text] = dot_nt(r.text_states[...], self.weight(name)[...])
            rows = r.text_rows[number]
            head = floor_div(iota((1, sz.channels), 1), HEAD)
            for one in range(HEADS):
                target[one * sz.text_pad : (one + 1) * sz.text_pad] = jnp.where(
                    head == one, rows, 0.0
                ).astype(LOW)
        r.query_rows[...] = dot_nt(r.widen[...], self.v.query_self[...]).astype(LOW)
        rows = iota((HEADS * 2 * HEAD, 1), 0)
        source = iota((1, sz.channels), 1)
        source = source + HEAD * floor_div(source, HEAD)
        r.value_rows[...] = (
            dot_nt(jnp.where(rows == source, 1.0, 0.0).astype(LOW), self.v.key_self[...])
            + dot_nt(jnp.where(rows == source + HEAD, 1.0, 0.0).astype(LOW), self.v.value_self[...])
        ).astype(LOW)
        r.osp[...] = dot_nn(r.widen[...], self.weight(self.r.out_self)[...]).astype(LOW)

    def attention(self):
        r, sz = self.r, self.sz
        keys, tokens, slot = sz.keys, sz.tokens, sz.slot
        self.in_pieces = self.gather_rows(r.act_in, 0, 1)
        lane_in = iota((LANES, LANES), 0)
        lane_out = iota((LANES, LANES), 1)

        def shift(by):
            return jnp.where((lane_in == lane_out + by) & (lane_out < HEAD), 1.0, 0.0).astype(LOW)

        def shift_wide(by):
            source = iota((LANES, slot), 0)
            target = iota((LANES, slot), 1)
            return jnp.where((source == target + by) & (target < HEAD), 1.0, 0.0).astype(LOW)

        def shift_rows(by):
            source = iota((slot, LANES), 1)
            target = iota((slot, LANES), 0)
            return jnp.where((source == target + by) & (target < HEAD), 1.0, 0.0).astype(LOW)

        query_out = jnp.where((lane_in + HEAD == lane_out) & (lane_in < HEAD), 1.0, 0.0).astype(LOW)
        lane = iota((1, LANES), 1)
        for start in range(0, keys, 2 * tokens):
            rows = slice(start, start + 2 * tokens)
            block = r.qkv[rows]
            valid = iota((2 * tokens, 1), 0) + start < self.height * sz.width
            r.qh[rows] = jnp.where(
                lane < HEAD, block.astype(F32), jnp.where(lane == HEAD, 1.0, 0.0)
            ).astype(LOW)
            bias = jnp.where((lane == HEAD) & jnp.logical_not(valid), -1e30, 0.0)
            r.kh[rows] = (dot_nn(block, shift(HEAD)) + bias).astype(LOW)
            ones = jnp.where((iota((1, slot), 1) >= HEAD) & (iota((1, slot), 1) < HEAD + 3), 1.0, 0.0)
            r.vh[rows] = (dot_nn(block, shift_wide(2 * HEAD)) + ones).astype(LOW)
            one_row = jnp.where(iota((slot, 1), 0) == HEAD, 1.0, 0.0)
            r.vt[:, rows] = (dot_nt(shift_rows(2 * HEAD), block) + one_row).astype(LOW)
            r.kt[:, rows] = dot_nt(shift_rows(HEAD), block).astype(LOW)
            r.qkv[rows] = dot_nn(block, query_out).astype(LOW)
        factor = self.scale * 1.4426950408889634
        base = self.used
        self.used += sz.seqs

        def send(target, step):
            return self.remote(
                r.mixed_send.at[target],
                r.mixed.at[pl.ds(pl.multiple_of(self.seq * slot, 16), slot)],
                (self.batch, target),
                base + step,
            )

        score_refs = (r.scores, r.scores_odd)

        def keep(step, parity):
            return pltpu.make_async_copy(
                r.probs.at[parity],
                r.kept_probs.at[self.far_first(step)],
                r.local_sems.at[len(Fetched._fields) + 2 + parity],
            )

        def own_scores(step, parity, start, top):
            target = self.far_first(step)
            queries = r.qh[pl.ds(pl.multiple_of(target * tokens, tokens), tokens)]
            scores = dot_nt(r.kh[start : start + tokens], queries)
            score_refs[parity][start : start + tokens] = scores
            part = jnp.max(scores.reshape(tokens // 8, 8, tokens), axis=0)
            top = part if top is None else jnp.maximum(top, part)
            if start + tokens == keys:
                r.tops[parity] = jnp.broadcast_to(jnp.max(top, axis=0, keepdims=True), (8, tokens))
            return top

        def finish(step, sums):
            target = self.far_first(step)
            inverse = 1.0 / sums[HEAD : HEAD + 1]
            mixed = jnp.where(iota((slot, 1), 0) < HEAD, sums * inverse, 0.0)
            r.mixed_full[target] = mixed
            r.mixed_send[target] = mixed.astype(LOW)
            r.inverse[target] = jnp.broadcast_to(inverse, (8, tokens))

        def half_step(step, parity, with_next, with_last, wait_kept):
            if wait_kept:
                keep(step - 2, parity).wait()
            offset = r.tops[parity, 0:1] * factor
            top = sums = None
            for start in range(0, keys, tokens):
                if with_next:
                    top = own_scores(step + 1, 1 - parity, start, top)
                for inner in range(start, start + tokens, LANES):
                    powers = jnp.exp2(score_refs[parity][inner : inner + LANES] * factor - offset)
                    r.probs[parity, inner : inner + LANES] = powers.astype(LOW)
                if with_last:
                    part = dot_nn(
                        r.vt[:, start : start + tokens], r.probs[1 - parity, start : start + tokens]
                    )
                    sums = part if sums is None else sums + part
            keep(step, parity).start()
            if with_last:
                finish(step - 1, sums)
                send(self.far_first(step - 1), step - 1).start()

        top = None
        for start in range(0, keys, tokens):
            top = own_scores(0, 0, start, top)
        half_step(0, 0, True, False, False)
        half_step(1, 1, True, True, False)

        def pair(number, carry):
            step = 2 + 2 * number
            half_step(step, 0, True, True, True)
            half_step(step + 1, 1, True, True, True)
            return carry

        lax.fori_loop(0, sz.seqs // 2 - 2, pair, 0)
        half_step(sz.seqs - 2, 0, True, True, True)
        half_step(sz.seqs - 1, 1, False, True, True)
        finish(sz.seqs - 1, dot_nn(r.vt[...], r.probs[1]))
        keep(sz.seqs - 2, 0).wait()
        keep(sz.seqs - 1, 1).wait()
        self.recall(0).start()
        r.mixed[pl.ds(pl.multiple_of(self.seq * slot, 16), slot)] = r.mixed_send[self.seq]
        for step in range(sz.seqs - 1):
            send(self.far_first(step), step).wait()

    def local_block(self):
        r, sz = self.r, self.sz
        tokens, channels = sz.tokens, sz.channels
        pad = sz.text_pad
        r.stream[...] = r.stream_in[...] + dot_tn(r.mixed[...], r.osp[...])
        for start, size in self.chunks(tokens):
            rows = slice(start, start + size)
            self.layer_norm(r.stream[rows], r.gain_cross, rows, r.normed_cross, r.hat_cross, r.scale_cross)
        r.query_text[...] = dot_nn(r.normed_cross[...], self.weight(self.r.query_cross)[...]).astype(LOW)
        r.cross[...] = dot_nt(r.text_key[...], r.query_text[...])
        for head in range(HEADS):
            rows = slice(head * pad, (head + 1) * pad)
            valid = iota((pad, 1), 0) < sz.text
            scores = jnp.where(valid, r.cross[rows] * self.scale, -1e30)
            powers = jnp.exp(scores - jnp.max(scores, axis=0, keepdims=True))
            attention = powers / jnp.sum(powers, axis=0, keepdims=True)
            r.cross[rows] = attention
            r.cross_low[rows] = attention.astype(LOW)
        r.cross_mixed[...] = dot_tn(r.cross_low[...], r.text_value[...]).astype(LOW)
        r.stream[...] = r.stream[...] + dot_nn(r.cross_mixed[...], self.weight(self.r.out_cross)[...])
        for start, size in self.chunks(tokens):
            rows = slice(start, start + size)
            self.layer_norm(r.stream[rows], r.gain_feed, rows, r.normed_feed, r.hat_feed, r.scale_feed)
        feed_up = self.weight(self.r.feed_up)
        joined = r.scores
        root = 0.7071067811865476
        block = 2 * LANES
        pieces = sz.hidden // block
        for piece in range(pieces):
            for place in (piece, piece + pieces):
                joined[place * tokens : (place + 1) * tokens] = dot_nn(
                    r.normed_feed[...], feed_up[:, place * block : (place + 1) * block]
                )
            for start, size in self.chunks(tokens):
                values = joined[piece * tokens + start : piece * tokens + start + size]
                gates_at = (piece + pieces) * tokens + start
                gates = joined[gates_at : gates_at + size]
                half = 0.5 * (1.0 + lax.erf(gates * root))
                slope = half + gates * (jnp.exp(-0.5 * gates * gates) * 0.3989422804014327)
                active = gates * half
                r.gated[start : start + size, piece * block : (piece + 1) * block] = (
                    values * active
                ).astype(LOW)
                joined[piece * tokens + start : piece * tokens + start + size] = active
                joined[gates_at : gates_at + size] = values * slope

        low = (
            r.stream[...] + dot_nt(r.gated[...], self.weight(self.r.feed_down)[...])
        ).astype(LOW)
        r.stream_low[...] = low
        project_out = self.weight(self.r.project_out)
        r.tmp[...] = dot_nn(r.stream_low[...], project_out[...])
        for start, size in self.chunks(tokens):
            rows = slice(start, start + size)
            wide = slice(start + sz.width, start + sz.width + size)
            mask = self.wide_mask(start + sz.width, size)
            r.output_own[rows] = (r.res6[wide] + r.tmp[rows]) * mask
            r.grad_branch[rows] = (r.cot6[wide] * mask).astype(LOW)
        self.put(r.output_own, r.output)
        r.grad[...] = dot_nt(r.grad_branch[...], project_out[...])
        r.grad_feed_low[...] = r.grad[...].astype(LOW)
        for piece in range(pieces):
            lanes = slice(piece * block, (piece + 1) * block)
            gate_lanes = slice(sz.hidden + piece * block, sz.hidden + (piece + 1) * block)
            r.grad_gated[...] = dot_nn(r.grad_feed_low[...], self.v.feed_down[:, lanes])
            for start, size in self.chunks(tokens):
                rows = slice(start, start + size)
                active = joined[piece * tokens + start : piece * tokens + start + size]
                gates_at = (piece + pieces) * tokens + start
                grads = r.grad_gated[rows]
                r.grad_joined[rows, lanes] = (grads * active).astype(LOW)
                r.grad_joined[rows, gate_lanes] = (grads * joined[gates_at : gates_at + size]).astype(LOW)
        r.tmp[...] = dot_nt(r.grad_joined[...], self.v.feed_up[...])
        self.layer_step(r.hat_feed, r.scale_feed, r.gain_feed, 3, r.grad_cross_low)
        r.grad_cross_mixed[...] = dot_nt(r.grad_cross_low[...], self.v.out_cross[...]).astype(LOW)
        r.scores[0 : HEADS * pad] = dot_nt(r.text_value[...], r.grad_cross_mixed[...])
        for head in range(HEADS):
            rows = slice(head * pad, (head + 1) * pad)
            attention = r.cross[rows]
            grads = r.scores[rows]
            delta = jnp.sum(attention * grads, axis=0, keepdims=True)
            r.cross_scores[rows] = (attention * (grads - delta)).astype(LOW)
        r.grad_query_text[...] = (
            dot_tn(r.cross_scores[...], r.text_key[...]) * self.scale
        ).astype(LOW)
        r.tmp[...] = dot_nt(r.grad_query_text[...], self.v.query_cross[...])
        self.layer_step(r.hat_cross, r.scale_cross, r.gain_cross, 4, r.grad_self_low)
        r.gm_send[...] = dot_nt(r.osp[...], r.grad_self_low[...]).astype(LOW)
        slot = sz.slot
        copies = [
            self.remote(
                r.gm_send.at[pl.ds(pl.multiple_of(other * slot, 16), slot)],
                r.gm.at[self.seq],
                (self.batch, other),
            )
            for other in self.seq_others
        ]
        self.start(copies)
        self.gm_copies = copies
        r.gm[self.seq] = r.gm_send[pl.ds(pl.multiple_of(self.seq * slot, 16), slot)]

    def layer_step(self, hat, scale, gain, place, target):
        r = self.r
        gains = None
        for start, size in self.chunks(self.sz.tokens):
            rows = slice(start, start + size)
            part, gain_part = self.layer_back(hat[rows], scale[rows, 0:1], r.tmp[rows], row_of(gain))
            total = r.grad[rows] + part
            r.grad[rows] = total
            target[rows] = total.astype(LOW)
            gains = gain_part if gains is None else gains + gain_part
        r.gain_parts[place : place + 1] = gains

    def text_grads(self):
        r, sz = self.r, self.sz
        pad = sz.text_pad
        head_of = floor_div(iota((1, sz.channels), 1), HEAD)
        keys = dot_nn(r.cross_scores[...], r.query_text[...]) * self.scale
        values = dot_nn(r.cross_low[...], r.grad_cross_mixed[...])
        packed = None
        for number, grads in enumerate((keys, values)):
            total = None
            for head in range(HEADS):
                part = jnp.where(head_of == head, grads[head * pad : (head + 1) * pad], 0.0)
                total = part if total is None else total + part
            part = dot_nn(total.astype(LOW), r.place[number])
            packed = part if packed is None else packed + part
        r.text_send[...] = packed.astype(LOW)
        copies = [
            self.remote(
                r.text_send.at[:, pl.ds(pl.multiple_of(other * LANES, LANES), LANES)],
                r.text_recv.at[self.seq],
                (self.batch, other),
            )
            for other in self.seq_others
        ]
        self.start(copies)
        r.text_recv[self.seq] = r.text_send[
            :, pl.ds(pl.multiple_of(self.seq * LANES, LANES), LANES)
        ]
        self.text_copies = copies

    def text_second(self):
        r = self.r
        self.wait(self.text_copies)
        total = r.text_recv[0].astype(F32)
        for place in range(1, self.sz.seqs):
            total = total + r.text_recv[place].astype(F32)
        r.text_sum[...] = total
        self.put(r.text_sum, r.text_total.at[self.batch])
        copies = self.to_batch(r.text_sum, r.text_total.at[self.batch])
        self.start(copies)
        self.text_copies = copies

    def store_pack(self, start, rows, values):
        for shard in range(self.sz.seqs):
            self.r.pack[shard % 2, shard // 2, start + rows.start : start + rows.stop] = values[
                :, shard * LANES : (shard + 1) * LANES
            ].astype(LOW)

    def early_grads(self):
        r, sz = self.r, self.sz
        channels = sz.channels
        rows = iota((2 * channels, 1), 0)
        target = jnp.where(rows >= channels, rows + (3 * LANES - channels), rows)
        spread = jnp.where(iota((1, 6 * LANES), 1) == target, 1.0, 0.0).astype(LOW)
        for z in range(sz.seqs // 2):
            wide = 2 * channels
            grads = dot_nn(r.grad_joined[:, z * wide : (z + 1) * wide], spread).astype(LOW)
            sums = dot_tn(r.normed_feed[...], grads)
            for tile in range(6):
                start = sz.start.up + (tile % 3) * channels
                r.pack[tile // 3, z, start : start + channels] = sums[
                    :, tile * LANES : (tile + 1) * LANES
                ].astype(LOW)
        size = sz.down_rows
        tail = sz.hidden - 2 * size
        placed = [dot_nn(r.grad_feed_low[...], r.place[number]).astype(LOW) for number in range(3)]
        sums = dot_tn(r.gated[:, 0:size], placed[0]) + dot_tn(r.gated[:, size : 2 * size], placed[1])
        extra = dot_tn(r.gated[:, 2 * size :], placed[2])
        self.store_pack(sz.start.down, slice(0, tail), sums[0:tail] + extra)
        self.store_pack(sz.start.down, slice(tail, size), sums[tail:])
        sums = (
            dot_tn(r.stream_low[...], dot_nn(r.grad_branch[...], r.place[0]).astype(LOW))
            + dot_tn(r.cross_mixed[...], dot_nn(r.grad_cross_low[...], r.place[1]).astype(LOW))
            + dot_tn(r.normed_cross[...], dot_nn(r.grad_query_text[...], r.place[2]).astype(LOW))
        )
        self.store_pack(sz.start.trio, slice(0, channels), sums)

    def recall(self, step):
        r = self.r
        return pltpu.make_async_copy(
            r.kept_probs.at[lax.rem(self.seq + step, self.sz.seqs)],
            r.probs.at[lax.rem(step, 2)],
            r.local_sems.at[len(Fetched._fields) + 2 + lax.rem(step, 2)],
        )

    def attention_back(self):
        r, sz = self.r, self.sz
        keys, tokens, slot = sz.keys, sz.tokens, sz.slot
        self.wait(self.gm_copies)
        base = self.used
        self.used += sz.seqs
        own_slot = pl.ds(pl.multiple_of(self.seq * slot, 16), slot)

        def send(step):
            target = lax.rem(self.seq + step, sz.seqs)
            return self.remote(
                r.dq_send.at[target], r.dq.at[own_slot], (self.batch, target), base + step
            )

        self.in_pieces += self.gather_rows(r.act_in, 2, sz.rows)
        r.scores[0:keys, 0:LANES] = jnp.zeros((keys, LANES), F32)
        row = iota((slot, 1), 0)
        to_values = jnp.where(
            (iota((slot, LANES), 0) + 2 * HEAD == iota((slot, LANES), 1))
            & (iota((slot, LANES), 0) < HEAD),
            1.0,
            0.0,
        ).astype(LOW)

        def block(step, carry):
            source = lax.rem(self.seq + step, sz.seqs)
            slot_now = lax.rem(step, 2)
            self.recall(step).wait()

            @pl.when(step < sz.seqs - 1)
            def _():
                self.recall(step + 1).start()

            scaled = (r.gm[source].astype(F32) * r.inverse[source, 0:1]).astype(LOW).astype(F32)
            delta = -jnp.sum(r.mixed_full[source] * scaled, axis=0, keepdims=True)
            high = delta.astype(LOW).astype(F32)
            middle = (delta - high).astype(LOW).astype(F32)
            rest = delta - high - middle
            extended = jnp.where(row == HEAD, high, scaled)
            extended = jnp.where(row == HEAD + 1, middle, extended)
            extended = jnp.where(row == HEAD + 2, rest, extended).astype(LOW)
            query_rows = pl.ds(pl.multiple_of(source * tokens, tokens), tokens)
            token_grads = dot_tn(scaled.astype(LOW), to_values).astype(LOW)
            queries = r.qkv[query_rows]
            grad_query = None
            for start in range(0, keys, tokens):
                rows = slice(start, start + tokens)
                grads = dot_nn(r.vh[rows], extended)
                powers = r.probs[slot_now, rows]
                low = (powers.astype(F32) * grads).astype(LOW)
                r.scores[rows, 0:LANES] += dot_nn(low, queries) + dot_nn(powers, token_grads)
                part = dot_nn(r.kt[:, rows], low)
                grad_query = part if grad_query is None else grad_query + part
            r.dq_send[source] = (grad_query * self.scale).astype(LOW)

            @pl.when(step > 0)
            def _():
                send(step).start()

            return carry

        lax.fori_loop(0, 2, block, 0)
        self.sums_batch(0)
        self.sums_batch(1)
        lax.fori_loop(2, sz.seqs, block, 0)
        factor = jnp.where(iota((1, LANES), 1) < 2 * HEAD, self.scale, 1.0)
        pick = jnp.where(
            iota((2 * HEAD, LANES), 1) == iota((2 * HEAD, LANES), 0) + HEAD, 1.0, 0.0
        ).astype(LOW)
        wide = 2 * HEAD
        for place in range(sz.seqs):
            rows = slice(place * tokens, (place + 1) * tokens)
            grads = (r.scores[rows, 0:LANES] * factor).astype(LOW)
            r.dkv_send[place * wide : (place + 1) * wide] = dot_nt(pick, grads).astype(LOW)
        own_wide = pl.ds(pl.multiple_of(self.seq * wide, 16), wide)
        copies = [
            self.remote(
                r.dkv_send.at[pl.ds(pl.multiple_of(other * wide, 16), wide)],
                r.dkv.at[own_wide],
                (self.batch, other),
            )
            for other in self.seq_others
        ]
        self.start(copies)
        r.dkv[own_wide] = r.dkv_send[own_wide]
        r.dq[own_slot] = r.dq_send[self.seq]
        self.gp_copies = copies + [send(step) for step in range(1, sz.seqs)]
        self.text_second()
        for start, size in self.chunks(sz.wide):
            rows = slice(start, start + size)
            r.normed_mid[rows], r.slope_mid[rows] = self.slope(r.mid6, 1, r.gain_mid, start, size)
        outer = dot_nn(r.mixed[...], dot_nn(r.grad_self_low[...], r.place[0]).astype(LOW))
        self.store_pack(sz.start.pair, slice(0, HEADS * slot), outer)

    def norm_sums(self, number, rows_of):
        first = second = None
        mean, inverse = self.norm(number)
        for start, size in self.chunks(self.sz.tokens):
            grads, values = rows_of(start, size)
            one, two = col_sum(grads), col_sum(grads * ((values - mean) * inverse))
            first = one if first is None else first + one
            second = two if second is None else second + two
        return first, second

    def norm_factors(self, number, gain, total):
        gains = row_of(gain)
        sums = self.grouped(total * gains) / self.count()
        mean, inverse = self.norm(number)
        return mean, inverse, gains * inverse, sums[0:1] * inverse, sums[1:2] * inverse

    def slope(self, source, number, gain, start, size):
        mean, inverse = self.norm(number)
        normed = (source[start : start + size] - mean) * inverse
        values = normed * row_of(gain)
        gate = sigmoid(values)
        return normed, gate * (1.0 + values * (1.0 - gate)) * self.wide_mask(start, size)

    def residual_back(self):
        r, sz = self.r, self.sz
        width, tokens, channels = sz.width, sz.tokens, sz.channels
        self.wait(self.gp_copies)
        r.tmp[...] = dot_tn(r.dq[...], r.query_rows[...]) + dot_tn(r.dkv[...], r.value_rows[...])
        self.layer_step(r.hat_self, r.scale_self, r.gain_self, 5, r.grad_in_low)
        r.gblk6[width : width + tokens] = dot_nt(r.grad_in_low[...], self.v.project_in[...])
        halo = self.halo(r.gblk6)
        halo.start()

        def block_rows(start, size):
            wide = slice(start + width, start + width + size)
            return r.gblk6[wide], r.res6[wide]

        self.stats_store(3, self.norm_sums(2, block_rows))
        stats = self.stats_start(3)
        self.wait(self.late)
        self.late = []
        self.gather_in = self.gather_forward(r.act_in, self.in_pieces)
        self.sums_cross(0)
        self.sums_cross(1)
        self.middle_grads()
        self.sums_core(2)
        halo.wait()
        self.wait(stats)
        total = self.stats_total(3)
        r.gain_parts[2:3] = total[1:2]
        mean, inverse, factor, first, second = self.norm_factors(2, r.gain_block, total)
        for start, size in self.chunks(sz.wide):
            rows = slice(start, start + size)
            mask = self.wide_mask(start, size)
            normed = (r.res6[rows] - mean) * inverse
            grads = r.cot6[rows] * mask + r.gblk6[rows] * factor - mask * (first + normed * second)
            r.cot6[rows] = grads
            self.shifts(r.shift_grad, start, size, grads * self.inside_mask(start, size))
        near = [self.remote(r.shift_grad.at[1, pl.ds(width, tokens)], r.near_grads, self.partner)]
        self.start(near)
        r.gact6[width : width + tokens] = self.conv_back(r.shift_grad, self.v.conv_second)
        halo = self.halo(r.gact6)
        halo.start()

        def mid_rows(start, size):
            wide = slice(start + width, start + width + size)
            return r.gact6[wide] * r.slope_mid[wide], r.mid6[wide]

        self.stats_store(4, self.norm_sums(1, mid_rows))
        stats = self.stats_start(4)
        self.sums_batch(2)
        self.sums_z(0)
        self.wait(near)
        self.conv_pack(sz.start.second)
        self.start(self.stages[3][1])
        halo.wait()
        self.wait(stats)
        total = self.stats_total(4)
        r.gain_parts[1:2] = total[1:2]
        mean, inverse, factor, first, second = self.norm_factors(1, r.gain_mid, total)
        time_total = None
        for start, size in self.chunks(sz.wide):
            rows = slice(start, start + size)
            grads = r.gact6[rows] * r.slope_mid[rows] * factor - self.wide_mask(start, size) * (
                first + r.normed_mid[rows] * second
            )
            self.shifts(r.shift_grad, start, size, grads)
            if width <= start < width + tokens:
                part = col_sum(grads)
                time_total = part if time_total is None else time_total + part
        first_copies = self.conv_send(r.shift_grad, r.first_send, r.first_grads)
        r.gblk6[width : width + tokens] = self.conv_back(r.shift_grad, self.v.conv_first)

        def in_rows(start, size):
            wide = slice(start + width, start + width + size)
            normed, slope = self.slope(r.lat6, 0, r.gain_in, start + width, size)
            return r.gblk6[wide] * slope, r.lat6[wide]

        parts = r.gain_parts
        self.stats_store(5, self.norm_sums(0, in_rows))
        stats = self.stats_start(5)
        r.extra_send[...] = jnp.zeros(r.extra_send.shape, F32)
        r.extra_send[2:3] = time_total
        r.extra_send[3:6] = parts[3:6]
        r.extra_recv[self.seq] = r.extra_send[...]
        extras = self.to_seq(lambda other: r.extra_send, r.extra_recv.at[self.seq])
        self.start(extras)
        self.sums_gather(0)
        self.sums_cross(2)
        self.sums_z(1)
        self.sums_cross(3)
        self.sums_z(2)
        first_copies = self.conv_grads(
            first_copies, self.gather_in, r.first_grads, r.act_in, r.first_part, r.first_recv
        )
        self.wait(stats)
        total = self.stats_total(5)
        mean, inverse, factor, first, second = self.norm_factors(0, r.gain_in, total)
        self.wait(extras)
        sums = r.extra_recv[0]
        for place in range(1, sz.seqs):
            sums = sums + r.extra_recv[place]
        r.final_send[...] = sums
        r.final_send[1:2] = total[1:2]
        r.final_send[0:1] = parts[1:2]
        r.final_send[6:7] = parts[2:3]
        self.put(r.final_send, r.final_recv.at[self.batch])
        self.final_copies = self.to_batch(r.final_send, r.final_recv.at[self.batch])
        self.start(self.final_copies)
        for start, size in self.chunks(tokens):
            wide = slice(start + width, start + width + size)
            normed, slope = self.slope(r.lat6, 0, r.gain_in, start + width, size)
            r.latent_own[start : start + size] = (
                r.cot6[wide]
                + r.gblk6[wide] * slope * factor
                - self.wide_mask(start + width, size) * (first + normed * second)
            )
        self.put(r.latent_own, r.latent_grad)
        self.sums_gather(1)
        self.sums_z(3)
        first_copies = self.conv_gather(first_copies, r.first_part, r.first_recv, r.conv_first_sum)
        self.sums_gather(2)
        self.sums_gather(3)
        self.wait(first_copies)

    def middle_grads(self):
        r, sz = self.r, self.sz
        queries = dot_nn(r.dq[...], r.normed_self[...]).astype(LOW)
        values = dot_nn(r.dkv[...], r.normed_self[...]).astype(LOW)
        slot, wide = sz.slot, 2 * HEAD
        for shard in range(sz.seqs):
            for tile, (start, size) in enumerate(self.lane_tiles()):
                target = r.pack.at[shard % 2, shard // 2]
                at = sz.start.heads + tile * LANES
                if size < LANES:
                    target[at : at + LANES] = jnp.zeros((LANES, LANES), LOW)
                lanes = slice(start, start + size)
                target[at : at + slot, 0:size] = queries[shard * slot : (shard + 1) * slot, lanes]
                target[at + slot : at + LANES, 0:size] = values[shard * wide : (shard + 1) * wide, lanes]
        inner = dot_tn(r.normed_block[...], dot_nn(r.grad_in_low[...], r.place[1]).astype(LOW))
        for shard in range(sz.seqs):
            rows = slice(sz.start.pair, sz.start.pair + sz.channels)
            outer = r.pack[shard % 2, shard // 2, rows].astype(F32)
            lanes = slice(shard * LANES, (shard + 1) * LANES)
            r.pack[shard % 2, shard // 2, rows] = (outer + inner[:, lanes]).astype(LOW)

    def conv_pack(self, start):
        r, sz = self.r, self.sz
        own = r.shift_grad[1, sz.width : sz.width + sz.tokens]
        placed = [dot_nn(own, r.place_half[number]).astype(LOW) for number in range(3)]
        near = [dot_nn(r.near_grads[...], r.place_half[number]).astype(LOW) for number in range(3)]
        for col in range(3):
            total = None
            for row in range(3):
                rows = slice(row * sz.width, row * sz.width + sz.tokens)
                part = dot_tn(r.shifted[col, rows], placed[row])
                part = part + dot_tn(r.near_shifted[col, rows], near[row])
                total = part if total is None else total + part
            at = start + col * sz.channels
            for z in range(sz.seqs // 2):
                r.recv_core[z, at : at + sz.channels] = total[:, z * LANES : (z + 1) * LANES].astype(LOW)

    def sums_setup(self):
        r, sz = self.r, self.sz
        half, batches = sz.seqs // 2, sz.batches
        self.stages = []
        for start, size in sz.chunks:
            rows = pl.ds(start, size)
            part = size // batches
            quarter = pl.ds(start // batches, part)
            one = []
            if start < sz.start.second:
                one.append(
                    self.remote(r.pack.at[1 - self.core, :, rows], r.recv_core.at[:, rows], self.partner)
                )
            pair = half // 2
            x_rows = pl.ds(pl.multiple_of(start + 2 * (1 - self.batch_x) * part, 16), 2 * part)
            y_rows = pl.ds(pl.multiple_of(start + 2 * (1 - self.batch_y) * part, 16), 2 * part)
            two = [
                self.remote(
                    r.recv_core.at[pl.ds(place * pair, pair), far_rows],
                    r.recv_first.at[place, :, pl.ds(start // 2, 2 * part)],
                    peer,
                )
                for place, (far_rows, peer) in enumerate(((x_rows, self.x_peer), (y_rows, self.y_peer)))
            ]
            far_y = 2 * self.batch_x + 1 - self.batch_y
            far_x = 2 * self.batch_y + 1 - self.batch_x
            cross = [
                self.remote(
                    r.recv_core.at[
                        pl.ds(place * pair, pair), pl.ds(pl.multiple_of(start + far * part, 16), part)
                    ],
                    r.recv_second.at[pl.ds(place * pair, pair), quarter],
                    peer,
                )
                for place, (far, peer) in enumerate(((far_y, self.y_peer), (far_x, self.x_peer)))
            ]
            three = [
                self.remote(
                    r.recv_second.at[other, quarter],
                    r.recv_z.at[step, quarter],
                    (self.batch, other * 2 + self.core),
                )
                for step, other in enumerate(self.z_others)
            ]
            own = pl.ds(pl.multiple_of(start + self.quarter_of(self.z_pos) * part, 16), part)
            four = self.to_batch(r.sum_own.at[quarter], r.gathered.at[own])
            self.stages.append((one, two, cross, three, four))

    def quarter_of(self, z):
        second = z // (self.sz.seqs // 4)
        x, y = self.batch_x, self.batch_y
        return (1 - second) * (2 * x + y) + second * (2 * y + x)

    def sums_core(self, number):
        self.start(self.stages[number][0])

    def sums_batch(self, number):
        r, sz = self.r, self.sz
        start, size = sz.chunks[number]
        self.wait(self.stages[number][0])

        @pl.loop(0, sz.seqs // 2)
        def add(z):
            rows = pl.ds(start, size)
            r.recv_core[z, rows] = (
                r.pack[self.core, z, rows].astype(F32) + r.recv_core[z, rows].astype(F32)
            ).astype(LOW)

        self.start(self.stages[number][1])

    def sums_cross(self, number):
        r, sz = self.r, self.sz
        start, size = sz.chunks[number]
        part = size // sz.batches
        pair = sz.seqs // 4
        self.wait(self.stages[number][1])

        def add(target, source):
            r.recv_core[target] = (r.recv_core[target].astype(F32) + source.astype(F32)).astype(LOW)

        @pl.loop(0, pair)
        def sums(z):
            for place, near in enumerate((self.batch_x, self.batch_y)):
                rows = pl.ds(pl.multiple_of(start + 2 * near * part, 16), 2 * part)
                add((z + place * pair, rows), r.recv_first[place, z, pl.ds(start // 2, 2 * part)])

        self.start(self.stages[number][2])

    def sums_z(self, number):
        r, sz = self.r, self.sz
        start, size = sz.chunks[number]
        part = size // sz.batches
        quarter = pl.ds(start // sz.batches, part)
        self.wait(self.stages[number][2])

        @pl.loop(0, sz.seqs // 2)
        def add(z):
            own = r.recv_core[z, pl.ds(pl.multiple_of(start + self.quarter_of(z) * part, 16), part)]
            r.recv_second[z, quarter] = (
                own.astype(F32) + r.recv_second[z, quarter].astype(F32)
            ).astype(LOW)

        self.start(self.stages[number][3])

    def sums_gather(self, number):
        r, sz = self.r, self.sz
        start, size = sz.chunks[number]
        part = size // sz.batches
        quarter = pl.ds(start // sz.batches, part)
        self.wait(self.stages[number][3])
        total = r.recv_second[self.z_pos, quarter].astype(F32)
        for step in range(sz.seqs // 2 - 1):
            total = total + r.recv_z[step, quarter].astype(F32)
        own = pl.ds(pl.multiple_of(start + self.quarter_of(self.z_pos) * part, 16), part)
        r.sum_own[quarter] = total.astype(LOW)
        self.put(r.sum_own.at[quarter], r.gathered.at[own])
        self.start(self.stages[number][4])

    def run(self):
        self.entry()
        self.sums_setup()
        self.residual()
        self.attention()
        self.in_pieces += self.gather_rows(self.r.act_in, 1, 2)
        self.local_block()
        self.text_grads()
        self.early_grads()
        self.sums_core(0)
        self.sums_core(1)
        self.attention_back()
        self.residual_back()
        for stages in self.stages:
            self.wait(stages[4])
        self.wait(self.text_copies)
        self.wait(self.final_copies)
        self.wait(self.puts)
        assert self.used <= SEMAPHORES


def fused_call(sz, operands):
    t, c = sz.tokens, sz.channels
    outs = dict(
        output=((t, c), F32),
        latent_grad=((t, c), F32),
        final_recv=((sz.batches, 8, c), F32),
        time_all=((sz.batches, 8, sz.emb), F32),
        text_all=((sz.batches, sz.text_pad, sz.context), LOW),
        text_total=((sz.batches, sz.text_pad, LANES), F32),
        gathered=((sz.pack_rows, LANES), LOW),
        conv_first_sum=((sz.conv_rows, c), LOW),
        kept_probs=((sz.seqs, sz.keys, t), LOW),
    )
    scratch = buffers(sz)
    vmem = pl.BlockSpec(memory_space=pltpu.VMEM)
    anywhere = pl.BlockSpec(memory_space=pl.ANY)
    fetched = [getattr(operands, name) for name in Fetched._fields]
    specs = operands._replace(**{name: vmem for name in Inputs._fields})
    specs = specs._replace(**{name: anywhere for name in Fetched._fields})
    specs = specs._replace(
        latents=anywhere, cotangent=anywhere, heights=pl.BlockSpec(memory_space=pltpu.SMEM)
    )
    names = list(Inputs._fields) + list(outs) + list(scratch)
    shapes = [pltpu.VMEM(shape, kind) for shape, kind in scratch.values()]
    shapes += [pltpu.VMEM(operand.shape, operand.dtype) for operand in fetched]
    shapes += [pltpu.SemaphoreType.DMA((2, SEMAPHORES)), pltpu.SemaphoreType.DMA((len(fetched) + 24,))]

    def body(*refs):
        count = len(names)
        named = types.SimpleNamespace(**dict(zip(names, refs[:count])))
        named.sems, named.local_sems = refs[-2:]
        Fused(sz, named, Fetched(*refs[count:-2])).run()

    return pl.pallas_call(
        body,
        out_shape=tuple(jax.ShapeDtypeStruct(shape, kind) for shape, kind in outs.values()),
        in_specs=list(specs),
        out_specs=(anywhere,) * len(outs),
        scratch_shapes=shapes,
        compiler_params=pltpu.CompilerParams(
            collective_id=5, has_side_effects=True, vmem_limit_bytes=63 << 20
        ),
    )(*operands)


class Outputs(typing.NamedTuple):
    output: typing.Any
    latent_grad: typing.Any
    gain_in: typing.Any
    conv_first: typing.Any
    time_weight: typing.Any
    gain_mid: typing.Any
    conv_second: typing.Any
    gain_block: typing.Any
    project_in: typing.Any
    gain_self: typing.Any
    query_self: typing.Any
    key_self: typing.Any
    value_self: typing.Any
    out_self: typing.Any
    gain_cross: typing.Any
    query_cross: typing.Any
    key_cross: typing.Any
    value_cross: typing.Any
    out_cross: typing.Any
    gain_feed: typing.Any
    feed_up: typing.Any
    feed_down: typing.Any
    project_out: typing.Any


class Large(typing.NamedTuple):
    feed_up: typing.Any
    feed_down: typing.Any
    conv_second: typing.Any
    conv_first: typing.Any
    key_cross: typing.Any
    value_cross: typing.Any
    time_weight: typing.Any


LARGE = Large._fields


def unpack_kernel(sz, count, *refs):
    given = refs[:count]
    outs = Outputs(*refs[count : count + len(Outputs._fields)])
    held = refs[count + len(Outputs._fields) : -1]
    sems = refs[-1]
    channels = sz.channels
    pending = []

    def move(source, target):
        pending.append(pltpu.make_async_copy(source, target, sems.at[len(pending)]))
        pending[-1].start()
        return pending[-1]

    order = (6, 7, 0, 1, 2, 3, 4, 5)
    loads = {place: move(given[place], held[place]) for place in order}
    output, latent_grad, final_recv, time_all, text_all, text_total, gathered, first_sum = held[:count]
    finals = outs
    outs = outs._replace(**dict(zip(LARGE, held[count:])))
    moves = []
    loads[6].wait()
    eye = jnp.where(iota((LANES, LANES), 0) == iota((LANES, LANES), 1), 1.0, 0.0).astype(LOW)

    def turned(start, rows):
        return dot_nt(eye, gathered[start : start + rows])

    def three(values, *targets):
        for place, target in enumerate(targets):
            target[...] = values[place * HEAD : (place + 1) * HEAD]

    for tile in range(3):
        lanes = slice(tile * LANES, min((tile + 1) * LANES, outs.feed_up.shape[1]))
        start = sz.start.up + tile * channels
        outs.feed_up[:, lanes] = gathered[start : start + channels, : lanes.stop - lanes.start].astype(F32)
    values = turned(sz.start.down, sz.down_rows)
    for place in range(3):
        lanes = slice(place * sz.down_rows, min((place + 1) * sz.down_rows, sz.hidden))
        outs.feed_down[:, lanes] = values[
            place * HEAD : (place + 1) * HEAD, : lanes.stop - lanes.start
        ]
    moves.append(move(outs.feed_up, finals.feed_up))
    moves.append(move(outs.feed_down, finals.feed_down))
    three(turned(sz.start.trio, channels), outs.project_out, outs.out_cross, outs.query_cross)
    for tile in range(sz.sizes.heads // LANES):
        lanes = slice(tile * LANES, min((tile + 1) * LANES, channels))
        start = sz.start.heads + tile * LANES
        values = gathered[start : start + LANES].astype(F32)[:, : lanes.stop - lanes.start]
        outs.query_self[:, lanes] = values[:HEAD]
        outs.key_self[:, lanes] = values[sz.slot : sz.slot + HEAD]
        outs.value_self[:, lanes] = values[sz.slot + HEAD :]
    outs.project_in[...] = turned(sz.start.pair, channels)[HEAD : 2 * HEAD]
    wide = turned(sz.start.pair, HEADS * sz.slot)[:HEAD].astype(LOW)
    source = iota((1, channels), 1)
    target = source + (sz.slot - HEAD) * floor_div(source, HEAD)
    squeeze = jnp.where(iota((HEADS * sz.slot, 1), 0) == target, 1.0, 0.0).astype(LOW)
    outs.out_self[...] = dot_nn(wide, squeeze)
    for col in range(3):
        values = turned(sz.start.second + col * channels, channels)
        for row in range(3):
            outs.conv_second[row, col] = values[row * HEAD : (row + 1) * HEAD]
    moves.append(move(outs.conv_second, finals.conv_second))
    loads[0].wait()
    moves.append(move(output, finals.output))
    loads[1].wait()
    moves.append(move(latent_grad, finals.latent_grad))
    loads[7].wait()
    for row in range(3):
        values = first_sum[row * LANES : (row + 1) * LANES].astype(F32)
        for col in range(3):
            outs.conv_first[row, col] = values[col * HEAD : (col + 1) * HEAD]
    moves.append(move(outs.conv_first, finals.conv_first))
    for place in range(2, 6):
        loads[place].wait()
    text = None
    for place in range(sz.batches):
        grads = text_total[place]
        high = grads.astype(LOW)
        rest = (grads - high.astype(F32)).astype(LOW)
        part = dot_tn(high, text_all[place]) + dot_tn(rest, text_all[place])
        text = part if text is None else text + part
    three(text, outs.key_cross, outs.value_cross)
    moves.append(move(outs.key_cross, finals.key_cross))
    moves.append(move(outs.value_cross, finals.value_cross))
    pick = jnp.where(
        (iota((channels, LANES), 0) == iota((channels, LANES), 1) + lax.axis_index(SEQ) * HEAD)
        & (iota((channels, LANES), 1) < HEAD),
        1.0,
        0.0,
    ).astype(LOW)
    total = time = None
    for place in range(sz.batches):
        rows = final_recv[place]
        total = rows if total is None else total + rows
        picked = dot_nn(split_three(jnp.where(iota((8, 1), 0) == 2, rows, 0.0)), pick)
        act = time_all[place]
        act = pltpu.roll(act, 2, 0)
        part = dot_tn(picked.astype(LOW), jnp.concatenate([act, act, act], axis=0).astype(LOW))
        time = part if time is None else time + part
    outs.time_weight[...] = time[:HEAD]
    moves.append(move(outs.time_weight, finals.time_weight))
    gains = sum_three(dot_nn(split_three(total), pick))
    order = (
        outs.gain_mid,
        outs.gain_in,
        None,
        outs.gain_feed,
        outs.gain_cross,
        outs.gain_self,
        outs.gain_block,
    )
    for place, out in enumerate(order):
        if out is not None:
            out[...] = gains[place : place + 1, :HEAD]
    for one in moves:
        one.wait()


def unpack_call(sz, results):
    channels, hidden = sz.channels, sz.hidden
    square = jax.ShapeDtypeStruct((HEAD, channels), F32)
    gain = jax.ShapeDtypeStruct((1, HEAD), F32)
    image = jax.ShapeDtypeStruct((sz.tokens, channels), F32)
    conv = jax.ShapeDtypeStruct((3, 3, HEAD, channels), F32)
    context = jax.ShapeDtypeStruct((HEAD, sz.context), F32)
    shapes = Outputs(*[square] * len(Outputs._fields))._replace(
        output=image,
        latent_grad=image,
        gain_in=gain,
        gain_mid=gain,
        gain_block=gain,
        gain_self=gain,
        gain_cross=gain,
        gain_feed=gain,
        conv_first=conv,
        conv_second=conv,
        time_weight=jax.ShapeDtypeStruct((HEAD, sz.emb), F32),
        key_cross=context,
        value_cross=context,
        feed_up=jax.ShapeDtypeStruct((channels, 2 * hidden // sz.seqs), F32),
        feed_down=jax.ShapeDtypeStruct((HEAD, hidden), F32),
    )
    vmem = pl.BlockSpec(memory_space=pltpu.VMEM)
    anywhere = pl.BlockSpec(memory_space=pl.ANY)
    specs = Outputs(*[vmem] * len(shapes))._replace(**{name: anywhere for name in LARGE})
    specs = specs._replace(output=anywhere, latent_grad=anywhere)
    held = list(results) + [getattr(shapes, name) for name in LARGE]
    return Outputs(
        *pl.pallas_call(
            lambda *refs: unpack_kernel(sz, len(results), *refs),
            out_shape=tuple(shapes),
            in_specs=[anywhere] * len(results),
            out_specs=tuple(specs),
            scratch_shapes=[pltpu.VMEM(one.shape, one.dtype) for one in held]
            + [pltpu.SemaphoreType.DMA((len(results) + len(LARGE) + 2,))],
            compiler_params=pltpu.CompilerParams(vmem_limit_bytes=60 << 20),
        )(*results)
    )


def fast_device(*arguments):
    given = Inputs(*arguments)
    latents = given.latents
    sz = Sizes(
        lax.axis_size(BATCH),
        lax.axis_size(SEQ),
        latents,
        given.time_vector,
        given.text_states,
        given.feed_down,
    )
    channels = sz.channels
    flat = given._replace(
        latents=latents.reshape(sz.tokens, channels),
        cotangent=given.cotangent.reshape(sz.tokens, channels),
        text_states=given.text_states.reshape(sz.text, sz.context),
        time_weight=given.time_weight.T,
        key_cross=given.key_cross.T,
        value_cross=given.value_cross.T,
        feed_down=given.feed_down.T,
    )
    results = fused_call(sz, flat)[:-1]
    outs = unpack_call(sz, results)
    shaped = outs._replace(
        output=outs.output.reshape(latents.shape), latent_grad=outs.latent_grad.reshape(latents.shape)
    )
    shaped = [jnp.swapaxes(one, -2, -1) if one.shape[-2] == HEAD else one for one in shaped]
    return tuple(one.reshape(-1) if one.shape[0] == 1 and one.ndim == 2 else one for one in shaped)


def on_device(
    latents,
    heights,
    time_vector,
    text_states,
    gain_in,
    conv_first,
    time_weight,
    gain_mid,
    conv_second,
    gain_block,
    project_in,
    gain_self,
    query_self,
    key_self,
    value_self,
    out_self,
    gain_cross,
    query_cross,
    key_cross,
    value_cross,
    out_cross,
    gain_feed,
    feed_up,
    feed_down,
    project_out,
    cotangent,
):
    images_in, rows_in, col_count, channels = latents.shape
    seq_size = lax.axis_size(SEQ)
    seq_index = lax.axis_index(SEQ)
    block_rows = rows_in * col_count
    keys_count = block_rows * seq_size
    score_scale = HEAD ** (-0.5)
    row_ids = seq_index * rows_in + jnp.arange(rows_in, dtype=jnp.int32)

    def spread_fn(values):
        return values

    def pick_fn(values):
        return values

    images, row_count = (latents.shape[0], latents.shape[1])
    tok_rows = row_count * col_count
    tokens = images * tok_rows
    row_valid = (row_ids[None, :] < heights[:, None]).astype(jnp.int32)
    row_mask = row_valid.astype(jnp.float32)
    cell_mask = row_mask[:, :, None, None]
    key_rows = jnp.arange(keys_count, dtype=jnp.int32) // col_count
    key_mask = (key_rows[None, :] < heights[:, None]).astype(jnp.int32)
    cell_counts = (heights * (col_count * (channels // GROUPS))).astype(jnp.float32)

    def res_piece(values, norm_gain, sum_first, sum_second):
        return (
            jax.nn.silu(group_apply(values, norm_gain, sum_first, sum_second, cell_counts))
            * cell_mask
        )

    def block_piece(values, norm_gain, sum_first, sum_second):
        return group_apply(values, norm_gain, sum_first, sum_second, cell_counts)

    first_in, second_in = norm_stats(latents, row_mask, spread_fn, pick_fn)
    act_in = res_piece(latents, gain_in, first_in, second_in).astype(jnp.bfloat16)
    padded_in = rows_halo(act_in)
    conv_out = conv_rows(padded_in, conv_first)
    time_act = jax.nn.silu(time_vector.astype(jnp.float32)).astype(jnp.bfloat16)
    time_term = jnp.dot(time_act, time_weight, preferred_element_type=jnp.float32)
    mid_in = conv_out + time_term[:, None, None, :]
    first_mid, second_mid = norm_stats(mid_in, row_mask, spread_fn, pick_fn)
    act_mid = res_piece(mid_in, gain_mid, first_mid, second_mid).astype(jnp.bfloat16)
    padded_mid = rows_halo(act_mid)
    resid = latents + conv_rows(padded_mid, conv_second)
    first_block, second_block = norm_stats(resid, row_mask, spread_fn, pick_fn)
    normed_block = (
        block_piece(resid, gain_block, first_block, second_block)
        .reshape(tokens, channels)
        .astype(jnp.bfloat16)
    )
    stream_in = jnp.dot(normed_block, project_in, preferred_element_type=jnp.float32)
    normed_self = layer_norm(stream_in, gain_self).astype(jnp.bfloat16)
    joined_self = jnp.concatenate((query_self, key_self, value_self), axis=1)
    projected = (
        jnp.dot(normed_self, joined_self, preferred_element_type=jnp.float32)
        .astype(jnp.bfloat16)
        .reshape(images, tok_rows, 3 * channels)
    )
    queries = projected[:, :, :channels]
    keys_local = projected[:, :, channels : 2 * channels]
    values_local = projected[:, :, 2 * channels :]
    keys_all = lax.all_gather(keys_local, SEQ, axis=1, tiled=True)
    values_all = lax.all_gather(values_local, SEQ, axis=1, tiled=True)

    def forward_image(bundle):
        image_queries, image_keys, image_values, image_mask = bundle
        query_blocks = image_queries.reshape(-1, block_rows, channels)
        return lax.map(
            lambda part: self_forward((part, image_keys, image_values, image_mask), score_scale),
            query_blocks,
        )

    attn_mixed, log_totals = lax.map(forward_image, (queries, keys_all, values_all, key_mask))
    mixed_flat = attn_mixed.reshape(tokens, channels)
    stream_self = stream_in + jnp.dot(mixed_flat, out_self, preferred_element_type=jnp.float32)
    normed_cross = layer_norm(stream_self, gain_cross).astype(jnp.bfloat16)
    query_text = (
        jnp.dot(normed_cross, query_cross, preferred_element_type=jnp.float32)
        .astype(jnp.bfloat16)
        .reshape(images, tok_rows, HEADS, HEAD)
    )
    text_flat = text_states.reshape(-1, text_states.shape[2])
    text_pairs = (
        jnp.dot(
            text_flat,
            jnp.concatenate((key_cross, value_cross), axis=1),
            preferred_element_type=jnp.float32,
        )
        .astype(jnp.bfloat16)
        .reshape(images, -1, 2, HEADS, HEAD)
    )
    text_keys = text_pairs[:, :, 0]
    text_values = text_pairs[:, :, 1]
    cross_scores = (
        jnp.einsum("iqhd,ikhd->ihqk", query_text, text_keys, preferred_element_type=jnp.float32)
        * score_scale
    )
    cross_attn = jnp.exp(cross_scores - jax.nn.logsumexp(cross_scores, axis=-1, keepdims=True))
    cross_low = cross_attn.astype(jnp.bfloat16)
    cross_mixed = (
        jnp.einsum("ihqk,ikhd->iqhd", cross_low, text_values, preferred_element_type=jnp.float32)
        .astype(jnp.bfloat16)
        .reshape(tokens, channels)
    )
    stream_cross = stream_self + jnp.dot(cross_mixed, out_cross, preferred_element_type=jnp.float32)
    normed_feed = layer_norm(stream_cross, gain_feed).astype(jnp.bfloat16)
    joined_feed = jnp.dot(normed_feed, feed_up, preferred_element_type=jnp.float32)
    gated = geglu(joined_feed).astype(jnp.bfloat16)
    stream_feed = stream_cross + jnp.dot(gated, feed_down, preferred_element_type=jnp.float32)
    stream_low = stream_feed.astype(jnp.bfloat16)
    branch_out = jnp.dot(stream_low, project_out, preferred_element_type=jnp.float32).reshape(
        images, row_count, col_count, channels
    )
    output = (resid + branch_out) * cell_mask
    grad_output = cotangent * cell_mask
    grad_branch = grad_output.reshape(tokens, channels).astype(jnp.bfloat16)
    grad_project_out = grad_dot(stream_low, grad_branch)
    grad_stream = back_dot(grad_branch, project_out)
    grad_feed_low = grad_stream.astype(jnp.bfloat16)
    grad_feed_down = grad_dot(gated, grad_feed_low)
    grad_gated = back_dot(grad_feed_low, feed_down)
    unused, pull_geglu = jax.vjp(geglu, joined_feed)
    grad_joined = pull_geglu(grad_gated)[0].astype(jnp.bfloat16)
    grad_feed_up = grad_dot(normed_feed, grad_joined)
    unused, pull_norm = jax.vjp(layer_norm, stream_cross, gain_feed)
    grad_part, grad_gain_feed = pull_norm(back_dot(grad_joined, feed_up))
    grad_stream = grad_stream + grad_part
    grad_cross_low = grad_stream.astype(jnp.bfloat16)
    grad_out_cross = grad_dot(cross_mixed, grad_cross_low)
    grad_cross_mixed = (
        back_dot(grad_cross_low, out_cross)
        .astype(jnp.bfloat16)
        .reshape(images, tok_rows, HEADS, HEAD)
    )
    grad_text_values = jnp.einsum(
        "ihqk,iqhd->ikhd", cross_low, grad_cross_mixed, preferred_element_type=jnp.float32
    )
    grad_cross_attn = jnp.einsum(
        "iqhd,ikhd->ihqk", grad_cross_mixed, text_values, preferred_element_type=jnp.float32
    )
    cross_delta = jnp.sum(cross_attn * grad_cross_attn, axis=-1, keepdims=True)
    grad_cross_scores = (cross_attn * (grad_cross_attn - cross_delta)).astype(jnp.bfloat16)
    grad_query_text = (
        (
            jnp.einsum(
                "ihqk,ikhd->iqhd", grad_cross_scores, text_keys, preferred_element_type=jnp.float32
            )
            * score_scale
        )
        .astype(jnp.bfloat16)
        .reshape(tokens, channels)
    )
    grad_text_keys = (
        jnp.einsum(
            "ihqk,iqhd->ikhd", grad_cross_scores, query_text, preferred_element_type=jnp.float32
        )
        * score_scale
    )
    text_wide = text_flat.astype(jnp.float32)
    grad_key_cross = exact_grad_dot(text_wide, grad_text_keys.reshape(-1, channels))
    grad_value_cross = exact_grad_dot(text_wide, grad_text_values.reshape(-1, channels))
    grad_query_cross = grad_dot(normed_cross, grad_query_text)
    unused, pull_norm = jax.vjp(layer_norm, stream_self, gain_cross)
    grad_part, grad_gain_cross = pull_norm(back_dot(grad_query_text, query_cross))
    grad_stream = grad_stream + grad_part
    grad_self_low = grad_stream.astype(jnp.bfloat16)
    grad_out_self = grad_dot(mixed_flat, grad_self_low)
    grad_mixed = (
        back_dot(grad_self_low, out_self).astype(jnp.bfloat16).reshape(images, tok_rows, channels)
    )

    def backward_image(bundle):
        image_queries, image_grads, image_totals, image_keys, image_values, image_mask = bundle
        query_blocks = image_queries.reshape(-1, block_rows, channels)
        grad_blocks = image_grads.reshape(-1, block_rows, channels)
        return lax.map(
            lambda part: query_side(
                (part[0], part[1], part[2], image_keys, image_values, image_mask), score_scale
            ),
            (query_blocks, grad_blocks, image_totals),
        )

    grad_queries, kept_attn, kept_grads = lax.map(
        backward_image, (queries, grad_mixed, log_totals, keys_all, values_all, key_mask)
    )
    grads_four = grad_mixed.reshape(images, -1, block_rows, HEADS, HEAD)
    queries_four = queries.reshape(images, -1, block_rows, HEADS, HEAD)
    row_total = tok_rows * lax.axis_size(SEQ)
    value_terms = jnp.einsum(
        "inhqk,inqhd->kihd", kept_attn, grads_four, preferred_element_type=jnp.float32
    )
    key_terms_part = (
        jnp.einsum(
            "inhqk,inqhd->kihd", kept_grads, queries_four, preferred_element_type=jnp.float32
        )
        * score_scale
    )
    summed = lax.psum_scatter(
        jnp.stack(
            (
                key_terms_part.reshape(row_total, images, -1),
                value_terms.reshape(row_total, images, -1),
            ),
            2,
        ).astype(jnp.bfloat16),
        SEQ,
        scatter_dimension=0,
        tiled=True,
    ).astype(jnp.float32)
    grad_keys = jnp.swapaxes(summed[:, :, 0], 0, 1)
    grad_values = jnp.swapaxes(summed[:, :, 1], 0, 1)
    grad_projected = jnp.concatenate(
        (
            grad_queries.reshape(images, tok_rows, channels),
            grad_keys.astype(jnp.bfloat16),
            grad_values.astype(jnp.bfloat16),
        ),
        axis=2,
    ).reshape(tokens, 3 * channels)
    grad_joined_self = grad_dot(normed_self, grad_projected)
    unused, pull_norm = jax.vjp(layer_norm, stream_in, gain_self)
    grad_part, grad_gain_self = pull_norm(back_dot(grad_projected, joined_self))
    grad_stream = grad_stream + grad_part
    grad_stream_low = grad_stream.astype(jnp.bfloat16)
    grad_project_in = grad_dot(normed_block, grad_stream_low)
    grad_block = back_dot(grad_stream_low, project_in).reshape(
        images, row_count, col_count, channels
    )
    grad_resid_part, grad_gain_block = norm_backward(
        block_piece,
        resid,
        gain_block,
        first_block,
        second_block,
        grad_block,
        row_mask,
        spread_fn,
        pick_fn,
    )
    grad_resid = grad_output + grad_resid_part
    grad_second_low = grad_resid.astype(jnp.bfloat16)
    grad_conv_second = conv_weight_grad(padded_mid, grad_second_low)
    grad_act_mid = conv_rows(grads_halo(grad_second_low), flipped(conv_second))
    grad_mid, grad_gain_mid = norm_backward(
        res_piece,
        mid_in,
        gain_mid,
        first_mid,
        second_mid,
        grad_act_mid,
        row_mask,
        spread_fn,
        pick_fn,
    )
    grad_time = jnp.sum(grad_mid, axis=(1, 2))
    grad_time_weight = exact_grad_dot(time_act.astype(jnp.float32), grad_time)
    grad_first_low = grad_mid.astype(jnp.bfloat16)
    grad_conv_first = conv_weight_grad(padded_in, grad_first_low)
    grad_act_in = conv_rows(grads_halo(grad_first_low), flipped(conv_first))
    grad_in_part, grad_gain_in = norm_backward(
        res_piece, latents, gain_in, first_in, second_in, grad_act_in, row_mask, spread_fn, pick_fn
    )
    latent_grad = grad_resid + grad_in_part
    shares = (
        lax.psum_scatter(
            grad_gain_in.reshape(1, -1).astype(jnp.bfloat16), SEQ, scatter_dimension=1, tiled=True
        ).astype(jnp.float32),
        lax.psum_scatter(
            grad_conv_first.reshape(-1, channels).astype(jnp.bfloat16),
            SEQ,
            scatter_dimension=1,
            tiled=True,
        ).astype(jnp.float32),
        lax.psum_scatter(
            grad_time_weight.astype(jnp.bfloat16), SEQ, scatter_dimension=1, tiled=True
        ).astype(jnp.float32),
        lax.psum_scatter(
            grad_gain_mid.reshape(1, -1).astype(jnp.bfloat16),
            SEQ,
            scatter_dimension=1,
            tiled=True,
        ).astype(jnp.float32),
        lax.psum_scatter(
            grad_conv_second.reshape(-1, channels).astype(jnp.bfloat16),
            SEQ,
            scatter_dimension=1,
            tiled=True,
        ).astype(jnp.float32),
        lax.psum_scatter(
            grad_gain_block.reshape(1, -1).astype(jnp.bfloat16),
            SEQ,
            scatter_dimension=1,
            tiled=True,
        ).astype(jnp.float32),
        lax.psum_scatter(
            grad_project_in.astype(jnp.bfloat16), SEQ, scatter_dimension=1, tiled=True
        ).astype(jnp.float32),
        lax.psum_scatter(
            grad_gain_self.reshape(1, -1).astype(jnp.bfloat16),
            SEQ,
            scatter_dimension=1,
            tiled=True,
        ).astype(jnp.float32),
        lax.psum_scatter(
            grad_joined_self[:, :channels].astype(jnp.bfloat16),
            SEQ,
            scatter_dimension=1,
            tiled=True,
        ).astype(jnp.float32),
        lax.psum_scatter(
            grad_joined_self[:, channels : 2 * channels].astype(jnp.bfloat16),
            SEQ,
            scatter_dimension=1,
            tiled=True,
        ).astype(jnp.float32),
        lax.psum_scatter(
            grad_joined_self[:, 2 * channels :].astype(jnp.bfloat16),
            SEQ,
            scatter_dimension=1,
            tiled=True,
        ).astype(jnp.float32),
        lax.psum_scatter(
            grad_out_self.astype(jnp.bfloat16), SEQ, scatter_dimension=1, tiled=True
        ).astype(jnp.float32),
        lax.psum_scatter(
            grad_gain_cross.reshape(1, -1).astype(jnp.bfloat16),
            SEQ,
            scatter_dimension=1,
            tiled=True,
        ).astype(jnp.float32),
        lax.psum_scatter(
            grad_query_cross.astype(jnp.bfloat16), SEQ, scatter_dimension=1, tiled=True
        ).astype(jnp.float32),
        lax.psum_scatter(
            grad_key_cross.astype(jnp.bfloat16), SEQ, scatter_dimension=1, tiled=True
        ).astype(jnp.float32),
        lax.psum_scatter(
            grad_value_cross.astype(jnp.bfloat16), SEQ, scatter_dimension=1, tiled=True
        ).astype(jnp.float32),
        lax.psum_scatter(
            grad_out_cross.astype(jnp.bfloat16), SEQ, scatter_dimension=1, tiled=True
        ).astype(jnp.float32),
        lax.psum_scatter(
            grad_gain_feed.reshape(1, -1).astype(jnp.bfloat16),
            SEQ,
            scatter_dimension=1,
            tiled=True,
        ).astype(jnp.float32),
        lax.psum_scatter(
            grad_feed_up.astype(jnp.bfloat16), SEQ, scatter_dimension=1, tiled=True
        ).astype(jnp.float32),
        lax.psum_scatter(
            grad_feed_down.astype(jnp.bfloat16), SEQ, scatter_dimension=1, tiled=True
        ).astype(jnp.float32),
        lax.psum_scatter(
            grad_project_out.astype(jnp.bfloat16), SEQ, scatter_dimension=1, tiled=True
        ).astype(jnp.float32),
    )
    totals = (
        lax.psum(shares[0].astype(jnp.bfloat16), BATCH).astype(jnp.float32),
        lax.psum(shares[1].astype(jnp.bfloat16), BATCH).astype(jnp.float32),
        lax.psum(shares[2].astype(jnp.bfloat16), BATCH).astype(jnp.float32),
        lax.psum(shares[3].astype(jnp.bfloat16), BATCH).astype(jnp.float32),
        lax.psum(shares[4].astype(jnp.bfloat16), BATCH).astype(jnp.float32),
        lax.psum(shares[5].astype(jnp.bfloat16), BATCH).astype(jnp.float32),
        lax.psum(shares[6].astype(jnp.bfloat16), BATCH).astype(jnp.float32),
        lax.psum(shares[7].astype(jnp.bfloat16), BATCH).astype(jnp.float32),
        lax.psum(shares[8].astype(jnp.bfloat16), BATCH).astype(jnp.float32),
        lax.psum(shares[9].astype(jnp.bfloat16), BATCH).astype(jnp.float32),
        lax.psum(shares[10].astype(jnp.bfloat16), BATCH).astype(jnp.float32),
        lax.psum(shares[11].astype(jnp.bfloat16), BATCH).astype(jnp.float32),
        lax.psum(shares[12].astype(jnp.bfloat16), BATCH).astype(jnp.float32),
        lax.psum(shares[13].astype(jnp.bfloat16), BATCH).astype(jnp.float32),
        lax.psum(shares[14].astype(jnp.bfloat16), BATCH).astype(jnp.float32),
        lax.psum(shares[15].astype(jnp.bfloat16), BATCH).astype(jnp.float32),
        lax.psum(shares[16].astype(jnp.bfloat16), BATCH).astype(jnp.float32),
        lax.psum(shares[17].astype(jnp.bfloat16), BATCH).astype(jnp.float32),
        lax.psum(shares[18].astype(jnp.bfloat16), BATCH).astype(jnp.float32),
        lax.psum(shares[19].astype(jnp.bfloat16), BATCH).astype(jnp.float32),
        lax.psum(shares[20].astype(jnp.bfloat16), BATCH).astype(jnp.float32),
    )
    return (
        output,
        latent_grad,
        totals[0].reshape(-1),
        totals[1].reshape(3, 3, channels, -1),
        totals[2],
        totals[3].reshape(-1),
        totals[4].reshape(3, 3, channels, -1),
        totals[5].reshape(-1),
        totals[6],
        totals[7].reshape(-1),
        totals[8],
        totals[9],
        totals[10],
        totals[11],
        totals[12].reshape(-1),
        totals[13],
        totals[14],
        totals[15],
        totals[16],
        totals[17].reshape(-1),
        totals[18],
        totals[19],
        totals[20],
    )


def solution(mesh):
    in_specs = (
        P(BATCH, SEQ, None, None),
        P(BATCH),
        P(BATCH, None),
        P(BATCH, None, None),
        P(),
        P(),
        P(),
        P(),
        P(),
        P(),
        P(),
        P(),
        P(),
        P(),
        P(),
        P(),
        P(),
        P(),
        P(),
        P(),
        P(),
        P(),
        P(),
        P(),
        P(),
        P(BATCH, SEQ, None, None),
    )
    out_specs = (
        P(BATCH, SEQ, None, None),
        P(BATCH, SEQ, None, None),
        P(SEQ),
        P(None, None, None, SEQ),
        P(None, SEQ),
        P(SEQ),
        P(None, None, None, SEQ),
        P(SEQ),
        P(None, SEQ),
        P(SEQ),
        P(None, SEQ),
        P(None, SEQ),
        P(None, SEQ),
        P(None, SEQ),
        P(SEQ),
        P(None, SEQ),
        P(None, SEQ),
        P(None, SEQ),
        P(None, SEQ),
        P(SEQ),
        P(None, SEQ),
        P(None, SEQ),
        P(None, SEQ),
    )
    device_fn = fast_device if mesh.shape[SEQ] == HEADS and mesh.shape[BATCH] == 4 else on_device
    return jax.shard_map(
        device_fn, mesh=mesh, in_specs=in_specs, out_specs=out_specs, check_vma=False
    )
```
